32 devices in a mesh: seq: 4 (over z), dp: 8 (over y, x, core).
Axes of the slice: x: 2, y: 2, z: 4, core: 2. Of those that a mesh axis runs over, the one named last changes fastest.
Arguments:
- block_input: bfloat16 [8, 2048, 1536], P('dp', 'seq'), may hold values from -6 to 6
- document_number: int32 [8, 2048], P('dp', 'seq'), may hold values from 0 to 3, never falling along the last dimension, each value on 1 to 1024 neighbouring positions
- key_present: int32 [8, 2048], P('dp', 'seq'), may hold values 0 or 1
- routes: int32 [8, 2048, 6], P('dp', 'seq'), may hold values from 0 to 15, all different within a row; in each aligned block of 512 rows (0 to 511, 512 to 1023, ..., all dimensions but the last counted through in order) at most 256 rows name the same one
- sequence_adapter: int32 [8], P('dp'), may hold values from 0 to 7
- output_gradient: bfloat16 [8, 2048, 1536], P('dp', 'seq'), may hold values from -6 to 6
- norm_scale_pair: bfloat16 [2, 1536], P(None, ('seq', 'dp')), may hold values from 0.5 to 1.5
- query_key_value_weight: bfloat16 [1536, 2560], P(('seq', 'dp')), may hold values from -0.15625 to 0.15625
- attention_output_weight: bfloat16 [1536, 1536], P(('seq', 'dp')), may hold values from -0.625 to 0.625
- router_weight: bfloat16 [1536, 16], P(('seq', 'dp')), may hold values from -0.078125 to 0.078125
- shared_gate_up_weight: bfloat16 [1536, 2, 1024], P(('seq', 'dp')), may hold values from -0.15625 to 0.15625
- shared_down_weight: bfloat16 [1024, 1536], P(('seq', 'dp')), may hold values from -0.375 to 0.375
- routed_gate_up_weight: bfloat16 [16, 1536, 2, 512], P('dp', 'seq'), may hold values from -0.15625 to 0.15625
- routed_down_weight: bfloat16 [16, 512, 1536], P('dp', 'seq'), may hold values from -1 to 1
- dense_first_factor: bfloat16 [1536, 6, 128], P(('seq', 'dp')), may hold values from -0.15625 to 0.15625
- shared_down_first_factor: bfloat16 [1024, 128], P(('seq', 'dp')), may hold values from -0.1875 to 0.1875
- dense_second_factor: bfloat16 [128, 7680], P(None, ('seq', 'dp')), may hold values from -0.75 to 0.75
- routed_first_factor: bfloat16 [16, 1536, 2, 128], P('dp', 'seq'), may hold values from -0.15625 to 0.15625
- routed_down_first_factor: bfloat16 [16, 512, 128], P('dp', 'seq'), may hold values from -0.25 to 0.25
- routed_second_factor: bfloat16 [16, 128, 2560], P('dp', None, 'seq'), may hold values from -0.75 to 0.75
Outputs:
- hidden_out: bfloat16 [8, 2048, 1536], P('dp', 'seq')
- grad_hidden: float32 [8, 2048, 1536], P('dp', 'seq')
- gradient_first_factor: float32 [1536, 6, 128], P(('seq', 'dp'))
- gradient_shared_down_factor: float32 [1024, 128], P(('seq', 'dp'))
- gradient_second_factor: float32 [128, 7680], P(None, ('seq', 'dp'))
- grad_expert_lora_a: float32 [16, 1536, 2, 128], P('dp', 'seq')
- grad_expert_lora_a_down: float32 [16, 512, 128], P('dp', 'seq')
- grad_expert_lora_b: float32 [16, 128, 2560], P('dp', None, 'seq')
The draws below stay inside these ranges and needn't reach their ends.
Inputs may be any that keep to these rules, and one draw needn't show every extreme that they name: `routes`: in each aligned block of 512 positions of a sequence, every expert is named by at most 256 tokens; each token names 6 different experts. `document_number`: never falling along a sequence; a document spans at most 1024 positions.
All inputs are finite; a program needn't handle non-finite values. No bound on the sum of `key_present` on one device may be relied on, other than what follows from the above.
Results may differ from the reference program's by a relative error of at most 0.022.
Values may be sent and summed in bfloat16 or wider, within the bound.
No kernel may reach another device: no remote copies, remote signals or barrier semaphores. Data moves between devices by JAX's collectives and lax.ppermute only.
A program may use at most 384 MiB of HBM per device.

```python
import math
import jax
import jax.numpy as jnp
import numpy as np
from jax import lax

MODEL_WIDTH = 1536
HEADS = 12
KV_HEADS = 4
HEAD_DIM = 128
EXPERT_HIDDEN = 512
SHARED_HIDDEN = 1024
TOPK = 6
NADAPT = 8
ADAPTER_RANK = 16
LENGTH = 2048
SEQUENCES = 8
BLK = 512
ROUTED_EXPERTS = 16
CAP = 256
ADAPTER_COLUMNS = 128
QKV = 2560
DENSE_COLUMNS = 7680
EXPERT_COLUMNS = 2560
N_SEQ = 4


def with_ends(entries, own_key, low, largest):
    longest = entries.shape.index(max(entries.shape))
    spots = []
    for shift in (0, 1):
        where = [jax.random.randint(jax.random.fold_in(own_key, axis), (), 0, length) for axis, length in enumerate(entries.shape)]
        where[longest] = (where[longest] + shift) % entries.shape[longest]
        spots.append(tuple(where))
    return entries.at[spots[0]].set(low).at[spots[1]].set(largest)


def block_levels(rng, shape, cuts, smallest, high):
    loudness = 1.0
    for position, parts in cuts:
        draws = jax.random.uniform(jax.random.fold_in(jax.random.fold_in(rng, 6), position), (parts,), jnp.float32, smallest / len(cuts), high / len(cuts))
        loudness = loudness * jnp.repeat(jnp.exp(draws), shape[position] // parts).reshape((-1,) + (1,) * (len(shape) - 1 - position))
    return loudness


def length_profile(amount, total, bound, skew):
    portions = [(1 << 20) // math.isqrt(grade ** skew) + 1 for grade in range(2, amount + 1)]
    spare, given = total - bound - (amount - 1), [1] * (amount - 1)
    while spare > 0:
        movable = [i for i in range(amount - 1) if given[i] < bound]
        mass, left = sum([portions[i] for i in movable]), spare
        for i in movable:
            extra = min(bound - given[i], max(1, left * portions[i] // mass), spare)
            given[i] = given[i] + extra
            spare = spare - extra
    return np.array([bound] + given)


def uneven(rng, count, total, reach, slope):
    if count == 2:
        one = jax.random.randint(rng, (), max(1, total - reach), min(reach, total - 1) + 1)
        return jnp.stack([one, total - one])
    sizes = jnp.asarray(length_profile(count, total, reach, slope), jnp.int32)
    couples = (count - 1) // 2
    source_of, sink = sizes[1:1 + 2 * couples:2], sizes[2:2 + 2 * couples:2]
    slack = jnp.minimum(source_of - 1, reach - sink)
    shifted = jax.random.randint(jax.random.fold_in(rng, 1), (couples,), 0, 1 << 20) % (slack + 1)
    sizes = sizes.at[1:1 + 2 * couples:2].set(source_of - shifted).at[2:2 + 2 * couples:2].set(sink + shifted)
    return sizes[jax.random.permutation(jax.random.fold_in(rng, 2), count)]


def deal_out(own_key, own, number, rows, number_of, top, limit, skew):
    sequence = jax.random.permutation(own_key, number_of)
    packed, common = load_shares(number_of, rows * top, limit, skew, True), load_shares(number_of, rows * top, limit, skew, False)
    places = jnp.arange(number_of)

    def named(sizes, offset_by):
        used = int((sizes > 0).sum())
        fixed = max(1, used // 4)
        moved = fixed + (places - fixed + offset_by * (used - fixed)) % max(1, number_of - fixed)
        return jnp.zeros((number_of,), jnp.int32).at[sequence[jnp.where(places < fixed, places, moved)]].set(jnp.asarray(sizes, jnp.int32))

    sizes = jnp.where(number % 4 == 0, named(packed, number // 4), named(common, number - number // 4 - 1))
    mixed = jax.random.permutation(jax.random.fold_in(own, 3), number_of)
    donor, sink = mixed[0:number_of // 2 * 2:2], mixed[1:number_of // 2 * 2:2]
    margin = jnp.minimum(sizes[donor] - 1, limit - sizes[sink]) // 2
    margin = jnp.where((donor == sequence[0]) | (sink == sequence[0]) | (sizes[sink] == 0), 0, jnp.maximum(margin, 0))
    moved = jax.random.randint(jax.random.fold_in(own, 4), (number_of // 2,), 0, 1 << 20) % (margin + 1)
    sizes = sizes.at[donor].add(-moved).at[sink].add(moved)
    labels = jnp.searchsorted(jnp.cumsum(sizes), jnp.arange(rows * top), side="right").astype(jnp.int32)
    table = labels.reshape(top, rows).T
    table = table[jax.random.permutation(jax.random.fold_in(own, 1), rows)]
    offset_by = jax.random.randint(jax.random.fold_in(own, 2), (rows, 1), 0, top)
    return jnp.take_along_axis(table, (jnp.arange(top)[None, :] + offset_by) % top, axis=1)


def load_shares(amount, total, bound, lean, full):
    loads = [(1 << 20) // math.isqrt(grade ** lean) + 1 for grade in range(1, amount + 1)]
    largest = bound if full else min(bound, max(-(-total // amount), total * loads[0] // sum(loads)))
    least = 1 if total - largest >= amount - 1 else 0
    holding, rest = [largest] + [least] * (amount - 1), total - largest - least * (amount - 1)
    while rest > 0:
        movable = [i for i in range(1, amount) if holding[i] < largest] or [i for i in range(1, amount) if holding[i] < bound]
        pool, remaining = sum([loads[i] for i in movable]), rest
        for i in movable:
            addition = min(bound - holding[i], max(1, remaining * loads[i] // pool), rest)
            holding[i] = holding[i] + addition
            rest = rest - addition
    return np.array(holding)


def gaussian(key, dims, scale, most, split=(), kind=jnp.bfloat16):
    array = jax.random.normal(key, dims, jnp.float32) * scale
    if len(split) > 0:
        array = block_levels(key, dims, split, -0.22, 0.18) * array
    return jnp.clip(array, min=-most, max=most).astype(kind)


def setup_inputs(seed: int = 0) -> dict:
    key_of = jax.random.split(jax.random.key(seed), 21)
    block_input = gaussian(key_of[0], (SEQUENCES, LENGTH, MODEL_WIDTH), 1.0, 6.0, ((0, 8), (1, 4)))
    document_number = jax.vmap(lambda own: jnp.searchsorted(jnp.cumsum(uneven(own, 4, LENGTH, LENGTH // 2, 0)), jnp.arange(LENGTH), side="right"))(jax.random.split(key_of[1], SEQUENCES)).reshape((SEQUENCES, LENGTH)).astype(jnp.int32)
    key_present = with_ends((jax.random.randint(key_of[2], (SEQUENCES, LENGTH), 0, 8) < 7).astype(jnp.int32), jax.random.fold_in(key_of[2], 1), 0, 1)
    routes_keys = jax.random.split(jax.random.fold_in(key_of[3], 1), SEQUENCES * LENGTH // BLK)
    routes_turns = jax.random.permutation(jax.random.fold_in(key_of[3], 3), SEQUENCES * LENGTH // BLK)
    routes = jax.vmap(lambda own, number: deal_out(jax.random.fold_in(key_of[3], 2), own, number, BLK, ROUTED_EXPERTS, TOPK, CAP, 1))(routes_keys, routes_turns).reshape((SEQUENCES, LENGTH, TOPK))
    sequence_adapter = with_ends(jax.random.randint(key_of[4], (SEQUENCES,), 0, NADAPT), jax.random.fold_in(key_of[4], 1), 0, NADAPT - 1).astype(jnp.int32)
    output_gradient = gaussian(key_of[5], (SEQUENCES, LENGTH, MODEL_WIDTH), 1.0, 6.0, ((0, 8), (1, 4)))
    norm_scale_pair = jnp.clip(1.0 + 0.1 * jax.random.normal(key_of[6], (2, MODEL_WIDTH), jnp.float32), 0.5, 1.5).astype(jnp.bfloat16)
    query_key_value_weight = gaussian(key_of[7], (MODEL_WIDTH, QKV), MODEL_WIDTH ** -0.5, 0.15625, ((0, 32),))
    attention_output_weight = gaussian(key_of[8], (MODEL_WIDTH, MODEL_WIDTH), (MODEL_WIDTH // 16) ** -0.5, 0.625, ((0, 32),))
    router_weight = gaussian(key_of[9], (MODEL_WIDTH, ROUTED_EXPERTS), (4 * MODEL_WIDTH) ** -0.5, 0.078125, ((0, 32),))
    shared_gate_up_weight = gaussian(key_of[10], (MODEL_WIDTH, 2, SHARED_HIDDEN), MODEL_WIDTH ** -0.5, 0.15625, ((0, 32),))
    shared_down_weight = gaussian(key_of[11], (SHARED_HIDDEN, MODEL_WIDTH), (SHARED_HIDDEN // 4) ** -0.5, 0.375, ((0, 32),))
    routed_gate_up_weight = gaussian(key_of[12], (ROUTED_EXPERTS, MODEL_WIDTH, 2, EXPERT_HIDDEN), MODEL_WIDTH ** -0.5, 0.15625, ((0, 8), (1, 4)))
    routed_down_weight = gaussian(key_of[13], (ROUTED_EXPERTS, EXPERT_HIDDEN, MODEL_WIDTH), (EXPERT_HIDDEN // 16) ** -0.5, 1.0, ((0, 8), (1, 4)))
    dense_first_factor = gaussian(key_of[14], (MODEL_WIDTH, 6, ADAPTER_COLUMNS), MODEL_WIDTH ** -0.5, 0.15625, ((0, 32),))
    shared_down_first_factor = gaussian(key_of[15], (SHARED_HIDDEN, ADAPTER_COLUMNS), SHARED_HIDDEN ** -0.5, 0.1875, ((0, 32),))
    dense_second_factor = gaussian(key_of[16], (ADAPTER_COLUMNS, DENSE_COLUMNS), (4 * ADAPTER_RANK) ** -0.5, 0.75, ((1, 32),))
    routed_first_factor = gaussian(key_of[17], (ROUTED_EXPERTS, MODEL_WIDTH, 2, ADAPTER_COLUMNS), MODEL_WIDTH ** -0.5, 0.15625, ((0, 8), (1, 4)))
    routed_down_first_factor = gaussian(key_of[18], (ROUTED_EXPERTS, EXPERT_HIDDEN, ADAPTER_COLUMNS), EXPERT_HIDDEN ** -0.5, 0.25, ((0, 8), (1, 4)))
    routed_second_factor = gaussian(key_of[19], (ROUTED_EXPERTS, ADAPTER_COLUMNS, EXPERT_COLUMNS), (4 * ADAPTER_RANK) ** -0.5, 0.75, ((0, 8), (2, 4)))
    return dict(block_input=block_input, document_number=document_number, key_present=key_present, routes=routes, sequence_adapter=sequence_adapter, output_gradient=output_gradient, norm_scale_pair=norm_scale_pair, query_key_value_weight=query_key_value_weight, attention_output_weight=attention_output_weight, router_weight=router_weight, shared_gate_up_weight=shared_gate_up_weight, shared_down_weight=shared_down_weight, routed_gate_up_weight=routed_gate_up_weight, routed_down_weight=routed_down_weight, dense_first_factor=dense_first_factor, shared_down_first_factor=shared_down_first_factor, dense_second_factor=dense_second_factor, routed_first_factor=routed_first_factor, routed_down_first_factor=routed_down_first_factor, routed_second_factor=routed_second_factor)


EPSILON = 1e-05
HIGHEST = lax.Precision.HIGHEST

@jax.custom_vjp
def low(v):
    return lax.optimization_barrier(v.astype(jnp.bfloat16)).astype(jnp.float32)

@jax.custom_vjp
def low_back(v):
    return v

def low_keep(v):
    return (low(v), None)

def low_pass(kept, grad):
    return (grad,)

def back_keep(v):
    return (v, None)

def back_low(kept, grad):
    return (low(grad),)
low.defvjp(low_keep, low_pass)
low_back.defvjp(back_keep, back_low)

def both_ways(values):
    return low_back(low(values))

def matmul(left, right):
    return jnp.dot(left, right, precision=HIGHEST)

def rms_norm(values, gain):
    return values * lax.rsqrt(lax.optimization_barrier(jnp.mean(values * values, axis=-1, keepdims=True)) + EPSILON) * gain

def swiglu(gate_up):
    half_width = gate_up.shape[-1] // 2
    return jax.nn.silu(gate_up[:, :half_width]) * gate_up[:, half_width:]

def split_columns(matrix, widths):
    parts_list = []
    offset = 0
    for span_width in widths:
        parts_list.append(matrix[:, offset:offset + span_width])
        offset += span_width
    return parts_list

def adapter(inputs, a_cols, b_parts, select):
    group_count, rank_width = (a_cols.shape[1], a_cols.shape[2])
    low_rank = matmul(inputs, a_cols.reshape(a_cols.shape[0], group_count * rank_width))
    low_rank = both_ways(low_rank.reshape(inputs.shape[0], group_count, rank_width) * select)
    return jnp.concatenate([matmul(low_rank[:, g], b_parts[g]) for g in range(group_count)], axis=1)

def expert_apply(inputs, gate_up_w, down_w, first_gu, first_down, second, select):
    gate_up = low_back(matmul(inputs, gate_up_w.reshape(MODEL_WIDTH, 2 * EXPERT_HIDDEN)) + adapter(inputs, first_gu, [second[:, :EXPERT_HIDDEN], second[:, EXPERT_HIDDEN:2 * EXPERT_HIDDEN]], select))
    hidden = low(swiglu(gate_up))
    return matmul(hidden, down_w) + adapter(hidden, first_down[:, None], [second[:, 2 * EXPERT_HIDDEN:]], select)

def sequence_forward(tokens, segs, valid, rts, adapter_id, frozen, learned_params):
    gains, qkv_w, out_w, router_w, sgu_w, sdown_w, egu_w, edown_w = frozen
    first_a, first_down, second_b, expert_a, expert_a_down, expert_b = learned_params
    length = tokens.shape[0]
    query_width = HEADS * HEAD_DIM
    kv_width = KV_HEADS * HEAD_DIM
    groups = HEADS // KV_HEADS
    b_parts = split_columns(second_b, [query_width, kv_width, kv_width, MODEL_WIDTH, SHARED_HIDDEN, SHARED_HIDDEN, MODEL_WIDTH])
    select = (jnp.arange(NADAPT * ADAPTER_RANK, dtype=jnp.int32) // ADAPTER_RANK == adapter_id).astype(jnp.float32)
    normed = low(rms_norm(tokens, gains[0]))
    qkv = both_ways(matmul(normed, qkv_w) + adapter(normed, first_a[:, 0:3], b_parts[0:3], select))
    query = qkv[:, :query_width].reshape(length, KV_HEADS, groups, HEAD_DIM)
    keys = qkv[:, query_width:query_width + kv_width].reshape(length, KV_HEADS, HEAD_DIM)
    values = qkv[:, query_width + kv_width:].reshape(length, KV_HEADS, HEAD_DIM)
    qblock = math.gcd(length, 512)
    key_pos = jnp.arange(length, dtype=jnp.int32)

    def attend(start):
        query_part = lax.dynamic_slice_in_dim(query, start, qblock, 0)
        scores = low_back(jnp.einsum('qkgd,pkd->kgqp', query_part, keys, precision=HIGHEST) * HEAD_DIM ** (-0.5))
        query_pos = start + jnp.arange(qblock, dtype=jnp.int32)
        seg_part = lax.dynamic_slice_in_dim(segs, start, qblock, 0)
        permit = (key_pos[None, :] <= query_pos[:, None]) & (segs[None, :] == seg_part[:, None])
        permit = permit & ((valid[None, :] == 1) | (key_pos[None, :] == query_pos[:, None]))
        scores = jnp.where(permit[None, None], scores, -jnp.inf)
        probs = jax.nn.softmax(scores, axis=-1)
        return jnp.einsum('kgqp,pkd->qkgd', low(probs), values, precision=HIGHEST)
    starts = jnp.arange(length // qblock, dtype=jnp.int32) * qblock
    attn = both_ways(lax.map(jax.checkpoint(attend), starts).reshape(length, query_width))
    y_attn = low_back(matmul(attn, out_w) + adapter(attn, first_a[:, 3:4], b_parts[3:4], select))
    mid = tokens + y_attn
    normed2 = low(rms_norm(mid, gains[1]))
    logits = matmul(normed2, router_w)
    chosen = jnp.take_along_axis(logits, rts, axis=1)
    gates = jax.nn.softmax(chosen, axis=-1)
    shared_gu = low_back(matmul(normed2, sgu_w.reshape(MODEL_WIDTH, 2 * SHARED_HIDDEN)) + adapter(normed2, first_a[:, 4:6], b_parts[4:6], select))
    shared_hidden = low(swiglu(shared_gu))
    y_shared = low_back(matmul(shared_hidden, sdown_w) + adapter(shared_hidden, first_down[:, None], b_parts[6:7], select))
    experts = router_w.shape[1]
    room = CAP * N_SEQ
    hits = (rts[:, :, None] == jnp.arange(experts, dtype=jnp.int32)).astype(jnp.int32)
    flags = lax.optimization_barrier(jnp.sum(hits, axis=1))
    ranks = jnp.cumsum(flags, axis=0) - flags
    slot_ids = lax.optimization_barrier(jnp.sum(hits * ranks[:, None, :], axis=2))
    dest = (rts * room + slot_ids).astype(jnp.int32)
    token_ids = jnp.broadcast_to(jnp.arange(length, dtype=jnp.int32)[:, None], dest.shape)
    table = jnp.full((experts * room,), length, dtype=jnp.int32).at[dest.reshape(-1)].set(token_ids.reshape(-1))
    padded = jnp.concatenate([normed2, jnp.zeros((1, MODEL_WIDTH), normed2.dtype)], axis=0)
    routed = low_back(padded[table].reshape(experts, room, MODEL_WIDTH))
    expert_out = jax.vmap(expert_apply, in_axes=(0, 0, 0, 0, 0, 0, None))(routed, egu_w, edown_w, expert_a, expert_a_down, expert_b, select)
    taken = both_ways(expert_out).reshape(experts * room, MODEL_WIDTH)[dest]
    moe = lax.optimization_barrier(jnp.sum(gates[:, :, None] * taken, axis=1))
    return mid + moe + y_shared

def reference(block_input, document_number, key_present, routes, sequence_adapter, output_gradient, norm_scale_pair, query_key_value_weight, attention_output_weight, router_weight, shared_gate_up_weight, shared_down_weight, routed_gate_up_weight, routed_down_weight, dense_first_factor, shared_down_first_factor, dense_second_factor, routed_first_factor, routed_down_first_factor, routed_second_factor):
    frozen = tuple((route_weight.astype(jnp.float32) for route_weight in (norm_scale_pair, query_key_value_weight, attention_output_weight, router_weight, shared_gate_up_weight, shared_down_weight, routed_gate_up_weight, routed_down_weight)))
    learned_params = tuple((route_weight.astype(jnp.float32) for route_weight in (dense_first_factor, shared_down_first_factor, dense_second_factor, routed_first_factor, routed_down_first_factor, routed_second_factor)))

    def forward(inputs, adapters):

        def one_sequence(item):
            return sequence_forward(item[0], item[1], item[2], item[3], item[4], frozen, adapters)
        return lax.map(jax.checkpoint(one_sequence), (inputs, document_number, key_present, routes, sequence_adapter))
    result, pull = jax.vjp(forward, block_input.astype(jnp.float32), learned_params)
    grad_in, grads = pull(output_gradient.astype(jnp.float32))
    return (result.astype(jnp.bfloat16), grad_in, grads[0], grads[1], grads[2], grads[3], grads[4], grads[5])
```

```python
import functools
import math

import jax
import jax.numpy as jnp
from jax import lax
from jax.experimental import pallas as pl
from jax.experimental.pallas import tpu as pltpu
from jax.sharding import PartitionSpec as P

HEADS = 12
KV_HEADS = 4
HEAD_DIM = 128
EXPERT_HIDDEN = 512
SHARED_HIDDEN = 1024
ADAPTER_RANK = 16
DOCUMENT_SPAN = 1024

EPSILON = 1e-05
MASKED_SCORE = -1e30
LOG2E = 1.4426950408889634
SCALE = HEAD_DIM ** (-0.5)
LANES = 128
VMEM_LIMIT = 60 * 1024 * 1024

F32 = jnp.float32
BF16 = jnp.bfloat16


def dot_nn(left, right):
    return jnp.dot(left, right, preferred_element_type=F32)


def dot_tn(left, right):
    return lax.dot_general(left, right, (((0,), (0,)), ((), ())), preferred_element_type=F32)


def dot_nt(left, right):
    return lax.dot_general(left, right, (((1,), (1,)), ((), ())), preferred_element_type=F32)


def rms_norm(values, gain):
    return values * lax.rsqrt(jnp.mean(values * values, axis=-1, keepdims=True) + EPSILON) * gain


def swiglu(gate_up):
    half_width = gate_up.shape[-1] // 2
    return jax.nn.silu(gate_up[:, :half_width]) * gate_up[:, half_width:]


def query_tiles(rows, hops):
    tile = math.gcd(rows, 256)
    spans = []
    for first in range(0, rows, tile):
        oldest = max(0, hops * rows + first - (DOCUMENT_SPAN - 1)) // tile * tile
        spans.append((first, tile, oldest, hops * rows + first + tile - oldest))
    return spans


def fill_bias(spans, shift, query_tag, key_tag, bias):
    for first, tile, oldest, span in spans:
        keys = oldest + lax.broadcasted_iota(jnp.int32, (span, tile), 0)
        queries = shift + first + lax.broadcasted_iota(jnp.int32, (span, tile), 1)
        same = key_tag[oldest : oldest + span, :] == query_tag[:, first : first + tile]
        permit = (keys <= queries) & (same | (keys == queries))
        bias[oldest : oldest + span, first : first + tile] = jnp.where(permit, 0.0, MASKED_SCORE)


def attend_kernel(spans, shift, q_ref, k_ref, v_ref, qt_ref, kt_ref, out_ref, lse_ref, bias):
    @pl.when(pl.program_id(0) == 0)
    def _():
        fill_bias(spans, shift, qt_ref, kt_ref, bias)

    groups = q_ref.shape[1] // HEAD_DIM
    for first, tile, oldest, span in spans:
        keys = k_ref[oldest : oldest + span, :]
        values = v_ref[oldest : oldest + span, :]
        mask = bias[oldest : oldest + span, first : first + tile]
        for h in range(groups):
            columns = slice(h * HEAD_DIM, (h + 1) * HEAD_DIM)
            scores = dot_nt(keys, q_ref[first : first + tile, columns]) * (SCALE * LOG2E) + mask
            top = jnp.max(scores, axis=0, keepdims=True)
            weights = jnp.exp2(scores - top)
            total = jnp.sum(weights, axis=0, keepdims=True)
            mixed = dot_tn(values, weights.astype(BF16)) / total
            out_ref[first : first + tile, columns] = mixed.T.astype(BF16)
            lse_ref[0, h : h + 1, first : first + tile] = top + jnp.log2(total)


def attend(qkv, kv_all, query_tag, key_tag, hops):
    rows = qkv.shape[0]
    groups = HEADS // KV_HEADS
    span = kv_all.shape[0]
    spans = query_tiles(rows, hops)
    return pl.pallas_call(
        functools.partial(attend_kernel, spans, hops * rows),
        grid=(KV_HEADS,),
        in_specs=[
            pl.BlockSpec((rows, groups * HEAD_DIM), lambda g: (0, g)),
            pl.BlockSpec((span, HEAD_DIM), lambda g: (0, g)),
            pl.BlockSpec((span, HEAD_DIM), lambda g: (0, KV_HEADS + g)),
            pl.BlockSpec((1, rows), lambda g: (0, 0)),
            pl.BlockSpec((span, 1), lambda g: (0, 0)),
        ],
        out_specs=[
            pl.BlockSpec((rows, groups * HEAD_DIM), lambda g: (0, g)),
            pl.BlockSpec((1, groups, rows), lambda g: (g, 0, 0)),
        ],
        out_shape=[
            jax.ShapeDtypeStruct((rows, HEADS * HEAD_DIM), BF16),
            jax.ShapeDtypeStruct((KV_HEADS, groups, rows), F32),
        ],
        scratch_shapes=[pltpu.VMEM((span, rows), F32)],
        compiler_params=pltpu.CompilerParams(vmem_limit_bytes=VMEM_LIMIT),
        cost_estimate=pl.CostEstimate(
            flops=4 * HEADS * rows * span * HEAD_DIM, bytes_accessed=8 * rows * 1536, transcendentals=HEADS * rows * span
        ),
        name="attend",
    )(qkv, kv_all, kv_all, query_tag, key_tag)


def attend_back_kernel(
    spans, shift, q_ref, k_ref, v_ref, g_ref, lse_ref, qt_ref, kt_ref, dq_ref, dk_ref, dv_ref, bias, dk_acc, dv_acc
):
    @pl.when(pl.program_id(0) == 0)
    def _():
        fill_bias(spans, shift, qt_ref, kt_ref, bias)

    dk_acc[...] = jnp.zeros_like(dk_acc)
    dv_acc[...] = jnp.zeros_like(dv_acc)
    groups = q_ref.shape[1] // HEAD_DIM
    for first, tile, oldest, span in spans:
        keys = k_ref[oldest : oldest + span, :]
        values = v_ref[oldest : oldest + span, :]
        mask = bias[oldest : oldest + span, first : first + tile]
        for h in range(groups):
            columns = slice(h * HEAD_DIM, (h + 1) * HEAD_DIM)
            query = q_ref[first : first + tile, columns]
            grad = g_ref[first : first + tile, columns]
            lse = lse_ref[0, h : h + 1, first : first + tile]
            probs = jnp.exp2(dot_nt(keys, query) * (SCALE * LOG2E) + mask - lse)
            dv_acc[oldest : oldest + span, :] += dot_nn(probs.astype(BF16), grad)
            grad_probs = dot_nt(values, grad)
            delta = jnp.sum(probs * grad_probs, axis=0, keepdims=True)
            grad_scores = (probs * (grad_probs - delta)).astype(BF16)
            dk_acc[oldest : oldest + span, :] += dot_nn(grad_scores, query) * SCALE
            dq_ref[first : first + tile, columns] = (dot_tn(grad_scores, keys) * SCALE).astype(BF16)
    dk_ref[...] = dk_acc[...].astype(dk_ref.dtype)
    dv_ref[...] = dv_acc[...].astype(dv_ref.dtype)


def attend_back(qkv, kv_all, grad_attn, lse, query_tag, key_tag, hops):
    rows = qkv.shape[0]
    groups = HEADS // KV_HEADS
    span = kv_all.shape[0]
    spans = query_tiles(rows, hops)
    return pl.pallas_call(
        functools.partial(attend_back_kernel, spans, hops * rows),
        grid=(KV_HEADS,),
        in_specs=[
            pl.BlockSpec((rows, groups * HEAD_DIM), lambda g: (0, g)),
            pl.BlockSpec((span, HEAD_DIM), lambda g: (0, g)),
            pl.BlockSpec((span, HEAD_DIM), lambda g: (0, KV_HEADS + g)),
            pl.BlockSpec((rows, groups * HEAD_DIM), lambda g: (0, g)),
            pl.BlockSpec((1, groups, rows), lambda g: (g, 0, 0)),
            pl.BlockSpec((1, rows), lambda g: (0, 0)),
            pl.BlockSpec((span, 1), lambda g: (0, 0)),
        ],
        out_specs=[
            pl.BlockSpec((rows, groups * HEAD_DIM), lambda g: (0, g)),
            pl.BlockSpec((span, HEAD_DIM), lambda g: (0, g)),
            pl.BlockSpec((span, HEAD_DIM), lambda g: (0, g)),
        ],
        out_shape=[
            jax.ShapeDtypeStruct((rows, HEADS * HEAD_DIM), BF16),
            jax.ShapeDtypeStruct((span, KV_HEADS * HEAD_DIM), BF16),
            jax.ShapeDtypeStruct((span, KV_HEADS * HEAD_DIM), BF16),
        ],
        scratch_shapes=[
            pltpu.VMEM((span, rows), F32),
            pltpu.VMEM((span, HEAD_DIM), F32),
            pltpu.VMEM((span, HEAD_DIM), F32),
        ],
        compiler_params=pltpu.CompilerParams(vmem_limit_bytes=VMEM_LIMIT),
        cost_estimate=pl.CostEstimate(
            flops=10 * HEADS * rows * span * HEAD_DIM, bytes_accessed=16 * rows * 1536, transcendentals=HEADS * rows * span
        ),
        name="attend_back",
    )(qkv, kv_all, kv_all, grad_attn, lse, query_tag, key_tag)


def expert_kernel(count, experts, with_prior, *refs):
    meta, up_ref, down_ref, second_ref = refs[:4]
    refs = refs[4:]
    token_refs, refs = refs[:count], refs[count:]
    grad_refs, refs = refs[:count], refs[count:]
    prior_moe, prior_back = (), ()
    if with_prior:
        prior_moe, refs = refs[:count], refs[count:]
        prior_back, refs = refs[:count], refs[count:]
    moe_refs, refs = refs[:count], refs[count:]
    back_refs, refs = refs[:count], refs[count:]
    first_grad, down_grad, second_grad = refs[:3]
    tokens_buf, grad_buf, moe_buf, back_buf, in_sem, out_sem = refs[3:]

    step = pl.program_id(0)
    slot = lax.rem(step, 2)
    rows, wide = tokens_buf.shape[1:]
    model = wide - LANES
    hidden = EXPERT_HIDDEN
    capacity = rows // 2
    rank = LANES

    def incoming(k, to):
        pairs = [(token_refs[k], tokens_buf, 0), (grad_refs[k], grad_buf, 1)]
        if with_prior:
            pairs += [(prior_moe[k], moe_buf, 2), (prior_back[k], back_buf, 3)]
        return [pltpu.make_async_copy(src, dst.at[to], in_sem.at[to, n]) for src, dst, n in pairs]

    def outgoing(k, at):
        return [
            pltpu.make_async_copy(moe_buf.at[at], moe_refs[k], out_sem.at[at, 0]),
            pltpu.make_async_copy(back_buf.at[at], back_refs[k], out_sem.at[at, 1]),
        ]

    @pl.when(step == 0)
    def _():
        for copy in incoming(0, 0):
            copy.start()
        first_grad[...] = jnp.zeros_like(first_grad)
        down_grad[...] = jnp.zeros_like(down_grad)
        second_grad[...] = jnp.zeros_like(second_grad)

    for k in range(count):

        @pl.when(step == k)
        def _(k=k):
            for copy in incoming(k, k % 2):
                copy.wait()
            if k >= 1:
                for copy in outgoing(k - 1, (k - 1) % 2):
                    copy.wait()
            if k + 1 < count:
                for copy in incoming(k + 1, (k + 1) % 2):
                    copy.start()

    expert = meta[0]
    adapter = meta[1 + step]
    lane = lax.broadcasted_iota(jnp.int32, (1, LANES), 1)
    select = (lane // ADAPTER_RANK == adapter).astype(F32)
    select_two = jnp.concatenate([select, select], axis=1)

    extra = tokens_buf[slot, :, model:].astype(F32)
    slot_column = jnp.sum(jnp.where(lane == expert, extra, 0.0), axis=1, keepdims=True)
    extra_t = extra.T
    sub = lax.broadcasted_iota(jnp.int32, (LANES, 1), 0)
    slot_row = jnp.sum(jnp.where(sub == expert, extra_t, 0.0), axis=0, keepdims=True)
    place = (lax.broadcasted_iota(jnp.int32, (rows, capacity), 1).astype(F32) == slot_column).astype(F32).astype(BF16)
    pick = (lax.broadcasted_iota(jnp.int32, (capacity, rows), 0).astype(F32) == slot_row).astype(F32).astype(BF16)

    picked_extra = dot_nn(pick, tokens_buf[slot, :, model:])
    gate = jnp.sum(
        jnp.where((lane == experts + expert) | (lane == 2 * experts + expert), picked_extra, 0.0), axis=1, keepdims=True
    )
    inputs = dot_nn(pick, tokens_buf[slot, :, :model]).astype(BF16)
    low = (dot_nn(inputs, up_ref[:, 2 * hidden :]) * select_two).astype(BF16)
    gate_part = dot_nn(inputs, up_ref[:, :hidden]) + dot_nn(low[:, :rank], second_ref[:, :hidden])
    up_part = dot_nn(inputs, up_ref[:, hidden : 2 * hidden]) + dot_nn(low[:, rank:], second_ref[:, hidden : 2 * hidden])
    sigmoid = 1.0 / (1.0 + jnp.exp(-gate_part))
    silu = gate_part * sigmoid
    act = (silu * up_part).astype(BF16)
    low_down = (dot_nn(act, down_ref[:, model:]) * select).astype(BF16)
    output = (dot_nn(act, down_ref[:, :model]) + dot_nn(low_down, second_ref[:, 2 * hidden :])).astype(BF16).astype(F32)
    grad_rows = dot_nn(pick, grad_buf[slot])
    grad_gate = jnp.sum(output * grad_rows, axis=1, keepdims=True)
    moe = dot_nn(place, (gate * output).astype(BF16))
    if with_prior:
        moe = moe + moe_buf[slot].astype(F32)
    moe_buf[slot] = moe.astype(BF16)

    grad_y = (gate * grad_rows).astype(BF16)
    glow_down = (dot_nt(grad_y, second_ref[:, 2 * hidden :]) * select).astype(BF16)
    second_grad[:, 2 * hidden :] += dot_tn(low_down, grad_y)
    down_grad[...] += dot_tn(glow_down, act)
    grad_act = dot_nt(grad_y, down_ref[:, :model]) + dot_nt(glow_down, down_ref[:, model:])
    grad_up = (grad_act * silu).astype(BF16)
    grad_gp = (grad_act * up_part * (sigmoid * (1.0 + gate_part * (1.0 - sigmoid)))).astype(BF16)
    glow = jnp.concatenate(
        [
            dot_nt(grad_gp, second_ref[:, :hidden]) * select,
            dot_nt(grad_up, second_ref[:, hidden : 2 * hidden]) * select,
        ],
        axis=1,
    ).astype(BF16)
    second_grad[:, :hidden] += dot_tn(low[:, :rank], grad_gp)
    second_grad[:, hidden : 2 * hidden] += dot_tn(low[:, rank:], grad_up)
    first_grad[...] += dot_tn(glow, inputs)
    grad_in = (
        dot_nt(grad_gp, up_ref[:, :hidden])
        + dot_nt(grad_up, up_ref[:, hidden : 2 * hidden])
        + dot_nt(glow, up_ref[:, 2 * hidden :])
    ).astype(BF16)
    gate_hi = grad_gate.astype(BF16).astype(F32)
    gate_lo = grad_gate - gate_hi
    extra_out = (
        jnp.where(lane == expert, gate_hi, 0.0) + jnp.where(lane == experts + expert, gate_lo, 0.0)
    ).astype(BF16)
    back = dot_nn(place, grad_in)
    back_extra = dot_nn(place, extra_out)
    if with_prior:
        back = back + back_buf[slot, :, :model].astype(F32)
        back_extra = back_extra + back_buf[slot, :, model:].astype(F32)
    back_buf[slot, :, :model] = back.astype(BF16)
    back_buf[slot, :, model:] = back_extra.astype(BF16)

    for k in range(count):

        @pl.when(step == k)
        def _(k=k):
            for copy in outgoing(k, k % 2):
                copy.start()
            if k == count - 1:
                for copy in outgoing(k, k % 2):
                    copy.wait()


def expert_call(meta, up, down, second, tokens, grads, prior, experts):
    count = len(tokens)
    rows, wide = tokens[0].shape
    model = wide - LANES
    whole = lambda a: pl.BlockSpec(a.shape, lambda i: (0,) * a.ndim, pipeline_mode=pl.Buffered(1))
    anywhere = pl.BlockSpec(memory_space=pl.ANY)
    prior = [] if prior is None else list(prior[0]) + list(prior[1])
    moe_shape = jax.ShapeDtypeStruct((rows, model), BF16)
    back_shape = jax.ShapeDtypeStruct((rows, wide), BF16)
    grad_shapes = [
        jax.ShapeDtypeStruct((2 * LANES, model), F32),
        jax.ShapeDtypeStruct((LANES, EXPERT_HIDDEN), F32),
        jax.ShapeDtypeStruct(second.shape, F32),
    ]
    outs = pl.pallas_call(
        functools.partial(expert_kernel, count, experts, bool(prior)),
        grid=(count,),
        in_specs=[pl.BlockSpec(memory_space=pltpu.SMEM), whole(up), whole(down), whole(second)]
        + [anywhere] * (2 * count + len(prior)),
        out_specs=[anywhere] * (2 * count)
        + [pl.BlockSpec(s.shape, lambda i: (0, 0), pipeline_mode=pl.Buffered(1)) for s in grad_shapes],
        out_shape=[moe_shape] * count + [back_shape] * count + grad_shapes,
        scratch_shapes=[
            pltpu.VMEM((2, rows, wide), BF16),
            pltpu.VMEM((2, rows, model), BF16),
            pltpu.VMEM((2, rows, model), BF16),
            pltpu.VMEM((2, rows, wide), BF16),
            pltpu.SemaphoreType.DMA((2, 4)),
            pltpu.SemaphoreType.DMA((2, 2)),
        ],
        compiler_params=pltpu.CompilerParams(vmem_limit_bytes=VMEM_LIMIT),
        cost_estimate=pl.CostEstimate(
            flops=count * 2 * 2800000000 * rows // 512, bytes_accessed=12000000, transcendentals=count * rows * 512
        ),
        name="expert",
    )(meta, up, down, second, *tokens, *grads, *prior)
    return outs[:count], outs[count : 2 * count], outs[2 * count :]


def swap(array, bit, size):
    return lax.ppermute(array, "dp", [(i, i ^ bit) for i in range(size)])


def plane_gather(array, size):
    half = array.shape[0] // 2
    across = {0: array, 2: swap(array, 2, size), 4: swap(array, 4, size)}
    across[6] = jnp.concatenate([swap(across[4][:half], 2, size), swap(across[2][half:], 4, size)], axis=0)
    blocks = [None] * size
    for k in (0, 2, 4, 6):
        blocks[k] = across[k]
        blocks[k + 1] = swap(across[k], 1, size)
    return blocks


def plane_reduce(parts, size):
    def add(*terms):
        total = terms[0].astype(F32)
        for term in terms[1:]:
            total = total + term.astype(F32)
        return total.astype(BF16)

    half = parts[0].shape[0] // 2
    pair = {k: add(parts[k], swap(parts[k + 1], 1, size)) for k in (6, 2, 4, 0)}
    top = add(pair[4][:half], swap(pair[6][:half], 2, size))
    low = add(pair[2][half:], swap(pair[6][half:], 4, size))
    from_x = swap(jnp.concatenate([pair[2][:half], low], axis=0), 2, size)
    from_y = swap(jnp.concatenate([top, pair[4][half:]], axis=0), 4, size)
    return add(pair[0], from_x, from_y)


def dense_gather(shard, me, size):
    along = lax.all_gather(shard, "seq", axis=0)
    depth, rows, width = along.shape
    whole = jnp.zeros((depth, size, rows, width), shard.dtype)
    for k, block in enumerate(plane_gather(along, size)):
        whole = lax.dynamic_update_slice(whole, block[:, None], (0, me ^ k, 0, 0))
    return whole.reshape(depth * size * rows, width)


def pad_rows(array, rows):
    return jnp.pad(array, ((0, rows - array.shape[0]), (0, 0)))


def per_device(
    depth,
    size,
    block_input,
    document_number,
    key_present,
    routes,
    sequence_adapter,
    output_gradient,
    norm_scale_pair,
    query_key_value_weight,
    attention_output_weight,
    router_weight,
    shared_gate_up_weight,
    shared_down_weight,
    routed_gate_up_weight,
    routed_down_weight,
    dense_first_factor,
    shared_down_first_factor,
    dense_second_factor,
    routed_first_factor,
    routed_down_first_factor,
    routed_second_factor,
):
    _, rows, model = block_input.shape
    me = lax.axis_index("dp")
    experts = router_weight.shape[1]
    local_experts = routed_gate_up_weight.shape[0]
    shard_rows = query_key_value_weight.shape[0]
    shared_rows = shared_down_weight.shape[0]
    rank_all = dense_second_factor.shape[0]
    second_columns = dense_second_factor.shape[1]
    query_width = HEADS * HEAD_DIM
    kv_width = KV_HEADS * HEAD_DIM
    hops = min(depth - 1, -(-(DOCUMENT_SPAN - 1) // rows))
    rank = ADAPTER_RANK

    adapters_all = lax.all_gather(sequence_adapter, "dp", axis=0, tiled=True)
    adapter = sequence_adapter[0]

    pack_one = jnp.concatenate(
        [
            query_key_value_weight,
            dense_first_factor.reshape(shard_rows, 6 * rank_all),
            dense_second_factor.T.reshape(shard_rows, second_columns * rank_all // shard_rows),
            jnp.pad(
                jnp.concatenate([router_weight, norm_scale_pair.T], axis=1), ((0, 0), (0, LANES - experts - 2))
            ),
        ],
        axis=1,
    )
    pack_two = jnp.concatenate(
        [
            attention_output_weight,
            shared_gate_up_weight.reshape(shard_rows, 2 * SHARED_HIDDEN),
            pad_rows(jnp.concatenate([shared_down_weight, shared_down_first_factor], axis=1), shard_rows),
        ],
        axis=1,
    )
    one = dense_gather(pack_one, me, size)
    two = dense_gather(pack_two, me, size)
    qkv_w = one[:, : query_width + 2 * kv_width]
    offset = query_width + 2 * kv_width
    first_all = one[:, offset : offset + 6 * rank_all].reshape(model, 6, rank_all)
    offset += 6 * rank_all
    second_width = second_columns * rank_all // shard_rows
    second_t = one[:, offset : offset + second_width].reshape(depth * size * second_columns, rank_all)
    offset += second_width
    router_w = one[:, offset : offset + experts]
    gains = one[:, offset + experts : offset + experts + 2].astype(F32).T
    out_w = two[:, :model]
    sgu_w = two[:, model : model + 2 * SHARED_HIDDEN]
    shared_down = two[:, model + 2 * SHARED_HIDDEN :].reshape(depth * size, shard_rows, model + rank_all)
    shared_down = shared_down[:, :shared_rows].reshape(SHARED_HIDDEN, model + rank_all)
    sdown_w = shared_down[:, :model]
    first = lax.dynamic_slice_in_dim(first_all, adapter * rank, rank, 2)
    first_down = lax.dynamic_slice_in_dim(shared_down[:, model:], adapter * rank, rank, 1)
    second = lax.dynamic_slice_in_dim(second_t, adapter * rank, rank, 1).T
    widths = [query_width, kv_width, kv_width, model, SHARED_HIDDEN, SHARED_HIDDEN, model]
    edges = [sum(widths[:n]) for n in range(len(widths) + 1)]
    b_parts = [second[:, edges[n] : edges[n + 1]] for n in range(len(widths))]

    second_experts = lax.all_gather(routed_second_factor, "seq", axis=2, tiled=True)
    up_experts, down_experts = [], []
    for j in range(local_experts):
        up_shard = jnp.concatenate(
            [
                routed_gate_up_weight[j].reshape(-1, 2 * EXPERT_HIDDEN),
                routed_first_factor[j].reshape(-1, 2 * rank_all),
            ],
            axis=1,
        )
        up_experts.append(lax.all_gather(up_shard, "seq", axis=0, tiled=True))
        down_shard = jnp.concatenate([routed_down_weight[j], routed_down_first_factor[j]], axis=1)
        down_experts.append(lax.all_gather(down_shard, "seq", axis=0, tiled=True))

    grad_out_b = output_gradient[0]
    grad_blocks = plane_gather(grad_out_b, size)

    present_tag = jnp.where(key_present == 1, document_number, -1).astype(F32)
    tag_blocks = [
        lax.ppermute(present_tag + 1.0, "seq", [(i, i + h) for i in range(depth - h)]) - 1.0 for h in range(hops, 0, -1)
    ] + [present_tag]
    key_tag = jnp.concatenate(tag_blocks, axis=1).reshape((hops + 1) * rows, 1)
    query_tag = document_number.astype(F32)

    x_flat = block_input[0].astype(F32)
    normed = rms_norm(x_flat, gains[0]).astype(BF16)
    qkv_low = dot_nn(normed, first[:, 0:3].reshape(model, 3 * rank)).astype(BF16)
    qkv_extra = jnp.concatenate([dot_nn(qkv_low[:, n * rank : (n + 1) * rank], b_parts[n]) for n in range(3)], axis=1)
    qkv = (dot_nn(normed, qkv_w) + qkv_extra).astype(BF16)
    own_kv = qkv[:, query_width:]
    kv_blocks = [own_kv]
    for _ in range(hops):
        kv_blocks.append(lax.ppermute(kv_blocks[-1], "seq", [(i, i + 1) for i in range(depth - 1)]))
    kv_all = jnp.concatenate(kv_blocks[::-1], axis=0)
    attn, lse = attend(qkv, kv_all, query_tag, key_tag, hops)
    out_low = dot_nn(attn, first[:, 3]).astype(BF16)
    mid = x_flat + dot_nn(attn, out_w) + dot_nn(out_low, b_parts[3])
    normed2 = rms_norm(mid, gains[1]).astype(BF16)

    logits = dot_nn(normed2, router_w)
    route_rows = routes[0]
    flags = jnp.sum((route_rows[..., None] == jnp.arange(experts, dtype=jnp.int32)).astype(F32), axis=1)
    before = (jnp.arange(rows)[:, None] > jnp.arange(rows)[None, :]).astype(BF16)
    ranks = dot_nn(before, flags.astype(BF16))
    slots = jnp.where(flags > 0, ranks, -1.0)
    top = jnp.max(jnp.where(flags > 0, logits, -jnp.inf), axis=-1, keepdims=True)
    weights = jnp.where(flags > 0, jnp.exp(logits - top), 0.0)
    gates = weights / jnp.sum(weights, axis=-1, keepdims=True)
    gates_hi = gates.astype(BF16)
    gates_lo = (gates - gates_hi.astype(F32)).astype(BF16)
    extra = jnp.concatenate([slots.astype(BF16), gates_hi, gates_lo], axis=1)
    payload = jnp.concatenate([normed2, jnp.pad(extra, ((0, 0), (0, LANES - 3 * experts)))], axis=1)
    token_blocks = plane_gather(payload, size)

    shared_low = dot_nn(normed2, first[:, 4:6].reshape(model, 2 * rank)).astype(BF16)
    shared_gu = dot_nn(normed2, sgu_w) + jnp.concatenate(
        [dot_nn(shared_low[:, :rank], b_parts[4]), dot_nn(shared_low[:, rank:], b_parts[5])], axis=1
    )
    shared_hidden = swiglu(shared_gu).astype(BF16)
    sdown_low = dot_nn(shared_hidden, first_down).astype(BF16)
    y_shared = dot_nn(shared_hidden, sdown_w) + dot_nn(sdown_low, b_parts[6])
    grad_out = grad_out_b.astype(F32)
    glow_sdown = dot_nt(grad_out_b, b_parts[6]).astype(BF16)
    grad_b_sdown = dot_tn(sdown_low, grad_out_b)
    grad_a_sdown = dot_tn(shared_hidden, glow_sdown)
    grad_shared_hidden = dot_nt(grad_out_b, sdown_w) + dot_nt(glow_sdown, first_down)
    _, swiglu_back = jax.vjp(swiglu, shared_gu)
    grad_sgu = swiglu_back(grad_shared_hidden)[0].astype(BF16)
    glow_sgu = jnp.concatenate(
        [dot_nt(grad_sgu[:, :SHARED_HIDDEN], b_parts[4]), dot_nt(grad_sgu[:, SHARED_HIDDEN:], b_parts[5])], axis=1
    ).astype(BF16)
    grad_b_sgu = [
        dot_tn(shared_low[:, :rank], grad_sgu[:, :SHARED_HIDDEN]),
        dot_tn(shared_low[:, rank:], grad_sgu[:, SHARED_HIDDEN:]),
    ]
    grad_a_sgu = dot_tn(normed2, glow_sgu)
    grad_normed2 = dot_nt(grad_sgu, sgu_w) + dot_nt(glow_sgu, first[:, 4:6].reshape(model, 2 * rank))

    groups = ((6, 7, 2, 3), (4, 5, 1, 0))
    moe_parts, back_parts = [None] * size, [None] * size
    grads_first, grads_down, grads_second = [], [], []
    for j in range(local_experts):
        sums = None
        for group in groups:
            meta = jnp.stack([me * local_experts + j] + [adapters_all[me ^ k] for k in group]).astype(jnp.int32)
            prior = None if j == 0 else ([moe_parts[k] for k in group], [back_parts[k] for k in group])
            moe_out, back_out, grads = expert_call(
                meta,
                up_experts[j],
                down_experts[j],
                second_experts[j],
                [token_blocks[k] for k in group],
                [grad_blocks[k] for k in group],
                prior,
                experts,
            )
            for n, k in enumerate(group):
                moe_parts[k], back_parts[k] = moe_out[n], back_out[n]
            sums = grads if sums is None else [a + b for a, b in zip(sums, grads)]
        grads_first.append(sums[0])
        grads_down.append(sums[1])
        grads_second.append(sums[2])
    back = plane_reduce(back_parts, size).astype(F32)
    moe = plane_reduce(moe_parts, size).astype(F32)
    hidden_out = (mid + moe + y_shared).astype(BF16)[None]

    owner_rows = model // depth
    first_sum = jnp.stack(grads_first).astype(BF16).transpose(0, 2, 1)
    grad_expert_a = lax.psum_scatter(first_sum, "seq", scatter_dimension=1, tiled=True).astype(F32)
    grad_expert_a = grad_expert_a.reshape(local_experts, owner_rows, 2, rank_all)
    down_sum = jnp.stack(grads_down).astype(BF16).transpose(0, 2, 1)
    grad_expert_a_down = lax.psum_scatter(down_sum, "seq", scatter_dimension=1, tiled=True).astype(F32)
    second_sum = jnp.stack(grads_second).astype(BF16)
    grad_expert_b = lax.psum_scatter(second_sum, "seq", scatter_dimension=2, tiled=True).astype(F32)

    grad_gates = back[:, model : model + experts] + back[:, model + experts : model + 2 * experts]
    grad_logits = gates * (grad_gates - jnp.sum(gates * grad_gates, axis=-1, keepdims=True))
    grad_normed2 = grad_normed2 + back[:, :model]
    grad_normed2 = grad_normed2 + jnp.einsum(
        "re,de->rd", grad_logits, router_w.astype(F32), precision=lax.Precision.HIGHEST
    )
    _, norm2_back = jax.vjp(lambda values_in: rms_norm(values_in, gains[1]), mid)
    grad_mid = grad_out + norm2_back(grad_normed2)[0]
    grad_mid_b = grad_mid.astype(BF16)
    glow_out = dot_nt(grad_mid_b, b_parts[3]).astype(BF16)
    grad_b_out = dot_tn(out_low, grad_mid_b)
    grad_a_out = dot_tn(attn, glow_out)
    grad_attn = (dot_nt(grad_mid_b, out_w) + dot_nt(glow_out, first[:, 3])).astype(BF16)

    grad_q, grad_k, grad_v = attend_back(qkv, kv_all, grad_attn, lse, query_tag, key_tag, hops)
    grad_kv = jnp.concatenate([grad_k, grad_v], axis=1)
    moving = None
    for h in range(hops + 1):
        part = grad_kv[h * rows : (h + 1) * rows].astype(F32)
        if moving is not None:
            part = part + lax.ppermute(moving, "seq", [(i + 1, i) for i in range(depth - 1)]).astype(F32)
        moving = part.astype(BF16)
    grad_qkv = jnp.concatenate([grad_q, moving], axis=1)
    parts = [grad_qkv[:, edges[n] : edges[n + 1]] for n in range(3)]
    glow_qkv = jnp.concatenate([dot_nt(parts[n], b_parts[n]) for n in range(3)], axis=1).astype(BF16)
    grad_b_qkv = [dot_tn(qkv_low[:, n * rank : (n + 1) * rank], parts[n]) for n in range(3)]
    grad_a_qkv = dot_tn(normed, glow_qkv)
    grad_normed = dot_nt(grad_qkv, qkv_w) + dot_nt(glow_qkv, first[:, 0:3].reshape(model, 3 * rank))
    _, norm1_back = jax.vjp(lambda values_in: rms_norm(values_in, gains[0]), x_flat)
    grad_hidden = (grad_mid + norm1_back(grad_normed)[0])[None]

    first_compact = jnp.concatenate([grad_a_qkv, grad_a_out, grad_a_sgu], axis=1)
    second_compact = jnp.concatenate(grad_b_qkv + [grad_b_out] + grad_b_sgu + [grad_b_sdown], axis=1)
    compact = jnp.concatenate(
        [
            first_compact.reshape(depth * size, shard_rows * 6 * rank),
            grad_a_sdown.reshape(depth * size, shared_rows * rank),
            second_compact.T.reshape(depth * size, second_columns * rank),
        ],
        axis=1,
    ).reshape(depth, size, -1)
    compact = lax.psum_scatter(compact, "seq", scatter_dimension=0, tiled=True)[0]
    compact = lax.all_to_all(compact, "dp", split_axis=0, concat_axis=0, tiled=True)
    of_adapter = (adapters_all[:, None] == jnp.arange(rank_all // rank, dtype=jnp.int32)[None, :]).astype(F32)
    spread = jnp.sum(of_adapter[:, :, None] * compact[:, None, :], axis=0)
    cut_one = shard_rows * 6 * rank
    cut_two = cut_one + shared_rows * rank
    grad_first = spread[:, :cut_one].reshape(-1, shard_rows, 6, rank).transpose(1, 2, 0, 3)
    grad_first = grad_first.reshape(shard_rows, 6, rank_all)
    grad_first_down = spread[:, cut_one:cut_two].reshape(-1, shared_rows, rank).transpose(1, 0, 2)
    grad_first_down = grad_first_down.reshape(shared_rows, rank_all)
    grad_second = spread[:, cut_two:].reshape(-1, second_columns, rank).transpose(0, 2, 1)
    grad_second = grad_second.reshape(rank_all, second_columns)
    return (
        hidden_out,
        grad_hidden,
        grad_first,
        grad_first_down,
        grad_second,
        grad_expert_a,
        grad_expert_a_down,
        grad_expert_b,
    )


def solution(mesh):
    in_specs = (
        P("dp", "seq", None),
        P("dp", "seq"),
        P("dp", "seq"),
        P("dp", "seq", None),
        P("dp"),
        P("dp", "seq", None),
        P(None, ("seq", "dp")),
        P(("seq", "dp"), None),
        P(("seq", "dp"), None),
        P(("seq", "dp"), None),
        P(("seq", "dp"), None, None),
        P(("seq", "dp"), None),
        P("dp", "seq", None, None),
        P("dp", "seq", None),
        P(("seq", "dp"), None, None),
        P(("seq", "dp"), None),
        P(None, ("seq", "dp")),
        P("dp", "seq", None, None),
        P("dp", "seq", None),
        P("dp", None, "seq"),
    )
    out_specs = (
        P("dp", "seq", None),
        P("dp", "seq", None),
        P(("seq", "dp"), None, None),
        P(("seq", "dp"), None),
        P(None, ("seq", "dp")),
        P("dp", "seq", None, None),
        P("dp", "seq", None),
        P("dp", None, "seq"),
    )
    return jax.shard_map(
        functools.partial(per_device, mesh.shape["seq"], mesh.shape["dp"]),
        mesh=mesh,
        in_specs=in_specs,
        out_specs=out_specs,
        check_vma=False,
    )
```

```python
import functools
import math

import jax
import jax.numpy as jnp
from jax import lax
from jax.experimental import pallas as pl
from jax.experimental.pallas import tpu as pltpu
from jax.sharding import PartitionSpec as P

HEADS = 12
KV_HEADS = 4
HEAD_DIM = 128
EXPERT_HIDDEN = 512
SHARED_HIDDEN = 1024
ADAPTER_RANK = 16
DOCUMENT_SPAN = 1024

EPSILON = 1e-05
MASKED_SCORE = -1e30
LOG2E = 1.4426950408889634
SCALE = HEAD_DIM ** (-0.5)
LANES = 128
VMEM_LIMIT = 60 * 1024 * 1024

F32 = jnp.float32
BF16 = jnp.bfloat16


def dot_nn(left, right):
    return jnp.dot(left, right, preferred_element_type=F32)


def dot_tn(left, right):
    return lax.dot_general(left, right, (((0,), (0,)), ((), ())), preferred_element_type=F32)


def dot_nt(left, right):
    return lax.dot_general(left, right, (((1,), (1,)), ((), ())), preferred_element_type=F32)


def rms_norm(values, gain):
    return values * lax.rsqrt(jnp.mean(values * values, axis=-1, keepdims=True) + EPSILON) * gain


def cost(microseconds):
    return pl.CostEstimate(flops=int(1153500000 * microseconds), bytes_accessed=1000000, transcendentals=0)


def query_tiles(rows, hops):
    tile = math.gcd(rows, 256)
    spans = []
    for first in range(0, rows, tile):
        oldest = max(0, hops * rows + first - (DOCUMENT_SPAN - 1)) // tile * tile
        spans.append((first, tile, oldest, hops * rows + first + tile - oldest))
    return spans


def fill_bias(spans, shift, query_tag, key_tag, bias):
    for first, tile, oldest, span in spans:
        keys = oldest + lax.broadcasted_iota(jnp.int32, (span, tile), 0)
        queries = shift + first + lax.broadcasted_iota(jnp.int32, (span, tile), 1)
        same = key_tag[oldest : oldest + span, :] == query_tag[:, first : first + tile]
        permit = (keys <= queries) & (same | (keys == queries))
        bias[oldest : oldest + span, first : first + tile] = jnp.where(permit, 0.0, MASKED_SCORE)


def attend_kernel(spans, shift, waits, q_ref, k_ref, v_ref, qt_ref, kt_ref, *rest):
    out_ref, lse_ref, bias = rest[waits:]

    @pl.when(pl.program_id(0) == 0)
    def _():
        fill_bias(spans, shift, qt_ref, kt_ref, bias)

    groups = q_ref.shape[1] // HEAD_DIM
    for first, tile, oldest, span in spans:
        keys = k_ref[oldest : oldest + span, :]
        values = v_ref[oldest : oldest + span, :]
        mask = bias[oldest : oldest + span, first : first + tile]
        for h in range(groups):
            columns = slice(h * HEAD_DIM, (h + 1) * HEAD_DIM)
            scores = dot_nt(keys, q_ref[first : first + tile, columns]) * (SCALE * LOG2E) + mask
            top = jnp.max(scores, axis=0, keepdims=True)
            weights = jnp.exp2(scores - top)
            total = jnp.sum(weights, axis=0, keepdims=True)
            mixed = dot_tn(values, weights.astype(BF16)) / total
            out_ref[first : first + tile, columns] = mixed.T.astype(BF16)
            lse_ref[0, h : h + 1, first : first + tile] = top + jnp.log2(total)


def attend(query, kv_all, query_tag, key_tag, hops, deps=()):
    rows = query.shape[0]
    groups = HEADS // KV_HEADS
    span = kv_all.shape[0]
    spans = query_tiles(rows, hops)
    return pl.pallas_call(
        functools.partial(attend_kernel, spans, hops * rows, len(deps)),
        grid=(KV_HEADS,),
        in_specs=[
            pl.BlockSpec((rows, groups * HEAD_DIM), lambda g: (0, g)),
            pl.BlockSpec((span, HEAD_DIM), lambda g: (0, g)),
            pl.BlockSpec((span, HEAD_DIM), lambda g: (0, KV_HEADS + g)),
            pl.BlockSpec((1, rows), lambda g: (0, 0)),
            pl.BlockSpec((span, 1), lambda g: (0, 0)),
        ]
        + [pl.BlockSpec(memory_space=pl.ANY)] * len(deps),
        out_specs=[
            pl.BlockSpec((rows, groups * HEAD_DIM), lambda g: (0, g)),
            pl.BlockSpec((1, groups, rows), lambda g: (g, 0, 0)),
        ],
        out_shape=[
            jax.ShapeDtypeStruct((rows, HEADS * HEAD_DIM), BF16),
            jax.ShapeDtypeStruct((KV_HEADS, groups, rows), F32),
        ],
        scratch_shapes=[pltpu.VMEM((span, rows), F32)],
        compiler_params=pltpu.CompilerParams(vmem_limit_bytes=VMEM_LIMIT),
        cost_estimate=cost(23.0),
        name="attend",
    )(query, kv_all, kv_all, query_tag, key_tag, *deps)


def attend_back_kernel(
    spans, shift, waits, q_ref, k_ref, v_ref, g_ref, lse_ref, qt_ref, kt_ref, *rest
):
    dq_ref, dkv_ref, bias, dk_acc, dv_acc = rest[waits:]

    @pl.when(pl.program_id(0) == 0)
    def _():
        fill_bias(spans, shift, qt_ref, kt_ref, bias)

    dk_acc[...] = jnp.zeros_like(dk_acc)
    dv_acc[...] = jnp.zeros_like(dv_acc)
    groups = q_ref.shape[1] // HEAD_DIM
    for first, tile, oldest, span in spans:
        keys = k_ref[oldest : oldest + span, :]
        values = v_ref[oldest : oldest + span, :]
        mask = bias[oldest : oldest + span, first : first + tile]
        for h in range(groups):
            columns = slice(h * HEAD_DIM, (h + 1) * HEAD_DIM)
            query = q_ref[first : first + tile, columns]
            grad = g_ref[first : first + tile, columns]
            lse = lse_ref[0, h : h + 1, first : first + tile]
            probs = jnp.exp2(dot_nt(keys, query) * (SCALE * LOG2E) + mask - lse)
            dv_acc[oldest : oldest + span, :] += dot_nn(probs.astype(BF16), grad)
            grad_probs = dot_nt(values, grad)
            delta = jnp.sum(probs * grad_probs, axis=0, keepdims=True)
            grad_scores = (probs * (grad_probs - delta)).astype(BF16)
            dk_acc[oldest : oldest + span, :] += dot_nn(grad_scores, query) * SCALE
            dq_ref[first : first + tile, columns] = (dot_tn(grad_scores, keys) * SCALE).astype(BF16)
    dkv_ref[:, :HEAD_DIM] = dk_acc[...].astype(dkv_ref.dtype)
    dkv_ref[:, HEAD_DIM:] = dv_acc[...].astype(dkv_ref.dtype)


def attend_back(query, kv_all, grad_attn, lse, query_tag, key_tag, hops, head, count, deps=()):
    rows = query.shape[0]
    groups = HEADS // KV_HEADS
    span = kv_all.shape[0]
    spans = query_tiles(rows, hops)
    return pl.pallas_call(
        functools.partial(attend_back_kernel, spans, hops * rows, len(deps)),
        grid=(count,),
        in_specs=[
            pl.BlockSpec((rows, groups * HEAD_DIM), lambda g: (0, head + g)),
            pl.BlockSpec((span, HEAD_DIM), lambda g: (0, head + g)),
            pl.BlockSpec((span, HEAD_DIM), lambda g: (0, KV_HEADS + head + g)),
            pl.BlockSpec((rows, groups * HEAD_DIM), lambda g: (0, head + g)),
            pl.BlockSpec((1, groups, rows), lambda g: (head + g, 0, 0)),
            pl.BlockSpec((1, rows), lambda g: (0, 0)),
            pl.BlockSpec((span, 1), lambda g: (0, 0)),
        ]
        + [pl.BlockSpec(memory_space=pl.ANY)] * len(deps),
        out_specs=[
            pl.BlockSpec((rows, groups * HEAD_DIM), lambda g: (0, g)),
            pl.BlockSpec((span, 2 * HEAD_DIM), lambda g: (0, g)),
        ],
        out_shape=[
            jax.ShapeDtypeStruct((rows, count * groups * HEAD_DIM), BF16),
            jax.ShapeDtypeStruct((span, count * 2 * HEAD_DIM), BF16),
        ],
        scratch_shapes=[
            pltpu.VMEM((span, rows), F32),
            pltpu.VMEM((span, HEAD_DIM), F32),
            pltpu.VMEM((span, HEAD_DIM), F32),
        ],
        compiler_params=pltpu.CompilerParams(vmem_limit_bytes=VMEM_LIMIT),
        cost_estimate=cost(2.0 * count),
        name="attend_back",
    )(query, kv_all, kv_all, grad_attn, lse, query_tag, key_tag, *deps)


BACK_ROWS = 2 * ADAPTER_RANK


def expert_kernel(count, splits, experts, capacity, with_prior, with_shared, waits, *refs):
    meta, refs = refs[0], refs[1:]
    weight_count = 5 if with_shared else 3
    weight_refs, refs = refs[:weight_count], refs[weight_count:]
    token_refs, grad_refs = [], []
    for split in splits:
        token_refs.append(refs[:split])
        refs = refs[split:]
    for split in splits:
        grad_refs.append(refs[:split])
        refs = refs[split:]
    prior_moe, prior_back = (), ()
    if with_prior:
        prior_moe, refs = refs[:count], refs[count:]
        prior_back, refs = refs[:count], refs[count:]
    refs = refs[waits:]
    moe_refs, refs = refs[:count], refs[count:]
    back_refs, refs = refs[:count], refs[count:]
    grad_count = 4 if with_shared else 3
    grad_outs, refs = refs[:grad_count], refs[grad_count:]
    grad_sums, refs = refs[:grad_count], refs[grad_count:]
    first_grad, down_grad, second_grad = grad_sums[:3]
    weight_bufs, refs = refs[:weight_count], refs[weight_count:]
    tokens_buf, grad_buf, moe_buf, back_buf, in_sem, out_sem, weight_sem, sum_sem = refs

    step = pl.program_id(0)
    steps = count // 2
    slots = min(2, steps)
    slot = lax.rem(step, slots)
    rows, wide = tokens_buf.shape[2:]
    model = wide - LANES
    hidden = EXPERT_HIDDEN
    rank = ADAPTER_RANK
    up_ref, down_ref, second_ref = weight_bufs[:3]

    def weight_copy(n):
        return pltpu.make_async_copy(weight_refs[n], weight_bufs[n], weight_sem.at[n])

    def incoming(k, i, kinds):
        copies = []
        to, source = k % slots, 2 * k + i
        for n, (refs_of, buf) in enumerate(((token_refs, tokens_buf), (grad_refs, grad_buf))):
            size = rows // len(refs_of[source])
            for p, piece in enumerate(refs_of[source] if n in kinds else ()):
                part = buf.at[to, i, pl.ds(p * size, size)]
                copies.append(pltpu.make_async_copy(piece, part, in_sem.at[to, i, 2 * n + p]))
        if with_prior and 2 in kinds:
            copies.append(pltpu.make_async_copy(prior_moe[source], moe_buf.at[to, i], in_sem.at[to, i, 4]))
            copies.append(pltpu.make_async_copy(prior_back[source], back_buf.at[to, i], in_sem.at[to, i, 5]))
        return copies

    def outgoing(k, i, kinds=(0, 1)):
        at, source = k % slots, 2 * k + i
        pairs = ((moe_buf, moe_refs), (back_buf, back_refs))
        return [pltpu.make_async_copy(pairs[n][0].at[at, i], pairs[n][1][source], out_sem.at[at, i, n]) for n in kinds]

    def at_step(action, first=0, last=steps):
        for k in range(first, last):
            pl.when(step == k)(functools.partial(action, k))

    def wait_in(i, kind):
        def action(k):
            for copy in incoming(k, i, (kind,)):
                copy.wait()

        at_step(action)

    def start_out(i, n):
        at_step(lambda k: outgoing(k, i, (n,))[0].start())

    def turn(k):
        for i in (0, 1):
            if k >= 1:
                for copy in outgoing(k - 1, i):
                    copy.wait()
            if k + 1 < steps:
                for copy in incoming(k + 1, i, (0, 1, 2)):
                    copy.start()

    def sum_copy(n):
        return pltpu.make_async_copy(grad_sums[n], grad_outs[n], sum_sem.at[n])

    @pl.when(step == 0)
    def _():
        for i in (0, 1):
            for copy in incoming(0, i, (0,)):
                copy.start()
        for i in (0, 1):
            for copy in incoming(0, i, (1,)):
                copy.start()
        for n in range(weight_count):
            weight_copy(n).start()
        for i in (0, 1):
            for copy in incoming(0, i, (2,)):
                copy.start()
        for total in grad_sums:
            total[...] = jnp.zeros_like(total)

    expert = meta[0]
    lane = lax.broadcasted_iota(jnp.int32, (1, LANES), 1)
    sub = lax.broadcasted_iota(jnp.int32, (LANES, 1), 0)
    places, picks, gates_of, selects, adapters = [], [], [], [], []
    inputs, grad_rows = [], []
    for i in (0, 1):
        wait_in(i, 0)
        extra_b = tokens_buf[slot, i, :, model:]
        extra = extra_b.astype(F32)
        own = 3 * experts + 3 * rank
        adapter = extra[0:1, own : own + 1]
        select = ((lane // rank).astype(F32) == adapter).astype(F32)
        slot_column = jnp.sum(jnp.where(lane == expert, extra, 0.0), axis=1, keepdims=True)
        slot_row = jnp.sum(jnp.where(sub == expert, extra.T, 0.0), axis=0, keepdims=True)
        place = lax.broadcasted_iota(jnp.int32, (rows, capacity), 1).astype(F32) == slot_column
        pick = lax.broadcasted_iota(jnp.int32, (capacity, rows), 0).astype(F32) == slot_row
        place, pick = place.astype(F32).astype(BF16), pick.astype(F32).astype(BF16)
        picked_extra = dot_nn(pick, extra_b)
        chosen = (lane == experts + expert) | (lane == 2 * experts + expert)
        gates_of.append(jnp.sum(jnp.where(chosen, picked_extra, 0.0), axis=1, keepdims=True))
        inputs.append(dot_nn(pick, tokens_buf[slot, i, :, :model]).astype(BF16))
        picks.append(pick)
        places.append(place)
        adapters.append(adapter)
        selects.append(jnp.broadcast_to(select, (capacity, LANES)))
    for i in (0, 1):
        wait_in(i, 1)
        grad_rows.append(dot_nn(picks[i], grad_buf[slot, i]))
    at_step(turn)
    inputs = jnp.concatenate(inputs, axis=0)
    grad_rows = jnp.concatenate(grad_rows, axis=0)
    gate = jnp.concatenate(gates_of, axis=0)
    select = jnp.concatenate(selects, axis=0)
    select_two = jnp.concatenate([select, select], axis=1)

    @pl.when(step == 0)
    def _():
        for n in range(weight_count):
            weight_copy(n).wait()

    low = (dot_nn(inputs, up_ref[:, 2 * hidden : 2 * hidden + 2 * LANES]) * select_two).astype(BF16)
    gate_part = dot_nn(inputs, up_ref[:, :hidden]) + dot_nn(low[:, :LANES], second_ref[:, :hidden])
    up_part = dot_nn(inputs, up_ref[:, hidden : 2 * hidden]) + dot_nn(low[:, LANES:], second_ref[:, hidden : 2 * hidden])
    sigmoid = 1.0 / (1.0 + jnp.exp(-gate_part))
    silu = gate_part * sigmoid
    act = (silu * up_part).astype(BF16)
    low_down = (dot_nn(act, down_ref[:, model:]) * select).astype(BF16)
    output = (dot_nn(act, down_ref[:, :model]) + dot_nn(low_down, second_ref[:, 2 * hidden :])).astype(BF16).astype(F32)
    grad_gate = jnp.sum(output * grad_rows, axis=1, keepdims=True)
    weighted = (gate * output).astype(BF16)

    grad_y = (gate * grad_rows).astype(BF16)
    glow_down = (dot_nt(grad_y, second_ref[:, 2 * hidden :]) * select).astype(BF16)
    second_grad[:, 2 * hidden :] += dot_tn(low_down, grad_y)
    down_grad[...] += dot_tn(act, glow_down)
    grad_act = dot_nt(grad_y, down_ref[:, :model]) + dot_nt(glow_down, down_ref[:, model:])
    grad_up = (grad_act * silu).astype(BF16)
    grad_gp = (grad_act * up_part * (sigmoid * (1.0 + gate_part * (1.0 - sigmoid)))).astype(BF16)
    glow = jnp.concatenate(
        [
            dot_nt(grad_gp, second_ref[:, :hidden]) * select,
            dot_nt(grad_up, second_ref[:, hidden : 2 * hidden]) * select,
        ],
        axis=1,
    ).astype(BF16)
    second_grad[:, :hidden] += dot_tn(low[:, :LANES], grad_gp)
    second_grad[:, hidden : 2 * hidden] += dot_tn(low[:, LANES:], grad_up)
    first_grad[...] += dot_tn(inputs, glow)
    grad_in = (
        dot_nt(grad_gp, up_ref[:, :hidden])
        + dot_nt(grad_up, up_ref[:, hidden : 2 * hidden])
        + dot_nt(glow, up_ref[:, 2 * hidden : 2 * hidden + 2 * LANES])
    ).astype(BF16)
    gate_hi = grad_gate.astype(BF16).astype(F32)
    gate_lo = grad_gate - gate_hi
    extra_out = (
        jnp.where(lane == expert, gate_hi, 0.0) + jnp.where(lane == experts + expert, gate_lo, 0.0)
    ).astype(BF16)

    @pl.when(step == steps - 1)
    def _():
        for n in range(3):
            sum_copy(n).start()

    for i in (0, 1):
        mine = slice(i * capacity, (i + 1) * capacity)
        wait_in(i, 2)
        moe = dot_nn(places[i], weighted[mine])
        back = dot_nn(places[i], grad_in[mine])
        back_extra = dot_nn(places[i], extra_out[mine])
        if with_prior:
            moe = moe + moe_buf[slot, i].astype(F32)
            back = back + back_buf[slot, i, :rows, :model].astype(F32)
            back_extra = back_extra + back_buf[slot, i, :rows, model:].astype(F32)
        if not with_prior:
            back_buf[slot, i, rows:, :] = jnp.zeros((BACK_ROWS, wide), BF16)
        if with_shared:
            sdown_ref, sb_ref = weight_bufs[3:]
            units = sdown_ref.shape[0]
            first_gate, first_up, first_down = 3 * experts, 3 * experts + rank, 3 * experts + 2 * rank
            tokens = tokens_buf[slot, i, :, :model]
            extra_b = tokens_buf[slot, i, :, model:]
            grads = grad_buf[slot, i]
            offset = (lane - sub).astype(F32) - adapters[i] * float(rank)

            def spread(base):
                inside = (sub >= base) & (sub < base + rank)
                return (inside & (offset == float(-base))).astype(F32).astype(BF16)

            to_gate = dot_nt(spread(first_gate), sb_ref[:units]).astype(BF16)
            to_up = dot_nt(spread(first_up), sb_ref[units:]).astype(BF16)
            to_down = dot_nt(spread(first_down), sdown_ref[:, model:]).astype(BF16)
            shared_up = up_ref[:, 2 * hidden + 2 * LANES :]
            gate_up = dot_nn(tokens, shared_up)
            s_gate = gate_up[:, :units] + dot_nn(extra_b, to_gate)
            s_up = gate_up[:, units:] + dot_nn(extra_b, to_up)
            s_sig = 1.0 / (1.0 + jnp.exp(-s_gate))
            s_silu = s_gate * s_sig
            s_act = (s_silu * s_up).astype(BF16)
            moe = moe + dot_nn(s_act, sdown_ref[:, :model])
            s_grad = dot_nt(grads, sdown_ref[:, :model]) + dot_nn(extra_b, to_down)
            grad_sums[3][...] += dot_tn(s_act, dot_nn(extra_b, spread(first_down)).astype(BF16))
            s_gu = (s_grad * s_silu).astype(BF16)
            s_gg = (s_grad * s_up * (s_sig * (1.0 + s_gate * (1.0 - s_sig)))).astype(BF16)
            back_extra = back_extra + dot_nt(s_act, to_down) + dot_nt(s_gg, to_gate) + dot_nt(s_gu, to_up)
            back = back + dot_nt(jnp.concatenate([s_gg, s_gu], axis=1), shared_up)
            columns = pl.ds(pl.multiple_of(meta[1] * units, units), units)
            grad_bg = dot_tn(extra_b, s_gg)[first_gate : first_gate + rank]
            grad_bu = dot_tn(extra_b, s_gu)[first_up : first_up + rank]
            back_buf[slot, i, rows : rows + rank, columns] = grad_bg.astype(BF16)
            back_buf[slot, i, rows + rank :, columns] = grad_bu.astype(BF16)
        moe_buf[slot, i] = moe.astype(BF16)
        start_out(i, 0)
        back_buf[slot, i, :rows, :model] = back.astype(BF16)
        back_buf[slot, i, :rows, model:] = back_extra.astype(BF16)
        start_out(i, 1)

    @pl.when(step == steps - 1)
    def _():
        for n in range(3, grad_count):
            sum_copy(n).start()
        for i in (0, 1):
            for copy in outgoing(steps - 1, i):
                copy.wait()
        for n in range(grad_count):
            sum_copy(n).wait()


def expert_call(meta, weights, tokens, grads, prior, experts, capacity, deps=()):
    count = len(tokens)
    with_shared = len(weights) > 3
    splits = [len(pieces) for pieces in tokens]
    rows, model = sum(piece.shape[0] for piece in grads[0]), grads[0][0].shape[1]
    wide = model + LANES
    slots = min(2, count // 2)
    anywhere = pl.BlockSpec(memory_space=pl.ANY)
    prior = [] if prior is None else list(prior[0]) + list(prior[1])
    flat = [piece for pieces in tokens for piece in pieces] + [piece for pieces in grads for piece in pieces]
    grad_shapes = [
        jax.ShapeDtypeStruct((model, 2 * LANES), F32),
        jax.ShapeDtypeStruct((EXPERT_HIDDEN, LANES), F32),
        jax.ShapeDtypeStruct(weights[2].shape, F32),
    ]
    if with_shared:
        grad_shapes.append(jax.ShapeDtypeStruct((weights[3].shape[0], LANES), F32))
    back_rows = rows + BACK_ROWS
    outs = pl.pallas_call(
        functools.partial(expert_kernel, count, splits, experts, capacity, bool(prior), with_shared, len(deps)),
        grid=(count // 2,),
        in_specs=[pl.BlockSpec(memory_space=pltpu.SMEM)]
        + [anywhere] * (len(weights) + len(flat) + len(prior) + len(deps)),
        out_specs=[anywhere] * (2 * count + len(grad_shapes)),
        out_shape=[jax.ShapeDtypeStruct((rows, model), BF16)] * count
        + [jax.ShapeDtypeStruct((back_rows, wide), BF16)] * count
        + grad_shapes,
        scratch_shapes=[pltpu.VMEM(s.shape, F32) for s in grad_shapes]
        + [pltpu.VMEM(w.shape, BF16) for w in weights]
        + [
            pltpu.VMEM((slots, 2, rows, wide), BF16),
            pltpu.VMEM((slots, 2, rows, model), BF16),
            pltpu.VMEM((slots, 2, rows, model), BF16),
            pltpu.VMEM((slots, 2, back_rows, wide), BF16),
            pltpu.SemaphoreType.DMA((slots, 2, 6)),
            pltpu.SemaphoreType.DMA((slots, 2, 2)),
            pltpu.SemaphoreType.DMA((len(weights),)),
            pltpu.SemaphoreType.DMA((len(grad_shapes),)),
        ],
        compiler_params=pltpu.CompilerParams(vmem_limit_bytes=VMEM_LIMIT),
        cost_estimate=cost(12.0 * count),
        name="expert",
    )(meta, *weights, *flat, *prior, *deps)
    return outs[:count], outs[count : 2 * count], outs[2 * count :]


def swap(array, bit, size):
    return lax.ppermute(array, "dp", [(i, i ^ bit) for i in range(size)])


def plane_gather(array, size):
    half = array.shape[0] // 2
    x, y = swap(array, 2, size), swap(array, 4, size)
    across = {0: (array,), 2: (x,), 4: (y,), 6: (swap(y[:half], 2, size), swap(x[half:], 4, size))}
    blocks = [None] * size
    for k in (0, 2, 4, 6):
        blocks[k] = across[k]
        blocks[k + 1] = tuple(swap(piece, 1, size) for piece in across[k])
    return blocks


def add(*terms):
    total = terms[0].astype(F32)
    for term in terms[1:]:
        total = total + term.astype(F32)
    return total.astype(BF16)


def tie_kernel(*refs):
    del refs


def tie_all(arrays, *others):
    anywhere = pl.BlockSpec(memory_space=pl.ANY)
    return pl.pallas_call(
        tie_kernel,
        in_specs=[anywhere] * (len(arrays) + len(others)),
        out_specs=[anywhere] * len(arrays),
        out_shape=[jax.ShapeDtypeStruct(array.shape, array.dtype) for array in arrays],
        input_output_aliases={n: n for n in range(len(arrays))},
        name="tie",
    )(*arrays, *others)


def tie(array, *others):
    return tie_all([array], *others)[0]


def assemble_kernel(splits, widths, waits, me_ref, *refs):
    pieces, outs = refs[: sum(splits)], refs[sum(splits) + waits : -3]
    whole, in_sem, out_sem = refs[-3:]
    copies, at = [], 0
    for k, split in enumerate(splits):
        start = 0
        for piece in pieces[at : at + split]:
            target = whole.at[pl.ds(start, piece.shape[0]), me_ref[0] ^ k]
            copies.append(pltpu.make_async_copy(piece, target, in_sem.at[len(copies)]))
            start += piece.shape[0]
        at += split
    for copy in copies:
        copy.start()
    for copy in copies:
        copy.wait()
    copies, column = [], 0
    for out, (count, width) in zip(outs, widths):
        for n in range(count):
            source = whole.at[:, :, :, pl.ds(column, width)]
            copies.append(pltpu.make_async_copy(source, out.at[:, :, n], out_sem.at[len(copies)]))
            column += width
    for copy in copies:
        copy.start()
    for copy in copies:
        copy.wait()


def assemble(blocks, widths, me, deps=()):
    depth, rows, _ = blocks[0][0].shape
    size = len(blocks)
    splits = [len(pieces) for pieces in blocks]
    flat = [piece for pieces in blocks for piece in pieces]
    outs = pl.pallas_call(
        functools.partial(assemble_kernel, splits, widths, len(deps)),
        in_specs=[pl.BlockSpec(memory_space=pltpu.SMEM)] + [pl.BlockSpec(memory_space=pl.ANY)] * (len(flat) + len(deps)),
        out_specs=[pl.BlockSpec(memory_space=pl.ANY)] * len(widths),
        out_shape=[jax.ShapeDtypeStruct((depth, size, count, rows, width), BF16) for count, width in widths],
        scratch_shapes=[
            pltpu.VMEM((depth, size, rows, sum(count * width for count, width in widths)), BF16),
            pltpu.SemaphoreType.DMA((len(flat),)),
            pltpu.SemaphoreType.DMA((sum(count for count, _ in widths),)),
        ],
        compiler_params=pltpu.CompilerParams(vmem_limit_bytes=VMEM_LIMIT),
        name="assemble",
    )(me.astype(jnp.int32).reshape(1), *flat, *deps)
    return [out.reshape(-1, out.shape[-1]) for out in outs]


def per_device(
    depth,
    size,
    block_input,
    document_number,
    key_present,
    routes,
    sequence_adapter,
    output_gradient,
    norm_scale_pair,
    query_key_value_weight,
    attention_output_weight,
    router_weight,
    shared_gate_up_weight,
    shared_down_weight,
    routed_gate_up_weight,
    routed_down_weight,
    dense_first_factor,
    shared_down_first_factor,
    dense_second_factor,
    routed_first_factor,
    routed_down_first_factor,
    routed_second_factor,
):
    _, rows, model = block_input.shape
    topk = routes.shape[2]
    me = lax.axis_index("dp")
    experts = router_weight.shape[1]
    local_experts = routed_gate_up_weight.shape[0]
    shard_rows = query_key_value_weight.shape[0]
    shared_rows = shared_down_weight.shape[0]
    rank_all = dense_second_factor.shape[0]
    second_columns = dense_second_factor.shape[1]
    capacity = 4 * topk * rows // (3 * experts)
    query_width = HEADS * HEAD_DIM
    kv_width = KV_HEADS * HEAD_DIM
    hops = min(depth - 1, -(-(DOCUMENT_SPAN - 1) // rows))
    rank = ADAPTER_RANK
    units = SHARED_HIDDEN // size
    adapter = sequence_adapter[0]
    forward = [(i, i + 1) for i in range(depth - 1)]
    backward = [(i + 1, i) for i in range(depth - 1)]

    def over_seq(shard):
        return lax.all_gather(shard, "seq", axis=0)

    first_shard = dense_first_factor.reshape(shard_rows, 6 * rank_all)
    second_width = second_columns * rank_all // shard_rows
    groups = second_width // rank_all
    pack_kv = jnp.concatenate(
        [
            query_key_value_weight[:, query_width:],
            first_shard[:, rank_all : 3 * rank_all],
            dense_second_factor.T.reshape(groups, shard_rows, rank_all).transpose(1, 0, 2).reshape(shard_rows, -1),
            jnp.pad(
                jnp.concatenate([router_weight, norm_scale_pair.T], axis=1), ((0, 0), (0, LANES - experts - 2))
            ),
        ],
        axis=1,
    )
    pack_q = jnp.concatenate(
        [
            query_key_value_weight[:, :query_width],
            first_shard[:, :rank_all],
            first_shard[:, 3 * rank_all :],
            attention_output_weight,
        ],
        axis=1,
    )
    seq_kv = over_seq(pack_kv)
    seq_q = over_seq(tie(pack_q, seq_kv))

    present_tag = jnp.where(key_present == 1, document_number, -1).astype(F32)
    tag_blocks = [
        lax.ppermute(present_tag + 1.0, "seq", [(i, i + h) for i in range(depth - h)]) - 1.0 for h in range(hops, 0, -1)
    ] + [present_tag]
    key_tag = jnp.concatenate(tag_blocks, axis=1).reshape((hops + 1) * rows, 1)
    query_tag = document_number.astype(F32)

    flags = jnp.sum((routes[0][..., None] == jnp.arange(experts, dtype=jnp.int32)).astype(F32), axis=1)
    before = (jnp.arange(rows)[:, None] > jnp.arange(rows)[None, :]).astype(BF16)
    slots = jnp.where(flags > 0, dot_nn(before, flags.astype(BF16)), -1.0).astype(BF16)

    def own_columns(matrix):
        return lax.dynamic_slice_in_dim(matrix, adapter * rank, rank, 1)

    def own_factors(matrix):
        count = matrix.shape[1] // rank_all
        return jnp.concatenate([own_columns(matrix[:, n * rank_all : (n + 1) * rank_all]) for n in range(count)], axis=1)

    grad_out_b = output_gradient[0]
    grads_x, grads_y = swap(grad_out_b, 2, size), swap(grad_out_b, 4, size)
    kv_gathered = plane_gather(tie(seq_kv, grads_x, grads_y), size)
    grads_x, grads_y = tie_all([grads_x, grads_y], kv_gathered[2][0], kv_gathered[4][0])
    far_grads = (swap(grads_y[: rows // 2], 2, size), swap(grads_x[rows // 2 :], 4, size))
    grad_blocks = [(grad_out_b,), None, (grads_x,), None, (grads_y,), None, far_grads, None]
    kv_w, kv_first, second_t, small = assemble(
        kv_gathered, ((1, 2 * kv_width), (1, 2 * rank_all), (groups, rank_all), (1, LANES)), me, tag_blocks[:hops]
    )
    router_w = small[:, :experts]
    gains = small[:, experts : experts + 2].astype(F32).T
    second = own_columns(second_t).T
    first_kv = own_factors(kv_first)
    widths = [query_width, kv_width, kv_width, model, SHARED_HIDDEN, SHARED_HIDDEN, model]
    edges = [sum(widths[:n]) for n in range(len(widths) + 1)]
    b_parts = [second[:, edges[n] : edges[n + 1]] for n in range(len(widths))]

    x_flat = block_input[0].astype(F32)
    normed = rms_norm(x_flat, gains[0]).astype(BF16)
    low_kv = dot_nn(normed, first_kv).astype(BF16)
    kv_extra = jnp.concatenate([dot_nn(low_kv[:, :rank], b_parts[1]), dot_nn(low_kv[:, rank:], b_parts[2])], axis=1)
    kv_blocks = [(dot_nn(normed, kv_w) + kv_extra).astype(BF16)]
    q_blocks = plane_gather(tie(seq_q, *far_grads), size)
    for k in range(1, size, 2):
        grad_blocks[k] = tuple(swap(piece, 1, size) for piece in grad_blocks[k - 1])
    for h in range(hops):
        block = kv_blocks[-1] if h == 0 else tie(kv_blocks[-1], q_blocks[2][0], q_blocks[4][0])
        kv_blocks.append(lax.ppermute(block, "seq", forward))
        kv_blocks[h] = block
    kv_all = jnp.concatenate(kv_blocks[::-1], axis=0)

    down_rows = routed_down_weight.shape[1]
    second_cut = rank_all * routed_second_factor.shape[2] // down_rows
    up_shards, down_shards = [], []
    for j in range(local_experts):
        up_parts = [
            routed_gate_up_weight[j].reshape(-1, 2 * EXPERT_HIDDEN),
            routed_first_factor[j].reshape(-1, 2 * rank_all),
        ]
        down_parts = [
            routed_down_weight[j],
            routed_down_first_factor[j],
            routed_second_factor[j].reshape(down_rows, -1),
        ]
        if j == 0:
            gate_up = shared_gate_up_weight.reshape(shard_rows, 2, depth, size, units // depth)
            gate_up = gate_up.transpose(3, 0, 1, 2, 4).reshape(size, shard_rows, 2 * units)
            gate_up = lax.all_to_all(tie(gate_up, kv_gathered[2][0], kv_gathered[4][0]), "dp", split_axis=0, concat_axis=0, tiled=True)
            up_parts.append(gate_up.reshape(size * shard_rows, 2 * units))
            shared_down = jnp.concatenate([shared_down_weight, shared_down_first_factor], axis=1)
            down_parts.append(shared_down.reshape(down_rows, -1))
        up_shards.append(jnp.concatenate(up_parts, axis=1))
        down_shards.append(jnp.concatenate(down_parts, axis=1))
    seq_up, seq_down = [], []
    for j in range(local_experts):
        seq_up.append(over_seq(tie(up_shards[j], seq_q if j == 0 else seq_up[j - 1])))
        seq_down.append(over_seq(tie(down_shards[j], seq_q if j == 0 else seq_up[j - 1])))

    q_w, q_first, out_w = assemble(q_blocks, ((1, query_width), (1, 4 * rank_all), (1, model)), me)
    q_first = own_factors(q_first)
    first_q, first_o, first_gu = q_first[:, :rank], q_first[:, rank : 2 * rank], q_first[:, 2 * rank :]
    low_q = dot_nn(normed, first_q).astype(BF16)
    query = (dot_nn(normed, q_w) + dot_nn(low_q, b_parts[0])).astype(BF16)
    glow_sdown = dot_nt(grad_out_b, b_parts[6]).astype(BF16)
    attn, lse = attend(query, kv_all, query_tag, key_tag, hops, (*grad_blocks[3], *grad_blocks[5], *grad_blocks[7]))
    out_low = dot_nn(attn, first_o).astype(BF16)
    mid = x_flat + dot_nn(attn, out_w) + dot_nn(out_low, b_parts[3])
    normed2 = rms_norm(mid, gains[1]).astype(BF16)

    logits = dot_nn(normed2, router_w)
    top = jnp.max(jnp.where(flags > 0, logits, -jnp.inf), axis=-1, keepdims=True)
    weights = jnp.where(flags > 0, jnp.exp(logits - top), 0.0)
    gates = weights / jnp.sum(weights, axis=-1, keepdims=True)
    gates_hi = gates.astype(BF16)
    gates_lo = (gates - gates_hi.astype(F32)).astype(BF16)
    shared_low = dot_nn(normed2, first_gu).astype(BF16)
    own_adapter = jnp.full((rows, LANES - 3 * experts - 3 * rank), adapter.astype(F32)).astype(BF16)
    payload = jnp.concatenate([normed2, slots, gates_hi, gates_lo, shared_low, glow_sdown, own_adapter], axis=1)
    token_blocks = [None] * size
    token_blocks[0], token_blocks[1] = (payload,), (swap(payload, 1, size),)
    tokens_x, tokens_y = swap(payload, 2, size), swap(payload, 4, size)

    def gather_far(tokens_x, tokens_y, *done):
        tokens_x, tokens_y = tie_all([tokens_x, tokens_y], *done)
        half = rows // 2
        token_blocks[2], token_blocks[3] = (tokens_x,), (swap(tokens_x, 1, size),)
        token_blocks[4], token_blocks[5] = (tokens_y,), (swap(tokens_y, 1, size),)
        return swap(tokens_y[:half], 2, size), swap(tokens_x[half:], 4, size)

    def gather_farthest(far, *done):
        far = tuple(tie_all(far, *done))
        token_blocks[6], token_blocks[7] = far, tuple(swap(piece, 1, size) for piece in far)


    moe_parts, back_parts, grad_sums = [None] * size, [None] * size, []
    wide = model + rank_all

    def weights_of(j):
        second_j = seq_down[j][:, :, wide : wide + second_cut]
        second_j = second_j.reshape(depth, rank_all, -1).transpose(1, 0, 2).reshape(rank_all, -1)
        args = [seq_up[j].reshape(model, -1), seq_down[j][:, :, :wide].reshape(EXPERT_HIDDEN, wide), second_j]
        if j == 0:
            args.append(seq_down[j][:, :, wide + second_cut :].reshape(units, wide))
            slices = [
                lax.dynamic_slice_in_dim(second_t[edges[n] : edges[n + 1]].reshape(depth, size, -1, rank_all), me, 1, 1)
                for n in (4, 5)
            ]
            args.append(jnp.concatenate([part.reshape(units, rank_all) for part in slices], axis=0))
        return args

    def run_expert(j, args, group, prior, deps):
        meta = jnp.stack([me * local_experts + j, me]).astype(jnp.int32)
        prior = ([moe_parts[k] for k in group], [back_parts[k] for k in group]) if prior else None
        moe_out, back_out, grads = expert_call(
            meta,
            args,
            [token_blocks[k] for k in group],
            [grad_blocks[k] for k in group],
            prior,
            experts,
            capacity,
            deps,
        )
        for n, k in enumerate(group):
            moe_parts[k], back_parts[k] = moe_out[n], back_out[n]
        grad_sums[-1] = list(grads) if grad_sums[-1] is None else [a + b for a, b in zip(grad_sums[-1], grads)]

    for j in range(local_experts - 1):
        grad_sums.append(None)
        args = weights_of(j)
        previous = ()
        for group in ((0, 1), (2, 3), (4, 5), (6, 7)):
            run_expert(j, args, group, j > 0, previous)
            previous = (back_parts[group[0]],)
            if j == 0 and group == (0, 1):
                far = gather_far(tokens_x, tokens_y, *previous)
            if j == 0 and group == (2, 3):
                gather_farthest(far, *previous)
    if local_experts == 1:
        gather_farthest(gather_far(tokens_x, tokens_y))
    grad_sums.append(None)
    j, prior, half = local_experts - 1, local_experts > 1, (rows + BACK_ROWS) // 2
    args = weights_of(j)
    run_expert(j, args, (6, 7), prior, (back_parts[6],) if prior else ())
    pair_six = add(back_parts[6], swap(back_parts[7], 1, size))
    run_expert(j, args, (2, 3), prior, (pair_six,))
    from_diagonal_x, from_diagonal_y = swap(pair_six[:half], 2, size), swap(pair_six[half:], 4, size)
    pair_two = add(back_parts[2], swap(back_parts[3], 1, size))
    run_expert(j, args, (4, 5), prior, (pair_two,))
    pair_four = add(back_parts[4], swap(tie(back_parts[5], from_diagonal_x, from_diagonal_y), 1, size))
    to_x = jnp.concatenate([pair_two[:half], add(pair_two[half:], from_diagonal_y)], axis=0)
    to_y = jnp.concatenate([add(pair_four[:half], from_diagonal_x), pair_four[half:]], axis=0)
    run_expert(j, args, (0, 1), prior, (to_x, to_y))
    back_sum = add(back_parts[0], swap(back_parts[1], 1, size), swap(to_x, 2, size), swap(to_y, 4, size))
    back = back_sum.astype(F32)

    half = rows // 2
    far_parts = dict(zip((6, 2, 4, 0), tie_all([moe_parts[k + 1] for k in (6, 2, 4, 0)], back_sum)))
    pair = {k: add(moe_parts[k], swap(far_parts[k], 1, size)) for k in (6, 2, 4, 0)}
    moe_to_x = jnp.concatenate([pair[2][:half], add(pair[2][half:], swap(pair[6][half:], 4, size))], axis=0)
    moe_to_y = jnp.concatenate([add(pair[4][:half], swap(pair[6][:half], 2, size)), pair[4][half:]], axis=0)
    moe_from_x, moe_from_y = swap(moe_to_x, 2, size), swap(moe_to_y, 4, size)
    moe = pair[0].astype(F32) + moe_from_x.astype(F32) + moe_from_y.astype(F32)
    tail = back[:rows, model:]
    low_sdown = tail[:, 3 * experts + 2 * rank : 3 * experts + 3 * rank].astype(BF16)

    owner_rows = model // depth
    packed = [grads[0].astype(BF16).reshape(depth, owner_rows, 2 * rank_all) for grads in grad_sums]
    packed.append(
        jnp.concatenate([g[1] for g in grad_sums], axis=1).astype(BF16).reshape(depth, -1, 2 * rank_all)
    )
    for grads in grad_sums:
        packed.append(
            grads[2].astype(BF16).reshape(rank_all, depth, -1).transpose(1, 0, 2).reshape(depth, -1, 2 * rank_all)
        )
    packed.append(grad_sums[0][3].astype(BF16).reshape(depth, -1, 2 * rank_all))
    lines = [part.shape[1] for part in packed]
    packed_sum = lax.psum_scatter(jnp.concatenate(packed, axis=1), "seq", scatter_dimension=0, tiled=True)
    packed = packed_sum[0].astype(F32)
    cuts = [sum(lines[:n]) for n in range(len(lines) + 1)]
    pieces = [packed[cuts[n] : cuts[n + 1]] for n in range(len(lines))]
    grad_expert_a = jnp.stack(pieces[:local_experts]).reshape(local_experts, owner_rows, 2, rank_all)
    grad_expert_a_down = pieces[local_experts].reshape(down_rows, local_experts, rank_all).transpose(1, 0, 2)
    grad_expert_b = jnp.stack(pieces[local_experts + 1 : -1]).reshape(local_experts, rank_all, -1)
    grad_first_down = pieces[-1].reshape(shared_rows, rank_all)

    grad_out = grad_out_b.astype(F32)
    grad_gates = tail[:, :experts] + tail[:, experts : 2 * experts]
    glow_sgu = tail[:, 3 * experts : 3 * experts + 2 * rank].astype(BF16)
    grad_logits = gates * (grad_gates - jnp.sum(gates * grad_gates, axis=-1, keepdims=True))
    grad_normed2 = back[:rows, :model] + dot_nt(glow_sgu, first_gu)
    grad_normed2 = grad_normed2 + jnp.einsum(
        "re,de->rd", grad_logits, router_w.astype(F32), precision=lax.Precision.HIGHEST
    )
    _, norm2_back = jax.vjp(lambda values_in: rms_norm(values_in, gains[1]), mid)
    grad_mid = grad_out + norm2_back(grad_normed2)[0]
    grad_mid_b = grad_mid.astype(BF16)
    glow_out = dot_nt(grad_mid_b, b_parts[3]).astype(BF16)
    grad_attn = (dot_nt(grad_mid_b, out_w) + dot_nt(glow_out, first_o)).astype(BF16)

    def spread_out(flat, pieces):
        width = sum(p.size // (depth * size) for p in pieces)
        flat = flat.astype(F32)
        chosen = (flat[:, width : width + 1] == jnp.arange(rank_all // rank, dtype=F32)[None, :]).astype(F32)
        spread = jnp.sum(chosen[:, :, None] * flat[:, None, :width], axis=0)
        outs, at = [], 0
        for p in pieces:
            count = p.shape[0] // (depth * size)
            outs.append(spread[:, at : at + count * p.shape[1]].reshape(-1, count, p.shape[1]))
            at += count * p.shape[1]
        return outs

    def tagged(flat):
        return jnp.concatenate([flat, jnp.full((flat.shape[0], LANES), adapter.astype(F32)).astype(flat.dtype)], axis=1)

    def shared_columns(block):
        block = block[:, :SHARED_HIDDEN].reshape(rank, size, depth, units // depth)
        return block.transpose(0, 2, 1, 3).reshape(rank, SHARED_HIDDEN).T

    def pack_for_owners(pieces):
        return tagged(jnp.concatenate([p.astype(BF16).reshape(depth * size, -1) for p in pieces], axis=1))

    count = KV_HEADS // 2
    grad_q_one, grad_kv_one = attend_back(query, kv_all, grad_attn, lse, query_tag, key_tag, hops, 0, count, (pair[6], pair[2], pair[4]))
    one = grad_kv_one[:rows]
    hop_one = lax.ppermute(one, "seq", backward)
    grad_q_two, grad_kv_two = attend_back(
        query, kv_all, grad_attn, lse, query_tag, key_tag, hops, count, count, (moe_to_x, moe_to_y)
    )
    two = tie(grad_kv_two[:rows], hop_one)
    hop_two = lax.ppermute(two, "seq", backward)
    for h in range(hops):
        own = slice((h + 1) * rows, (h + 2) * rows)
        from_one = hop_one if h == 0 else lax.ppermute(one, "seq", backward)
        from_two = hop_two if h == 0 else lax.ppermute(tie(two, from_one), "seq", backward)
        one, two = add(grad_kv_one[own], from_one), add(grad_kv_two[own], from_two)
    late_deps = (hop_two, moe_from_x, moe_from_y)
    glow_out_t, glow_sgu_t, out_low_t, shared_rows_t, low_sdown_t, grad_q = tie_all(
        [glow_out, glow_sgu, out_low, back[rows:], low_sdown, jnp.concatenate([grad_q_one, grad_q_two], axis=1)],
        *late_deps,
    )
    hidden_out = (mid + moe + dot_nn(low_sdown_t, b_parts[6])).astype(BF16)[None]

    early = [
        jnp.concatenate([dot_tn(attn, glow_out_t), dot_tn(normed2, glow_sgu_t)], axis=1),
        jnp.concatenate(
            [
                jnp.zeros((query_width + 2 * kv_width, rank), F32),
                dot_tn(grad_mid_b, out_low_t),
                shared_columns(shared_rows_t[:rank]),
                shared_columns(shared_rows_t[rank:]),
                dot_tn(grad_out_b, low_sdown_t),
            ],
            axis=0,
        ),
    ]
    early_packed = pack_for_owners(early)
    early_flat = lax.all_to_all(early_packed, ("seq", "dp"), split_axis=0, concat_axis=0, tiled=True)
    one, two = tie_all([one, two], early_packed)
    grad_kvs = [half_[:, 2 * n * HEAD_DIM : 2 * (n + 1) * HEAD_DIM] for half_ in (one, two) for n in range(count)]
    glow_q = dot_nt(grad_q, b_parts[0]).astype(BF16)
    grad_normed = dot_nt(grad_q, q_w) + dot_nt(glow_q, first_q)
    grad_k = jnp.concatenate([piece[:, :HEAD_DIM] for piece in grad_kvs], axis=1)
    grad_v = jnp.concatenate([piece[:, HEAD_DIM:] for piece in grad_kvs], axis=1)
    glow_kv = jnp.concatenate([dot_nt(grad_k, b_parts[1]), dot_nt(grad_v, b_parts[2])], axis=1).astype(BF16)
    late = [
        jnp.concatenate([dot_tn(normed, glow_q), dot_tn(normed, glow_kv)], axis=1).astype(BF16),
        jnp.concatenate(
            [
                dot_tn(grad_q, low_q).astype(BF16),
                dot_tn(grad_k, low_kv[:, :rank]).astype(BF16),
                dot_tn(grad_v, low_kv[:, rank:]).astype(BF16),
                jnp.zeros((edges[-1] - edges[3], rank), BF16),
            ],
            axis=0,
        ),
    ]
    late_flat = lax.all_to_all(pack_for_owners(late), ("seq", "dp"), split_axis=0, concat_axis=0, tiled=True)
    grad_normed = grad_normed + dot_nt(jnp.concatenate([grad_k, grad_v], axis=1), kv_w) + dot_nt(glow_kv, first_kv)
    _, norm1_back = jax.vjp(lambda values_in: rms_norm(values_in, gains[0]), x_flat)
    grad_hidden = (grad_mid + norm1_back(grad_normed)[0])[None]
    early_parts, late_parts = spread_out(early_flat, early), spread_out(late_flat, late)
    grad_first = jnp.concatenate([late_parts[0], early_parts[0]], axis=2)
    grad_first = grad_first.reshape(-1, shard_rows, 6, rank).transpose(1, 2, 0, 3).reshape(shard_rows, 6, rank_all)
    grad_second = (early_parts[1] + late_parts[1]).transpose(0, 2, 1).reshape(rank_all, second_columns)
    return (
        hidden_out,
        grad_hidden,
        grad_first,
        grad_first_down,
        grad_second,
        grad_expert_a,
        grad_expert_a_down,
        grad_expert_b,
    )


def solution(mesh):
    in_specs = (
        P("dp", "seq", None),
        P("dp", "seq"),
        P("dp", "seq"),
        P("dp", "seq", None),
        P("dp"),
        P("dp", "seq", None),
        P(None, ("seq", "dp")),
        P(("seq", "dp"), None),
        P(("seq", "dp"), None),
        P(("seq", "dp"), None),
        P(("seq", "dp"), None, None),
        P(("seq", "dp"), None),
        P("dp", "seq", None, None),
        P("dp", "seq", None),
        P(("seq", "dp"), None, None),
        P(("seq", "dp"), None),
        P(None, ("seq", "dp")),
        P("dp", "seq", None, None),
        P("dp", "seq", None),
        P("dp", None, "seq"),
    )
    out_specs = (
        P("dp", "seq", None),
        P("dp", "seq", None),
        P(("seq", "dp"), None, None),
        P(("seq", "dp"), None),
        P(None, ("seq", "dp")),
        P("dp", "seq", None, None),
        P("dp", "seq", None),
        P("dp", None, "seq"),
    )
    return jax.shard_map(
        functools.partial(per_device, mesh.shape["seq"], mesh.shape["dp"]),
        mesh=mesh,
        in_specs=in_specs,
        out_specs=out_specs,
        check_vma=False,
    )
```

```python
import functools
import math

import jax
import jax.numpy as jnp
from jax import lax
from jax.experimental import pallas as pl
from jax.experimental.pallas import tpu as pltpu
from jax.sharding import PartitionSpec as P

HEADS = 12
KV_HEADS = 4
HEAD_DIM = 128
EXPERT_HIDDEN = 512
SHARED_HIDDEN = 1024
ADAPTER_RANK = 16
DOCUMENT_SPAN = 1024

EPSILON = 1e-05
MASKED_SCORE = -1e30
LOG2E = 1.4426950408889634
SCALE = HEAD_DIM ** (-0.5)
LANES = 128
VMEM_LIMIT = 60 * 1024 * 1024

F32 = jnp.float32
BF16 = jnp.bfloat16


def dot_nn(left, right):
    return jnp.dot(left, right, preferred_element_type=F32)


def dot_tn(left, right):
    return lax.dot_general(left, right, (((0,), (0,)), ((), ())), preferred_element_type=F32)


def dot_nt(left, right):
    return lax.dot_general(left, right, (((1,), (1,)), ((), ())), preferred_element_type=F32)


def rms_norm(values, gain):
    return values * lax.rsqrt(jnp.mean(values * values, axis=-1, keepdims=True) + EPSILON) * gain


def cost(microseconds):
    return pl.CostEstimate(flops=int(1153500000 * microseconds), bytes_accessed=1000000, transcendentals=0)


def query_tiles(rows, hops):
    tile = math.gcd(rows, 256)
    spans = []
    for first in range(0, rows, tile):
        oldest = max(0, hops * rows + first - (DOCUMENT_SPAN - 1)) // tile * tile
        spans.append((first, tile, oldest, hops * rows + first + tile - oldest))
    return spans


def fill_bias(spans, shift, query_tag, key_tag, bias):
    for first, tile, oldest, span in spans:
        keys = oldest + lax.broadcasted_iota(jnp.int32, (span, tile), 0)
        queries = shift + first + lax.broadcasted_iota(jnp.int32, (span, tile), 1)
        same = key_tag[oldest : oldest + span, :] == query_tag[:, first : first + tile]
        permit = (keys <= queries) & (same | (keys == queries))
        bias[oldest : oldest + span, first : first + tile] = jnp.where(permit, 0.0, MASKED_SCORE)


def attend_kernel(spans, shift, waits, q_ref, k_ref, v_ref, qt_ref, kt_ref, *rest):
    out_ref, lse_ref, bias = rest[waits:]

    @pl.when(pl.program_id(0) == 0)
    def _():
        fill_bias(spans, shift, qt_ref, kt_ref, bias)

    groups = q_ref.shape[1] // HEAD_DIM
    for first, tile, oldest, span in spans:
        keys = k_ref[oldest : oldest + span, :]
        values = v_ref[oldest : oldest + span, :]
        mask = bias[oldest : oldest + span, first : first + tile]
        for h in range(groups):
            columns = slice(h * HEAD_DIM, (h + 1) * HEAD_DIM)
            scores = dot_nt(keys, q_ref[first : first + tile, columns]) * (SCALE * LOG2E) + mask
            top = jnp.max(scores, axis=0, keepdims=True)
            weights = jnp.exp2(scores - top)
            total = jnp.sum(weights, axis=0, keepdims=True)
            mixed = dot_tn(values, weights.astype(BF16)) / total
            out_ref[first : first + tile, columns] = mixed.T.astype(BF16)
            lse_ref[0, h : h + 1, first : first + tile] = top + jnp.log2(total)


def attend(query, kv_all, query_tag, key_tag, hops, deps=()):
    rows = query.shape[0]
    groups = HEADS // KV_HEADS
    span = kv_all.shape[0]
    spans = query_tiles(rows, hops)
    return pl.pallas_call(
        functools.partial(attend_kernel, spans, hops * rows, len(deps)),
        grid=(KV_HEADS,),
        in_specs=[
            pl.BlockSpec((rows, groups * HEAD_DIM), lambda g: (0, g)),
            pl.BlockSpec((span, HEAD_DIM), lambda g: (0, g)),
            pl.BlockSpec((span, HEAD_DIM), lambda g: (0, KV_HEADS + g)),
            pl.BlockSpec((1, rows), lambda g: (0, 0)),
            pl.BlockSpec((span, 1), lambda g: (0, 0)),
        ]
        + [pl.BlockSpec(memory_space=pl.ANY)] * len(deps),
        out_specs=[
            pl.BlockSpec((rows, groups * HEAD_DIM), lambda g: (0, g)),
            pl.BlockSpec((1, groups, rows), lambda g: (g, 0, 0)),
        ],
        out_shape=[
            jax.ShapeDtypeStruct((rows, HEADS * HEAD_DIM), BF16),
            jax.ShapeDtypeStruct((KV_HEADS, groups, rows), F32),
        ],
        scratch_shapes=[pltpu.VMEM((span, rows), F32)],
        compiler_params=pltpu.CompilerParams(vmem_limit_bytes=VMEM_LIMIT),
        cost_estimate=cost(23.0),
        name="attend",
    )(query, kv_all, kv_all, query_tag, key_tag, *deps)


def attend_back_kernel(
    spans, shift, waits, q_ref, k_ref, v_ref, g_ref, lse_ref, qt_ref, kt_ref, *rest
):
    dq_ref, dkv_ref, bias, dk_acc, dv_acc = rest[waits:]

    @pl.when(pl.program_id(0) == 0)
    def _():
        fill_bias(spans, shift, qt_ref, kt_ref, bias)

    dk_acc[...] = jnp.zeros_like(dk_acc)
    dv_acc[...] = jnp.zeros_like(dv_acc)
    groups = q_ref.shape[1] // HEAD_DIM
    for first, tile, oldest, span in spans:
        keys = k_ref[oldest : oldest + span, :]
        values = v_ref[oldest : oldest + span, :]
        mask = bias[oldest : oldest + span, first : first + tile]
        for h in range(groups):
            columns = slice(h * HEAD_DIM, (h + 1) * HEAD_DIM)
            query = q_ref[first : first + tile, columns]
            grad = g_ref[first : first + tile, columns]
            lse = lse_ref[0, h : h + 1, first : first + tile]
            probs = jnp.exp2(dot_nt(keys, query) * (SCALE * LOG2E) + mask - lse)
            dv_acc[oldest : oldest + span, :] += dot_nn(probs.astype(BF16), grad)
            grad_probs = dot_nt(values, grad)
            delta = jnp.sum(probs * grad_probs, axis=0, keepdims=True)
            grad_scores = (probs * (grad_probs - delta)).astype(BF16)
            dk_acc[oldest : oldest + span, :] += dot_nn(grad_scores, query) * SCALE
            dq_ref[first : first + tile, columns] = (dot_tn(grad_scores, keys) * SCALE).astype(BF16)
    dkv_ref[:, :HEAD_DIM] = dk_acc[...].astype(dkv_ref.dtype)
    dkv_ref[:, HEAD_DIM:] = dv_acc[...].astype(dkv_ref.dtype)


def attend_back(query, kv_all, grad_attn, lse, query_tag, key_tag, hops, head, count, deps=()):
    rows = query.shape[0]
    groups = HEADS // KV_HEADS
    span = kv_all.shape[0]
    spans = query_tiles(rows, hops)
    return pl.pallas_call(
        functools.partial(attend_back_kernel, spans, hops * rows, len(deps)),
        grid=(count,),
        in_specs=[
            pl.BlockSpec((rows, groups * HEAD_DIM), lambda g: (0, head + g)),
            pl.BlockSpec((span, HEAD_DIM), lambda g: (0, head + g)),
            pl.BlockSpec((span, HEAD_DIM), lambda g: (0, KV_HEADS + head + g)),
            pl.BlockSpec((rows, groups * HEAD_DIM), lambda g: (0, head + g)),
            pl.BlockSpec((1, groups, rows), lambda g: (head + g, 0, 0)),
            pl.BlockSpec((1, rows), lambda g: (0, 0)),
            pl.BlockSpec((span, 1), lambda g: (0, 0)),
        ]
        + [pl.BlockSpec(memory_space=pl.ANY)] * len(deps),
        out_specs=[
            pl.BlockSpec((rows, groups * HEAD_DIM), lambda g: (0, g)),
            pl.BlockSpec((span, 2 * HEAD_DIM), lambda g: (0, g)),
        ],
        out_shape=[
            jax.ShapeDtypeStruct((rows, count * groups * HEAD_DIM), BF16),
            jax.ShapeDtypeStruct((span, count * 2 * HEAD_DIM), BF16),
        ],
        scratch_shapes=[
            pltpu.VMEM((span, rows), F32),
            pltpu.VMEM((span, HEAD_DIM), F32),
            pltpu.VMEM((span, HEAD_DIM), F32),
        ],
        compiler_params=pltpu.CompilerParams(vmem_limit_bytes=VMEM_LIMIT),
        cost_estimate=cost(2.0 * count),
        name="attend_back",
    )(query, kv_all, kv_all, grad_attn, lse, query_tag, key_tag, *deps)


BACK_ROWS = 2 * ADAPTER_RANK


def expert_kernel(count, splits, experts, capacity, depth, with_prior, with_shared, with_sums, packed, waits, *refs):
    meta, refs = refs[0], refs[1:]
    weight_count = 5 if with_shared else 3
    weight_refs, refs = refs[:weight_count], refs[weight_count:]
    token_refs, grad_refs = [], []
    for split in splits:
        token_refs.append(refs[:split])
        refs = refs[split:]
    for split in splits:
        grad_refs.append(refs[:split])
        refs = refs[split:]
    prior_moe, prior_back = (), ()
    if with_prior:
        prior_moe, refs = refs[:count], refs[count:]
        prior_back, refs = refs[:count], refs[count:]
    grad_count = 4 if with_shared else 3
    sums_in = ()
    if with_sums:
        sums_in, refs = refs[:grad_count], refs[grad_count:]
    refs = refs[waits:]
    moe_refs, refs = refs[:count], refs[count:]
    back_refs, refs = refs[:count], refs[count:]
    out_count = 1 if packed else grad_count
    grad_outs, refs = refs[:out_count], refs[out_count:]
    grad_sums, refs = refs[:grad_count], refs[grad_count:]
    first_grad, down_grad, second_grad = grad_sums[:3]
    weight_bufs, refs = refs[:weight_count], refs[weight_count:]
    if packed:
        pack_buf, refs = refs[0], refs[1:]
    tokens_buf, grad_buf, moe_buf, back_buf, in_sem, out_sem, weight_sem, sum_sem, sum_in_sem = refs

    step = pl.program_id(0)
    steps = count // 2
    slots = min(2, steps)
    slot = lax.rem(step, slots)
    rows, wide = tokens_buf.shape[2:]
    model = wide - LANES
    hidden = EXPERT_HIDDEN
    rank = ADAPTER_RANK
    up_ref, down_ref, second_ref = weight_bufs[:3]

    def weight_copy(n):
        return pltpu.make_async_copy(weight_refs[n], weight_bufs[n], weight_sem.at[n])

    def incoming(k, i, kinds):
        copies = []
        to, source = k % slots, 2 * k + i
        for n, (refs_of, buf) in enumerate(((token_refs, tokens_buf), (grad_refs, grad_buf))):
            size = rows // len(refs_of[source])
            for p, piece in enumerate(refs_of[source] if n in kinds else ()):
                part = buf.at[to, i, pl.ds(p * size, size)]
                copies.append(pltpu.make_async_copy(piece, part, in_sem.at[to, i, 2 * n + p]))
        if with_prior and 2 in kinds:
            copies.append(pltpu.make_async_copy(prior_moe[source], moe_buf.at[to, i], in_sem.at[to, i, 4]))
            copies.append(pltpu.make_async_copy(prior_back[source], back_buf.at[to, i], in_sem.at[to, i, 5]))
        return copies

    def outgoing(k, i, kinds=(0, 1)):
        at, source = k % slots, 2 * k + i
        pairs = ((moe_buf, moe_refs), (back_buf, back_refs))
        return [pltpu.make_async_copy(pairs[n][0].at[at, i], pairs[n][1][source], out_sem.at[at, i, n]) for n in kinds]

    def at_step(action, first=0, last=steps):
        for k in range(first, last):
            pl.when(step == k)(functools.partial(action, k))

    def wait_in(i, kind):
        def action(k):
            for copy in incoming(k, i, (kind,)):
                copy.wait()

        at_step(action)

    def start_out(i, n):
        at_step(lambda k: outgoing(k, i, (n,))[0].start())

    def turn(k):
        for i in (0, 1):
            if k >= 1:
                for copy in outgoing(k - 1, i):
                    copy.wait()
            if k + 1 < steps:
                for copy in incoming(k + 1, i, (0, 1, 2)):
                    copy.start()

    def sum_copy(n):
        return pltpu.make_async_copy(pack_buf if packed else grad_sums[n], grad_outs[n], sum_sem.at[n])

    def sum_in(n):
        return pltpu.make_async_copy(sums_in[n], grad_sums[n], sum_in_sem.at[n])

    @pl.when(step == 0)
    def _():
        for i in (0, 1):
            for copy in incoming(0, i, (0,)):
                copy.start()
        for i in (0, 1):
            for copy in incoming(0, i, (1,)):
                copy.start()
        for n in range(weight_count):
            weight_copy(n).start()
        for i in (0, 1):
            for copy in incoming(0, i, (2,)):
                copy.start()
        for n, total in enumerate(grad_sums):
            if with_sums:
                sum_in(n).start()
            else:
                total[...] = jnp.zeros_like(total)

    expert = meta[0]
    lane = lax.broadcasted_iota(jnp.int32, (1, LANES), 1)
    sub = lax.broadcasted_iota(jnp.int32, (LANES, 1), 0)
    places, picks, gates_of, selects, adapters = [], [], [], [], []
    inputs, grad_rows = [], []
    for i in (0, 1):
        wait_in(i, 0)
        extra_b = tokens_buf[slot, i, :, model:]
        extra = extra_b.astype(F32)
        own = 3 * experts + 3 * rank
        adapter = extra[0:1, own : own + 1]
        select = ((lane // rank).astype(F32) == adapter).astype(F32)
        slot_column = jnp.sum(jnp.where(lane == expert, extra, 0.0), axis=1, keepdims=True)
        slot_row = jnp.sum(jnp.where(sub == expert, extra.T, 0.0), axis=0, keepdims=True)
        place = lax.broadcasted_iota(jnp.int32, (rows, capacity), 1).astype(F32) == slot_column
        pick = lax.broadcasted_iota(jnp.int32, (capacity, rows), 0).astype(F32) == slot_row
        place, pick = place.astype(F32).astype(BF16), pick.astype(F32).astype(BF16)
        picked_extra = dot_nn(pick, extra_b)
        chosen = (lane == experts + expert) | (lane == 2 * experts + expert)
        gates_of.append(jnp.sum(jnp.where(chosen, picked_extra, 0.0), axis=1, keepdims=True))
        inputs.append(dot_nn(pick, tokens_buf[slot, i, :, :model]).astype(BF16))
        picks.append(pick)
        places.append(place)
        adapters.append(adapter)
        selects.append(jnp.broadcast_to(select, (capacity, LANES)))
    for i in (0, 1):
        wait_in(i, 1)
        grad_rows.append(dot_nn(picks[i], grad_buf[slot, i]))
    at_step(turn)
    inputs = jnp.concatenate(inputs, axis=0)
    grad_rows = jnp.concatenate(grad_rows, axis=0)
    gate = jnp.concatenate(gates_of, axis=0)
    select = jnp.concatenate(selects, axis=0)
    select_two = jnp.concatenate([select, select], axis=1)

    @pl.when(step == 0)
    def _():
        for n in range(weight_count):
            weight_copy(n).wait()

    low = (dot_nn(inputs, up_ref[:, 2 * hidden : 2 * hidden + 2 * LANES]) * select_two).astype(BF16)
    gate_part = dot_nn(inputs, up_ref[:, :hidden]) + dot_nn(low[:, :LANES], second_ref[:, :hidden])
    up_part = dot_nn(inputs, up_ref[:, hidden : 2 * hidden]) + dot_nn(low[:, LANES:], second_ref[:, hidden : 2 * hidden])
    sigmoid = 1.0 / (1.0 + jnp.exp(-gate_part))
    silu = gate_part * sigmoid
    act = (silu * up_part).astype(BF16)
    low_down = (dot_nn(act, down_ref[:, model:]) * select).astype(BF16)
    output = (dot_nn(act, down_ref[:, :model]) + dot_nn(low_down, second_ref[:, 2 * hidden :])).astype(BF16).astype(F32)
    grad_gate = jnp.sum(output * grad_rows, axis=1, keepdims=True)
    weighted = (gate * output).astype(BF16)

    if with_sums:

        @pl.when(step == 0)
        def _():
            for n in range(grad_count):
                sum_in(n).wait()

    grad_y = (gate * grad_rows).astype(BF16)
    glow_down = (dot_nt(grad_y, second_ref[:, 2 * hidden :]) * select).astype(BF16)
    second_grad[:, 2 * hidden :] += dot_tn(low_down, grad_y)
    down_grad[...] += dot_tn(act, glow_down)
    grad_act = dot_nt(grad_y, down_ref[:, :model]) + dot_nt(glow_down, down_ref[:, model:])
    grad_up = (grad_act * silu).astype(BF16)
    grad_gp = (grad_act * up_part * (sigmoid * (1.0 + gate_part * (1.0 - sigmoid)))).astype(BF16)
    glow = jnp.concatenate(
        [
            dot_nt(grad_gp, second_ref[:, :hidden]) * select,
            dot_nt(grad_up, second_ref[:, hidden : 2 * hidden]) * select,
        ],
        axis=1,
    ).astype(BF16)
    second_grad[:, :hidden] += dot_tn(low[:, :LANES], grad_gp)
    second_grad[:, hidden : 2 * hidden] += dot_tn(low[:, LANES:], grad_up)
    first_grad[...] += dot_tn(inputs, glow)
    grad_in = (
        dot_nt(grad_gp, up_ref[:, :hidden])
        + dot_nt(grad_up, up_ref[:, hidden : 2 * hidden])
        + dot_nt(glow, up_ref[:, 2 * hidden : 2 * hidden + 2 * LANES])
    ).astype(BF16)
    gate_hi = grad_gate.astype(BF16).astype(F32)
    gate_lo = grad_gate - gate_hi
    extra_out = (
        jnp.where(lane == expert, gate_hi, 0.0) + jnp.where(lane == experts + expert, gate_lo, 0.0)
    ).astype(BF16)

    @pl.when(step == steps - 1)
    def _():
        if not packed:
            for n in range(3):
                sum_copy(n).start()
            return
        second_t = second_grad[...].T
        parts = [first_grad[:, :LANES], first_grad[:, LANES:], down_grad[...], second_t]
        at = 0
        for part in parts:
            size = part.shape[0] // depth
            for z in range(depth):
                pack_buf[z, at : at + size, :] = part[z * size : (z + 1) * size].astype(BF16)
            at += size

    for i in (0, 1):
        mine = slice(i * capacity, (i + 1) * capacity)
        wait_in(i, 2)
        moe = dot_nn(places[i], weighted[mine])
        back = dot_nn(places[i], grad_in[mine])
        back_extra = dot_nn(places[i], extra_out[mine])
        if with_prior:
            moe = moe + moe_buf[slot, i].astype(F32)
            back = back + back_buf[slot, i, :rows, :model].astype(F32)
            back_extra = back_extra + back_buf[slot, i, :rows, model:].astype(F32)
        if not with_prior:
            back_buf[slot, i, rows:, :] = jnp.zeros((BACK_ROWS, wide), BF16)
        if with_shared:
            sdown_ref, sb_ref = weight_bufs[3:]
            units = sdown_ref.shape[0]
            first_gate, first_up, first_down = 3 * experts, 3 * experts + rank, 3 * experts + 2 * rank
            tokens = tokens_buf[slot, i, :, :model]
            extra_b = tokens_buf[slot, i, :, model:]
            grads = grad_buf[slot, i]
            offset = (lane - sub).astype(F32) - adapters[i] * float(rank)

            def spread(base):
                inside = (sub >= base) & (sub < base + rank)
                return (inside & (offset == float(-base))).astype(F32).astype(BF16)

            to_gate = dot_nt(spread(first_gate), sb_ref[:units]).astype(BF16)
            to_up = dot_nt(spread(first_up), sb_ref[units:]).astype(BF16)
            to_down = dot_nt(spread(first_down), sdown_ref[:, model:]).astype(BF16)
            shared_up = up_ref[:, 2 * hidden + 2 * LANES :]
            gate_up = dot_nn(tokens, shared_up)
            s_gate = gate_up[:, :units] + dot_nn(extra_b, to_gate)
            s_up = gate_up[:, units:] + dot_nn(extra_b, to_up)
            s_sig = 1.0 / (1.0 + jnp.exp(-s_gate))
            s_silu = s_gate * s_sig
            s_act = (s_silu * s_up).astype(BF16)
            moe = moe + dot_nn(s_act, sdown_ref[:, :model])
            s_grad = dot_nt(grads, sdown_ref[:, :model]) + dot_nn(extra_b, to_down)
            grad_sums[3][...] += dot_tn(s_act, dot_nn(extra_b, spread(first_down)).astype(BF16))
            s_gu = (s_grad * s_silu).astype(BF16)
            s_gg = (s_grad * s_up * (s_sig * (1.0 + s_gate * (1.0 - s_sig)))).astype(BF16)
            back_extra = back_extra + dot_nt(s_act, to_down) + dot_nt(s_gg, to_gate) + dot_nt(s_gu, to_up)
            back = back + dot_nt(jnp.concatenate([s_gg, s_gu], axis=1), shared_up)
            columns = pl.ds(pl.multiple_of(meta[1] * units, units), units)
            grad_bg = dot_tn(extra_b, s_gg)[first_gate : first_gate + rank]
            grad_bu = dot_tn(extra_b, s_gu)[first_up : first_up + rank]
            back_buf[slot, i, rows : rows + rank, columns] = grad_bg.astype(BF16)
            back_buf[slot, i, rows + rank :, columns] = grad_bu.astype(BF16)
        moe_buf[slot, i] = moe.astype(BF16)
        start_out(i, 0)
        back_buf[slot, i, :rows, :model] = back.astype(BF16)
        back_buf[slot, i, :rows, model:] = back_extra.astype(BF16)
        start_out(i, 1)

    @pl.when(step == steps - 1)
    def _():
        if packed and with_shared:
            size = grad_sums[3].shape[0] // depth
            for z in range(depth):
                part = grad_sums[3][z * size : (z + 1) * size, :]
                if size % 16:
                    part = jnp.concatenate([part, jnp.zeros((16 - size % 16, LANES), F32)], axis=0)
                pack_buf[z, pack_buf.shape[1] - part.shape[0] :, :] = part.astype(BF16)
        for n in range(0 if packed else 3, out_count):
            sum_copy(n).start()
        for i in (0, 1):
            for copy in outgoing(steps - 1, i):
                copy.wait()
        for n in range(out_count):
            sum_copy(n).wait()


def expert_call(meta, weights, tokens, grads, prior, sums, packed, experts, capacity, depth, deps=()):
    count = len(tokens)
    with_shared = len(weights) > 3
    splits = [len(pieces) for pieces in tokens]
    rows, model = sum(piece.shape[0] for piece in grads[0]), grads[0][0].shape[1]
    wide = model + LANES
    slots = min(2, count // 2)
    anywhere = pl.BlockSpec(memory_space=pl.ANY)
    prior = [] if prior is None else list(prior[0]) + list(prior[1])
    flat = [piece for pieces in tokens for piece in pieces] + [piece for pieces in grads for piece in pieces]
    grad_shapes = [
        jax.ShapeDtypeStruct((model, 2 * LANES), F32),
        jax.ShapeDtypeStruct((EXPERT_HIDDEN, LANES), F32),
        jax.ShapeDtypeStruct(weights[2].shape, F32),
    ]
    if with_shared:
        grad_shapes.append(jax.ShapeDtypeStruct((weights[3].shape[0], LANES), F32))
    out_shapes = grad_shapes
    if packed:
        lines = sum(s.shape[0] for s in grad_shapes[:2]) + model + weights[2].shape[1]
        lines = lines // depth
        if with_shared:
            lines += -(-weights[3].shape[0] // depth // 16) * 16
        out_shapes = [jax.ShapeDtypeStruct((depth, lines, LANES), BF16)]
    back_rows = rows + BACK_ROWS
    outs = pl.pallas_call(
        functools.partial(
            expert_kernel, count, splits, experts, capacity, depth, bool(prior), with_shared, bool(sums), packed, len(deps)
        ),
        grid=(count // 2,),
        in_specs=[pl.BlockSpec(memory_space=pltpu.SMEM)]
        + [anywhere] * (len(weights) + len(flat) + len(prior) + len(sums) + len(deps)),
        out_specs=[anywhere] * (2 * count + len(out_shapes)),
        out_shape=[jax.ShapeDtypeStruct((rows, model), BF16)] * count
        + [jax.ShapeDtypeStruct((back_rows, wide), BF16)] * count
        + out_shapes,
        scratch_shapes=[pltpu.VMEM(s.shape, F32) for s in grad_shapes]
        + [pltpu.VMEM(w.shape, BF16) for w in weights]
        + ([pltpu.VMEM(out_shapes[0].shape, BF16)] if packed else [])
        + [
            pltpu.VMEM((slots, 2, rows, wide), BF16),
            pltpu.VMEM((slots, 2, rows, model), BF16),
            pltpu.VMEM((slots, 2, rows, model), BF16),
            pltpu.VMEM((slots, 2, back_rows, wide), BF16),
            pltpu.SemaphoreType.DMA((slots, 2, 6)),
            pltpu.SemaphoreType.DMA((slots, 2, 2)),
            pltpu.SemaphoreType.DMA((len(weights),)),
            pltpu.SemaphoreType.DMA((len(grad_shapes),)),
            pltpu.SemaphoreType.DMA((len(grad_shapes),)),
        ],
        compiler_params=pltpu.CompilerParams(vmem_limit_bytes=VMEM_LIMIT),
        cost_estimate=cost(12.0 * count),
        name="expert",
    )(meta, *weights, *flat, *prior, *sums, *deps)
    return outs[:count], outs[count : 2 * count], outs[2 * count :]


def swap(array, bit, size):
    return lax.ppermute(array, "dp", [(i, i ^ bit) for i in range(size)])


def plane_gather(array, size):
    half = array.shape[0] // 2
    x, y = swap(array, 2, size), swap(array, 4, size)
    across = {0: (array,), 2: (x,), 4: (y,), 6: (swap(y[:half], 2, size), swap(x[half:], 4, size))}
    blocks = [None] * size
    for k in (0, 2, 4, 6):
        blocks[k] = across[k]
        blocks[k + 1] = tuple(swap(piece, 1, size) for piece in across[k])
    return blocks


def add(*terms):
    total = terms[0].astype(F32)
    for term in terms[1:]:
        total = total + term.astype(F32)
    return total.astype(BF16)


def tie_kernel(*refs):
    del refs


def tie_all(arrays, *others):
    anywhere = pl.BlockSpec(memory_space=pl.ANY)
    return pl.pallas_call(
        tie_kernel,
        in_specs=[anywhere] * (len(arrays) + len(others)),
        out_specs=[anywhere] * len(arrays),
        out_shape=[jax.ShapeDtypeStruct(array.shape, array.dtype) for array in arrays],
        input_output_aliases={n: n for n in range(len(arrays))},
        name="tie",
    )(*arrays, *others)


def tie(array, *others):
    return tie_all([array], *others)[0]


def assemble_kernel(splits, widths, waits, me_ref, *refs):
    pieces, outs = refs[: sum(splits)], refs[sum(splits) + waits : -3]
    whole, in_sem, out_sem = refs[-3:]
    copies, at = [], 0
    for k, split in enumerate(splits):
        start = 0
        for piece in pieces[at : at + split]:
            target = whole.at[pl.ds(start, piece.shape[0]), me_ref[0] ^ k]
            copies.append(pltpu.make_async_copy(piece, target, in_sem.at[len(copies)]))
            start += piece.shape[0]
        at += split
    for copy in copies:
        copy.start()
    for copy in copies:
        copy.wait()
    copies, column = [], 0
    for out, (count, width) in zip(outs, widths):
        for n in range(count):
            source = whole.at[:, :, :, pl.ds(column, width)]
            copies.append(pltpu.make_async_copy(source, out.at[:, :, n], out_sem.at[len(copies)]))
            column += width
    for copy in copies:
        copy.start()
    for copy in copies:
        copy.wait()


def assemble(blocks, widths, me, deps=()):
    depth, rows, _ = blocks[0][0].shape
    size = len(blocks)
    splits = [len(pieces) for pieces in blocks]
    flat = [piece for pieces in blocks for piece in pieces]
    outs = pl.pallas_call(
        functools.partial(assemble_kernel, splits, widths, len(deps)),
        in_specs=[pl.BlockSpec(memory_space=pltpu.SMEM)] + [pl.BlockSpec(memory_space=pl.ANY)] * (len(flat) + len(deps)),
        out_specs=[pl.BlockSpec(memory_space=pl.ANY)] * len(widths),
        out_shape=[jax.ShapeDtypeStruct((depth, size, count, rows, width), BF16) for count, width in widths],
        scratch_shapes=[
            pltpu.VMEM((depth, size, rows, sum(count * width for count, width in widths)), BF16),
            pltpu.SemaphoreType.DMA((len(flat),)),
            pltpu.SemaphoreType.DMA((sum(count for count, _ in widths),)),
        ],
        compiler_params=pltpu.CompilerParams(vmem_limit_bytes=VMEM_LIMIT),
        name="assemble",
    )(me.astype(jnp.int32).reshape(1), *flat, *deps)
    return [out.reshape(-1, out.shape[-1]) for out in outs]


def query_back_kernel(q_one, q_two, normed, low_q, q_w, first_q, second_q, grad_normed, first_query, second_query):
    half = q_one.shape[1]
    glow_q = (dot_nt(q_one[...], second_q[:, :half]) + dot_nt(q_two[...], second_q[:, half:])).astype(BF16)
    grad_normed[...] = (
        dot_nt(q_one[...], q_w[:, :half]) + dot_nt(q_two[...], q_w[:, half:]) + dot_nt(glow_q, first_q[...])
    )
    first_query[...] = dot_tn(normed[...], glow_q)
    second_query[:, :half] = dot_tn(low_q[...], q_one[...])
    second_query[:, half:] = dot_tn(low_q[...], q_two[...])


def query_back(args):
    rows, model = args[2].shape
    vmem = pl.BlockSpec(memory_space=pltpu.VMEM)
    shapes = [(rows, model), (model, ADAPTER_RANK), (ADAPTER_RANK, HEADS * HEAD_DIM)]
    return pl.pallas_call(
        query_back_kernel,
        in_specs=[vmem] * len(args),
        out_specs=[vmem] * len(shapes),
        out_shape=[jax.ShapeDtypeStruct(shape, F32) for shape in shapes],
        compiler_params=pltpu.CompilerParams(vmem_limit_bytes=VMEM_LIMIT),
        cost_estimate=cost(2.0),
        name="query_back",
    )(*args)


def middle_kernel(waits, attn, glow_out, normed2, glow_sgu, grad_mid, out_low, grad_out, low_sdown, *rest):
    first_early, second_out, second_down = rest[waits:]
    rank = ADAPTER_RANK
    first_early[:, :rank] = dot_tn(attn[...], glow_out[...])
    first_early[:, rank:] = dot_tn(normed2[...], glow_sgu[...])
    second_out[...] = dot_tn(out_low[...], grad_mid[...])
    second_down[...] = dot_tn(low_sdown[...], grad_out[...])


def middle(args, deps):
    model = args[0].shape[1]
    rank = ADAPTER_RANK
    vmem = pl.BlockSpec(memory_space=pltpu.VMEM)
    shapes = [(model, 3 * rank), (rank, model), (rank, model)]
    return pl.pallas_call(
        functools.partial(middle_kernel, len(deps)),
        in_specs=[vmem] * len(args) + [pl.BlockSpec(memory_space=pl.ANY)] * len(deps),
        out_specs=[vmem] * len(shapes),
        out_shape=[jax.ShapeDtypeStruct(shape, F32) for shape in shapes],
        compiler_params=pltpu.CompilerParams(vmem_limit_bytes=VMEM_LIMIT),
        cost_estimate=cost(2.0),
        name="middle",
    )(*args, *deps)


def last_kernel(
    owners, one, two, normed, low_kv, kv_w, first_kv, second_k, second_v, hidden, gain, grad_mid, grad_normed_q,
    first_query, first_early, second_query, second_early, adapter, grad_hidden, first_out, second_out
):
    rank = ADAPTER_RANK
    count = one.shape[1] // (2 * HEAD_DIM)
    heads = [(half, n) for half in (one, two) for n in range(count)]
    grad_k = jnp.concatenate([half[:, 2 * n * HEAD_DIM : (2 * n + 1) * HEAD_DIM] for half, n in heads], axis=1)
    grad_v = jnp.concatenate([half[:, (2 * n + 1) * HEAD_DIM : (2 * n + 2) * HEAD_DIM] for half, n in heads], axis=1)
    width = grad_k.shape[1]
    glow_k = dot_nt(grad_k, second_k[...]).astype(BF16)
    glow_v = dot_nt(grad_v, second_v[...]).astype(BF16)
    grad_normed = grad_normed_q[...] + dot_nt(grad_k, kv_w[:, :width]) + dot_nt(grad_v, kv_w[:, width:])
    grad_normed = grad_normed + dot_nt(glow_k, first_kv[:, :rank]) + dot_nt(glow_v, first_kv[:, rank:])
    values = hidden[...].astype(F32)
    scale = lax.rsqrt(jnp.mean(values * values, axis=-1, keepdims=True) + EPSILON)
    scaled = grad_normed * gain[...]
    mean = jnp.mean(values * scaled, axis=-1, keepdims=True)
    grad_hidden[...] = grad_mid[...] + scale * scaled - values * (scale * scale * scale * mean)
    firsts = [first_query[...], dot_tn(normed[...], glow_k), dot_tn(normed[...], glow_v), first_early[...]]
    tags = jnp.broadcast_to(adapter[...], (first_query.shape[0], LANES - 6 * rank))
    first_out[...] = jnp.concatenate(firsts + [tags], axis=1).astype(BF16)
    seconds = [second_query[...], dot_tn(low_kv[:, :rank], grad_k), dot_tn(low_kv[:, rank:], grad_v), second_early[...]]
    seconds = jnp.concatenate(seconds, axis=1)
    columns = seconds.shape[1] // owners
    padding = jnp.zeros((rank, second_out.shape[1] // rank * LANES - columns), F32)
    for n in range(owners):
        piece = jnp.concatenate([seconds[:, n * columns : (n + 1) * columns], padding], axis=1).astype(BF16)
        for c in range(piece.shape[1] // LANES):
            second_out[n, c * rank : (c + 1) * rank, :] = piece[:, c * LANES : (c + 1) * LANES]


def last(owners, args):
    rows, model = args[8].shape
    columns = (args[14].shape[1] + 2 * KV_HEADS * HEAD_DIM + args[15].shape[1]) // owners
    vmem = pl.BlockSpec(memory_space=pltpu.VMEM)
    return pl.pallas_call(
        functools.partial(last_kernel, owners),
        in_specs=[vmem] * len(args),
        out_specs=[vmem] * 3,
        out_shape=[
            jax.ShapeDtypeStruct((rows, model), F32),
            jax.ShapeDtypeStruct((model, LANES), BF16),
            jax.ShapeDtypeStruct((owners, -(-columns // LANES) * ADAPTER_RANK, LANES), BF16),
        ],
        compiler_params=pltpu.CompilerParams(vmem_limit_bytes=VMEM_LIMIT),
        cost_estimate=cost(2.0),
        name="last",
    )(*args)


def spread_kernel(depth, lines, flat, first_out, second_out):
    rank = ADAPTER_RANK
    size = flat.shape[0] // depth
    row = lax.broadcasted_iota(jnp.int32, (LANES, 1), 0).astype(F32)
    column = lax.broadcasted_iota(jnp.int32, (1, first_out.shape[1]), 1)
    inside = column % LANES
    target = (column // LANES * rank + inside).astype(F32)
    owner = (inside // rank).astype(F32)
    short = lax.broadcasted_iota(jnp.int32, (1, rank), 1).astype(F32)
    chunks = (flat.shape[1] - lines) // rank
    first, second = None, [None] * chunks
    for d in range(size):
        adapter = flat[d, 0:1, 6 * rank : 6 * rank + 1].astype(F32)
        total = flat[d].astype(F32)
        for z in range(1, depth):
            total = total + flat[z * size + d].astype(F32)
        total = total.astype(BF16)
        place = ((target - adapter * float(rank) == row) & (owner == adapter)).astype(F32).astype(BF16)
        lift = (row - adapter * float(rank) == short).astype(F32).astype(BF16)
        part = dot_nn(total[:lines], place)
        first = part if first is None else first + part
        for c in range(chunks):
            part = dot_nn(lift, total[lines + c * rank : lines + (c + 1) * rank])
            second[c] = part if second[c] is None else second[c] + part
    first_out[...] = first
    for c in range(chunks):
        second_out[:, c * LANES : (c + 1) * LANES] = second[c]


def spread(flat, depth, lines):
    vmem = pl.BlockSpec(memory_space=pltpu.VMEM)
    chunks = (flat.shape[1] - lines) // ADAPTER_RANK
    return pl.pallas_call(
        functools.partial(spread_kernel, depth, lines),
        in_specs=[vmem],
        out_specs=[vmem] * 2,
        out_shape=[jax.ShapeDtypeStruct((lines, 6 * LANES), F32), jax.ShapeDtypeStruct((LANES, chunks * LANES), F32)],
        compiler_params=pltpu.CompilerParams(vmem_limit_bytes=VMEM_LIMIT),
        cost_estimate=cost(2.0),
        name="spread",
    )(flat)


def per_device(
    depth,
    size,
    block_input,
    document_number,
    key_present,
    routes,
    sequence_adapter,
    output_gradient,
    norm_scale_pair,
    query_key_value_weight,
    attention_output_weight,
    router_weight,
    shared_gate_up_weight,
    shared_down_weight,
    routed_gate_up_weight,
    routed_down_weight,
    dense_first_factor,
    shared_down_first_factor,
    dense_second_factor,
    routed_first_factor,
    routed_down_first_factor,
    routed_second_factor,
):
    _, rows, model = block_input.shape
    topk = routes.shape[2]
    me = lax.axis_index("dp")
    experts = router_weight.shape[1]
    local_experts = routed_gate_up_weight.shape[0]
    shard_rows = query_key_value_weight.shape[0]
    shared_rows = shared_down_weight.shape[0]
    rank_all = dense_second_factor.shape[0]
    second_columns = dense_second_factor.shape[1]
    capacity = 4 * topk * rows // (3 * experts)
    query_width = HEADS * HEAD_DIM
    kv_width = KV_HEADS * HEAD_DIM
    hops = min(depth - 1, -(-(DOCUMENT_SPAN - 1) // rows))
    rank = ADAPTER_RANK
    units = SHARED_HIDDEN // size
    adapter = sequence_adapter[0]
    forward = [(i, i + 1) for i in range(depth - 1)]
    backward = [(i + 1, i) for i in range(depth - 1)]

    def over_seq(shard):
        return lax.all_gather(shard, "seq", axis=0)

    first_shard = dense_first_factor.reshape(shard_rows, 6 * rank_all)
    second_width = second_columns * rank_all // shard_rows
    groups = second_width // rank_all
    pack_kv = jnp.concatenate(
        [
            query_key_value_weight[:, query_width:],
            first_shard[:, rank_all : 3 * rank_all],
            dense_second_factor.T.reshape(groups, shard_rows, rank_all).transpose(1, 0, 2).reshape(shard_rows, -1),
            jnp.pad(
                jnp.concatenate([router_weight, norm_scale_pair.T], axis=1), ((0, 0), (0, LANES - experts - 2))
            ),
        ],
        axis=1,
    )
    pack_q = jnp.concatenate(
        [
            query_key_value_weight[:, :query_width],
            first_shard[:, :rank_all],
            first_shard[:, 3 * rank_all :],
            attention_output_weight,
        ],
        axis=1,
    )
    seq_kv = over_seq(pack_kv)
    seq_q = over_seq(tie(pack_q, seq_kv))

    flags = jnp.sum((routes[0][..., None] == jnp.arange(experts, dtype=jnp.int32)).astype(F32), axis=1)
    before = (jnp.arange(rows)[:, None] > jnp.arange(rows)[None, :]).astype(BF16)
    slots = jnp.where(flags > 0, dot_nn(before, flags.astype(BF16)), -1.0).astype(BF16)

    def own_columns(matrix):
        return lax.dynamic_slice_in_dim(matrix, adapter * rank, rank, 1)

    def own_factors(matrix):
        count = matrix.shape[1] // rank_all
        return jnp.concatenate([own_columns(matrix[:, n * rank_all : (n + 1) * rank_all]) for n in range(count)], axis=1)

    grad_out_b = output_gradient[0]
    grads_x, grads_y = swap(grad_out_b, 2, size), swap(grad_out_b, 4, size)
    gate_up = shared_gate_up_weight.reshape(shard_rows, 2, depth, size, units // depth)
    gate_up = gate_up.transpose(3, 0, 1, 2, 4).reshape(size, shard_rows, 2 * units)
    gate_up = lax.all_to_all(gate_up, "dp", split_axis=0, concat_axis=0, tiled=True)
    kv_gathered = plane_gather(tie(seq_kv, grads_x, grads_y, gate_up), size)
    grads_x, grads_y = tie_all([grads_x, grads_y], *kv_gathered[6])
    far_grads = (swap(grads_y[: rows // 2], 2, size), swap(grads_x[rows // 2 :], 4, size))
    grad_blocks = [(grad_out_b,), None, (grads_x,), None, (grads_y,), None, far_grads, None]
    kv_w, kv_first, second_t, small = assemble(
        kv_gathered, ((1, 2 * kv_width), (1, 2 * rank_all), (groups, rank_all), (1, LANES)), me
    )
    router_w = small[:, :experts]
    gains = small[:, experts : experts + 2].astype(F32).T
    second = own_columns(second_t).T
    first_kv = own_factors(kv_first)
    widths = [query_width, kv_width, kv_width, model, SHARED_HIDDEN, SHARED_HIDDEN, model]
    edges = [sum(widths[:n]) for n in range(len(widths) + 1)]
    b_parts = [second[:, edges[n] : edges[n + 1]] for n in range(len(widths))]

    x_flat = block_input[0].astype(F32)
    normed = rms_norm(x_flat, gains[0]).astype(BF16)
    low_kv = dot_nn(normed, first_kv).astype(BF16)
    kv_extra = jnp.concatenate([dot_nn(low_kv[:, :rank], b_parts[1]), dot_nn(low_kv[:, rank:], b_parts[2])], axis=1)
    present_tag = jnp.where(key_present == 1, document_number + 1, 0).astype(BF16)
    tag_columns = jnp.broadcast_to(present_tag.reshape(rows, 1), (rows, LANES))
    kv_blocks = [jnp.concatenate([(dot_nn(normed, kv_w) + kv_extra).astype(BF16), tag_columns], axis=1)]
    q_blocks = plane_gather(tie(seq_q, *far_grads), size)
    for k in range(1, size, 2):
        grad_blocks[k] = tuple(swap(piece, 1, size) for piece in grad_blocks[k - 1])
    for h in range(hops):
        block = kv_blocks[-1] if h == 0 else tie(kv_blocks[-1], q_blocks[2][0], q_blocks[4][0])
        kv_blocks.append(lax.ppermute(block, "seq", forward))
        kv_blocks[h] = block
    kv_all = jnp.concatenate(kv_blocks[::-1], axis=0)
    key_tag = kv_all[:, 2 * kv_width : 2 * kv_width + 1].astype(F32)
    query_tag = (document_number + 1).astype(F32)

    down_rows = routed_down_weight.shape[1]
    second_cut = rank_all * routed_second_factor.shape[2] // down_rows
    up_shards, down_shards = [], []
    for j in range(local_experts):
        up_parts = [
            routed_gate_up_weight[j].reshape(-1, 2 * EXPERT_HIDDEN),
            routed_first_factor[j].reshape(-1, 2 * rank_all),
        ]
        down_parts = [
            routed_down_weight[j],
            routed_down_first_factor[j],
            routed_second_factor[j].reshape(down_rows, -1),
        ]
        if j == 0:
            up_parts.append(gate_up.reshape(size * shard_rows, 2 * units))
            shared_down = jnp.concatenate([shared_down_weight, shared_down_first_factor], axis=1)
            down_parts.append(shared_down.reshape(down_rows, -1))
        up_shards.append(jnp.concatenate(up_parts, axis=1))
        down_shards.append(jnp.concatenate(down_parts, axis=1))
    seq_up, seq_down = [], []
    for j in range(local_experts):
        seq_up.append(over_seq(tie(up_shards[j], seq_kv if j == 0 else seq_up[j - 1])))
        seq_down.append(over_seq(tie(down_shards[j], seq_kv if j == 0 else seq_up[j - 1])))

    q_w, q_first, out_w = assemble(q_blocks, ((1, query_width), (1, 4 * rank_all), (1, model)), me)
    q_first = own_factors(q_first)
    first_q, first_o, first_gu = q_first[:, :rank], q_first[:, rank : 2 * rank], q_first[:, 2 * rank :]
    low_q = dot_nn(normed, first_q).astype(BF16)
    query = (dot_nn(normed, q_w) + dot_nn(low_q, b_parts[0])).astype(BF16)
    glow_sdown = dot_nt(grad_out_b, b_parts[6]).astype(BF16)
    attn, lse = attend(query, kv_all, query_tag, key_tag, hops, (*grad_blocks[3], *grad_blocks[5], *grad_blocks[7]))
    out_low = dot_nn(attn, first_o).astype(BF16)
    mid = x_flat + dot_nn(attn, out_w) + dot_nn(out_low, b_parts[3])
    normed2 = rms_norm(mid, gains[1]).astype(BF16)

    logits = dot_nn(normed2, router_w)
    top = jnp.max(jnp.where(flags > 0, logits, -jnp.inf), axis=-1, keepdims=True)
    weights = jnp.where(flags > 0, jnp.exp(logits - top), 0.0)
    gates = weights / jnp.sum(weights, axis=-1, keepdims=True)
    gates_hi = gates.astype(BF16)
    gates_lo = (gates - gates_hi.astype(F32)).astype(BF16)
    shared_low = dot_nn(normed2, first_gu).astype(BF16)
    own_adapter = jnp.full((rows, LANES - 3 * experts - 3 * rank), adapter.astype(F32)).astype(BF16)
    payload = jnp.concatenate([normed2, slots, gates_hi, gates_lo, shared_low, glow_sdown, own_adapter], axis=1)
    token_blocks = [None] * size
    token_blocks[0], token_blocks[1] = (payload,), (swap(payload, 1, size),)
    tokens_x, tokens_y = swap(payload, 2, size), swap(payload, 4, size)

    def gather_far(tokens_x, tokens_y, *done):
        tokens_x, tokens_y = tie_all([tokens_x, tokens_y], *done)
        half = rows // 2
        token_blocks[2], token_blocks[3] = (tokens_x,), (swap(tokens_x, 1, size),)
        token_blocks[4], token_blocks[5] = (tokens_y,), (swap(tokens_y, 1, size),)
        return swap(tokens_y[:half], 2, size), swap(tokens_x[half:], 4, size)

    def gather_farthest(far, *done):
        far = tuple(tie_all(far, *done))
        token_blocks[6], token_blocks[7] = far, tuple(swap(piece, 1, size) for piece in far)


    moe_parts, back_parts, grad_sums = [None] * size, [None] * size, []
    wide = model + rank_all

    def weights_of(j):
        second_j = seq_down[j][:, :, wide : wide + second_cut]
        second_j = second_j.reshape(depth, rank_all, -1).transpose(1, 0, 2).reshape(rank_all, -1)
        args = [seq_up[j].reshape(model, -1), seq_down[j][:, :, :wide].reshape(EXPERT_HIDDEN, wide), second_j]
        if j == 0:
            args.append(seq_down[j][:, :, wide + second_cut :].reshape(units, wide))
            slices = [
                lax.dynamic_slice_in_dim(second_t[edges[n] : edges[n + 1]].reshape(depth, size, -1, rank_all), me, 1, 1)
                for n in (4, 5)
            ]
            args.append(jnp.concatenate([part.reshape(units, rank_all) for part in slices], axis=0))
        return args

    def run_expert(j, args, group, prior, deps, packed=False):
        meta = jnp.stack([me * local_experts + j, me]).astype(jnp.int32)
        prior = ([moe_parts[k] for k in group], [back_parts[k] for k in group]) if prior else None
        moe_out, back_out, grads = expert_call(
            meta,
            args,
            [token_blocks[k] for k in group],
            [grad_blocks[k] for k in group],
            prior,
            grad_sums[-1],
            packed,
            experts,
            capacity,
            depth,
            deps,
        )
        for n, k in enumerate(group):
            moe_parts[k], back_parts[k] = moe_out[n], back_out[n]
        grad_sums[-1] = list(grads)

    for j in range(local_experts - 1):
        grad_sums.append([])
        args = weights_of(j)
        previous = ()
        for group in ((0, 1), (2, 3), (4, 5), (6, 7)):
            run_expert(j, args, group, j > 0, previous, group == (6, 7))
            previous = (back_parts[group[0]],)
            if j == 0 and group == (0, 1):
                far = gather_far(tokens_x, tokens_y, *previous)
            if j == 0 and group == (2, 3):
                gather_farthest(far, *previous)
    if local_experts == 1:
        gather_farthest(gather_far(tokens_x, tokens_y))

    def scatter(packed):
        return lax.psum_scatter(packed, "seq", scatter_dimension=0, tiled=True)

    packed_sums = [scatter(grads[0]) for grads in grad_sums]
    grad_sums.append([])
    j, prior, half = local_experts - 1, local_experts > 1, (rows + BACK_ROWS) // 2
    args = weights_of(j)
    run_expert(j, args, (6, 7), prior, (back_parts[6],) if prior else ())
    pair_six = add(back_parts[6], swap(back_parts[7], 1, size))
    run_expert(j, args, (2, 3), prior, (pair_six,))
    from_diagonal_x, from_diagonal_y = swap(pair_six[:half], 2, size), swap(pair_six[half:], 4, size)
    pair_two = add(back_parts[2], swap(back_parts[3], 1, size))
    run_expert(j, args, (4, 5), prior, (pair_two, *packed_sums))
    pair_four = add(back_parts[4], swap(tie(back_parts[5], from_diagonal_x, from_diagonal_y), 1, size))
    to_x = jnp.concatenate([pair_two[:half], add(pair_two[half:], from_diagonal_y)], axis=0)
    to_y = jnp.concatenate([add(pair_four[:half], from_diagonal_x), pair_four[half:]], axis=0)
    run_expert(j, args, (0, 1), prior, (to_x, to_y), True)
    packed_sums.append(scatter(grad_sums[-1][0]))
    from_x, from_y = swap(to_x, 2, size), swap(to_y, 4, size)
    back_sum = add(back_parts[0], swap(tie(back_parts[1], from_x, from_y), 1, size), from_x, from_y)
    back = back_sum.astype(F32)

    half = rows // 2
    far_parts = dict(zip((6, 2, 4, 0), tie_all([moe_parts[k + 1] for k in (6, 2, 4, 0)], back_sum)))
    pair = {k: add(moe_parts[k], swap(far_parts[k], 1, size)) for k in (6, 2, 4, 0)}
    moe_to_x = jnp.concatenate([pair[2][:half], add(pair[2][half:], swap(pair[6][half:], 4, size))], axis=0)
    moe_to_y = jnp.concatenate([add(pair[4][:half], swap(pair[6][:half], 2, size)), pair[4][half:]], axis=0)
    moe_from_x, moe_from_y = swap(moe_to_x, 2, size), swap(moe_to_y, 4, size)
    moe = pair[0].astype(F32) + moe_from_x.astype(F32) + moe_from_y.astype(F32)
    tail = back[:rows, model:]
    low_sdown = tail[:, 3 * experts + 2 * rank : 3 * experts + 3 * rank].astype(BF16)

    owner_rows = model // depth
    firsts, downs, seconds = [], [], []
    for packed in packed_sums:
        packed = packed[0].astype(F32)
        firsts.append(jnp.stack([packed[:owner_rows], packed[owner_rows : 2 * owner_rows]], axis=1))
        at = 2 * owner_rows + down_rows
        downs.append(packed[2 * owner_rows : at])
        seconds.append(packed[at : at + routed_second_factor.shape[2]].T)
    at += routed_second_factor.shape[2]
    grad_expert_a, grad_expert_a_down, grad_expert_b = jnp.stack(firsts), jnp.stack(downs), jnp.stack(seconds)
    grad_first_down = packed_sums[0][0, at : at + shared_rows].astype(F32)

    grad_out = grad_out_b.astype(F32)
    grad_gates = tail[:, :experts] + tail[:, experts : 2 * experts]
    glow_sgu = tail[:, 3 * experts : 3 * experts + 2 * rank].astype(BF16)
    grad_logits = gates * (grad_gates - jnp.sum(gates * grad_gates, axis=-1, keepdims=True))
    grad_normed2 = back[:rows, :model] + dot_nt(glow_sgu, first_gu)
    grad_normed2 = grad_normed2 + jnp.einsum(
        "re,de->rd", grad_logits, router_w.astype(F32), precision=lax.Precision.HIGHEST
    )
    _, norm2_back = jax.vjp(lambda values_in: rms_norm(values_in, gains[1]), mid)
    grad_mid = grad_out + norm2_back(grad_normed2)[0]
    grad_mid_b = grad_mid.astype(BF16)
    glow_out = dot_nt(grad_mid_b, b_parts[3]).astype(BF16)
    grad_attn = (dot_nt(grad_mid_b, out_w) + dot_nt(glow_out, first_o)).astype(BF16)

    def shared_columns(block):
        block = block[:, :SHARED_HIDDEN].reshape(rank, size, depth, units // depth)
        return block.transpose(0, 2, 1, 3).reshape(rank, SHARED_HIDDEN)

    count = KV_HEADS // 2
    grad_q_one, grad_kv_one = attend_back(query, kv_all, grad_attn, lse, query_tag, key_tag, hops, 0, count, (pair[6], pair[2], pair[4]))
    one = grad_kv_one[:rows]
    hop_one = lax.ppermute(one, "seq", backward)
    grad_q_two, grad_kv_two = attend_back(
        query, kv_all, grad_attn, lse, query_tag, key_tag, hops, count, count, (moe_to_x, moe_to_y, packed_sums[-1])
    )
    two = tie(grad_kv_two[:rows], hop_one)
    hop_two = lax.ppermute(two, "seq", backward)
    grad_normed_q, first_query, second_query = query_back(
        [grad_q_one, grad_q_two, normed, low_q, q_w, first_q, b_parts[0]]
    )
    for h in range(hops):
        own = slice((h + 1) * rows, (h + 2) * rows)
        from_one = hop_one if h == 0 else lax.ppermute(one, "seq", backward)
        from_two = hop_two if h == 0 else lax.ppermute(tie(two, from_one, first_query), "seq", backward)
        one, two = add(grad_kv_one[own], from_one), add(grad_kv_two[own], from_two)
    first_early, second_out, second_down = middle(
        [attn, glow_out, normed2, glow_sgu, grad_mid_b, out_low, grad_out_b, low_sdown], (hop_two,)
    )
    hidden_out = (mid + moe + dot_nn(low_sdown, b_parts[6])).astype(BF16)[None]
    second_early = jnp.concatenate(
        [second_out, shared_columns(back[rows : rows + rank]), shared_columns(back[rows + rank :]), second_down], axis=1
    )
    grad_hidden, first_flat, second_flat = last(
        depth * size,
        [one, two, normed, low_kv, kv_w, first_kv, b_parts[1], b_parts[2], block_input[0], gains[0:1], grad_mid]
        + [grad_normed_q, first_query, first_early, second_query, second_early, adapter.astype(F32).reshape(1, 1)],
    )
    flat = jnp.concatenate([first_flat.reshape(depth * size, shard_rows, LANES), second_flat], axis=1)
    flat = lax.all_to_all(flat, ("seq", "dp"), split_axis=0, concat_axis=0, tiled=True)
    grad_first, grad_second = spread(flat, depth, shard_rows)
    grad_first = grad_first.reshape(shard_rows, 6, rank_all)
    grad_second = grad_second[:, :second_columns]
    grad_hidden = grad_hidden[None]
    return (
        hidden_out,
        grad_hidden,
        grad_first,
        grad_first_down,
        grad_second,
        grad_expert_a,
        grad_expert_a_down,
        grad_expert_b,
    )


def solution(mesh):
    in_specs = (
        P("dp", "seq", None),
        P("dp", "seq"),
        P("dp", "seq"),
        P("dp", "seq", None),
        P("dp"),
        P("dp", "seq", None),
        P(None, ("seq", "dp")),
        P(("seq", "dp"), None),
        P(("seq", "dp"), None),
        P(("seq", "dp"), None),
        P(("seq", "dp"), None, None),
        P(("seq", "dp"), None),
        P("dp", "seq", None, None),
        P("dp", "seq", None),
        P(("seq", "dp"), None, None),
        P(("seq", "dp"), None),
        P(None, ("seq", "dp")),
        P("dp", "seq", None, None),
        P("dp", "seq", None),
        P("dp", None, "seq"),
    )
    out_specs = (
        P("dp", "seq", None),
        P("dp", "seq", None),
        P(("seq", "dp"), None, None),
        P(("seq", "dp"), None),
        P(None, ("seq", "dp")),
        P("dp", "seq", None, None),
        P("dp", "seq", None),
        P("dp", None, "seq"),
    )
    return jax.shard_map(
        functools.partial(per_device, mesh.shape["seq"], mesh.shape["dp"]),
        mesh=mesh,
        in_specs=in_specs,
        out_specs=out_specs,
        check_vma=False,
    )
```

```python
import functools
import math

import jax
import jax.numpy as jnp
from jax import lax
from jax.experimental import pallas as pl
from jax.experimental.pallas import tpu as pltpu
from jax.sharding import PartitionSpec as P

HEADS = 12
KV_HEADS = 4
HEAD_DIM = 128
EXPERT_HIDDEN = 512
SHARED_HIDDEN = 1024
ADAPTER_RANK = 16
DOCUMENT_SPAN = 1024

EPSILON = 1e-05
MASKED_SCORE = -1e30
LOG2E = 1.4426950408889634
SCALE = HEAD_DIM ** (-0.5)
LANES = 128
VMEM_LIMIT = 60 * 1024 * 1024

F32 = jnp.float32
BF16 = jnp.bfloat16


def dot_nn(left, right):
    return jnp.dot(left, right, preferred_element_type=F32)


def dot_tn(left, right):
    return lax.dot_general(left, right, (((0,), (0,)), ((), ())), preferred_element_type=F32)


def dot_nt(left, right):
    return lax.dot_general(left, right, (((1,), (1,)), ((), ())), preferred_element_type=F32)


def rms_norm(values, gain):
    return values * lax.rsqrt(jnp.mean(values * values, axis=-1, keepdims=True) + EPSILON) * gain


def cost(microseconds):
    return pl.CostEstimate(flops=int(1153500000 * microseconds), bytes_accessed=1000000, transcendentals=0)


def query_tiles(rows, hops):
    tile = math.gcd(rows, 256)
    spans = []
    for first in range(0, rows, tile):
        oldest = max(0, hops * rows + first - (DOCUMENT_SPAN - 1)) // tile * tile
        spans.append((first, tile, oldest, hops * rows + first + tile - oldest))
    return spans


def fill_bias(spans, shift, query_tag, key_tag, bias):
    for first, tile, oldest, span in spans:
        keys = oldest + lax.broadcasted_iota(jnp.int32, (span, tile), 0)
        queries = shift + first + lax.broadcasted_iota(jnp.int32, (span, tile), 1)
        same = key_tag[oldest : oldest + span, :] == query_tag[:, first : first + tile]
        permit = (keys <= queries) & (same | (keys == queries))
        bias[oldest : oldest + span, first : first + tile] = jnp.where(permit, 0.0, MASKED_SCORE)


def attend_kernel(spans, shift, waits, q_ref, k_ref, v_ref, qt_ref, kt_ref, *rest):
    out_ref, lse_ref, bias = rest[waits:]

    @pl.when(pl.program_id(0) == 0)
    def _():
        fill_bias(spans, shift, qt_ref, kt_ref, bias)

    groups = q_ref.shape[1] // HEAD_DIM
    for first, tile, oldest, span in spans:
        keys = k_ref[oldest : oldest + span, :]
        values = v_ref[oldest : oldest + span, :]
        mask = bias[oldest : oldest + span, first : first + tile]
        for h in range(groups):
            columns = slice(h * HEAD_DIM, (h + 1) * HEAD_DIM)
            scores = dot_nt(keys, q_ref[first : first + tile, columns]) * (SCALE * LOG2E) + mask
            top = jnp.max(scores, axis=0, keepdims=True)
            weights = jnp.exp2(scores - top)
            total = jnp.sum(weights, axis=0, keepdims=True)
            mixed = dot_tn(values, weights.astype(BF16)) / total
            out_ref[first : first + tile, columns] = mixed.T.astype(BF16)
            lse_ref[0, h : h + 1, first : first + tile] = top + jnp.log2(total)


def attend(query, kv_all, query_tag, key_tag, hops, deps=()):
    rows = query.shape[0]
    groups = HEADS // KV_HEADS
    span = kv_all.shape[0]
    spans = query_tiles(rows, hops)
    return pl.pallas_call(
        functools.partial(attend_kernel, spans, hops * rows, len(deps)),
        grid=(KV_HEADS,),
        in_specs=[
            pl.BlockSpec((rows, groups * HEAD_DIM), lambda g: (0, g)),
            pl.BlockSpec((span, HEAD_DIM), lambda g: (0, g)),
            pl.BlockSpec((span, HEAD_DIM), lambda g: (0, KV_HEADS + g)),
            pl.BlockSpec((1, rows), lambda g: (0, 0)),
            pl.BlockSpec((span, 1), lambda g: (0, 0)),
        ]
        + [pl.BlockSpec(memory_space=pl.ANY)] * len(deps),
        out_specs=[
            pl.BlockSpec((rows, groups * HEAD_DIM), lambda g: (0, g)),
            pl.BlockSpec((1, groups, rows), lambda g: (g, 0, 0)),
        ],
        out_shape=[
            jax.ShapeDtypeStruct((rows, HEADS * HEAD_DIM), BF16),
            jax.ShapeDtypeStruct((KV_HEADS, groups, rows), F32),
        ],
        scratch_shapes=[pltpu.VMEM((span, rows), F32)],
        compiler_params=pltpu.CompilerParams(vmem_limit_bytes=VMEM_LIMIT),
        cost_estimate=cost(23.0),
        name="attend",
    )(query, kv_all, kv_all, query_tag, key_tag, *deps)


def attend_back_kernel(
    spans, shift, waits, q_ref, k_ref, v_ref, g_ref, lse_ref, qt_ref, kt_ref, *rest
):
    dq_ref, dkv_ref, bias, dk_acc, dv_acc = rest[waits:]

    @pl.when(pl.program_id(0) == 0)
    def _():
        fill_bias(spans, shift, qt_ref, kt_ref, bias)

    dk_acc[...] = jnp.zeros_like(dk_acc)
    dv_acc[...] = jnp.zeros_like(dv_acc)
    groups = q_ref.shape[1] // HEAD_DIM
    for first, tile, oldest, span in spans:
        keys = k_ref[oldest : oldest + span, :]
        values = v_ref[oldest : oldest + span, :]
        mask = bias[oldest : oldest + span, first : first + tile]
        for h in range(groups):
            columns = slice(h * HEAD_DIM, (h + 1) * HEAD_DIM)
            query = q_ref[first : first + tile, columns]
            grad = g_ref[first : first + tile, columns]
            lse = lse_ref[0, h : h + 1, first : first + tile]
            probs = jnp.exp2(dot_nt(keys, query) * (SCALE * LOG2E) + mask - lse)
            dv_acc[oldest : oldest + span, :] += dot_nn(probs.astype(BF16), grad)
            grad_probs = dot_nt(values, grad)
            delta = jnp.sum(probs * grad_probs, axis=0, keepdims=True)
            grad_scores = (probs * (grad_probs - delta)).astype(BF16)
            dk_acc[oldest : oldest + span, :] += dot_nn(grad_scores, query) * SCALE
            dq_ref[first : first + tile, columns] = (dot_tn(grad_scores, keys) * SCALE).astype(BF16)
    dkv_ref[:, :HEAD_DIM] = dk_acc[...].astype(dkv_ref.dtype)
    dkv_ref[:, HEAD_DIM:] = dv_acc[...].astype(dkv_ref.dtype)


def attend_back(query, kv_all, grad_attn, lse, query_tag, key_tag, hops, head, count, deps=()):
    rows = query.shape[0]
    groups = HEADS // KV_HEADS
    span = kv_all.shape[0]
    spans = query_tiles(rows, hops)
    return pl.pallas_call(
        functools.partial(attend_back_kernel, spans, hops * rows, len(deps)),
        grid=(count,),
        in_specs=[
            pl.BlockSpec((rows, groups * HEAD_DIM), lambda g: (0, head + g)),
            pl.BlockSpec((span, HEAD_DIM), lambda g: (0, head + g)),
            pl.BlockSpec((span, HEAD_DIM), lambda g: (0, KV_HEADS + head + g)),
            pl.BlockSpec((rows, groups * HEAD_DIM), lambda g: (0, head + g)),
            pl.BlockSpec((1, groups, rows), lambda g: (head + g, 0, 0)),
            pl.BlockSpec((1, rows), lambda g: (0, 0)),
            pl.BlockSpec((span, 1), lambda g: (0, 0)),
        ]
        + [pl.BlockSpec(memory_space=pl.ANY)] * len(deps),
        out_specs=[
            pl.BlockSpec((rows, groups * HEAD_DIM), lambda g: (0, g)),
            pl.BlockSpec((span, 2 * HEAD_DIM), lambda g: (0, g)),
        ],
        out_shape=[
            jax.ShapeDtypeStruct((rows, count * groups * HEAD_DIM), BF16),
            jax.ShapeDtypeStruct((span, count * 2 * HEAD_DIM), BF16),
        ],
        scratch_shapes=[
            pltpu.VMEM((span, rows), F32),
            pltpu.VMEM((span, HEAD_DIM), F32),
            pltpu.VMEM((span, HEAD_DIM), F32),
        ],
        compiler_params=pltpu.CompilerParams(vmem_limit_bytes=VMEM_LIMIT),
        cost_estimate=cost(2.0 * count),
        name="attend_back",
    )(query, kv_all, kv_all, grad_attn, lse, query_tag, key_tag, *deps)


BACK_ROWS = 2 * ADAPTER_RANK


def expert_kernel(count, splits, experts, capacity, depth, with_prior, with_shared, with_sums, packed, waits, *refs):
    meta, refs = refs[0], refs[1:]
    weight_count = 5 if with_shared else 3
    weight_refs, refs = refs[:weight_count], refs[weight_count:]
    token_refs, grad_refs = [], []
    for split in splits:
        token_refs.append(refs[:split])
        refs = refs[split:]
    for split in splits:
        grad_refs.append(refs[:split])
        refs = refs[split:]
    prior_moe, prior_back = (), ()
    if with_prior:
        prior_moe, refs = refs[:count], refs[count:]
        prior_back, refs = refs[:count], refs[count:]
    grad_count = 4 if with_shared else 3
    sums_in = ()
    if with_sums:
        sums_in, refs = refs[:grad_count], refs[grad_count:]
    refs = refs[waits:]
    moe_refs, refs = refs[:count], refs[count:]
    back_refs, refs = refs[:count], refs[count:]
    out_count = 1 if packed else grad_count
    grad_outs, refs = refs[:out_count], refs[out_count:]
    grad_sums, refs = refs[:grad_count], refs[grad_count:]
    first_grad, down_grad, second_grad = grad_sums[:3]
    weight_bufs, refs = refs[:weight_count], refs[weight_count:]
    if packed:
        pack_buf, refs = refs[0], refs[1:]
    tokens_buf, grad_buf, moe_buf, back_buf, in_sem, out_sem, weight_sem, sum_sem, sum_in_sem = refs

    step = pl.program_id(0)
    steps = count // 2
    slots = min(2, steps)
    slot = lax.rem(step, slots)
    rows, wide = tokens_buf.shape[2:]
    model = wide - LANES
    hidden = EXPERT_HIDDEN
    rank = ADAPTER_RANK
    up_ref, down_ref, second_ref = weight_bufs[:3]

    def weight_copy(n):
        return pltpu.make_async_copy(weight_refs[n], weight_bufs[n], weight_sem.at[n])

    def incoming(k, i, kinds):
        copies = []
        to, source = k % slots, 2 * k + i
        for n, (refs_of, buf) in enumerate(((token_refs, tokens_buf), (grad_refs, grad_buf))):
            size = rows // len(refs_of[source])
            for p, piece in enumerate(refs_of[source] if n in kinds else ()):
                part = buf.at[to, i, pl.ds(p * size, size)]
                copies.append(pltpu.make_async_copy(piece, part, in_sem.at[to, i, 2 * n + p]))
        if with_prior and 2 in kinds:
            copies.append(pltpu.make_async_copy(prior_moe[source], moe_buf.at[to, i], in_sem.at[to, i, 4]))
            copies.append(pltpu.make_async_copy(prior_back[source], back_buf.at[to, i], in_sem.at[to, i, 5]))
        return copies

    def outgoing(k, i, kinds=(0, 1)):
        at, source = k % slots, 2 * k + i
        pairs = ((moe_buf, moe_refs), (back_buf, back_refs))
        return [pltpu.make_async_copy(pairs[n][0].at[at, i], pairs[n][1][source], out_sem.at[at, i, n]) for n in kinds]

    def at_step(action, first=0, last=steps):
        for k in range(first, last):
            pl.when(step == k)(functools.partial(action, k))

    def wait_in(i, kind):
        def action(k):
            for copy in incoming(k, i, (kind,)):
                copy.wait()

        at_step(action)

    def start_out(i, n):
        at_step(lambda k: outgoing(k, i, (n,))[0].start())

    def turn(k):
        for i in (0, 1):
            if k >= 1:
                for copy in outgoing(k - 1, i):
                    copy.wait()
            if k + 1 < steps:
                for copy in incoming(k + 1, i, (0, 1, 2)):
                    copy.start()

    def sum_copy(n):
        return pltpu.make_async_copy(pack_buf if packed else grad_sums[n], grad_outs[n], sum_sem.at[n])

    def sum_in(n):
        return pltpu.make_async_copy(sums_in[n], grad_sums[n], sum_in_sem.at[n])

    @pl.when(step == 0)
    def _():
        for i in (0, 1):
            for copy in incoming(0, i, (0,)):
                copy.start()
        for i in (0, 1):
            for copy in incoming(0, i, (1,)):
                copy.start()
        for n in range(weight_count):
            weight_copy(n).start()
        for i in (0, 1):
            for copy in incoming(0, i, (2,)):
                copy.start()
        for n, total in enumerate(grad_sums):
            if with_sums:
                sum_in(n).start()
            else:
                total[...] = jnp.zeros_like(total)

    expert = meta[0]
    lane = lax.broadcasted_iota(jnp.int32, (1, LANES), 1)
    sub = lax.broadcasted_iota(jnp.int32, (LANES, 1), 0)
    places, picks, gates_of, selects, adapters = [], [], [], [], []
    inputs, grad_rows = [], []
    for i in (0, 1):
        wait_in(i, 0)
        extra_b = tokens_buf[slot, i, :, model:]
        extra = extra_b.astype(F32)
        own = 3 * experts + 3 * rank
        adapter = extra[0:1, own : own + 1]
        select = ((lane // rank).astype(F32) == adapter).astype(F32)
        slot_column = jnp.sum(jnp.where(lane == expert, extra, 0.0), axis=1, keepdims=True)
        slot_row = jnp.sum(jnp.where(sub == expert, extra.T, 0.0), axis=0, keepdims=True)
        place = lax.broadcasted_iota(jnp.int32, (rows, capacity), 1).astype(F32) == slot_column
        pick = lax.broadcasted_iota(jnp.int32, (capacity, rows), 0).astype(F32) == slot_row
        place, pick = place.astype(F32).astype(BF16), pick.astype(F32).astype(BF16)
        picked_extra = dot_nn(pick, extra_b)
        chosen = (lane == experts + expert) | (lane == 2 * experts + expert)
        gates_of.append(jnp.sum(jnp.where(chosen, picked_extra, 0.0), axis=1, keepdims=True))
        inputs.append(dot_nn(pick, tokens_buf[slot, i, :, :model]).astype(BF16))
        picks.append(pick)
        places.append(place)
        adapters.append(adapter)
        selects.append(jnp.broadcast_to(select, (capacity, LANES)))
    for i in (0, 1):
        wait_in(i, 1)
        grad_rows.append(dot_nn(picks[i], grad_buf[slot, i]))
    at_step(turn)
    inputs = jnp.concatenate(inputs, axis=0)
    grad_rows = jnp.concatenate(grad_rows, axis=0)
    gate = jnp.concatenate(gates_of, axis=0)
    select = jnp.concatenate(selects, axis=0)
    select_two = jnp.concatenate([select, select], axis=1)

    @pl.when(step == 0)
    def _():
        for n in range(weight_count):
            weight_copy(n).wait()

    low = (dot_nn(inputs, up_ref[:, 2 * hidden : 2 * hidden + 2 * LANES]) * select_two).astype(BF16)
    gate_part = dot_nn(inputs, up_ref[:, :hidden]) + dot_nn(low[:, :LANES], second_ref[:, :hidden])
    up_part = dot_nn(inputs, up_ref[:, hidden : 2 * hidden]) + dot_nn(low[:, LANES:], second_ref[:, hidden : 2 * hidden])
    sigmoid = 1.0 / (1.0 + jnp.exp(-gate_part))
    silu = gate_part * sigmoid
    act = (silu * up_part).astype(BF16)
    low_down = (dot_nn(act, down_ref[:, model:]) * select).astype(BF16)
    output = (dot_nn(act, down_ref[:, :model]) + dot_nn(low_down, second_ref[:, 2 * hidden :])).astype(BF16).astype(F32)
    grad_gate = jnp.sum(output * grad_rows, axis=1, keepdims=True)
    weighted = (gate * output).astype(BF16)

    if with_sums:

        @pl.when(step == 0)
        def _():
            for n in range(grad_count):
                sum_in(n).wait()

    grad_y = (gate * grad_rows).astype(BF16)
    glow_down = (dot_nt(grad_y, second_ref[:, 2 * hidden :]) * select).astype(BF16)
    second_grad[:, 2 * hidden :] += dot_tn(low_down, grad_y)
    down_grad[...] += dot_tn(act, glow_down)
    grad_act = dot_nt(grad_y, down_ref[:, :model]) + dot_nt(glow_down, down_ref[:, model:])
    grad_up = (grad_act * silu).astype(BF16)
    grad_gp = (grad_act * up_part * (sigmoid * (1.0 + gate_part * (1.0 - sigmoid)))).astype(BF16)
    glow = jnp.concatenate(
        [
            dot_nt(grad_gp, second_ref[:, :hidden]) * select,
            dot_nt(grad_up, second_ref[:, hidden : 2 * hidden]) * select,
        ],
        axis=1,
    ).astype(BF16)
    second_grad[:, :hidden] += dot_tn(low[:, :LANES], grad_gp)
    second_grad[:, hidden : 2 * hidden] += dot_tn(low[:, LANES:], grad_up)
    first_grad[...] += dot_tn(inputs, glow)
    grad_in = (
        dot_nt(grad_gp, up_ref[:, :hidden])
        + dot_nt(grad_up, up_ref[:, hidden : 2 * hidden])
        + dot_nt(glow, up_ref[:, 2 * hidden : 2 * hidden + 2 * LANES])
    ).astype(BF16)
    gate_hi = grad_gate.astype(BF16).astype(F32)
    gate_lo = grad_gate - gate_hi
    extra_out = (
        jnp.where(lane == expert, gate_hi, 0.0) + jnp.where(lane == experts + expert, gate_lo, 0.0)
    ).astype(BF16)

    @pl.when(step == steps - 1)
    def _():
        if not packed:
            for n in range(3):
                sum_copy(n).start()
            return
        second_t = second_grad[...].T
        parts = [first_grad[:, :LANES], first_grad[:, LANES:], down_grad[...], second_t]
        at = 0
        for part in parts:
            size = part.shape[0] // depth
            for z in range(depth):
                pack_buf[z, at : at + size, :] = part[z * size : (z + 1) * size].astype(BF16)
            at += size

    for i in (0, 1):
        mine = slice(i * capacity, (i + 1) * capacity)
        wait_in(i, 2)
        moe = dot_nn(places[i], weighted[mine])
        back = dot_nn(places[i], grad_in[mine])
        back_extra = dot_nn(places[i], extra_out[mine])
        if with_prior:
            moe = moe + moe_buf[slot, i].astype(F32)
            back = back + back_buf[slot, i, :rows, :model].astype(F32)
            back_extra = back_extra + back_buf[slot, i, :rows, model:].astype(F32)
        if not with_prior:
            back_buf[slot, i, rows:, :] = jnp.zeros((BACK_ROWS, wide), BF16)
        if with_shared:
            sdown_ref, sb_ref = weight_bufs[3:]
            units = sdown_ref.shape[0]
            first_gate, first_up, first_down = 3 * experts, 3 * experts + rank, 3 * experts + 2 * rank
            tokens = tokens_buf[slot, i, :, :model]
            extra_b = tokens_buf[slot, i, :, model:]
            grads = grad_buf[slot, i]
            offset = (lane - sub).astype(F32) - adapters[i] * float(rank)

            def spread(base):
                inside = (sub >= base) & (sub < base + rank)
                return (inside & (offset == float(-base))).astype(F32).astype(BF16)

            to_gate = dot_nt(spread(first_gate), sb_ref[:units]).astype(BF16)
            to_up = dot_nt(spread(first_up), sb_ref[units:]).astype(BF16)
            to_down = dot_nt(spread(first_down), sdown_ref[:, model:]).astype(BF16)
            shared_up = up_ref[:, 2 * hidden + 2 * LANES :]
            gate_up = dot_nn(tokens, shared_up)
            s_gate = gate_up[:, :units] + dot_nn(extra_b, to_gate)
            s_up = gate_up[:, units:] + dot_nn(extra_b, to_up)
            s_sig = 1.0 / (1.0 + jnp.exp(-s_gate))
            s_silu = s_gate * s_sig
            s_act = (s_silu * s_up).astype(BF16)
            moe = moe + dot_nn(s_act, sdown_ref[:, :model])
            s_grad = dot_nt(grads, sdown_ref[:, :model]) + dot_nn(extra_b, to_down)
            grad_sums[3][...] += dot_tn(s_act, dot_nn(extra_b, spread(first_down)).astype(BF16))
            s_gu = (s_grad * s_silu).astype(BF16)
            s_gg = (s_grad * s_up * (s_sig * (1.0 + s_gate * (1.0 - s_sig)))).astype(BF16)
            back_extra = back_extra + dot_nt(s_act, to_down) + dot_nt(s_gg, to_gate) + dot_nt(s_gu, to_up)
            back = back + dot_nt(jnp.concatenate([s_gg, s_gu], axis=1), shared_up)
            columns = pl.ds(pl.multiple_of(meta[1] * units, units), units)
            grad_bg = dot_tn(extra_b, s_gg)[first_gate : first_gate + rank]
            grad_bu = dot_tn(extra_b, s_gu)[first_up : first_up + rank]
            back_buf[slot, i, rows : rows + rank, columns] = grad_bg.astype(BF16)
            back_buf[slot, i, rows + rank :, columns] = grad_bu.astype(BF16)
        moe_buf[slot, i] = moe.astype(BF16)
        start_out(i, 0)
        back_buf[slot, i, :rows, :model] = back.astype(BF16)
        back_buf[slot, i, :rows, model:] = back_extra.astype(BF16)
        start_out(i, 1)

    @pl.when(step == steps - 1)
    def _():
        if packed and with_shared:
            size = grad_sums[3].shape[0] // depth
            for z in range(depth):
                part = grad_sums[3][z * size : (z + 1) * size, :]
                if size % 16:
                    part = jnp.concatenate([part, jnp.zeros((16 - size % 16, LANES), F32)], axis=0)
                pack_buf[z, pack_buf.shape[1] - part.shape[0] :, :] = part.astype(BF16)
        for n in range(0 if packed else 3, out_count):
            sum_copy(n).start()
        for i in (0, 1):
            for copy in outgoing(steps - 1, i):
                copy.wait()
        for n in range(out_count):
            sum_copy(n).wait()


def expert_call(meta, weights, tokens, grads, prior, sums, packed, experts, capacity, depth, deps=()):
    count = len(tokens)
    with_shared = len(weights) > 3
    splits = [len(pieces) for pieces in tokens]
    rows, model = sum(piece.shape[0] for piece in grads[0]), grads[0][0].shape[1]
    wide = model + LANES
    slots = min(2, count // 2)
    anywhere = pl.BlockSpec(memory_space=pl.ANY)
    prior = [] if prior is None else list(prior[0]) + list(prior[1])
    flat = [piece for pieces in tokens for piece in pieces] + [piece for pieces in grads for piece in pieces]
    grad_shapes = [
        jax.ShapeDtypeStruct((model, 2 * LANES), F32),
        jax.ShapeDtypeStruct((EXPERT_HIDDEN, LANES), F32),
        jax.ShapeDtypeStruct(weights[2].shape, F32),
    ]
    if with_shared:
        grad_shapes.append(jax.ShapeDtypeStruct((weights[3].shape[0], LANES), F32))
    out_shapes = grad_shapes
    if packed:
        lines = sum(s.shape[0] for s in grad_shapes[:2]) + model + weights[2].shape[1]
        lines = lines // depth
        if with_shared:
            lines += -(-weights[3].shape[0] // depth // 16) * 16
        out_shapes = [jax.ShapeDtypeStruct((depth, lines, LANES), BF16)]
    back_rows = rows + BACK_ROWS
    outs = pl.pallas_call(
        functools.partial(
            expert_kernel, count, splits, experts, capacity, depth, bool(prior), with_shared, bool(sums), packed, len(deps)
        ),
        grid=(count // 2,),
        in_specs=[pl.BlockSpec(memory_space=pltpu.SMEM)]
        + [anywhere] * (len(weights) + len(flat) + len(prior) + len(sums) + len(deps)),
        out_specs=[anywhere] * (2 * count + len(out_shapes)),
        out_shape=[jax.ShapeDtypeStruct((rows, model), BF16)] * count
        + [jax.ShapeDtypeStruct((back_rows, wide), BF16)] * count
        + out_shapes,
        scratch_shapes=[pltpu.VMEM(s.shape, F32) for s in grad_shapes]
        + [pltpu.VMEM(w.shape, BF16) for w in weights]
        + ([pltpu.VMEM(out_shapes[0].shape, BF16)] if packed else [])
        + [
            pltpu.VMEM((slots, 2, rows, wide), BF16),
            pltpu.VMEM((slots, 2, rows, model), BF16),
            pltpu.VMEM((slots, 2, rows, model), BF16),
            pltpu.VMEM((slots, 2, back_rows, wide), BF16),
            pltpu.SemaphoreType.DMA((slots, 2, 6)),
            pltpu.SemaphoreType.DMA((slots, 2, 2)),
            pltpu.SemaphoreType.DMA((len(weights),)),
            pltpu.SemaphoreType.DMA((len(grad_shapes),)),
            pltpu.SemaphoreType.DMA((len(grad_shapes),)),
        ],
        compiler_params=pltpu.CompilerParams(vmem_limit_bytes=VMEM_LIMIT),
        cost_estimate=cost(12.0 * count),
        name="expert",
    )(meta, *weights, *flat, *prior, *sums, *deps)
    return outs[:count], outs[count : 2 * count], outs[2 * count :]


def swap(array, bit, size):
    return lax.ppermute(array, "dp", [(i, i ^ bit) for i in range(size)])


def plane_gather(array, size):
    half = array.shape[0] // 2
    x, y = swap(array, 2, size), swap(array, 4, size)
    across = {0: (array,), 2: (x,), 4: (y,), 6: (swap(y[:half], 2, size), swap(x[half:], 4, size))}
    blocks = [None] * size
    for k in (0, 2, 4, 6):
        blocks[k] = across[k]
        blocks[k + 1] = tuple(swap(piece, 1, size) for piece in across[k])
    return blocks


def add(*terms):
    total = terms[0].astype(F32)
    for term in terms[1:]:
        total = total + term.astype(F32)
    return total.astype(BF16)


def tie_kernel(*refs):
    del refs


def tie_all(arrays, *others):
    anywhere = pl.BlockSpec(memory_space=pl.ANY)
    return pl.pallas_call(
        tie_kernel,
        in_specs=[anywhere] * (len(arrays) + len(others)),
        out_specs=[anywhere] * len(arrays),
        out_shape=[jax.ShapeDtypeStruct(array.shape, array.dtype) for array in arrays],
        input_output_aliases={n: n for n in range(len(arrays))},
        name="tie",
    )(*arrays, *others)


def tie(array, *others):
    return tie_all([array], *others)[0]


def assemble_kernel(splits, widths, waits, me_ref, *refs):
    pieces, outs = refs[: sum(splits)], refs[sum(splits) + waits : -3]
    whole, in_sem, out_sem = refs[-3:]
    copies, at = [], 0
    for k, split in enumerate(splits):
        start = 0
        for piece in pieces[at : at + split]:
            target = whole.at[pl.ds(start, piece.shape[0]), me_ref[0] ^ k]
            copies.append(pltpu.make_async_copy(piece, target, in_sem.at[len(copies)]))
            start += piece.shape[0]
        at += split
    for copy in copies:
        copy.start()
    for copy in copies:
        copy.wait()
    copies, column = [], 0
    for out, (count, width) in zip(outs, widths):
        for n in range(count):
            source = whole.at[:, :, :, pl.ds(column, width)]
            copies.append(pltpu.make_async_copy(source, out.at[:, :, n], out_sem.at[len(copies)]))
            column += width
    for copy in copies:
        copy.start()
    for copy in copies:
        copy.wait()


def assemble(blocks, widths, me, deps=()):
    depth, rows, _ = blocks[0][0].shape
    size = len(blocks)
    splits = [len(pieces) for pieces in blocks]
    flat = [piece for pieces in blocks for piece in pieces]
    outs = pl.pallas_call(
        functools.partial(assemble_kernel, splits, widths, len(deps)),
        in_specs=[pl.BlockSpec(memory_space=pltpu.SMEM)] + [pl.BlockSpec(memory_space=pl.ANY)] * (len(flat) + len(deps)),
        out_specs=[pl.BlockSpec(memory_space=pl.ANY)] * len(widths),
        out_shape=[jax.ShapeDtypeStruct((depth, size, count, rows, width), BF16) for count, width in widths],
        scratch_shapes=[
            pltpu.VMEM((depth, size, rows, sum(count * width for count, width in widths)), BF16),
            pltpu.SemaphoreType.DMA((len(flat),)),
            pltpu.SemaphoreType.DMA((sum(count for count, _ in widths),)),
        ],
        compiler_params=pltpu.CompilerParams(vmem_limit_bytes=VMEM_LIMIT),
        name="assemble",
    )(me.astype(jnp.int32).reshape(1), *flat, *deps)
    return [out.reshape(-1, out.shape[-1]) for out in outs]


def turn_kernel(
    own, other, from_x, from_y, hidden, gates, first_gu, router, gain, grad_out, second_o, out_w, first_o,
    grad_mid_out, grad_mid_b_out, glow_out, glow_sgu, low_sdown, grad_attn, units_out
):
    rows, model = hidden.shape
    experts = gates.shape[1]
    rank = ADAPTER_RANK
    total = own[...].astype(F32) + other[...].astype(F32) + from_x[...].astype(F32) + from_y[...].astype(F32)
    units_out[...] = total[rows:, :]
    tail = total[:rows, model:]
    grad_gates = tail[:, :experts] + tail[:, experts : 2 * experts]
    glow = tail[:, 3 * experts : 3 * experts + 2 * rank].astype(BF16)
    glow_sgu[...] = glow
    low_sdown[...] = tail[:, 3 * experts + 2 * rank : 3 * experts + 3 * rank].astype(BF16)
    gate = gates[...]
    grad_logits = gate * (grad_gates - jnp.sum(gate * grad_gates, axis=-1, keepdims=True))
    logits_hi = grad_logits.astype(BF16)
    rest = grad_logits - logits_hi.astype(F32)
    logits_mid = rest.astype(BF16)
    logits_lo = (rest - logits_mid.astype(F32)).astype(BF16)
    grad_normed = total[:rows, :model] + dot_nt(glow, first_gu[...])
    for part in (logits_hi, logits_mid, logits_lo):
        grad_normed = grad_normed + dot_nt(part, router[...])
    values = hidden[...]
    scale = lax.rsqrt(jnp.mean(values * values, axis=-1, keepdims=True) + EPSILON)
    scaled = grad_normed * gain[...]
    mean = jnp.mean(values * scaled, axis=-1, keepdims=True)
    grad_mid = grad_out[...].astype(F32) + scale * scaled - values * (scale * scale * scale * mean)
    grad_mid_out[...] = grad_mid
    grad_mid_b = grad_mid.astype(BF16)
    grad_mid_b_out[...] = grad_mid_b
    glow = dot_nt(grad_mid_b, second_o[...]).astype(BF16)
    glow_out[...] = glow
    grad_attn[...] = (dot_nt(grad_mid_b, out_w[...]) + dot_nt(glow, first_o[...])).astype(BF16)


def turn(args):
    rows, model = args[4].shape
    rank = ADAPTER_RANK
    vmem = pl.BlockSpec(memory_space=pltpu.VMEM)
    shapes = [
        ((rows, model), F32),
        ((rows, model), BF16),
        ((rows, rank), BF16),
        ((rows, 2 * rank), BF16),
        ((rows, rank), BF16),
        ((rows, HEADS * HEAD_DIM), BF16),
        ((BACK_ROWS, args[0].shape[1]), F32),
    ]
    return pl.pallas_call(
        turn_kernel,
        in_specs=[vmem] * len(args),
        out_specs=[vmem] * len(shapes),
        out_shape=[jax.ShapeDtypeStruct(shape, dtype) for shape, dtype in shapes],
        compiler_params=pltpu.CompilerParams(vmem_limit_bytes=VMEM_LIMIT),
        cost_estimate=cost(4.0),
        name="turn",
    )(*args)


def query_back_kernel(waits, grad_q, normed, low_q, q_w, first_q, second_q, *rest):
    grad_normed, first_query, second_query = rest[waits:]
    glow_q = dot_nt(grad_q[...], second_q[...]).astype(BF16)
    grad_normed[...] = dot_nt(grad_q[...], q_w[...]) + dot_nt(glow_q, first_q[...])
    first_query[...] = dot_tn(normed[...], glow_q)
    second_query[...] = dot_tn(low_q[...], grad_q[...])


def query_back(args, deps):
    rows, model = args[1].shape
    vmem = pl.BlockSpec(memory_space=pltpu.VMEM)
    shapes = [(rows, model), (model, ADAPTER_RANK), (ADAPTER_RANK, HEADS * HEAD_DIM)]
    return pl.pallas_call(
        functools.partial(query_back_kernel, len(deps)),
        in_specs=[vmem] * len(args) + [pl.BlockSpec(memory_space=pl.ANY)] * len(deps),
        out_specs=[vmem] * len(shapes),
        out_shape=[jax.ShapeDtypeStruct(shape, F32) for shape in shapes],
        compiler_params=pltpu.CompilerParams(vmem_limit_bytes=VMEM_LIMIT),
        cost_estimate=cost(0.1),
        name="query_back",
    )(*args, *deps)


def middle_kernel(waits, attn, glow_out, normed2, glow_sgu, grad_mid, out_low, grad_out, low_sdown, *rest):
    first_early, second_out, second_down = rest[waits:]
    rank = ADAPTER_RANK
    first_early[:, :rank] = dot_tn(attn[...], glow_out[...])
    first_early[:, rank:] = dot_tn(normed2[...], glow_sgu[...])
    second_out[...] = dot_tn(out_low[...], grad_mid[...])
    second_down[...] = dot_tn(low_sdown[...], grad_out[...])


def middle(args, deps):
    model = args[0].shape[1]
    rank = ADAPTER_RANK
    vmem = pl.BlockSpec(memory_space=pltpu.VMEM)
    shapes = [(model, 3 * rank), (rank, model), (rank, model)]
    return pl.pallas_call(
        functools.partial(middle_kernel, len(deps)),
        in_specs=[vmem] * len(args) + [pl.BlockSpec(memory_space=pl.ANY)] * len(deps),
        out_specs=[vmem] * len(shapes),
        out_shape=[jax.ShapeDtypeStruct(shape, F32) for shape in shapes],
        compiler_params=pltpu.CompilerParams(vmem_limit_bytes=VMEM_LIMIT),
        cost_estimate=cost(0.1),
        name="middle",
    )(*args, *deps)


def last_kernel(
    owners, grad_kv, normed, low_kv, kv_w, first_kv, second_k, second_v, hidden, gain, grad_mid, grad_normed_q,
    first_query, first_early, second_query, second_early, adapter, grad_hidden, first_out, second_out
):
    rank = ADAPTER_RANK
    heads = range(grad_kv.shape[1] // (2 * HEAD_DIM))
    grad_k = jnp.concatenate([grad_kv[:, 2 * n * HEAD_DIM : (2 * n + 1) * HEAD_DIM] for n in heads], axis=1)
    grad_v = jnp.concatenate([grad_kv[:, (2 * n + 1) * HEAD_DIM : (2 * n + 2) * HEAD_DIM] for n in heads], axis=1)
    width = grad_k.shape[1]
    glow_k = dot_nt(grad_k, second_k[...]).astype(BF16)
    glow_v = dot_nt(grad_v, second_v[...]).astype(BF16)
    grad_normed = grad_normed_q[...] + dot_nt(grad_k, kv_w[:, :width]) + dot_nt(grad_v, kv_w[:, width:])
    grad_normed = grad_normed + dot_nt(glow_k, first_kv[:, :rank]) + dot_nt(glow_v, first_kv[:, rank:])
    values = hidden[...].astype(F32)
    scale = lax.rsqrt(jnp.mean(values * values, axis=-1, keepdims=True) + EPSILON)
    scaled = grad_normed * gain[...]
    mean = jnp.mean(values * scaled, axis=-1, keepdims=True)
    grad_hidden[...] = grad_mid[...] + scale * scaled - values * (scale * scale * scale * mean)
    firsts = [first_query[...], dot_tn(normed[...], glow_k), dot_tn(normed[...], glow_v), first_early[...]]
    tags = jnp.broadcast_to(adapter[...], (first_query.shape[0], LANES - 6 * rank))
    first_out[...] = jnp.concatenate(firsts + [tags], axis=1).astype(BF16)
    seconds = [second_query[...], dot_tn(low_kv[:, :rank], grad_k), dot_tn(low_kv[:, rank:], grad_v), second_early[...]]
    seconds = jnp.concatenate(seconds, axis=1)
    columns = seconds.shape[1] // owners
    padding = jnp.zeros((rank, second_out.shape[1] // rank * LANES - columns), F32)
    for n in range(owners):
        piece = jnp.concatenate([seconds[:, n * columns : (n + 1) * columns], padding], axis=1).astype(BF16)
        for c in range(piece.shape[1] // LANES):
            second_out[n, c * rank : (c + 1) * rank, :] = piece[:, c * LANES : (c + 1) * LANES]


def last(owners, args):
    rows, model = args[7].shape
    columns = (args[13].shape[1] + 2 * KV_HEADS * HEAD_DIM + args[14].shape[1]) // owners
    vmem = pl.BlockSpec(memory_space=pltpu.VMEM)
    return pl.pallas_call(
        functools.partial(last_kernel, owners),
        in_specs=[vmem] * len(args),
        out_specs=[vmem] * 3,
        out_shape=[
            jax.ShapeDtypeStruct((rows, model), F32),
            jax.ShapeDtypeStruct((model, LANES), BF16),
            jax.ShapeDtypeStruct((owners, -(-columns // LANES) * ADAPTER_RANK, LANES), BF16),
        ],
        compiler_params=pltpu.CompilerParams(vmem_limit_bytes=VMEM_LIMIT),
        cost_estimate=cost(2.0),
        name="last",
    )(*args)


def spread_kernel(depth, lines, flat, first_out, second_out):
    rank = ADAPTER_RANK
    size = flat.shape[0] // depth
    row = lax.broadcasted_iota(jnp.int32, (LANES, 1), 0).astype(F32)
    column = lax.broadcasted_iota(jnp.int32, (1, first_out.shape[1]), 1)
    inside = column % LANES
    target = (column // LANES * rank + inside).astype(F32)
    owner = (inside // rank).astype(F32)
    short = lax.broadcasted_iota(jnp.int32, (1, rank), 1).astype(F32)
    chunks = (flat.shape[1] - lines) // rank
    first, second = None, [None] * chunks
    for d in range(size):
        adapter = flat[d, 0:1, 6 * rank : 6 * rank + 1].astype(F32)
        total = flat[d].astype(F32)
        for z in range(1, depth):
            total = total + flat[z * size + d].astype(F32)
        total = total.astype(BF16)
        place = ((target - adapter * float(rank) == row) & (owner == adapter)).astype(F32).astype(BF16)
        lift = (row - adapter * float(rank) == short).astype(F32).astype(BF16)
        part = dot_nn(total[:lines], place)
        first = part if first is None else first + part
        for c in range(chunks):
            part = dot_nn(lift, total[lines + c * rank : lines + (c + 1) * rank])
            second[c] = part if second[c] is None else second[c] + part
    first_out[...] = first
    for c in range(chunks):
        second_out[:, c * LANES : (c + 1) * LANES] = second[c]


def spread(flat, depth, lines):
    vmem = pl.BlockSpec(memory_space=pltpu.VMEM)
    chunks = (flat.shape[1] - lines) // ADAPTER_RANK
    return pl.pallas_call(
        functools.partial(spread_kernel, depth, lines),
        in_specs=[vmem],
        out_specs=[vmem] * 2,
        out_shape=[jax.ShapeDtypeStruct((lines, 6 * LANES), F32), jax.ShapeDtypeStruct((LANES, chunks * LANES), F32)],
        compiler_params=pltpu.CompilerParams(vmem_limit_bytes=VMEM_LIMIT),
        cost_estimate=cost(2.0),
        name="spread",
    )(flat)


def per_device(
    depth,
    size,
    block_input,
    document_number,
    key_present,
    routes,
    sequence_adapter,
    output_gradient,
    norm_scale_pair,
    query_key_value_weight,
    attention_output_weight,
    router_weight,
    shared_gate_up_weight,
    shared_down_weight,
    routed_gate_up_weight,
    routed_down_weight,
    dense_first_factor,
    shared_down_first_factor,
    dense_second_factor,
    routed_first_factor,
    routed_down_first_factor,
    routed_second_factor,
):
    _, rows, model = block_input.shape
    topk = routes.shape[2]
    me = lax.axis_index("dp")
    experts = router_weight.shape[1]
    local_experts = routed_gate_up_weight.shape[0]
    shard_rows = query_key_value_weight.shape[0]
    shared_rows = shared_down_weight.shape[0]
    rank_all = dense_second_factor.shape[0]
    second_columns = dense_second_factor.shape[1]
    capacity = 4 * topk * rows // (3 * experts)
    query_width = HEADS * HEAD_DIM
    kv_width = KV_HEADS * HEAD_DIM
    hops = min(depth - 1, -(-(DOCUMENT_SPAN - 1) // rows))
    rank = ADAPTER_RANK
    units = SHARED_HIDDEN // size
    adapter = sequence_adapter[0]
    forward = [(i, i + 1) for i in range(depth - 1)]
    backward = [(i + 1, i) for i in range(depth - 1)]

    def over_seq(shard):
        return lax.all_gather(shard, "seq", axis=0)

    first_shard = dense_first_factor.reshape(shard_rows, 6 * rank_all)
    second_width = second_columns * rank_all // shard_rows
    groups = second_width // rank_all
    pack_kv = jnp.concatenate(
        [
            query_key_value_weight[:, query_width:],
            first_shard[:, rank_all : 3 * rank_all],
            dense_second_factor.T.reshape(groups, shard_rows, rank_all).transpose(1, 0, 2).reshape(shard_rows, -1),
            jnp.pad(
                jnp.concatenate([router_weight, norm_scale_pair.T], axis=1), ((0, 0), (0, LANES - experts - 2))
            ),
        ],
        axis=1,
    )
    pack_q = jnp.concatenate(
        [
            query_key_value_weight[:, :query_width],
            first_shard[:, :rank_all],
            first_shard[:, 3 * rank_all :],
            attention_output_weight,
        ],
        axis=1,
    )
    seq_kv = over_seq(pack_kv)
    seq_q = over_seq(tie(pack_q, seq_kv))

    flags = jnp.sum((routes[0][..., None] == jnp.arange(experts, dtype=jnp.int32)).astype(F32), axis=1)
    before = (jnp.arange(rows)[:, None] > jnp.arange(rows)[None, :]).astype(BF16)
    slots = jnp.where(flags > 0, dot_nn(before, flags.astype(BF16)), -1.0).astype(BF16)

    def own_columns(matrix):
        return lax.dynamic_slice_in_dim(matrix, adapter * rank, rank, 1)

    def own_factors(matrix):
        count = matrix.shape[1] // rank_all
        return jnp.concatenate([own_columns(matrix[:, n * rank_all : (n + 1) * rank_all]) for n in range(count)], axis=1)

    grad_out_b = output_gradient[0]
    grads_x, grads_y = swap(grad_out_b, 2, size), swap(grad_out_b, 4, size)
    gate_up = shared_gate_up_weight.reshape(shard_rows, 2, depth, size, units // depth)
    gate_up = gate_up.transpose(3, 0, 1, 2, 4).reshape(size, shard_rows, 2 * units)
    gate_up = lax.all_to_all(gate_up, "dp", split_axis=0, concat_axis=0, tiled=True)
    kv_gathered = plane_gather(tie(seq_kv, grads_x, grads_y, gate_up), size)
    grads_x, grads_y = tie_all([grads_x, grads_y], *kv_gathered[6])
    far_grads = (swap(grads_y[: rows // 2], 2, size), swap(grads_x[rows // 2 :], 4, size))
    grad_blocks = [(grad_out_b,), None, (grads_x,), None, (grads_y,), None, far_grads, None]
    kv_w, kv_first, second_t, small = assemble(
        kv_gathered, ((1, 2 * kv_width), (1, 2 * rank_all), (groups, rank_all), (1, LANES)), me
    )
    router_w = small[:, :experts]
    gains = small[:, experts : experts + 2].astype(F32).T
    second = own_columns(second_t).T
    first_kv = own_factors(kv_first)
    widths = [query_width, kv_width, kv_width, model, SHARED_HIDDEN, SHARED_HIDDEN, model]
    edges = [sum(widths[:n]) for n in range(len(widths) + 1)]
    b_parts = [second[:, edges[n] : edges[n + 1]] for n in range(len(widths))]

    x_flat = block_input[0].astype(F32)
    normed = rms_norm(x_flat, gains[0]).astype(BF16)
    low_kv = dot_nn(normed, first_kv).astype(BF16)
    kv_extra = jnp.concatenate([dot_nn(low_kv[:, :rank], b_parts[1]), dot_nn(low_kv[:, rank:], b_parts[2])], axis=1)
    present_tag = jnp.where(key_present == 1, document_number + 1, 0).astype(BF16)
    tag_columns = jnp.broadcast_to(present_tag.reshape(rows, 1), (rows, LANES))
    kv_blocks = [jnp.concatenate([(dot_nn(normed, kv_w) + kv_extra).astype(BF16), tag_columns], axis=1)]
    q_blocks = plane_gather(tie(seq_q, *far_grads), size)
    for k in range(1, size, 2):
        grad_blocks[k] = tuple(swap(piece, 1, size) for piece in grad_blocks[k - 1])
    for h in range(hops):
        block = kv_blocks[-1] if h == 0 else tie(kv_blocks[-1], q_blocks[2][0], q_blocks[4][0])
        kv_blocks.append(lax.ppermute(block, "seq", forward))
        kv_blocks[h] = block
    kv_all = jnp.concatenate(kv_blocks[::-1], axis=0)
    key_tag = kv_all[:, 2 * kv_width : 2 * kv_width + 1].astype(F32)
    query_tag = (document_number + 1).astype(F32)

    down_rows = routed_down_weight.shape[1]
    second_cut = rank_all * routed_second_factor.shape[2] // down_rows
    up_shards, down_shards = [], []
    for j in range(local_experts):
        up_parts = [
            routed_gate_up_weight[j].reshape(-1, 2 * EXPERT_HIDDEN),
            routed_first_factor[j].reshape(-1, 2 * rank_all),
        ]
        down_parts = [
            routed_down_weight[j],
            routed_down_first_factor[j],
            routed_second_factor[j].reshape(down_rows, -1),
        ]
        if j == 0:
            up_parts.append(gate_up.reshape(size * shard_rows, 2 * units))
            shared_down = jnp.concatenate([shared_down_weight, shared_down_first_factor], axis=1)
            down_parts.append(shared_down.reshape(down_rows, -1))
        up_shards.append(jnp.concatenate(up_parts, axis=1))
        down_shards.append(jnp.concatenate(down_parts, axis=1))
    seq_up, seq_down = [], []
    for j in range(local_experts):
        seq_up.append(over_seq(tie(up_shards[j], seq_kv if j == 0 else seq_up[j - 1])))
        seq_down.append(over_seq(tie(down_shards[j], kv_blocks[1] if j == 0 else seq_up[j - 1])))

    q_w, q_first, out_w = assemble(q_blocks, ((1, query_width), (1, 4 * rank_all), (1, model)), me)
    q_first = own_factors(q_first)
    first_q, first_o, first_gu = q_first[:, :rank], q_first[:, rank : 2 * rank], q_first[:, 2 * rank :]
    low_q = dot_nn(normed, first_q).astype(BF16)
    query = (dot_nn(normed, q_w) + dot_nn(low_q, b_parts[0])).astype(BF16)
    glow_sdown = dot_nt(grad_out_b, b_parts[6]).astype(BF16)
    attn, lse = attend(query, kv_all, query_tag, key_tag, hops, (*grad_blocks[3], *grad_blocks[5], *grad_blocks[7]))
    out_low = dot_nn(attn, first_o).astype(BF16)
    mid = x_flat + dot_nn(attn, out_w) + dot_nn(out_low, b_parts[3])
    normed2 = rms_norm(mid, gains[1]).astype(BF16)

    logits = dot_nn(normed2, router_w)
    top = jnp.max(jnp.where(flags > 0, logits, -jnp.inf), axis=-1, keepdims=True)
    weights = jnp.where(flags > 0, jnp.exp(logits - top), 0.0)
    gates = weights / jnp.sum(weights, axis=-1, keepdims=True)
    gates_hi = gates.astype(BF16)
    gates_lo = (gates - gates_hi.astype(F32)).astype(BF16)
    shared_low = dot_nn(normed2, first_gu).astype(BF16)
    own_adapter = jnp.full((rows, LANES - 3 * experts - 3 * rank), adapter.astype(F32)).astype(BF16)
    payload = jnp.concatenate([normed2, slots, gates_hi, gates_lo, shared_low, glow_sdown, own_adapter], axis=1)
    token_blocks = [None] * size
    token_blocks[0], token_blocks[1] = (payload,), (swap(payload, 1, size),)
    tokens_x, tokens_y = swap(payload, 2, size), swap(payload, 4, size)

    def gather_far(tokens_x, tokens_y, *done):
        tokens_x, tokens_y = tie_all([tokens_x, tokens_y], *done)
        half = rows // 2
        token_blocks[2], token_blocks[3] = (tokens_x,), (swap(tokens_x, 1, size),)
        token_blocks[4], token_blocks[5] = (tokens_y,), (swap(tokens_y, 1, size),)
        return swap(tokens_y[:half], 2, size), swap(tokens_x[half:], 4, size)

    def gather_farthest(far, *done):
        far = tuple(tie_all(far, *done))
        token_blocks[6], token_blocks[7] = far, tuple(swap(piece, 1, size) for piece in far)


    moe_parts, back_parts, grad_sums = [None] * size, [None] * size, []
    wide = model + rank_all

    def weights_of(j):
        second_j = seq_down[j][:, :, wide : wide + second_cut]
        second_j = second_j.reshape(depth, rank_all, -1).transpose(1, 0, 2).reshape(rank_all, -1)
        args = [seq_up[j].reshape(model, -1), seq_down[j][:, :, :wide].reshape(EXPERT_HIDDEN, wide), second_j]
        if j == 0:
            args.append(seq_down[j][:, :, wide + second_cut :].reshape(units, wide))
            slices = [
                lax.dynamic_slice_in_dim(second_t[edges[n] : edges[n + 1]].reshape(depth, size, -1, rank_all), me, 1, 1)
                for n in (4, 5)
            ]
            args.append(jnp.concatenate([part.reshape(units, rank_all) for part in slices], axis=0))
        return args

    def run_expert(j, args, group, prior, deps, packed=False):
        meta = jnp.stack([me * local_experts + j, me]).astype(jnp.int32)
        prior = ([moe_parts[k] for k in group], [back_parts[k] for k in group]) if prior else None
        moe_out, back_out, grads = expert_call(
            meta,
            args,
            [token_blocks[k] for k in group],
            [grad_blocks[k] for k in group],
            prior,
            grad_sums[-1],
            packed,
            experts,
            capacity,
            depth,
            deps,
        )
        for n, k in enumerate(group):
            moe_parts[k], back_parts[k] = moe_out[n], back_out[n]
        grad_sums[-1] = list(grads)

    for j in range(local_experts - 1):
        grad_sums.append([])
        args = weights_of(j)
        previous = ()
        for group in ((0, 1), (2, 3), (4, 5), (6, 7)):
            run_expert(j, args, group, j > 0, previous, group == (6, 7))
            previous = (back_parts[group[0]],)
            if j == 0 and group == (0, 1):
                far = gather_far(tokens_x, tokens_y, *previous)
            if j == 0 and group == (2, 3):
                gather_farthest(far, *previous)
    if local_experts == 1:
        gather_farthest(gather_far(tokens_x, tokens_y))

    def scatter(packed):
        return lax.psum_scatter(packed, "seq", scatter_dimension=0, tiled=True)

    packed_sums = [scatter(grads[0]) for grads in grad_sums]
    grad_sums.append([])
    j, prior, half = local_experts - 1, local_experts > 1, (rows + BACK_ROWS) // 2
    args = weights_of(j)
    run_expert(j, args, (6, 7), prior, (back_parts[6],) if prior else ())
    pair_six = add(back_parts[6], swap(back_parts[7], 1, size))
    run_expert(j, args, (2, 3), prior, (pair_six,))
    from_diagonal_x, from_diagonal_y = swap(pair_six[:half], 2, size), swap(pair_six[half:], 4, size)
    pair_two = add(back_parts[2], swap(back_parts[3], 1, size))
    run_expert(j, args, (4, 5), prior, (pair_two,))
    pair_four = add(back_parts[4], swap(tie(back_parts[5], from_diagonal_x, from_diagonal_y, *packed_sums), 1, size))
    to_x = jnp.concatenate([pair_two[:half], add(pair_two[half:], from_diagonal_y)], axis=0)
    to_y = jnp.concatenate([add(pair_four[:half], from_diagonal_x), pair_four[half:]], axis=0)
    run_expert(j, args, (0, 1), prior, (to_x, to_y), True)
    packed_sums.append(scatter(grad_sums[-1][0]))
    from_x, from_y = swap(to_x, 2, size), swap(to_y, 4, size)
    grad_mid, grad_mid_b, glow_out, glow_sgu, low_sdown, grad_attn, shared_units = turn(
        [back_parts[0], swap(tie(back_parts[1], from_x, from_y), 1, size), from_x, from_y, mid, gates, first_gu]
        + [router_w, gains[1:2], grad_out_b, b_parts[3], out_w, first_o]
    )

    half = rows // 2
    far_parts = dict(zip((6, 2, 4, 0), tie_all([moe_parts[k + 1] for k in (6, 2, 4, 0)], from_x, from_y)))
    pair = {k: add(moe_parts[k], swap(far_parts[k], 1, size)) for k in (6, 2, 4, 0)}
    moe_to_x = jnp.concatenate([pair[2][:half], add(pair[2][half:], swap(pair[6][half:], 4, size))], axis=0)
    moe_to_y = jnp.concatenate([add(pair[4][:half], swap(pair[6][:half], 2, size)), pair[4][half:]], axis=0)
    moe_from_x, moe_from_y = swap(moe_to_x, 2, size), swap(moe_to_y, 4, size)
    moe = pair[0].astype(F32) + moe_from_x.astype(F32) + moe_from_y.astype(F32)

    def shared_columns(block):
        block = block[:, :SHARED_HIDDEN].reshape(rank, size, depth, units // depth)
        return block.transpose(0, 2, 1, 3).reshape(rank, SHARED_HIDDEN)

    grad_q, grad_kv = attend_back(
        query, kv_all, grad_attn, lse, query_tag, key_tag, hops, 0, KV_HEADS, (pair[6], pair[2], pair[4])
    )
    moving, early_received = grad_kv[:rows], grad_q
    for h in range(hops):
        if h == 1:
            moving = tie(moving, moe_to_x, moe_to_y)
        received = lax.ppermute(moving, "seq", backward)
        moving = add(grad_kv[(h + 1) * rows : (h + 2) * rows], received)
        if h == 0:
            early_received = received
    grad_normed_q, first_query, second_query = query_back(
        [grad_q, normed, low_q, q_w, first_q, b_parts[0]], (early_received,)
    )
    first_early, second_out, second_down = middle(
        [attn, glow_out, normed2, glow_sgu, grad_mid_b, out_low, grad_out_b, low_sdown],
        (early_received,),
    )
    packed_sums = tie_all(packed_sums, early_received)
    owner_rows = model // depth
    firsts, downs, seconds = [], [], []
    for packed in packed_sums:
        packed = packed[0].astype(F32)
        firsts.append(jnp.stack([packed[:owner_rows], packed[owner_rows : 2 * owner_rows]], axis=1))
        at = 2 * owner_rows + down_rows
        downs.append(packed[2 * owner_rows : at])
        seconds.append(packed[at : at + routed_second_factor.shape[2]].T)
    at += routed_second_factor.shape[2]
    grad_expert_a, grad_expert_a_down, grad_expert_b = jnp.stack(firsts), jnp.stack(downs), jnp.stack(seconds)
    grad_first_down = packed_sums[0][0, at : at + shared_rows].astype(F32)

    hidden_out = (mid + moe + dot_nn(low_sdown, b_parts[6])).astype(BF16)[None]
    second_early = jnp.concatenate(
        [second_out, shared_columns(shared_units[:rank]), shared_columns(shared_units[rank:]), second_down], axis=1
    )
    grad_hidden, first_flat, second_flat = last(
        depth * size,
        [moving, normed, low_kv, kv_w, first_kv, b_parts[1], b_parts[2], block_input[0], gains[0:1], grad_mid]
        + [grad_normed_q, first_query, first_early, second_query, second_early, adapter.astype(F32).reshape(1, 1)],
    )
    flat = jnp.concatenate([first_flat.reshape(depth * size, shard_rows, LANES), second_flat], axis=1)
    flat = lax.all_to_all(flat, ("seq", "dp"), split_axis=0, concat_axis=0, tiled=True)
    grad_first, grad_second = spread(flat, depth, shard_rows)
    grad_first = grad_first.reshape(shard_rows, 6, rank_all)
    grad_second = grad_second[:, :second_columns]
    grad_hidden = grad_hidden[None]
    return (
        hidden_out,
        grad_hidden,
        grad_first,
        grad_first_down,
        grad_second,
        grad_expert_a,
        grad_expert_a_down,
        grad_expert_b,
    )


def solution(mesh):
    in_specs = (
        P("dp", "seq", None),
        P("dp", "seq"),
        P("dp", "seq"),
        P("dp", "seq", None),
        P("dp"),
        P("dp", "seq", None),
        P(None, ("seq", "dp")),
        P(("seq", "dp"), None),
        P(("seq", "dp"), None),
        P(("seq", "dp"), None),
        P(("seq", "dp"), None, None),
        P(("seq", "dp"), None),
        P("dp", "seq", None, None),
        P("dp", "seq", None),
        P(("seq", "dp"), None, None),
        P(("seq", "dp"), None),
        P(None, ("seq", "dp")),
        P("dp", "seq", None, None),
        P("dp", "seq", None),
        P("dp", None, "seq"),
    )
    out_specs = (
        P("dp", "seq", None),
        P("dp", "seq", None),
        P(("seq", "dp"), None, None),
        P(("seq", "dp"), None),
        P(None, ("seq", "dp")),
        P("dp", "seq", None, None),
        P("dp", "seq", None),
        P("dp", None, "seq"),
    )
    return jax.shard_map(
        functools.partial(per_device, mesh.shape["seq"], mesh.shape["dp"]),
        mesh=mesh,
        in_specs=in_specs,
        out_specs=out_specs,
        check_vma=False,
    )
```

```python
import functools
import math

import jax
import jax.numpy as jnp
from jax import lax
from jax.experimental import pallas as pl
from jax.experimental.pallas import tpu as pltpu
from jax.sharding import PartitionSpec as P

HEADS = 12
KV_HEADS = 4
HEAD_DIM = 128
EXPERT_HIDDEN = 512
SHARED_HIDDEN = 1024
ADAPTER_RANK = 16
DOCUMENT_SPAN = 1024

EPSILON = 1e-05
MASKED_SCORE = -1e30
LOG2E = 1.4426950408889634
SCALE = HEAD_DIM ** (-0.5)
LANES = 128
VMEM_LIMIT = 60 * 1024 * 1024

F32 = jnp.float32
BF16 = jnp.bfloat16


def dot_nn(left, right):
    return jnp.dot(left, right, preferred_element_type=F32)


def dot_tn(left, right):
    return lax.dot_general(left, right, (((0,), (0,)), ((), ())), preferred_element_type=F32)


def dot_nt(left, right):
    return lax.dot_general(left, right, (((1,), (1,)), ((), ())), preferred_element_type=F32)


def rms_norm(values, gain):
    return values * lax.rsqrt(jnp.mean(values * values, axis=-1, keepdims=True) + EPSILON) * gain


def cost(microseconds):
    return pl.CostEstimate(flops=int(1153500000 * microseconds), bytes_accessed=1000000, transcendentals=0)


def query_tiles(rows, hops):
    tile = math.gcd(rows, 256)
    spans = []
    for first in range(0, rows, tile):
        oldest = max(0, hops * rows + first - (DOCUMENT_SPAN - 1)) // tile * tile
        spans.append((first, tile, oldest, hops * rows + first + tile - oldest))
    return spans


def fill_bias(spans, shift, query_tag, key_tag, bias):
    for first, tile, oldest, span in spans:
        keys = oldest + lax.broadcasted_iota(jnp.int32, (span, tile), 0)
        queries = shift + first + lax.broadcasted_iota(jnp.int32, (span, tile), 1)
        same = key_tag[oldest : oldest + span, :] == query_tag[:, first : first + tile]
        permit = (keys <= queries) & (same | (keys == queries))
        bias[oldest : oldest + span, first : first + tile] = jnp.where(permit, 0.0, MASKED_SCORE)


def attend_kernel(spans, shift, waits, q_ref, k_ref, v_ref, qt_ref, kt_ref, *rest):
    out_ref, lse_ref, bias = rest[waits:]

    @pl.when(pl.program_id(0) == 0)
    def _():
        fill_bias(spans, shift, qt_ref, kt_ref, bias)

    groups = q_ref.shape[1] // HEAD_DIM
    for first, tile, oldest, span in spans:
        keys = k_ref[oldest : oldest + span, :]
        values = v_ref[oldest : oldest + span, :]
        mask = bias[oldest : oldest + span, first : first + tile]
        for h in range(groups):
            columns = slice(h * HEAD_DIM, (h + 1) * HEAD_DIM)
            scores = dot_nt(keys, q_ref[first : first + tile, columns]) * (SCALE * LOG2E) + mask
            top = jnp.max(scores, axis=0, keepdims=True)
            weights = jnp.exp2(scores - top)
            total = jnp.sum(weights, axis=0, keepdims=True)
            mixed = dot_tn(values, weights.astype(BF16)) / total
            out_ref[first : first + tile, columns] = mixed.T.astype(BF16)
            lse_ref[0, h : h + 1, first : first + tile] = top + jnp.log2(total)


def attend(query, kv_all, query_tag, key_tag, hops, deps=()):
    rows = query.shape[0]
    groups = HEADS // KV_HEADS
    span = kv_all.shape[0]
    spans = query_tiles(rows, hops)
    return pl.pallas_call(
        functools.partial(attend_kernel, spans, hops * rows, len(deps)),
        grid=(KV_HEADS,),
        in_specs=[
            pl.BlockSpec((rows, groups * HEAD_DIM), lambda g: (0, g)),
            pl.BlockSpec((span, HEAD_DIM), lambda g: (0, g)),
            pl.BlockSpec((span, HEAD_DIM), lambda g: (0, KV_HEADS + g)),
            pl.BlockSpec((1, rows), lambda g: (0, 0)),
            pl.BlockSpec((span, 1), lambda g: (0, 0)),
        ]
        + [pl.BlockSpec(memory_space=pl.ANY)] * len(deps),
        out_specs=[
            pl.BlockSpec((rows, groups * HEAD_DIM), lambda g: (0, g)),
            pl.BlockSpec((1, groups, rows), lambda g: (g, 0, 0)),
        ],
        out_shape=[
            jax.ShapeDtypeStruct((rows, HEADS * HEAD_DIM), BF16),
            jax.ShapeDtypeStruct((KV_HEADS, groups, rows), F32),
        ],
        scratch_shapes=[pltpu.VMEM((span, rows), F32)],
        compiler_params=pltpu.CompilerParams(vmem_limit_bytes=VMEM_LIMIT),
        cost_estimate=cost(23.0),
        name="attend",
    )(query, kv_all, kv_all, query_tag, key_tag, *deps)


def attend_back_kernel(
    spans, shift, waits, q_ref, k_ref, v_ref, g_ref, lse_ref, qt_ref, kt_ref, *rest
):
    dq_ref, dkv_ref, bias, dk_acc, dv_acc = rest[waits:]

    @pl.when(pl.program_id(0) == 0)
    def _():
        fill_bias(spans, shift, qt_ref, kt_ref, bias)

    dk_acc[...] = jnp.zeros_like(dk_acc)
    dv_acc[...] = jnp.zeros_like(dv_acc)
    groups = q_ref.shape[1] // HEAD_DIM
    for first, tile, oldest, span in spans:
        keys = k_ref[oldest : oldest + span, :]
        values = v_ref[oldest : oldest + span, :]
        mask = bias[oldest : oldest + span, first : first + tile]
        for h in range(groups):
            columns = slice(h * HEAD_DIM, (h + 1) * HEAD_DIM)
            query = q_ref[first : first + tile, columns]
            grad = g_ref[first : first + tile, columns]
            lse = lse_ref[0, h : h + 1, first : first + tile]
            probs = jnp.exp2(dot_nt(keys, query) * (SCALE * LOG2E) + mask - lse)
            dv_acc[oldest : oldest + span, :] += dot_nn(probs.astype(BF16), grad)
            grad_probs = dot_nt(values, grad)
            delta = jnp.sum(probs * grad_probs, axis=0, keepdims=True)
            grad_scores = (probs * (grad_probs - delta)).astype(BF16)
            dk_acc[oldest : oldest + span, :] += dot_nn(grad_scores, query) * SCALE
            dq_ref[first : first + tile, columns] = (dot_tn(grad_scores, keys) * SCALE).astype(BF16)
    dkv_ref[:, :HEAD_DIM] = dk_acc[...].astype(dkv_ref.dtype)
    dkv_ref[:, HEAD_DIM:] = dv_acc[...].astype(dkv_ref.dtype)


def attend_back(query, kv_all, grad_attn, lse, query_tag, key_tag, hops, head, count, deps=()):
    rows = query.shape[0]
    groups = HEADS // KV_HEADS
    span = kv_all.shape[0]
    spans = query_tiles(rows, hops)
    return pl.pallas_call(
        functools.partial(attend_back_kernel, spans, hops * rows, len(deps)),
        grid=(count,),
        in_specs=[
            pl.BlockSpec((rows, groups * HEAD_DIM), lambda g: (0, head + g)),
            pl.BlockSpec((span, HEAD_DIM), lambda g: (0, head + g)),
            pl.BlockSpec((span, HEAD_DIM), lambda g: (0, KV_HEADS + head + g)),
            pl.BlockSpec((rows, groups * HEAD_DIM), lambda g: (0, head + g)),
            pl.BlockSpec((1, groups, rows), lambda g: (head + g, 0, 0)),
            pl.BlockSpec((1, rows), lambda g: (0, 0)),
            pl.BlockSpec((span, 1), lambda g: (0, 0)),
        ]
        + [pl.BlockSpec(memory_space=pl.ANY)] * len(deps),
        out_specs=[
            pl.BlockSpec((rows, groups * HEAD_DIM), lambda g: (0, g)),
            pl.BlockSpec((span, 2 * HEAD_DIM), lambda g: (0, g)),
        ],
        out_shape=[
            jax.ShapeDtypeStruct((rows, count * groups * HEAD_DIM), BF16),
            jax.ShapeDtypeStruct((span, count * 2 * HEAD_DIM), BF16),
        ],
        scratch_shapes=[
            pltpu.VMEM((span, rows), F32),
            pltpu.VMEM((span, HEAD_DIM), F32),
            pltpu.VMEM((span, HEAD_DIM), F32),
        ],
        compiler_params=pltpu.CompilerParams(vmem_limit_bytes=VMEM_LIMIT),
        cost_estimate=cost(2.0 * count),
        name="attend_back",
    )(query, kv_all, kv_all, grad_attn, lse, query_tag, key_tag, *deps)


BACK_ROWS = 2 * ADAPTER_RANK


def expert_kernel(
    count, splits, experts, capacity, depth, direct, with_prior, with_shared, with_sums, packed, waits, *refs
):
    meta, refs = refs[0], refs[1:]
    weight_count = 5 if with_shared else 3
    given = weight_count - (2 if with_shared else 1) if direct else weight_count
    weight_refs, refs = refs[:given], refs[given:]
    token_refs, grad_refs = [], []
    for split in splits:
        token_refs.append(refs[:split])
        refs = refs[split:]
    for split in splits:
        grad_refs.append(refs[:split])
        refs = refs[split:]
    prior_moe, prior_back = (), ()
    if with_prior:
        prior_moe, refs = refs[:count], refs[count:]
        prior_back, refs = refs[:count], refs[count:]
    grad_count = 4 if with_shared else 3
    sums_in = ()
    if with_sums:
        sums_in, refs = refs[:grad_count], refs[grad_count:]
    refs = refs[waits:]
    moe_refs, refs = refs[:count], refs[count:]
    back_refs, refs = refs[:count], refs[count:]
    out_count = 1 if packed else grad_count
    grad_outs, refs = refs[:out_count], refs[out_count:]
    grad_sums, refs = refs[:grad_count], refs[grad_count:]
    first_grad, down_grad, second_grad = grad_sums[:3]
    weight_bufs, refs = refs[:weight_count], refs[weight_count:]
    if packed:
        pack_buf, refs = refs[0], refs[1:]
    tokens_buf, grad_buf, moe_buf, back_buf, in_sem, out_sem, weight_sem, sum_sem, sum_in_sem = refs

    step = pl.program_id(0)
    steps = count // 2
    slots = min(2, steps)
    slot = lax.rem(step, slots)
    rows, wide = tokens_buf.shape[2:]
    model = wide - LANES
    hidden = EXPERT_HIDDEN
    rank = ADAPTER_RANK
    up_ref, down_ref, second_ref = weight_bufs[:3]

    def weight_copies():
        pairs = list(zip(weight_refs, weight_bufs))
        if direct:
            raw, lines = weight_refs[1], weight_refs[1].shape[1]
            pairs, columns = pairs[:1], second_ref.shape[1] // depth
            for z in range(depth):
                pairs.append((raw.at[z, :, pl.ds(0, wide)], down_ref.at[pl.ds(z * lines, lines)]))
                part = raw.at[z, :, pl.ds(wide, columns)]
                pairs.append((part, second_ref.at[:, pl.ds(z * columns, columns)]))
            if with_shared:
                group, size = 4 * LANES, lines // 4
                for z in range(depth):
                    for q in range(4):
                        width = min(group, wide - q * group)
                        part = raw.at[z, pl.ds(q * size, size), pl.ds(wide + columns, width)]
                        target = weight_bufs[3].at[pl.ds(z * size, size), pl.ds(q * group, width)]
                        pairs.append((part, target))
                pairs.append((weight_refs[2], weight_bufs[4]))
        return [pltpu.make_async_copy(src, dst, weight_sem.at[n]) for n, (src, dst) in enumerate(pairs)]

    def incoming(k, i, kinds):
        copies = []
        to, source = k % slots, 2 * k + i
        for n, (refs_of, buf) in enumerate(((token_refs, tokens_buf), (grad_refs, grad_buf))):
            size = rows // len(refs_of[source])
            for p, piece in enumerate(refs_of[source] if n in kinds else ()):
                part = buf.at[to, i, pl.ds(p * size, size)]
                copies.append(pltpu.make_async_copy(piece, part, in_sem.at[to, i, 2 * n + p]))
        if with_prior and 2 in kinds:
            copies.append(pltpu.make_async_copy(prior_moe[source], moe_buf.at[to, i], in_sem.at[to, i, 4]))
            copies.append(pltpu.make_async_copy(prior_back[source], back_buf.at[to, i], in_sem.at[to, i, 5]))
        return copies

    def outgoing(k, i, kinds=(0, 1)):
        at, source = k % slots, 2 * k + i
        pairs = ((moe_buf, moe_refs), (back_buf, back_refs))
        return [pltpu.make_async_copy(pairs[n][0].at[at, i], pairs[n][1][source], out_sem.at[at, i, n]) for n in kinds]

    def at_step(action, first=0, last=steps):
        for k in range(first, last):
            pl.when(step == k)(functools.partial(action, k))

    def wait_in(i, kind):
        def action(k):
            for copy in incoming(k, i, (kind,)):
                copy.wait()

        at_step(action)

    def start_out(i, n):
        at_step(lambda k: outgoing(k, i, (n,))[0].start())

    def turn(k):
        for i in (0, 1):
            if k >= 1:
                for copy in outgoing(k - 1, i):
                    copy.wait()
            if k + 1 < steps:
                for copy in incoming(k + 1, i, (0, 1, 2)):
                    copy.start()

    def sum_copy(n):
        return pltpu.make_async_copy(pack_buf if packed else grad_sums[n], grad_outs[n], sum_sem.at[n])

    def sum_in(n):
        return pltpu.make_async_copy(sums_in[n], grad_sums[n], sum_in_sem.at[n])

    @pl.when(step == 0)
    def _():
        for i in (0, 1):
            for copy in incoming(0, i, (0,)):
                copy.start()
        for i in (0, 1):
            for copy in incoming(0, i, (1,)):
                copy.start()
        for copy in weight_copies():
            copy.start()
        for i in (0, 1):
            for copy in incoming(0, i, (2,)):
                copy.start()
        for n, total in enumerate(grad_sums):
            if with_sums:
                sum_in(n).start()
            else:
                total[...] = jnp.zeros_like(total)

    expert = meta[0]
    lane = lax.broadcasted_iota(jnp.int32, (1, LANES), 1)
    sub = lax.broadcasted_iota(jnp.int32, (LANES, 1), 0)
    places, picks, gates_of, selects, adapters = [], [], [], [], []
    inputs, grad_rows = [], []
    for i in (0, 1):
        wait_in(i, 0)
        extra_b = tokens_buf[slot, i, :, model:]
        extra = extra_b.astype(F32)
        own = 3 * experts + 3 * rank
        adapter = extra[0:1, own : own + 1]
        select = ((lane // rank).astype(F32) == adapter).astype(F32)
        slot_column = jnp.sum(jnp.where(lane == expert, extra, 0.0), axis=1, keepdims=True)
        slot_row = jnp.sum(jnp.where(sub == expert, extra.T, 0.0), axis=0, keepdims=True)
        place = lax.broadcasted_iota(jnp.int32, (rows, capacity), 1).astype(F32) == slot_column
        pick = lax.broadcasted_iota(jnp.int32, (capacity, rows), 0).astype(F32) == slot_row
        place, pick = place.astype(F32).astype(BF16), pick.astype(F32).astype(BF16)
        picked_extra = dot_nn(pick, extra_b)
        chosen = (lane == experts + expert) | (lane == 2 * experts + expert)
        gates_of.append(jnp.sum(jnp.where(chosen, picked_extra, 0.0), axis=1, keepdims=True))
        inputs.append(dot_nn(pick, tokens_buf[slot, i, :, :model]).astype(BF16))
        picks.append(pick)
        places.append(place)
        adapters.append(adapter)
        selects.append(jnp.broadcast_to(select, (capacity, LANES)))
    for i in (0, 1):
        wait_in(i, 1)
        grad_rows.append(dot_nn(picks[i], grad_buf[slot, i]))
    at_step(turn)
    inputs = jnp.concatenate(inputs, axis=0)
    grad_rows = jnp.concatenate(grad_rows, axis=0)
    gate = jnp.concatenate(gates_of, axis=0)
    select = jnp.concatenate(selects, axis=0)
    select_two = jnp.concatenate([select, select], axis=1)

    @pl.when(step == 0)
    def _():
        for copy in weight_copies():
            copy.wait()

    low = (dot_nn(inputs, up_ref[:, 2 * hidden : 2 * hidden + 2 * LANES]) * select_two).astype(BF16)
    gate_part = dot_nn(inputs, up_ref[:, :hidden]) + dot_nn(low[:, :LANES], second_ref[:, :hidden])
    up_part = dot_nn(inputs, up_ref[:, hidden : 2 * hidden]) + dot_nn(low[:, LANES:], second_ref[:, hidden : 2 * hidden])
    sigmoid = 1.0 / (1.0 + jnp.exp(-gate_part))
    silu = gate_part * sigmoid
    act = (silu * up_part).astype(BF16)
    low_down = (dot_nn(act, down_ref[:, model:]) * select).astype(BF16)
    output = (dot_nn(act, down_ref[:, :model]) + dot_nn(low_down, second_ref[:, 2 * hidden :])).astype(BF16).astype(F32)
    grad_gate = jnp.sum(output * grad_rows, axis=1, keepdims=True)
    weighted = (gate * output).astype(BF16)

    if with_sums:

        @pl.when(step == 0)
        def _():
            for n in range(grad_count):
                sum_in(n).wait()

    grad_y = (gate * grad_rows).astype(BF16)
    glow_down = (dot_nt(grad_y, second_ref[:, 2 * hidden :]) * select).astype(BF16)
    second_grad[:, 2 * hidden :] += dot_tn(low_down, grad_y)
    down_grad[...] += dot_tn(act, glow_down)
    grad_act = dot_nt(grad_y, down_ref[:, :model]) + dot_nt(glow_down, down_ref[:, model:])
    grad_up = (grad_act * silu).astype(BF16)
    grad_gp = (grad_act * up_part * (sigmoid * (1.0 + gate_part * (1.0 - sigmoid)))).astype(BF16)
    glow = jnp.concatenate(
        [
            dot_nt(grad_gp, second_ref[:, :hidden]) * select,
            dot_nt(grad_up, second_ref[:, hidden : 2 * hidden]) * select,
        ],
        axis=1,
    ).astype(BF16)
    second_grad[:, :hidden] += dot_tn(low[:, :LANES], grad_gp)
    second_grad[:, hidden : 2 * hidden] += dot_tn(low[:, LANES:], grad_up)
    first_grad[...] += dot_tn(inputs, glow)
    grad_in = (
        dot_nt(grad_gp, up_ref[:, :hidden])
        + dot_nt(grad_up, up_ref[:, hidden : 2 * hidden])
        + dot_nt(glow, up_ref[:, 2 * hidden : 2 * hidden + 2 * LANES])
    ).astype(BF16)
    gate_hi = grad_gate.astype(BF16).astype(F32)
    gate_lo = grad_gate - gate_hi
    extra_out = (
        jnp.where(lane == expert, gate_hi, 0.0) + jnp.where(lane == experts + expert, gate_lo, 0.0)
    ).astype(BF16)

    @pl.when(step == steps - 1)
    def _():
        if not packed:
            for n in range(3):
                sum_copy(n).start()
            return
        second_t = second_grad[...].T
        parts = [first_grad[:, :LANES], first_grad[:, LANES:], down_grad[...], second_t]
        at = 0
        for part in parts:
            size = part.shape[0] // depth
            for z in range(depth):
                pack_buf[z, at : at + size, :] = part[z * size : (z + 1) * size].astype(BF16)
            at += size

    for i in (0, 1):
        mine = slice(i * capacity, (i + 1) * capacity)
        wait_in(i, 2)
        moe = dot_nn(places[i], weighted[mine])
        back = dot_nn(places[i], grad_in[mine])
        back_extra = dot_nn(places[i], extra_out[mine])
        if with_prior:
            moe = moe + moe_buf[slot, i].astype(F32)
            back = back + back_buf[slot, i, :rows, :model].astype(F32)
            back_extra = back_extra + back_buf[slot, i, :rows, model:].astype(F32)
        if not with_prior:
            back_buf[slot, i, rows:, :] = jnp.zeros((BACK_ROWS, wide), BF16)
        if with_shared:
            sdown_ref, sb_ref = weight_bufs[3:]
            units = sdown_ref.shape[0]
            first_gate, first_up, first_down = 3 * experts, 3 * experts + rank, 3 * experts + 2 * rank
            tokens = tokens_buf[slot, i, :, :model]
            extra_b = tokens_buf[slot, i, :, model:]
            grads = grad_buf[slot, i]
            offset = (lane - sub).astype(F32) - adapters[i] * float(rank)

            def spread(base):
                inside = (sub >= base) & (sub < base + rank)
                return (inside & (offset == float(-base))).astype(F32).astype(BF16)

            to_gate = dot_nt(spread(first_gate), sb_ref[:units]).astype(BF16)
            to_up = dot_nt(spread(first_up), sb_ref[units:]).astype(BF16)
            to_down = dot_nt(spread(first_down), sdown_ref[:, model:]).astype(BF16)
            shared_up = up_ref[:, 2 * hidden + 2 * LANES :]
            gate_up = dot_nn(tokens, shared_up)
            s_gate = gate_up[:, :units] + dot_nn(extra_b, to_gate)
            s_up = gate_up[:, units:] + dot_nn(extra_b, to_up)
            s_sig = 1.0 / (1.0 + jnp.exp(-s_gate))
            s_silu = s_gate * s_sig
            s_act = (s_silu * s_up).astype(BF16)
            moe = moe + dot_nn(s_act, sdown_ref[:, :model])
            s_grad = dot_nt(grads, sdown_ref[:, :model]) + dot_nn(extra_b, to_down)
            grad_sums[3][...] += dot_tn(s_act, dot_nn(extra_b, spread(first_down)).astype(BF16))
            s_gu = (s_grad * s_silu).astype(BF16)
            s_gg = (s_grad * s_up * (s_sig * (1.0 + s_gate * (1.0 - s_sig)))).astype(BF16)
            back_extra = back_extra + dot_nt(s_act, to_down) + dot_nt(s_gg, to_gate) + dot_nt(s_gu, to_up)
            back = back + dot_nt(jnp.concatenate([s_gg, s_gu], axis=1), shared_up)
            columns = pl.ds(pl.multiple_of(meta[1] * units, units), units)
            grad_bg = dot_tn(extra_b, s_gg)[first_gate : first_gate + rank]
            grad_bu = dot_tn(extra_b, s_gu)[first_up : first_up + rank]
            back_buf[slot, i, rows : rows + rank, columns] = grad_bg.astype(BF16)
            back_buf[slot, i, rows + rank :, columns] = grad_bu.astype(BF16)
        moe_buf[slot, i] = moe.astype(BF16)
        start_out(i, 0)
        back_buf[slot, i, :rows, :model] = back.astype(BF16)
        back_buf[slot, i, :rows, model:] = back_extra.astype(BF16)
        start_out(i, 1)

    @pl.when(step == steps - 1)
    def _():
        if packed and with_shared:
            size = grad_sums[3].shape[0] // depth
            for z in range(depth):
                part = grad_sums[3][z * size : (z + 1) * size, :]
                if size % 16:
                    part = jnp.concatenate([part, jnp.zeros((16 - size % 16, LANES), F32)], axis=0)
                pack_buf[z, pack_buf.shape[1] - part.shape[0] :, :] = part.astype(BF16)
        for n in range(0 if packed else 3, out_count):
            sum_copy(n).start()
        for i in (0, 1):
            for copy in outgoing(steps - 1, i):
                copy.wait()
        for n in range(out_count):
            sum_copy(n).wait()


def expert_call(meta, weights, shapes, tokens, grads, prior, sums, packed, experts, capacity, depth, deps=()):
    count = len(tokens)
    with_shared = len(shapes) > 3
    direct = len(weights) < len(shapes)
    splits = [len(pieces) for pieces in tokens]
    rows, model = sum(piece.shape[0] for piece in grads[0]), grads[0][0].shape[1]
    wide = model + LANES
    slots = min(2, count // 2)
    anywhere = pl.BlockSpec(memory_space=pl.ANY)
    prior = [] if prior is None else list(prior[0]) + list(prior[1])
    flat = [piece for pieces in tokens for piece in pieces] + [piece for pieces in grads for piece in pieces]
    grad_shapes = [
        jax.ShapeDtypeStruct((model, 2 * LANES), F32),
        jax.ShapeDtypeStruct((EXPERT_HIDDEN, LANES), F32),
        jax.ShapeDtypeStruct(shapes[2], F32),
    ]
    if with_shared:
        grad_shapes.append(jax.ShapeDtypeStruct((shapes[3][0], LANES), F32))
    out_shapes = grad_shapes
    if packed:
        lines = sum(s.shape[0] for s in grad_shapes[:2]) + model + shapes[2][1]
        lines = lines // depth
        if with_shared:
            lines += -(-shapes[3][0] // depth // 16) * 16
        out_shapes = [jax.ShapeDtypeStruct((depth, lines, LANES), BF16)]
    back_rows = rows + BACK_ROWS
    outs = pl.pallas_call(
        functools.partial(
            expert_kernel,
            *(count, splits, experts, capacity, depth, direct, bool(prior), with_shared, bool(sums), packed, len(deps)),
        ),
        grid=(count // 2,),
        in_specs=[pl.BlockSpec(memory_space=pltpu.SMEM)]
        + [anywhere] * (len(weights) + len(flat) + len(prior) + len(sums) + len(deps)),
        out_specs=[anywhere] * (2 * count + len(out_shapes)),
        out_shape=[jax.ShapeDtypeStruct((rows, model), BF16)] * count
        + [jax.ShapeDtypeStruct((back_rows, wide), BF16)] * count
        + out_shapes,
        scratch_shapes=[pltpu.VMEM(s.shape, F32) for s in grad_shapes]
        + [pltpu.VMEM(shape, BF16) for shape in shapes]
        + ([pltpu.VMEM(out_shapes[0].shape, BF16)] if packed else [])
        + [
            pltpu.VMEM((slots, 2, rows, wide), BF16),
            pltpu.VMEM((slots, 2, rows, model), BF16),
            pltpu.VMEM((slots, 2, rows, model), BF16),
            pltpu.VMEM((slots, 2, back_rows, wide), BF16),
            pltpu.SemaphoreType.DMA((slots, 2, 6)),
            pltpu.SemaphoreType.DMA((slots, 2, 2)),
            pltpu.SemaphoreType.DMA((len(shapes) + 6 * depth,)),
            pltpu.SemaphoreType.DMA((len(grad_shapes),)),
            pltpu.SemaphoreType.DMA((len(grad_shapes),)),
        ],
        compiler_params=pltpu.CompilerParams(vmem_limit_bytes=VMEM_LIMIT),
        cost_estimate=cost(12.0 * count),
        name="expert",
    )(meta, *weights, *flat, *prior, *sums, *deps)
    return outs[:count], outs[count : 2 * count], outs[2 * count :]


def swap(array, bit, size):
    return lax.ppermute(array, "dp", [(i, i ^ bit) for i in range(size)])


def plane_gather(array, size):
    half = array.shape[0] // 2
    x, y = swap(array, 2, size), swap(array, 4, size)
    across = {0: (array,), 2: (x,), 4: (y,), 6: (swap(y[:half], 2, size), swap(x[half:], 4, size))}
    blocks = [None] * size
    for k in (0, 2, 4, 6):
        blocks[k] = across[k]
        blocks[k + 1] = tuple(swap(piece, 1, size) for piece in across[k])
    return blocks


def add(*terms):
    total = terms[0].astype(F32)
    for term in terms[1:]:
        total = total + term.astype(F32)
    return total.astype(BF16)


def tie_kernel(*refs):
    del refs


def tie_all(arrays, *others):
    anywhere = pl.BlockSpec(memory_space=pl.ANY)
    return pl.pallas_call(
        tie_kernel,
        in_specs=[anywhere] * (len(arrays) + len(others)),
        out_specs=[anywhere] * len(arrays),
        out_shape=[jax.ShapeDtypeStruct(array.shape, array.dtype) for array in arrays],
        input_output_aliases={n: n for n in range(len(arrays))},
        name="tie",
    )(*arrays, *others)


def tie(array, *others):
    return tie_all([array], *others)[0]


def assemble_kernel(splits, widths, waits, me_ref, *refs):
    pieces, outs = refs[: sum(splits)], refs[sum(splits) + waits : -3]
    whole, in_sem, out_sem = refs[-3:]
    copies, at = [], 0
    for k, split in enumerate(splits):
        start = 0
        for piece in pieces[at : at + split]:
            target = whole.at[pl.ds(start, piece.shape[0]), me_ref[0] ^ k]
            copies.append(pltpu.make_async_copy(piece, target, in_sem.at[len(copies)]))
            start += piece.shape[0]
        at += split
    for copy in copies:
        copy.start()
    for copy in copies:
        copy.wait()
    copies, column = [], 0
    for out, (count, width) in zip(outs, widths):
        for n in range(count):
            source = whole.at[:, :, :, pl.ds(column, width)]
            copies.append(pltpu.make_async_copy(source, out.at[:, :, n], out_sem.at[len(copies)]))
            column += width
    for copy in copies:
        copy.start()
    for copy in copies:
        copy.wait()


def assemble(blocks, widths, me, deps=()):
    depth, rows, _ = blocks[0][0].shape
    size = len(blocks)
    splits = [len(pieces) for pieces in blocks]
    flat = [piece for pieces in blocks for piece in pieces]
    outs = pl.pallas_call(
        functools.partial(assemble_kernel, splits, widths, len(deps)),
        in_specs=[pl.BlockSpec(memory_space=pltpu.SMEM)] + [pl.BlockSpec(memory_space=pl.ANY)] * (len(flat) + len(deps)),
        out_specs=[pl.BlockSpec(memory_space=pl.ANY)] * len(widths),
        out_shape=[jax.ShapeDtypeStruct((depth, size, count, rows, width), BF16) for count, width in widths],
        scratch_shapes=[
            pltpu.VMEM((depth, size, rows, sum(count * width for count, width in widths)), BF16),
            pltpu.SemaphoreType.DMA((len(flat),)),
            pltpu.SemaphoreType.DMA((sum(count for count, _ in widths),)),
        ],
        compiler_params=pltpu.CompilerParams(vmem_limit_bytes=VMEM_LIMIT),
        name="assemble",
    )(me.astype(jnp.int32).reshape(1), *flat, *deps)
    return [out.reshape(-1, out.shape[-1]) for out in outs]


def turn_kernel(
    own, other, from_x, from_y, hidden, gates, first_gu, router, gain, grad_out, second_o, out_w, first_o,
    grad_mid_out, grad_mid_b_out, glow_out, glow_sgu, low_sdown, grad_attn, units_out
):
    rows, model = hidden.shape
    experts = gates.shape[1]
    rank = ADAPTER_RANK
    total = own[...].astype(F32) + other[...].astype(F32) + from_x[...].astype(F32) + from_y[...].astype(F32)
    units_out[...] = total[rows:, :]
    tail = total[:rows, model:]
    grad_gates = tail[:, :experts] + tail[:, experts : 2 * experts]
    glow = tail[:, 3 * experts : 3 * experts + 2 * rank].astype(BF16)
    glow_sgu[...] = glow
    low_sdown[...] = tail[:, 3 * experts + 2 * rank : 3 * experts + 3 * rank].astype(BF16)
    gate = gates[...]
    grad_logits = gate * (grad_gates - jnp.sum(gate * grad_gates, axis=-1, keepdims=True))
    logits_hi = grad_logits.astype(BF16)
    rest = grad_logits - logits_hi.astype(F32)
    logits_mid = rest.astype(BF16)
    logits_lo = (rest - logits_mid.astype(F32)).astype(BF16)
    grad_normed = total[:rows, :model] + dot_nt(glow, first_gu[...])
    for part in (logits_hi, logits_mid, logits_lo):
        grad_normed = grad_normed + dot_nt(part, router[...])
    values = hidden[...]
    scale = lax.rsqrt(jnp.mean(values * values, axis=-1, keepdims=True) + EPSILON)
    scaled = grad_normed * gain[...]
    mean = jnp.mean(values * scaled, axis=-1, keepdims=True)
    grad_mid = grad_out[...].astype(F32) + scale * scaled - values * (scale * scale * scale * mean)
    grad_mid_out[...] = grad_mid
    grad_mid_b = grad_mid.astype(BF16)
    grad_mid_b_out[...] = grad_mid_b
    glow = dot_nt(grad_mid_b, second_o[...]).astype(BF16)
    glow_out[...] = glow
    grad_attn[...] = (dot_nt(grad_mid_b, out_w[...]) + dot_nt(glow, first_o[...])).astype(BF16)


def turn(args):
    rows, model = args[4].shape
    rank = ADAPTER_RANK
    vmem = pl.BlockSpec(memory_space=pltpu.VMEM)
    shapes = [
        ((rows, model), F32),
        ((rows, model), BF16),
        ((rows, rank), BF16),
        ((rows, 2 * rank), BF16),
        ((rows, rank), BF16),
        ((rows, HEADS * HEAD_DIM), BF16),
        ((BACK_ROWS, args[0].shape[1]), F32),
    ]
    return pl.pallas_call(
        turn_kernel,
        in_specs=[vmem] * len(args),
        out_specs=[vmem] * len(shapes),
        out_shape=[jax.ShapeDtypeStruct(shape, dtype) for shape, dtype in shapes],
        compiler_params=pltpu.CompilerParams(vmem_limit_bytes=VMEM_LIMIT),
        cost_estimate=cost(4.0),
        name="turn",
    )(*args)


def query_back_kernel(waits, grad_q, normed, low_q, q_w, first_q, second_q, *rest):
    grad_normed, first_query, second_query = rest[waits:]
    glow_q = dot_nt(grad_q[...], second_q[...]).astype(BF16)
    grad_normed[...] = dot_nt(grad_q[...], q_w[...]) + dot_nt(glow_q, first_q[...])
    first_query[...] = dot_tn(normed[...], glow_q)
    second_query[...] = dot_tn(low_q[...], grad_q[...])


def query_back(args, deps):
    rows, model = args[1].shape
    vmem = pl.BlockSpec(memory_space=pltpu.VMEM)
    shapes = [(rows, model), (model, ADAPTER_RANK), (ADAPTER_RANK, HEADS * HEAD_DIM)]
    return pl.pallas_call(
        functools.partial(query_back_kernel, len(deps)),
        in_specs=[vmem] * len(args) + [pl.BlockSpec(memory_space=pl.ANY)] * len(deps),
        out_specs=[vmem] * len(shapes),
        out_shape=[jax.ShapeDtypeStruct(shape, F32) for shape in shapes],
        compiler_params=pltpu.CompilerParams(vmem_limit_bytes=VMEM_LIMIT),
        cost_estimate=cost(0.1),
        name="query_back",
    )(*args, *deps)


def middle_kernel(waits, attn, glow_out, normed2, glow_sgu, grad_mid, out_low, grad_out, low_sdown, *rest):
    first_early, second_out, second_down = rest[waits:]
    rank = ADAPTER_RANK
    first_early[:, :rank] = dot_tn(attn[...], glow_out[...])
    first_early[:, rank:] = dot_tn(normed2[...], glow_sgu[...])
    second_out[...] = dot_tn(out_low[...], grad_mid[...])
    second_down[...] = dot_tn(low_sdown[...], grad_out[...])


def middle(args, deps):
    model = args[0].shape[1]
    rank = ADAPTER_RANK
    vmem = pl.BlockSpec(memory_space=pltpu.VMEM)
    shapes = [(model, 3 * rank), (rank, model), (rank, model)]
    return pl.pallas_call(
        functools.partial(middle_kernel, len(deps)),
        in_specs=[vmem] * len(args) + [pl.BlockSpec(memory_space=pl.ANY)] * len(deps),
        out_specs=[vmem] * len(shapes),
        out_shape=[jax.ShapeDtypeStruct(shape, F32) for shape in shapes],
        compiler_params=pltpu.CompilerParams(vmem_limit_bytes=VMEM_LIMIT),
        cost_estimate=cost(0.1),
        name="middle",
    )(*args, *deps)


def last_kernel(
    owners, grad_kv, normed, low_kv, kv_w, first_kv, second_k, second_v, hidden, gain, grad_mid, grad_normed_q,
    first_query, first_early, second_query, second_early, adapter, grad_hidden, first_out, second_out
):
    rank = ADAPTER_RANK
    heads = range(grad_kv.shape[1] // (2 * HEAD_DIM))
    grad_k = jnp.concatenate([grad_kv[:, 2 * n * HEAD_DIM : (2 * n + 1) * HEAD_DIM] for n in heads], axis=1)
    grad_v = jnp.concatenate([grad_kv[:, (2 * n + 1) * HEAD_DIM : (2 * n + 2) * HEAD_DIM] for n in heads], axis=1)
    width = grad_k.shape[1]
    glow_k = dot_nt(grad_k, second_k[...]).astype(BF16)
    glow_v = dot_nt(grad_v, second_v[...]).astype(BF16)
    grad_normed = grad_normed_q[...] + dot_nt(grad_k, kv_w[:, :width]) + dot_nt(grad_v, kv_w[:, width:])
    grad_normed = grad_normed + dot_nt(glow_k, first_kv[:, :rank]) + dot_nt(glow_v, first_kv[:, rank:])
    values = hidden[...].astype(F32)
    scale = lax.rsqrt(jnp.mean(values * values, axis=-1, keepdims=True) + EPSILON)
    scaled = grad_normed * gain[...]
    mean = jnp.mean(values * scaled, axis=-1, keepdims=True)
    grad_hidden[...] = grad_mid[...] + scale * scaled - values * (scale * scale * scale * mean)
    firsts = [first_query[...], dot_tn(normed[...], glow_k), dot_tn(normed[...], glow_v), first_early[...]]
    tags = jnp.broadcast_to(adapter[...], (first_query.shape[0], LANES - 6 * rank))
    first_out[...] = jnp.concatenate(firsts + [tags], axis=1).astype(BF16)
    seconds = [second_query[...], dot_tn(low_kv[:, :rank], grad_k), dot_tn(low_kv[:, rank:], grad_v), second_early[...]]
    seconds = jnp.concatenate(seconds, axis=1)
    columns = seconds.shape[1] // owners
    padding = jnp.zeros((rank, second_out.shape[1] // rank * LANES - columns), F32)
    for n in range(owners):
        piece = jnp.concatenate([seconds[:, n * columns : (n + 1) * columns], padding], axis=1).astype(BF16)
        for c in range(piece.shape[1] // LANES):
            second_out[n, c * rank : (c + 1) * rank, :] = piece[:, c * LANES : (c + 1) * LANES]


def last(owners, args):
    rows, model = args[7].shape
    columns = (args[13].shape[1] + 2 * KV_HEADS * HEAD_DIM + args[14].shape[1]) // owners
    vmem = pl.BlockSpec(memory_space=pltpu.VMEM)
    return pl.pallas_call(
        functools.partial(last_kernel, owners),
        in_specs=[vmem] * len(args),
        out_specs=[vmem] * 3,
        out_shape=[
            jax.ShapeDtypeStruct((rows, model), F32),
            jax.ShapeDtypeStruct((model, LANES), BF16),
            jax.ShapeDtypeStruct((owners, -(-columns // LANES) * ADAPTER_RANK, LANES), BF16),
        ],
        compiler_params=pltpu.CompilerParams(vmem_limit_bytes=VMEM_LIMIT),
        cost_estimate=cost(2.0),
        name="last",
    )(*args)


def spread_kernel(depth, lines, flat, first_out, second_out):
    rank = ADAPTER_RANK
    size = flat.shape[0] // depth
    row = lax.broadcasted_iota(jnp.int32, (LANES, 1), 0).astype(F32)
    column = lax.broadcasted_iota(jnp.int32, (1, first_out.shape[1]), 1)
    inside = column % LANES
    target = (column // LANES * rank + inside).astype(F32)
    owner = (inside // rank).astype(F32)
    short = lax.broadcasted_iota(jnp.int32, (1, rank), 1).astype(F32)
    chunks = (flat.shape[1] - lines) // rank
    first, second = None, [None] * chunks
    for d in range(size):
        adapter = flat[d, 0:1, 6 * rank : 6 * rank + 1].astype(F32)
        total = flat[d].astype(F32)
        for z in range(1, depth):
            total = total + flat[z * size + d].astype(F32)
        total = total.astype(BF16)
        place = ((target - adapter * float(rank) == row) & (owner == adapter)).astype(F32).astype(BF16)
        lift = (row - adapter * float(rank) == short).astype(F32).astype(BF16)
        part = dot_nn(total[:lines], place)
        first = part if first is None else first + part
        for c in range(chunks):
            part = dot_nn(lift, total[lines + c * rank : lines + (c + 1) * rank])
            second[c] = part if second[c] is None else second[c] + part
    first_out[...] = first
    for c in range(chunks):
        second_out[:, c * LANES : (c + 1) * LANES] = second[c]


def spread(flat, depth, lines):
    vmem = pl.BlockSpec(memory_space=pltpu.VMEM)
    chunks = (flat.shape[1] - lines) // ADAPTER_RANK
    return pl.pallas_call(
        functools.partial(spread_kernel, depth, lines),
        in_specs=[vmem],
        out_specs=[vmem] * 2,
        out_shape=[jax.ShapeDtypeStruct((lines, 6 * LANES), F32), jax.ShapeDtypeStruct((LANES, chunks * LANES), F32)],
        compiler_params=pltpu.CompilerParams(vmem_limit_bytes=VMEM_LIMIT),
        cost_estimate=cost(2.0),
        name="spread",
    )(flat)


def per_device(
    depth,
    size,
    block_input,
    document_number,
    key_present,
    routes,
    sequence_adapter,
    output_gradient,
    norm_scale_pair,
    query_key_value_weight,
    attention_output_weight,
    router_weight,
    shared_gate_up_weight,
    shared_down_weight,
    routed_gate_up_weight,
    routed_down_weight,
    dense_first_factor,
    shared_down_first_factor,
    dense_second_factor,
    routed_first_factor,
    routed_down_first_factor,
    routed_second_factor,
):
    _, rows, model = block_input.shape
    topk = routes.shape[2]
    me = lax.axis_index("dp")
    experts = router_weight.shape[1]
    local_experts = routed_gate_up_weight.shape[0]
    shard_rows = query_key_value_weight.shape[0]
    shared_rows = shared_down_weight.shape[0]
    rank_all = dense_second_factor.shape[0]
    second_columns = dense_second_factor.shape[1]
    capacity = 4 * topk * rows // (3 * experts)
    query_width = HEADS * HEAD_DIM
    kv_width = KV_HEADS * HEAD_DIM
    hops = min(depth - 1, -(-(DOCUMENT_SPAN - 1) // rows))
    rank = ADAPTER_RANK
    units = SHARED_HIDDEN // size
    adapter = sequence_adapter[0]
    forward = [(i, i + 1) for i in range(depth - 1)]
    backward = [(i + 1, i) for i in range(depth - 1)]

    def over_seq(shard):
        return lax.all_gather(shard, "seq", axis=0)

    first_shard = dense_first_factor.reshape(shard_rows, 6 * rank_all)
    second_width = second_columns * rank_all // shard_rows
    groups = second_width // rank_all
    pack_kv = jnp.concatenate(
        [
            query_key_value_weight[:, query_width:],
            first_shard[:, rank_all : 3 * rank_all],
            dense_second_factor.T.reshape(groups, shard_rows, rank_all).transpose(1, 0, 2).reshape(shard_rows, -1),
            jnp.pad(
                jnp.concatenate([router_weight, norm_scale_pair.T], axis=1), ((0, 0), (0, LANES - experts - 2))
            ),
        ],
        axis=1,
    )
    pack_q = jnp.concatenate(
        [
            query_key_value_weight[:, :query_width],
            first_shard[:, :rank_all],
            first_shard[:, 3 * rank_all :],
            attention_output_weight,
        ],
        axis=1,
    )
    seq_kv = over_seq(pack_kv)
    seq_q = over_seq(tie(pack_q, seq_kv))

    flags = jnp.sum((routes[0][..., None] == jnp.arange(experts, dtype=jnp.int32)).astype(F32), axis=1)
    before = (jnp.arange(rows)[:, None] > jnp.arange(rows)[None, :]).astype(BF16)
    slots = jnp.where(flags > 0, dot_nn(before, flags.astype(BF16)), -1.0).astype(BF16)

    def own_columns(matrix):
        return lax.dynamic_slice_in_dim(matrix, adapter * rank, rank, 1)

    def own_factors(matrix):
        count = matrix.shape[1] // rank_all
        return jnp.concatenate([own_columns(matrix[:, n * rank_all : (n + 1) * rank_all]) for n in range(count)], axis=1)

    grad_out_b = output_gradient[0]
    grads_x, grads_y = swap(grad_out_b, 2, size), swap(grad_out_b, 4, size)
    gate_up = shared_gate_up_weight.reshape(shard_rows, 2, depth, size, units // depth)
    gate_up = gate_up.transpose(3, 0, 1, 2, 4).reshape(size, shard_rows, 2 * units)
    gate_up = lax.all_to_all(gate_up, "dp", split_axis=0, concat_axis=0, tiled=True)
    kv_gathered = plane_gather(tie(seq_kv, grads_x, grads_y, gate_up), size)
    grads_x, grads_y = tie_all([grads_x, grads_y], *kv_gathered[6])
    far_grads = (swap(grads_y[: rows // 2], 2, size), swap(grads_x[rows // 2 :], 4, size))
    grad_blocks = [(grad_out_b,), None, (grads_x,), None, (grads_y,), None, far_grads, None]
    kv_w, kv_first, second_t, small = assemble(
        kv_gathered, ((1, 2 * kv_width), (1, 2 * rank_all), (groups, rank_all), (1, LANES)), me
    )
    router_w = small[:, :experts]
    gains = small[:, experts : experts + 2].astype(F32).T
    second = own_columns(second_t).T
    first_kv = own_factors(kv_first)
    widths = [query_width, kv_width, kv_width, model, SHARED_HIDDEN, SHARED_HIDDEN, model]
    edges = [sum(widths[:n]) for n in range(len(widths) + 1)]
    b_parts = [second[:, edges[n] : edges[n + 1]] for n in range(len(widths))]

    down_rows = routed_down_weight.shape[1]
    second_cut = rank_all * routed_second_factor.shape[2] // down_rows
    up_shards, down_shards = [], []
    for j in range(local_experts):
        up_parts = [
            routed_gate_up_weight[j].reshape(-1, 2 * EXPERT_HIDDEN),
            routed_first_factor[j].reshape(-1, 2 * rank_all),
        ]
        down_parts = [
            routed_down_weight[j],
            routed_down_first_factor[j],
            routed_second_factor[j].reshape(down_rows, -1),
        ]
        if j == 0:
            up_parts.append(gate_up.reshape(size * shard_rows, 2 * units))
            shared_down = jnp.concatenate([shared_down_weight, shared_down_first_factor], axis=1)
            shared_down = jnp.pad(shared_down, ((0, 0), (0, 16 * LANES - shared_down.shape[1])))
            shared_down = shared_down.reshape(shared_rows, 4, 4 * LANES).transpose(1, 0, 2)
            down_parts.append(shared_down.reshape(down_rows, -1))
        up_shards.append(jnp.concatenate(up_parts, axis=1))
        down_shards.append(jnp.concatenate(down_parts, axis=1))
    first_down = over_seq(tie(down_shards[0], seq_kv))

    x_flat = block_input[0].astype(F32)
    normed = rms_norm(x_flat, gains[0]).astype(BF16)
    low_kv = dot_nn(normed, first_kv).astype(BF16)
    kv_extra = jnp.concatenate([dot_nn(low_kv[:, :rank], b_parts[1]), dot_nn(low_kv[:, rank:], b_parts[2])], axis=1)
    present_tag = jnp.where(key_present == 1, document_number + 1, 0).astype(BF16)
    tag_columns = jnp.broadcast_to(present_tag.reshape(rows, 1), (rows, LANES))
    kv_blocks = [jnp.concatenate([(dot_nn(normed, kv_w) + kv_extra).astype(BF16), tag_columns], axis=1)]
    q_blocks = plane_gather(tie(seq_q, *far_grads), size)
    for k in range(1, size, 2):
        grad_blocks[k] = tuple(swap(piece, 1, size) for piece in grad_blocks[k - 1])
    for h in range(hops):
        block = kv_blocks[-1] if h == 0 else tie(kv_blocks[-1], q_blocks[2][0], q_blocks[4][0], first_down)
        kv_blocks.append(lax.ppermute(block, "seq", forward))
        kv_blocks[h] = block
    kv_all = jnp.concatenate(kv_blocks[::-1], axis=0)
    key_tag = kv_all[:, 2 * kv_width : 2 * kv_width + 1].astype(F32)
    query_tag = (document_number + 1).astype(F32)

    seq_up, seq_down = [over_seq(tie(up_shards[0], kv_blocks[hops]))], [first_down]
    for j in range(1, local_experts):
        seq_up.append(over_seq(tie(up_shards[j], seq_down[j - 1])))
        seq_down.append(over_seq(tie(down_shards[j], seq_up[j - 1])))

    q_w, q_first, out_w = assemble(q_blocks, ((1, query_width), (1, 4 * rank_all), (1, model)), me)
    q_first = own_factors(q_first)
    first_q, first_o, first_gu = q_first[:, :rank], q_first[:, rank : 2 * rank], q_first[:, 2 * rank :]
    low_q = dot_nn(normed, first_q).astype(BF16)
    query = (dot_nn(normed, q_w) + dot_nn(low_q, b_parts[0])).astype(BF16)
    glow_sdown = dot_nt(grad_out_b, b_parts[6]).astype(BF16)
    attn, lse = attend(query, kv_all, query_tag, key_tag, hops, (*grad_blocks[3], *grad_blocks[5], *grad_blocks[7]))
    out_low = dot_nn(attn, first_o).astype(BF16)
    mid = x_flat + dot_nn(attn, out_w) + dot_nn(out_low, b_parts[3])
    normed2 = rms_norm(mid, gains[1]).astype(BF16)

    logits = dot_nn(normed2, router_w)
    top = jnp.max(jnp.where(flags > 0, logits, -jnp.inf), axis=-1, keepdims=True)
    weights = jnp.where(flags > 0, jnp.exp(logits - top), 0.0)
    gates = weights / jnp.sum(weights, axis=-1, keepdims=True)
    gates_hi = gates.astype(BF16)
    gates_lo = (gates - gates_hi.astype(F32)).astype(BF16)
    shared_low = dot_nn(normed2, first_gu).astype(BF16)
    own_adapter = jnp.full((rows, LANES - 3 * experts - 3 * rank), adapter.astype(F32)).astype(BF16)
    payload = jnp.concatenate([normed2, slots, gates_hi, gates_lo, shared_low, glow_sdown, own_adapter], axis=1)
    token_blocks = [None] * size
    token_blocks[0], token_blocks[1] = (payload,), (swap(payload, 1, size),)
    tokens_x, tokens_y = swap(payload, 2, size), swap(payload, 4, size)

    def gather_far(tokens_x, tokens_y, *done):
        tokens_x, tokens_y = tie_all([tokens_x, tokens_y], *done)
        half = rows // 2
        token_blocks[2], token_blocks[3] = (tokens_x,), (swap(tokens_x, 1, size),)
        token_blocks[4], token_blocks[5] = (tokens_y,), (swap(tokens_y, 1, size),)
        return swap(tokens_y[:half], 2, size), swap(tokens_x[half:], 4, size)

    def gather_farthest(far, *done):
        far = tuple(tie_all(far, *done))
        token_blocks[6], token_blocks[7] = far, tuple(swap(piece, 1, size) for piece in far)


    moe_parts, back_parts, grad_sums = [None] * size, [None] * size, []
    wide = model + rank_all

    direct = down_rows == rank_all
    shapes = [None] * local_experts

    def weights_of(j):
        args = [seq_up[j].reshape(model, -1)]
        shapes[j] = [args[0].shape, (EXPERT_HIDDEN, wide), (rank_all, depth * second_cut * down_rows // rank_all)]
        if direct:
            args.append(seq_down[j])
        else:
            second_j = seq_down[j][:, :, wide : wide + second_cut]
            second_j = second_j.reshape(depth, rank_all, -1).transpose(1, 0, 2).reshape(rank_all, -1)
            args += [seq_down[j][:, :, :wide].reshape(EXPERT_HIDDEN, wide), second_j]
        if j == 0:
            if not direct:
                parts = seq_down[j][:, :, wide + second_cut :].reshape(depth, 4, shared_rows, 4 * LANES)
                args.append(parts.transpose(0, 2, 1, 3).reshape(units, -1)[:, :wide])
            slices = [
                lax.dynamic_slice_in_dim(second_t[edges[n] : edges[n + 1]].reshape(depth, size, -1, rank_all), me, 1, 1)
                for n in (4, 5)
            ]
            args.append(jnp.concatenate([part.reshape(units, rank_all) for part in slices], axis=0))
            shapes[j] += [(units, wide), args[-1].shape]
        return args

    def run_expert(j, args, group, prior, deps, packed=False):
        meta = jnp.stack([me * local_experts + j, me]).astype(jnp.int32)
        prior = ([moe_parts[k] for k in group], [back_parts[k] for k in group]) if prior else None
        moe_out, back_out, grads = expert_call(
            meta,
            args,
            shapes[j],
            [token_blocks[k] for k in group],
            [grad_blocks[k] for k in group],
            prior,
            grad_sums[-1],
            packed,
            experts,
            capacity,
            depth,
            deps,
        )
        for n, k in enumerate(group):
            moe_parts[k], back_parts[k] = moe_out[n], back_out[n]
        grad_sums[-1] = list(grads)

    for j in range(local_experts - 1):
        grad_sums.append([])
        args = weights_of(j)
        previous = ()
        for group in ((0, 1), (2, 3), (4, 5), (6, 7)):
            run_expert(j, args, group, j > 0, previous, group == (6, 7))
            previous = (back_parts[group[0]],)
            if j == 0 and group == (0, 1):
                far = gather_far(tokens_x, tokens_y, *previous)
            if j == 0 and group == (2, 3):
                gather_farthest(far, *previous)
    if local_experts == 1:
        gather_farthest(gather_far(tokens_x, tokens_y))

    def scatter(packed):
        return lax.psum_scatter(packed, "seq", scatter_dimension=0, tiled=True)

    packed_sums = [scatter(grads[0]) for grads in grad_sums]
    grad_sums.append([])
    j, prior, half = local_experts - 1, local_experts > 1, (rows + BACK_ROWS) // 2
    args = weights_of(j)
    run_expert(j, args, (6, 7), prior, (back_parts[6],) if prior else ())
    pair_six = add(back_parts[6], swap(back_parts[7], 1, size))
    run_expert(j, args, (2, 3), prior, (pair_six,))
    from_diagonal_x, from_diagonal_y = swap(pair_six[:half], 2, size), swap(pair_six[half:], 4, size)
    pair_two = add(back_parts[2], swap(back_parts[3], 1, size))
    run_expert(j, args, (4, 5), prior, (pair_two,))
    pair_four = add(back_parts[4], swap(tie(back_parts[5], from_diagonal_x, from_diagonal_y, *packed_sums), 1, size))
    to_x = jnp.concatenate([pair_two[:half], add(pair_two[half:], from_diagonal_y)], axis=0)
    to_y = jnp.concatenate([add(pair_four[:half], from_diagonal_x), pair_four[half:]], axis=0)
    run_expert(j, args, (0, 1), prior, (to_x, to_y), True)
    packed_sums.append(scatter(grad_sums[-1][0]))
    from_x, from_y = swap(to_x, 2, size), swap(to_y, 4, size)
    grad_mid, grad_mid_b, glow_out, glow_sgu, low_sdown, grad_attn, shared_units = turn(
        [back_parts[0], swap(tie(back_parts[1], from_x, from_y), 1, size), from_x, from_y, mid, gates, first_gu]
        + [router_w, gains[1:2], grad_out_b, b_parts[3], out_w, first_o]
    )

    half = rows // 2
    far_parts = dict(zip((6, 2, 4, 0), tie_all([moe_parts[k + 1] for k in (6, 2, 4, 0)], from_x, from_y)))
    pair = {k: add(moe_parts[k], swap(far_parts[k], 1, size)) for k in (6, 2, 4, 0)}
    moe_to_x = jnp.concatenate([pair[2][:half], add(pair[2][half:], swap(pair[6][half:], 4, size))], axis=0)
    moe_to_y = jnp.concatenate([add(pair[4][:half], swap(pair[6][:half], 2, size)), pair[4][half:]], axis=0)
    moe_from_x, moe_from_y = swap(moe_to_x, 2, size), swap(moe_to_y, 4, size)
    moe = pair[0].astype(F32) + moe_from_x.astype(F32) + moe_from_y.astype(F32)

    def shared_columns(block):
        block = block[:, :SHARED_HIDDEN].reshape(rank, size, depth, units // depth)
        return block.transpose(0, 2, 1, 3).reshape(rank, SHARED_HIDDEN)

    grad_q, grad_kv = attend_back(
        query, kv_all, grad_attn, lse, query_tag, key_tag, hops, 0, KV_HEADS, (pair[6], pair[2], pair[4])
    )
    moving, early_received = grad_kv[:rows], grad_q
    for h in range(hops):
        if h == 1:
            moving = tie(moving, moe_to_x, moe_to_y)
        received = lax.ppermute(moving, "seq", backward)
        moving = add(grad_kv[(h + 1) * rows : (h + 2) * rows], received)
        if h == 0:
            early_received = received
    grad_normed_q, first_query, second_query = query_back(
        [grad_q, normed, low_q, q_w, first_q, b_parts[0]], (early_received,)
    )
    first_early, second_out, second_down = middle(
        [attn, glow_out, normed2, glow_sgu, grad_mid_b, out_low, grad_out_b, low_sdown],
        (early_received,),
    )
    packed_sums = tie_all(packed_sums, early_received)
    owner_rows = model // depth
    firsts, downs, seconds = [], [], []
    for packed in packed_sums:
        packed = packed[0].astype(F32)
        firsts.append(jnp.stack([packed[:owner_rows], packed[owner_rows : 2 * owner_rows]], axis=1))
        at = 2 * owner_rows + down_rows
        downs.append(packed[2 * owner_rows : at])
        seconds.append(packed[at : at + routed_second_factor.shape[2]].T)
    at += routed_second_factor.shape[2]
    grad_expert_a, grad_expert_a_down, grad_expert_b = jnp.stack(firsts), jnp.stack(downs), jnp.stack(seconds)
    grad_first_down = packed_sums[0][0, at : at + shared_rows].astype(F32)

    hidden_out = (mid + moe + dot_nn(low_sdown, b_parts[6])).astype(BF16)[None]
    second_early = jnp.concatenate(
        [second_out, shared_columns(shared_units[:rank]), shared_columns(shared_units[rank:]), second_down], axis=1
    )
    grad_hidden, first_flat, second_flat = last(
        depth * size,
        [moving, normed, low_kv, kv_w, first_kv, b_parts[1], b_parts[2], block_input[0], gains[0:1], grad_mid]
        + [grad_normed_q, first_query, first_early, second_query, second_early, adapter.astype(F32).reshape(1, 1)],
    )
    flat = jnp.concatenate([first_flat.reshape(depth * size, shard_rows, LANES), second_flat], axis=1)
    flat = lax.all_to_all(flat, ("seq", "dp"), split_axis=0, concat_axis=0, tiled=True)
    grad_first, grad_second = spread(flat, depth, shard_rows)
    grad_first = grad_first.reshape(shard_rows, 6, rank_all)
    grad_second = grad_second[:, :second_columns]
    grad_hidden = grad_hidden[None]
    return (
        hidden_out,
        grad_hidden,
        grad_first,
        grad_first_down,
        grad_second,
        grad_expert_a,
        grad_expert_a_down,
        grad_expert_b,
    )


def solution(mesh):
    in_specs = (
        P("dp", "seq", None),
        P("dp", "seq"),
        P("dp", "seq"),
        P("dp", "seq", None),
        P("dp"),
        P("dp", "seq", None),
        P(None, ("seq", "dp")),
        P(("seq", "dp"), None),
        P(("seq", "dp"), None),
        P(("seq", "dp"), None),
        P(("seq", "dp"), None, None),
        P(("seq", "dp"), None),
        P("dp", "seq", None, None),
        P("dp", "seq", None),
        P(("seq", "dp"), None, None),
        P(("seq", "dp"), None),
        P(None, ("seq", "dp")),
        P("dp", "seq", None, None),
        P("dp", "seq", None),
        P("dp", None, "seq"),
    )
    out_specs = (
        P("dp", "seq", None),
        P("dp", "seq", None),
        P(("seq", "dp"), None, None),
        P(("seq", "dp"), None),
        P(None, ("seq", "dp")),
        P("dp", "seq", None, None),
        P("dp", "seq", None),
        P("dp", None, "seq"),
    )
    return jax.shard_map(
        functools.partial(per_device, mesh.shape["seq"], mesh.shape["dp"]),
        mesh=mesh,
        in_specs=in_specs,
        out_specs=out_specs,
        check_vma=False,
    )
```

```python
import functools
import math

import jax
import jax.numpy as jnp
from jax import lax
from jax.experimental import pallas as pl
from jax.experimental.pallas import tpu as pltpu
from jax.sharding import PartitionSpec as P

HEADS = 12
KV_HEADS = 4
HEAD_DIM = 128
EXPERT_HIDDEN = 512
SHARED_HIDDEN = 1024
ADAPTER_RANK = 16
DOCUMENT_SPAN = 1024

EPSILON = 1e-05
MASKED_SCORE = -1e30
LOG2E = 1.4426950408889634
SCALE = HEAD_DIM ** (-0.5)
LANES = 128
VMEM_LIMIT = 60 * 1024 * 1024

F32 = jnp.float32
BF16 = jnp.bfloat16


def dot_nn(left, right):
    return jnp.dot(left, right, preferred_element_type=F32)


def dot_tn(left, right):
    return lax.dot_general(left, right, (((0,), (0,)), ((), ())), preferred_element_type=F32)


def dot_nt(left, right):
    return lax.dot_general(left, right, (((1,), (1,)), ((), ())), preferred_element_type=F32)


def rms_norm(values, gain):
    return values * lax.rsqrt(jnp.mean(values * values, axis=-1, keepdims=True) + EPSILON) * gain


def cost(microseconds):
    return pl.CostEstimate(flops=int(1153500000 * microseconds), bytes_accessed=1000000, transcendentals=0)


def query_tiles(rows, hops):
    tile = math.gcd(rows, 256)
    spans = []
    for first in range(0, rows, tile):
        oldest = max(0, hops * rows + first - (DOCUMENT_SPAN - 1)) // tile * tile
        spans.append((first, tile, oldest, hops * rows + first + tile - oldest))
    return spans


def fill_bias(spans, shift, query_tag, key_tag, bias):
    for first, tile, oldest, span in spans:
        keys = oldest + lax.broadcasted_iota(jnp.int32, (span, tile), 0)
        queries = shift + first + lax.broadcasted_iota(jnp.int32, (span, tile), 1)
        same = key_tag[oldest : oldest + span, :] == query_tag[:, first : first + tile]
        permit = (keys <= queries) & (same | (keys == queries))
        bias[oldest : oldest + span, first : first + tile] = jnp.where(permit, 0.0, MASKED_SCORE)


def attend_kernel(spans, shift, waits, q_ref, k_ref, v_ref, qt_ref, kt_ref, *rest):
    out_ref, lse_ref, bias = rest[waits:]

    @pl.when(pl.program_id(0) == 0)
    def _():
        fill_bias(spans, shift, qt_ref, kt_ref, bias)

    groups = q_ref.shape[1] // HEAD_DIM
    for first, tile, oldest, span in spans:
        keys = k_ref[oldest : oldest + span, :]
        values = v_ref[oldest : oldest + span, :]
        mask = bias[oldest : oldest + span, first : first + tile]
        for h in range(groups):
            columns = slice(h * HEAD_DIM, (h + 1) * HEAD_DIM)
            scores = dot_nt(keys, q_ref[first : first + tile, columns]) * (SCALE * LOG2E) + mask
            top = jnp.max(scores, axis=0, keepdims=True)
            weights = jnp.exp2(scores - top)
            total = jnp.sum(weights, axis=0, keepdims=True)
            mixed = dot_tn(values, weights.astype(BF16)) / total
            out_ref[first : first + tile, columns] = mixed.T.astype(BF16)
            lse_ref[0, h : h + 1, first : first + tile] = top + jnp.log2(total)


def attend(query, kv_all, query_tag, key_tag, hops, deps=()):
    rows = query.shape[0]
    groups = HEADS // KV_HEADS
    span = kv_all.shape[0]
    spans = query_tiles(rows, hops)
    return pl.pallas_call(
        functools.partial(attend_kernel, spans, hops * rows, len(deps)),
        grid=(KV_HEADS,),
        in_specs=[
            pl.BlockSpec((rows, groups * HEAD_DIM), lambda g: (0, g)),
            pl.BlockSpec((span, HEAD_DIM), lambda g: (0, g)),
            pl.BlockSpec((span, HEAD_DIM), lambda g: (0, KV_HEADS + g)),
            pl.BlockSpec((1, rows), lambda g: (0, 0)),
            pl.BlockSpec((span, 1), lambda g: (0, 0)),
        ]
        + [pl.BlockSpec(memory_space=pl.ANY)] * len(deps),
        out_specs=[
            pl.BlockSpec((rows, groups * HEAD_DIM), lambda g: (0, g)),
            pl.BlockSpec((1, groups, rows), lambda g: (g, 0, 0)),
        ],
        out_shape=[
            jax.ShapeDtypeStruct((rows, HEADS * HEAD_DIM), BF16),
            jax.ShapeDtypeStruct((KV_HEADS, groups, rows), F32),
        ],
        scratch_shapes=[pltpu.VMEM((span, rows), F32)],
        compiler_params=pltpu.CompilerParams(vmem_limit_bytes=VMEM_LIMIT),
        cost_estimate=cost(23.0),
        name="attend",
    )(query, kv_all, kv_all, query_tag, key_tag, *deps)


def attend_back_kernel(
    spans, shift, waits, q_ref, k_ref, v_ref, g_ref, lse_ref, qt_ref, kt_ref, *rest
):
    dq_ref, dkv_ref, bias, dk_acc, dv_acc = rest[waits:]

    @pl.when(pl.program_id(0) == 0)
    def _():
        fill_bias(spans, shift, qt_ref, kt_ref, bias)

    dk_acc[...] = jnp.zeros_like(dk_acc)
    dv_acc[...] = jnp.zeros_like(dv_acc)
    groups = q_ref.shape[1] // HEAD_DIM
    for first, tile, oldest, span in spans:
        keys = k_ref[oldest : oldest + span, :]
        values = v_ref[oldest : oldest + span, :]
        mask = bias[oldest : oldest + span, first : first + tile]
        for h in range(groups):
            columns = slice(h * HEAD_DIM, (h + 1) * HEAD_DIM)
            query = q_ref[first : first + tile, columns]
            grad = g_ref[first : first + tile, columns]
            lse = lse_ref[0, h : h + 1, first : first + tile]
            probs = jnp.exp2(dot_nt(keys, query) * (SCALE * LOG2E) + mask - lse)
            dv_acc[oldest : oldest + span, :] += dot_nn(probs.astype(BF16), grad)
            grad_probs = dot_nt(values, grad)
            delta = jnp.sum(probs * grad_probs, axis=0, keepdims=True)
            grad_scores = (probs * (grad_probs - delta)).astype(BF16)
            dk_acc[oldest : oldest + span, :] += dot_nn(grad_scores, query) * SCALE
            dq_ref[first : first + tile, columns] = (dot_tn(grad_scores, keys) * SCALE).astype(BF16)
    dkv_ref[:, :HEAD_DIM] = dk_acc[...].astype(dkv_ref.dtype)
    dkv_ref[:, HEAD_DIM:] = dv_acc[...].astype(dkv_ref.dtype)


def attend_back(query, kv_all, grad_attn, lse, query_tag, key_tag, hops, head, count, deps=()):
    rows = query.shape[0]
    groups = HEADS // KV_HEADS
    span = kv_all.shape[0]
    spans = query_tiles(rows, hops)
    return pl.pallas_call(
        functools.partial(attend_back_kernel, spans, hops * rows, len(deps)),
        grid=(count,),
        in_specs=[
            pl.BlockSpec((rows, groups * HEAD_DIM), lambda g: (0, head + g)),
            pl.BlockSpec((span, HEAD_DIM), lambda g: (0, head + g)),
            pl.BlockSpec((span, HEAD_DIM), lambda g: (0, KV_HEADS + head + g)),
            pl.BlockSpec((rows, groups * HEAD_DIM), lambda g: (0, head + g)),
            pl.BlockSpec((1, groups, rows), lambda g: (head + g, 0, 0)),
            pl.BlockSpec((1, rows), lambda g: (0, 0)),
            pl.BlockSpec((span, 1), lambda g: (0, 0)),
        ]
        + [pl.BlockSpec(memory_space=pl.ANY)] * len(deps),
        out_specs=[
            pl.BlockSpec((rows, groups * HEAD_DIM), lambda g: (0, g)),
            pl.BlockSpec((span, 2 * HEAD_DIM), lambda g: (0, g)),
        ],
        out_shape=[
            jax.ShapeDtypeStruct((rows, count * groups * HEAD_DIM), BF16),
            jax.ShapeDtypeStruct((span, count * 2 * HEAD_DIM), BF16),
        ],
        scratch_shapes=[
            pltpu.VMEM((span, rows), F32),
            pltpu.VMEM((span, HEAD_DIM), F32),
            pltpu.VMEM((span, HEAD_DIM), F32),
        ],
        compiler_params=pltpu.CompilerParams(vmem_limit_bytes=VMEM_LIMIT),
        cost_estimate=cost(2.0 * count),
        name="attend_back",
    )(query, kv_all, kv_all, grad_attn, lse, query_tag, key_tag, *deps)


BACK_ROWS = 2 * ADAPTER_RANK


def expert_kernel(
    count, splits, experts, capacity, depth, direct, with_prior, with_shared, with_sums, packed, waits, *refs
):
    meta, refs = refs[0], refs[1:]
    weight_count = 5 if with_shared else 3
    given = weight_count - (2 if with_shared else 1) if direct else weight_count
    weight_refs, refs = refs[:given], refs[given:]
    token_refs, grad_refs = [], []
    for split in splits:
        token_refs.append(refs[:split])
        refs = refs[split:]
    for split in splits:
        grad_refs.append(refs[:split])
        refs = refs[split:]
    prior_moe, prior_back = (), ()
    if with_prior:
        prior_moe, refs = refs[:count], refs[count:]
        prior_back, refs = refs[:count], refs[count:]
    grad_count = 4 if with_shared else 3
    sums_in = ()
    if with_sums:
        sums_in, refs = refs[:grad_count], refs[grad_count:]
    refs = refs[waits:]
    moe_refs, refs = refs[:count], refs[count:]
    back_refs, refs = refs[:count], refs[count:]
    out_count = 1 if packed else grad_count
    grad_outs, refs = refs[:out_count], refs[out_count:]
    grad_sums, refs = refs[:grad_count], refs[grad_count:]
    first_grad, down_grad, second_grad = grad_sums[:3]
    weight_bufs, refs = refs[:weight_count], refs[weight_count:]
    if packed:
        pack_buf, refs = refs[0], refs[1:]
    tokens_buf, grad_buf, moe_buf, back_buf, in_sem, out_sem, weight_sem, sum_sem, sum_in_sem = refs

    step = pl.program_id(0)
    steps = count // 2
    slots = min(2, steps)
    slot = lax.rem(step, slots)
    rows, wide = tokens_buf.shape[2:]
    model = wide - LANES
    hidden = EXPERT_HIDDEN
    rank = ADAPTER_RANK
    up_ref, down_ref, second_ref = weight_bufs[:3]

    def weight_copies():
        pairs = list(zip(weight_refs, weight_bufs))
        if direct:
            raw, lines = weight_refs[1], weight_refs[1].shape[1]
            pairs, columns = pairs[:1], second_ref.shape[1] // depth
            for z in range(depth):
                pairs.append((raw.at[z, :, pl.ds(0, wide)], down_ref.at[pl.ds(z * lines, lines)]))
                part = raw.at[z, :, pl.ds(wide, columns)]
                pairs.append((part, second_ref.at[:, pl.ds(z * columns, columns)]))
            if with_shared:
                group, size = 4 * LANES, lines // 4
                for z in range(depth):
                    for q in range(4):
                        width = min(group, wide - q * group)
                        part = raw.at[z, pl.ds(q * size, size), pl.ds(wide + columns, width)]
                        target = weight_bufs[3].at[pl.ds(z * size, size), pl.ds(q * group, width)]
                        pairs.append((part, target))
                pairs.append((weight_refs[2], weight_bufs[4]))
        return [pltpu.make_async_copy(src, dst, weight_sem.at[n]) for n, (src, dst) in enumerate(pairs)]

    def incoming(k, i, kinds):
        copies = []
        to, source = k % slots, 2 * k + i
        for n, (refs_of, buf) in enumerate(((token_refs, tokens_buf), (grad_refs, grad_buf))):
            size = rows // len(refs_of[source])
            for p, piece in enumerate(refs_of[source] if n in kinds else ()):
                part = buf.at[to, i, pl.ds(p * size, size)]
                copies.append(pltpu.make_async_copy(piece, part, in_sem.at[to, i, 2 * n + p]))
        if with_prior and 2 in kinds:
            copies.append(pltpu.make_async_copy(prior_moe[source], moe_buf.at[to, i], in_sem.at[to, i, 4]))
            copies.append(pltpu.make_async_copy(prior_back[source], back_buf.at[to, i], in_sem.at[to, i, 5]))
        return copies

    def outgoing(k, i, kinds=(0, 1)):
        at, source = k % slots, 2 * k + i
        pairs = ((moe_buf, moe_refs), (back_buf, back_refs))
        return [pltpu.make_async_copy(pairs[n][0].at[at, i], pairs[n][1][source], out_sem.at[at, i, n]) for n in kinds]

    def at_step(action, first=0, last=steps):
        for k in range(first, last):
            pl.when(step == k)(functools.partial(action, k))

    def wait_in(i, kind):
        def action(k):
            for copy in incoming(k, i, (kind,)):
                copy.wait()

        at_step(action)

    def start_out(i, n):
        at_step(lambda k: outgoing(k, i, (n,))[0].start())

    def turn(k):
        for i in (0, 1):
            if k >= 1:
                for copy in outgoing(k - 1, i):
                    copy.wait()
            if k + 1 < steps:
                for copy in incoming(k + 1, i, (0, 1, 2)):
                    copy.start()

    def sum_copy(n):
        return pltpu.make_async_copy(pack_buf if packed else grad_sums[n], grad_outs[n], sum_sem.at[n])

    def sum_in(n):
        return pltpu.make_async_copy(sums_in[n], grad_sums[n], sum_in_sem.at[n])

    @pl.when(step == 0)
    def _():
        for i in (0, 1):
            for copy in incoming(0, i, (0,)):
                copy.start()
        for i in (0, 1):
            for copy in incoming(0, i, (1,)):
                copy.start()
        for copy in weight_copies():
            copy.start()
        for i in (0, 1):
            for copy in incoming(0, i, (2,)):
                copy.start()
        for n, total in enumerate(grad_sums):
            if with_sums:
                sum_in(n).start()
            else:
                total[...] = jnp.zeros_like(total)

    expert = meta[0]
    lane = lax.broadcasted_iota(jnp.int32, (1, LANES), 1)
    sub = lax.broadcasted_iota(jnp.int32, (LANES, 1), 0)
    places, picks, gates_of, selects, adapters = [], [], [], [], []
    inputs, grad_rows = [], []
    for i in (0, 1):
        wait_in(i, 0)
        extra_b = tokens_buf[slot, i, :, model:]
        extra = extra_b.astype(F32)
        own = 3 * experts + 3 * rank
        adapter = extra[0:1, own : own + 1]
        select = ((lane // rank).astype(F32) == adapter).astype(F32)
        slot_column = jnp.sum(jnp.where(lane == expert, extra, 0.0), axis=1, keepdims=True)
        slot_row = jnp.sum(jnp.where(sub == expert, extra.T, 0.0), axis=0, keepdims=True)
        place = lax.broadcasted_iota(jnp.int32, (rows, capacity), 1).astype(F32) == slot_column
        pick = lax.broadcasted_iota(jnp.int32, (capacity, rows), 0).astype(F32) == slot_row
        place, pick = place.astype(F32).astype(BF16), pick.astype(F32).astype(BF16)
        picked_extra = dot_nn(pick, extra_b)
        chosen = (lane == experts + expert) | (lane == 2 * experts + expert)
        gates_of.append(jnp.sum(jnp.where(chosen, picked_extra, 0.0), axis=1, keepdims=True))
        inputs.append(dot_nn(pick, tokens_buf[slot, i, :, :model]).astype(BF16))
        picks.append(pick)
        places.append(place)
        adapters.append(adapter)
        selects.append(jnp.broadcast_to(select, (capacity, LANES)))
    for i in (0, 1):
        wait_in(i, 1)
        grad_rows.append(dot_nn(picks[i], grad_buf[slot, i]))
    at_step(turn)
    inputs = jnp.concatenate(inputs, axis=0)
    grad_rows = jnp.concatenate(grad_rows, axis=0)
    gate = jnp.concatenate(gates_of, axis=0)
    select = jnp.concatenate(selects, axis=0)
    select_two = jnp.concatenate([select, select], axis=1)

    @pl.when(step == 0)
    def _():
        for copy in weight_copies():
            copy.wait()

    low = (dot_nn(inputs, up_ref[:, 2 * hidden : 2 * hidden + 2 * LANES]) * select_two).astype(BF16)
    gate_part = dot_nn(inputs, up_ref[:, :hidden]) + dot_nn(low[:, :LANES], second_ref[:, :hidden])
    up_part = dot_nn(inputs, up_ref[:, hidden : 2 * hidden]) + dot_nn(low[:, LANES:], second_ref[:, hidden : 2 * hidden])
    sigmoid = 1.0 / (1.0 + jnp.exp(-gate_part))
    silu = gate_part * sigmoid
    act = (silu * up_part).astype(BF16)
    low_down = (dot_nn(act, down_ref[:, model:]) * select).astype(BF16)
    output = (dot_nn(act, down_ref[:, :model]) + dot_nn(low_down, second_ref[:, 2 * hidden :])).astype(BF16).astype(F32)
    grad_gate = jnp.sum(output * grad_rows, axis=1, keepdims=True)
    weighted = (gate * output).astype(BF16)

    if with_sums:

        @pl.when(step == 0)
        def _():
            for n in range(grad_count):
                sum_in(n).wait()

    grad_y = (gate * grad_rows).astype(BF16)
    glow_down = (dot_nt(grad_y, second_ref[:, 2 * hidden :]) * select).astype(BF16)
    second_grad[:, 2 * hidden :] += dot_tn(low_down, grad_y)
    down_grad[...] += dot_tn(act, glow_down)
    grad_act = dot_nt(grad_y, down_ref[:, :model]) + dot_nt(glow_down, down_ref[:, model:])
    grad_up = (grad_act * silu).astype(BF16)
    grad_gp = (grad_act * up_part * (sigmoid * (1.0 + gate_part * (1.0 - sigmoid)))).astype(BF16)
    glow = jnp.concatenate(
        [
            dot_nt(grad_gp, second_ref[:, :hidden]) * select,
            dot_nt(grad_up, second_ref[:, hidden : 2 * hidden]) * select,
        ],
        axis=1,
    ).astype(BF16)
    second_grad[:, :hidden] += dot_tn(low[:, :LANES], grad_gp)
    second_grad[:, hidden : 2 * hidden] += dot_tn(low[:, LANES:], grad_up)
    first_grad[...] += dot_tn(inputs, glow)
    grad_in = (
        dot_nt(grad_gp, up_ref[:, :hidden])
        + dot_nt(grad_up, up_ref[:, hidden : 2 * hidden])
        + dot_nt(glow, up_ref[:, 2 * hidden : 2 * hidden + 2 * LANES])
    ).astype(BF16)
    gate_hi = grad_gate.astype(BF16).astype(F32)
    gate_lo = grad_gate - gate_hi
    extra_out = (
        jnp.where(lane == expert, gate_hi, 0.0) + jnp.where(lane == experts + expert, gate_lo, 0.0)
    ).astype(BF16)

    @pl.when(step == steps - 1)
    def _():
        if not packed:
            for n in range(3):
                sum_copy(n).start()
            return
        second_t = second_grad[...].T
        parts = [first_grad[:, :LANES], first_grad[:, LANES:], down_grad[...], second_t]
        at = 0
        for part in parts:
            size = part.shape[0] // depth
            for z in range(depth):
                pack_buf[z, at : at + size, :] = part[z * size : (z + 1) * size].astype(BF16)
            at += size

    for i in (0, 1):
        mine = slice(i * capacity, (i + 1) * capacity)
        wait_in(i, 2)
        moe = dot_nn(places[i], weighted[mine])
        back = dot_nn(places[i], grad_in[mine])
        back_extra = dot_nn(places[i], extra_out[mine])
        if with_prior:
            moe = moe + moe_buf[slot, i].astype(F32)
            back = back + back_buf[slot, i, :rows, :model].astype(F32)
            back_extra = back_extra + back_buf[slot, i, :rows, model:].astype(F32)
        if not with_prior:
            back_buf[slot, i, rows:, :] = jnp.zeros((BACK_ROWS, wide), BF16)
        if with_shared:
            sdown_ref, sb_ref = weight_bufs[3:]
            units = sdown_ref.shape[0]
            first_gate, first_up, first_down = 3 * experts, 3 * experts + rank, 3 * experts + 2 * rank
            tokens = tokens_buf[slot, i, :, :model]
            extra_b = tokens_buf[slot, i, :, model:]
            grads = grad_buf[slot, i]
            offset = (lane - sub).astype(F32) - adapters[i] * float(rank)

            def spread(base):
                inside = (sub >= base) & (sub < base + rank)
                return (inside & (offset == float(-base))).astype(F32).astype(BF16)

            to_gate = dot_nt(spread(first_gate), sb_ref[:units]).astype(BF16)
            to_up = dot_nt(spread(first_up), sb_ref[units:]).astype(BF16)
            to_down = dot_nt(spread(first_down), sdown_ref[:, model:]).astype(BF16)
            shared_up = up_ref[:, 2 * hidden + 2 * LANES :]
            gate_up = dot_nn(tokens, shared_up)
            s_gate = gate_up[:, :units] + dot_nn(extra_b, to_gate)
            s_up = gate_up[:, units:] + dot_nn(extra_b, to_up)
            s_sig = 1.0 / (1.0 + jnp.exp(-s_gate))
            s_silu = s_gate * s_sig
            s_act = (s_silu * s_up).astype(BF16)
            moe = moe + dot_nn(s_act, sdown_ref[:, :model])
            s_grad = dot_nt(grads, sdown_ref[:, :model]) + dot_nn(extra_b, to_down)
            grad_sums[3][...] += dot_tn(s_act, dot_nn(extra_b, spread(first_down)).astype(BF16))
            s_gu = (s_grad * s_silu).astype(BF16)
            s_gg = (s_grad * s_up * (s_sig * (1.0 + s_gate * (1.0 - s_sig)))).astype(BF16)
            back_extra = back_extra + dot_nt(s_act, to_down) + dot_nt(s_gg, to_gate) + dot_nt(s_gu, to_up)
            back = back + dot_nt(jnp.concatenate([s_gg, s_gu], axis=1), shared_up)
            columns = pl.ds(pl.multiple_of(meta[1] * units, units), units)
            grad_bg = dot_tn(extra_b, s_gg)[first_gate : first_gate + rank]
            grad_bu = dot_tn(extra_b, s_gu)[first_up : first_up + rank]
            back_buf[slot, i, rows : rows + rank, columns] = grad_bg.astype(BF16)
            back_buf[slot, i, rows + rank :, columns] = grad_bu.astype(BF16)
        moe_buf[slot, i] = moe.astype(BF16)
        start_out(i, 0)
        back_buf[slot, i, :rows, :model] = back.astype(BF16)
        back_buf[slot, i, :rows, model:] = back_extra.astype(BF16)
        start_out(i, 1)

    @pl.when(step == steps - 1)
    def _():
        if packed and with_shared:
            size = grad_sums[3].shape[0] // depth
            for z in range(depth):
                part = grad_sums[3][z * size : (z + 1) * size, :]
                if size % 16:
                    part = jnp.concatenate([part, jnp.zeros((16 - size % 16, LANES), F32)], axis=0)
                pack_buf[z, pack_buf.shape[1] - part.shape[0] :, :] = part.astype(BF16)
        for n in range(0 if packed else 3, out_count):
            sum_copy(n).start()
        for i in (0, 1):
            for copy in outgoing(steps - 1, i):
                copy.wait()
        for n in range(out_count):
            sum_copy(n).wait()


def expert_call(meta, weights, shapes, tokens, grads, prior, sums, packed, experts, capacity, depth, deps=()):
    count = len(tokens)
    with_shared = len(shapes) > 3
    direct = len(weights) < len(shapes)
    splits = [len(pieces) for pieces in tokens]
    rows, model = sum(piece.shape[0] for piece in grads[0]), grads[0][0].shape[1]
    wide = model + LANES
    slots = min(2, count // 2)
    anywhere = pl.BlockSpec(memory_space=pl.ANY)
    prior = [] if prior is None else list(prior[0]) + list(prior[1])
    flat = [piece for pieces in tokens for piece in pieces] + [piece for pieces in grads for piece in pieces]
    grad_shapes = [
        jax.ShapeDtypeStruct((model, 2 * LANES), F32),
        jax.ShapeDtypeStruct((EXPERT_HIDDEN, LANES), F32),
        jax.ShapeDtypeStruct(shapes[2], F32),
    ]
    if with_shared:
        grad_shapes.append(jax.ShapeDtypeStruct((shapes[3][0], LANES), F32))
    out_shapes = grad_shapes
    if packed:
        lines = sum(s.shape[0] for s in grad_shapes[:2]) + model + shapes[2][1]
        lines = lines // depth
        if with_shared:
            lines += -(-shapes[3][0] // depth // 16) * 16
        out_shapes = [jax.ShapeDtypeStruct((depth, lines, LANES), BF16)]
    back_rows = rows + BACK_ROWS
    outs = pl.pallas_call(
        functools.partial(
            expert_kernel,
            *(count, splits, experts, capacity, depth, direct, bool(prior), with_shared, bool(sums), packed, len(deps)),
        ),
        grid=(count // 2,),
        in_specs=[pl.BlockSpec(memory_space=pltpu.SMEM)]
        + [anywhere] * (len(weights) + len(flat) + len(prior) + len(sums) + len(deps)),
        out_specs=[anywhere] * (2 * count + len(out_shapes)),
        out_shape=[jax.ShapeDtypeStruct((rows, model), BF16)] * count
        + [jax.ShapeDtypeStruct((back_rows, wide), BF16)] * count
        + out_shapes,
        scratch_shapes=[pltpu.VMEM(s.shape, F32) for s in grad_shapes]
        + [pltpu.VMEM(shape, BF16) for shape in shapes]
        + ([pltpu.VMEM(out_shapes[0].shape, BF16)] if packed else [])
        + [
            pltpu.VMEM((slots, 2, rows, wide), BF16),
            pltpu.VMEM((slots, 2, rows, model), BF16),
            pltpu.VMEM((slots, 2, rows, model), BF16),
            pltpu.VMEM((slots, 2, back_rows, wide), BF16),
            pltpu.SemaphoreType.DMA((slots, 2, 6)),
            pltpu.SemaphoreType.DMA((slots, 2, 2)),
            pltpu.SemaphoreType.DMA((len(shapes) + 6 * depth,)),
            pltpu.SemaphoreType.DMA((len(grad_shapes),)),
            pltpu.SemaphoreType.DMA((len(grad_shapes),)),
        ],
        compiler_params=pltpu.CompilerParams(vmem_limit_bytes=VMEM_LIMIT),
        cost_estimate=cost(12.0 * count),
        name="expert",
    )(meta, *weights, *flat, *prior, *sums, *deps)
    return outs[:count], outs[count : 2 * count], outs[2 * count :]


def swap(array, bit, size):
    return lax.ppermute(array, "dp", [(i, i ^ bit) for i in range(size)])


def plane_gather(array, size):
    half = array.shape[0] // 2
    x, y = swap(array, 2, size), swap(array, 4, size)
    across = {0: (array,), 2: (x,), 4: (y,), 6: (swap(y[:half], 2, size), swap(x[half:], 4, size))}
    blocks = [None] * size
    for k in (0, 2, 4, 6):
        blocks[k] = across[k]
        blocks[k + 1] = tuple(swap(piece, 1, size) for piece in across[k])
    return blocks


def add(*terms):
    total = terms[0].astype(F32)
    for term in terms[1:]:
        total = total + term.astype(F32)
    return total.astype(BF16)


def tie_kernel(*refs):
    del refs


def tie_all(arrays, *others):
    anywhere = pl.BlockSpec(memory_space=pl.ANY)
    return pl.pallas_call(
        tie_kernel,
        in_specs=[anywhere] * (len(arrays) + len(others)),
        out_specs=[anywhere] * len(arrays),
        out_shape=[jax.ShapeDtypeStruct(array.shape, array.dtype) for array in arrays],
        input_output_aliases={n: n for n in range(len(arrays))},
        name="tie",
    )(*arrays, *others)


def tie(array, *others):
    return tie_all([array], *others)[0]


def assemble_kernel(splits, widths, waits, me_ref, *refs):
    pieces, outs = refs[: sum(splits)], refs[sum(splits) + waits : -3]
    whole, in_sem, out_sem = refs[-3:]
    copies, at = [], 0
    for k, split in enumerate(splits):
        start = 0
        for piece in pieces[at : at + split]:
            target = whole.at[pl.ds(start, piece.shape[0]), me_ref[0] ^ k]
            copies.append(pltpu.make_async_copy(piece, target, in_sem.at[len(copies)]))
            start += piece.shape[0]
        at += split
    for copy in copies:
        copy.start()
    for copy in copies:
        copy.wait()
    copies, column = [], 0
    for out, (count, width) in zip(outs, widths):
        for n in range(count):
            source = whole.at[:, :, :, pl.ds(column, width)]
            copies.append(pltpu.make_async_copy(source, out.at[:, :, n], out_sem.at[len(copies)]))
            column += width
    for copy in copies:
        copy.start()
    for copy in copies:
        copy.wait()


def assemble(blocks, widths, me, deps=()):
    depth, rows, _ = blocks[0][0].shape
    size = len(blocks)
    splits = [len(pieces) for pieces in blocks]
    flat = [piece for pieces in blocks for piece in pieces]
    outs = pl.pallas_call(
        functools.partial(assemble_kernel, splits, widths, len(deps)),
        in_specs=[pl.BlockSpec(memory_space=pltpu.SMEM)] + [pl.BlockSpec(memory_space=pl.ANY)] * (len(flat) + len(deps)),
        out_specs=[pl.BlockSpec(memory_space=pl.ANY)] * len(widths),
        out_shape=[jax.ShapeDtypeStruct((depth, size, count, rows, width), BF16) for count, width in widths],
        scratch_shapes=[
            pltpu.VMEM((depth, size, rows, sum(count * width for count, width in widths)), BF16),
            pltpu.SemaphoreType.DMA((len(flat),)),
            pltpu.SemaphoreType.DMA((sum(count for count, _ in widths),)),
        ],
        compiler_params=pltpu.CompilerParams(vmem_limit_bytes=VMEM_LIMIT),
        name="assemble",
    )(me.astype(jnp.int32).reshape(1), *flat, *deps)
    return [out.reshape(-1, out.shape[-1]) for out in outs]


def turn_kernel(
    waits, own, other, from_x, from_y, hidden, gates, first_gu, router, gain, grad_out, second_o, out_w, first_o, *rest
):
    grad_mid_out, grad_mid_b_out, glow_out, glow_sgu, low_sdown, grad_attn, units_out = rest[waits:]
    rows, model = hidden.shape
    experts = gates.shape[1]
    rank = ADAPTER_RANK
    total = own[...].astype(F32) + other[...].astype(F32) + from_x[...].astype(F32) + from_y[...].astype(F32)
    units_out[...] = total[rows:, :]
    tail = total[:rows, model:]
    grad_gates = tail[:, :experts] + tail[:, experts : 2 * experts]
    glow = tail[:, 3 * experts : 3 * experts + 2 * rank].astype(BF16)
    glow_sgu[...] = glow
    low_sdown[...] = tail[:, 3 * experts + 2 * rank : 3 * experts + 3 * rank].astype(BF16)
    gate = gates[...]
    grad_logits = gate * (grad_gates - jnp.sum(gate * grad_gates, axis=-1, keepdims=True))
    logits_hi = grad_logits.astype(BF16)
    left = grad_logits - logits_hi.astype(F32)
    logits_mid = left.astype(BF16)
    logits_lo = (left - logits_mid.astype(F32)).astype(BF16)
    grad_normed = total[:rows, :model] + dot_nt(glow, first_gu[...])
    for part in (logits_hi, logits_mid, logits_lo):
        grad_normed = grad_normed + dot_nt(part, router[...])
    values = hidden[...]
    scale = lax.rsqrt(jnp.mean(values * values, axis=-1, keepdims=True) + EPSILON)
    scaled = grad_normed * gain[...]
    mean = jnp.mean(values * scaled, axis=-1, keepdims=True)
    grad_mid = grad_out[...].astype(F32) + scale * scaled - values * (scale * scale * scale * mean)
    grad_mid_out[...] = grad_mid
    grad_mid_b = grad_mid.astype(BF16)
    grad_mid_b_out[...] = grad_mid_b
    glow = dot_nt(grad_mid_b, second_o[...]).astype(BF16)
    glow_out[...] = glow
    grad_attn[...] = (dot_nt(grad_mid_b, out_w[...]) + dot_nt(glow, first_o[...])).astype(BF16)


def turn(args, deps):
    rows, model = args[4].shape
    rank = ADAPTER_RANK
    vmem = pl.BlockSpec(memory_space=pltpu.VMEM)
    shapes = [
        ((rows, model), F32),
        ((rows, model), BF16),
        ((rows, rank), BF16),
        ((rows, 2 * rank), BF16),
        ((rows, rank), BF16),
        ((rows, HEADS * HEAD_DIM), BF16),
        ((BACK_ROWS, args[0].shape[1]), F32),
    ]
    return pl.pallas_call(
        functools.partial(turn_kernel, len(deps)),
        in_specs=[vmem] * len(args) + [pl.BlockSpec(memory_space=pl.ANY)] * len(deps),
        out_specs=[vmem] * len(shapes),
        out_shape=[jax.ShapeDtypeStruct(shape, dtype) for shape, dtype in shapes],
        compiler_params=pltpu.CompilerParams(vmem_limit_bytes=VMEM_LIMIT),
        cost_estimate=cost(4.0),
        name="turn",
    )(*args, *deps)


def query_back_kernel(waits, grad_q, normed, low_q, q_w, first_q, second_q, *rest):
    grad_normed, first_query, second_query = rest[waits:]
    glow_q = dot_nt(grad_q[...], second_q[...]).astype(BF16)
    grad_normed[...] = dot_nt(grad_q[...], q_w[...]) + dot_nt(glow_q, first_q[...])
    first_query[...] = dot_tn(normed[...], glow_q)
    second_query[...] = dot_tn(low_q[...], grad_q[...])


def query_back(args, deps):
    rows, model = args[1].shape
    vmem = pl.BlockSpec(memory_space=pltpu.VMEM)
    shapes = [(rows, model), (model, ADAPTER_RANK), (ADAPTER_RANK, HEADS * HEAD_DIM)]
    return pl.pallas_call(
        functools.partial(query_back_kernel, len(deps)),
        in_specs=[vmem] * len(args) + [pl.BlockSpec(memory_space=pl.ANY)] * len(deps),
        out_specs=[vmem] * len(shapes),
        out_shape=[jax.ShapeDtypeStruct(shape, F32) for shape in shapes],
        compiler_params=pltpu.CompilerParams(vmem_limit_bytes=VMEM_LIMIT),
        cost_estimate=cost(0.1),
        name="query_back",
    )(*args, *deps)


def middle_kernel(waits, attn, glow_out, normed2, glow_sgu, grad_mid, out_low, grad_out, low_sdown, *rest):
    first_early, second_out, second_down = rest[waits:]
    rank = ADAPTER_RANK
    first_early[:, :rank] = dot_tn(attn[...], glow_out[...])
    first_early[:, rank:] = dot_tn(normed2[...], glow_sgu[...])
    second_out[...] = dot_tn(out_low[...], grad_mid[...])
    second_down[...] = dot_tn(low_sdown[...], grad_out[...])


def middle(args, deps):
    model = args[0].shape[1]
    rank = ADAPTER_RANK
    vmem = pl.BlockSpec(memory_space=pltpu.VMEM)
    shapes = [(model, 3 * rank), (rank, model), (rank, model)]
    return pl.pallas_call(
        functools.partial(middle_kernel, len(deps)),
        in_specs=[vmem] * len(args) + [pl.BlockSpec(memory_space=pl.ANY)] * len(deps),
        out_specs=[vmem] * len(shapes),
        out_shape=[jax.ShapeDtypeStruct(shape, F32) for shape in shapes],
        compiler_params=pltpu.CompilerParams(vmem_limit_bytes=VMEM_LIMIT),
        cost_estimate=cost(0.1),
        name="middle",
    )(*args, *deps)


def last_kernel(
    owners, grad_kv, normed, low_kv, kv_w, first_kv, second_k, second_v, hidden, gain, grad_mid, grad_normed_q,
    first_query, first_early, second_query, second_early, adapter, grad_hidden, first_out, second_out
):
    rank = ADAPTER_RANK
    heads = range(grad_kv.shape[1] // (2 * HEAD_DIM))
    grad_k = jnp.concatenate([grad_kv[:, 2 * n * HEAD_DIM : (2 * n + 1) * HEAD_DIM] for n in heads], axis=1)
    grad_v = jnp.concatenate([grad_kv[:, (2 * n + 1) * HEAD_DIM : (2 * n + 2) * HEAD_DIM] for n in heads], axis=1)
    width = grad_k.shape[1]
    glow_k = dot_nt(grad_k, second_k[...]).astype(BF16)
    glow_v = dot_nt(grad_v, second_v[...]).astype(BF16)
    grad_normed = grad_normed_q[...] + dot_nt(grad_k, kv_w[:, :width]) + dot_nt(grad_v, kv_w[:, width:])
    grad_normed = grad_normed + dot_nt(glow_k, first_kv[:, :rank]) + dot_nt(glow_v, first_kv[:, rank:])
    values = hidden[...].astype(F32)
    scale = lax.rsqrt(jnp.mean(values * values, axis=-1, keepdims=True) + EPSILON)
    scaled = grad_normed * gain[...]
    mean = jnp.mean(values * scaled, axis=-1, keepdims=True)
    grad_hidden[...] = grad_mid[...] + scale * scaled - values * (scale * scale * scale * mean)
    firsts = [first_query[...], dot_tn(normed[...], glow_k), dot_tn(normed[...], glow_v), first_early[...]]
    tags = jnp.broadcast_to(adapter[...], (first_query.shape[0], LANES - 6 * rank))
    first_out[...] = jnp.concatenate(firsts + [tags], axis=1).astype(BF16)
    seconds = [second_query[...], dot_tn(low_kv[:, :rank], grad_k), dot_tn(low_kv[:, rank:], grad_v), second_early[...]]
    seconds = jnp.concatenate(seconds, axis=1)
    columns = seconds.shape[1] // owners
    padding = jnp.zeros((rank, second_out.shape[1] // rank * LANES - columns), F32)
    for n in range(owners):
        piece = jnp.concatenate([seconds[:, n * columns : (n + 1) * columns], padding], axis=1).astype(BF16)
        for c in range(piece.shape[1] // LANES):
            second_out[n, c * rank : (c + 1) * rank, :] = piece[:, c * LANES : (c + 1) * LANES]


def last(owners, args):
    rows, model = args[7].shape
    columns = (args[13].shape[1] + 2 * KV_HEADS * HEAD_DIM + args[14].shape[1]) // owners
    vmem = pl.BlockSpec(memory_space=pltpu.VMEM)
    return pl.pallas_call(
        functools.partial(last_kernel, owners),
        in_specs=[vmem] * len(args),
        out_specs=[vmem] * 3,
        out_shape=[
            jax.ShapeDtypeStruct((rows, model), F32),
            jax.ShapeDtypeStruct((model, LANES), BF16),
            jax.ShapeDtypeStruct((owners, -(-columns // LANES) * ADAPTER_RANK, LANES), BF16),
        ],
        compiler_params=pltpu.CompilerParams(vmem_limit_bytes=VMEM_LIMIT),
        cost_estimate=cost(2.0),
        name="last",
    )(*args)


def spread_kernel(depth, lines, flat, first_out, second_out):
    rank = ADAPTER_RANK
    size = flat.shape[0] // depth
    row = lax.broadcasted_iota(jnp.int32, (LANES, 1), 0).astype(F32)
    column = lax.broadcasted_iota(jnp.int32, (1, first_out.shape[1]), 1)
    inside = column % LANES
    target = (column // LANES * rank + inside).astype(F32)
    owner = (inside // rank).astype(F32)
    short = lax.broadcasted_iota(jnp.int32, (1, rank), 1).astype(F32)
    chunks = (flat.shape[1] - lines) // rank
    first, second = None, [None] * chunks
    for d in range(size):
        adapter = flat[d, 0:1, 6 * rank : 6 * rank + 1].astype(F32)
        total = flat[d].astype(F32)
        for z in range(1, depth):
            total = total + flat[z * size + d].astype(F32)
        total = total.astype(BF16)
        place = ((target - adapter * float(rank) == row) & (owner == adapter)).astype(F32).astype(BF16)
        lift = (row - adapter * float(rank) == short).astype(F32).astype(BF16)
        part = dot_nn(total[:lines], place)
        first = part if first is None else first + part
        for c in range(chunks):
            part = dot_nn(lift, total[lines + c * rank : lines + (c + 1) * rank])
            second[c] = part if second[c] is None else second[c] + part
    first_out[...] = first
    for c in range(chunks):
        second_out[:, c * LANES : (c + 1) * LANES] = second[c]


def spread(flat, depth, lines):
    vmem = pl.BlockSpec(memory_space=pltpu.VMEM)
    chunks = (flat.shape[1] - lines) // ADAPTER_RANK
    return pl.pallas_call(
        functools.partial(spread_kernel, depth, lines),
        in_specs=[vmem],
        out_specs=[vmem] * 2,
        out_shape=[jax.ShapeDtypeStruct((lines, 6 * LANES), F32), jax.ShapeDtypeStruct((LANES, chunks * LANES), F32)],
        compiler_params=pltpu.CompilerParams(vmem_limit_bytes=VMEM_LIMIT),
        cost_estimate=cost(2.0),
        name="spread",
    )(flat)


def per_device(
    depth,
    size,
    block_input,
    document_number,
    key_present,
    routes,
    sequence_adapter,
    output_gradient,
    norm_scale_pair,
    query_key_value_weight,
    attention_output_weight,
    router_weight,
    shared_gate_up_weight,
    shared_down_weight,
    routed_gate_up_weight,
    routed_down_weight,
    dense_first_factor,
    shared_down_first_factor,
    dense_second_factor,
    routed_first_factor,
    routed_down_first_factor,
    routed_second_factor,
):
    _, rows, model = block_input.shape
    topk = routes.shape[2]
    me = lax.axis_index("dp")
    experts = router_weight.shape[1]
    local_experts = routed_gate_up_weight.shape[0]
    shard_rows = query_key_value_weight.shape[0]
    shared_rows = shared_down_weight.shape[0]
    rank_all = dense_second_factor.shape[0]
    second_columns = dense_second_factor.shape[1]
    capacity = 4 * topk * rows // (3 * experts)
    query_width = HEADS * HEAD_DIM
    kv_width = KV_HEADS * HEAD_DIM
    hops = min(depth - 1, -(-(DOCUMENT_SPAN - 1) // rows))
    rank = ADAPTER_RANK
    units = SHARED_HIDDEN // size
    adapter = sequence_adapter[0]
    forward = [(i, i + 1) for i in range(depth - 1)]
    backward = [(i + 1, i) for i in range(depth - 1)]

    def over_seq(shard):
        return lax.all_gather(shard, "seq", axis=0)

    first_shard = dense_first_factor.reshape(shard_rows, 6 * rank_all)
    second_width = second_columns * rank_all // shard_rows
    groups = second_width // rank_all
    pack_kv = jnp.concatenate(
        [
            query_key_value_weight[:, query_width:],
            first_shard[:, rank_all : 3 * rank_all],
            dense_second_factor.T.reshape(groups, shard_rows, rank_all).transpose(1, 0, 2).reshape(shard_rows, -1),
            jnp.pad(
                jnp.concatenate([router_weight, norm_scale_pair.T], axis=1), ((0, 0), (0, LANES - experts - 2))
            ),
        ],
        axis=1,
    )
    pack_q = jnp.concatenate(
        [
            query_key_value_weight[:, :query_width],
            first_shard[:, :rank_all],
            first_shard[:, 3 * rank_all :],
            attention_output_weight,
        ],
        axis=1,
    )
    seq_kv = over_seq(pack_kv)
    seq_q = over_seq(tie(pack_q, seq_kv))

    flags = jnp.sum((routes[0][..., None] == jnp.arange(experts, dtype=jnp.int32)).astype(F32), axis=1)
    before = (jnp.arange(rows)[:, None] > jnp.arange(rows)[None, :]).astype(BF16)
    slots = jnp.where(flags > 0, dot_nn(before, flags.astype(BF16)), -1.0).astype(BF16)

    def own_columns(matrix):
        return lax.dynamic_slice_in_dim(matrix, adapter * rank, rank, 1)

    def own_factors(matrix):
        count = matrix.shape[1] // rank_all
        return jnp.concatenate([own_columns(matrix[:, n * rank_all : (n + 1) * rank_all]) for n in range(count)], axis=1)

    grad_out_b = output_gradient[0]
    grads_x, grads_y = swap(grad_out_b, 2, size), swap(grad_out_b, 4, size)
    gate_up = shared_gate_up_weight.reshape(shard_rows, 2, depth, size, units // depth)
    gate_up = gate_up.transpose(3, 0, 1, 2, 4).reshape(size, shard_rows, 2 * units)
    gate_up = lax.all_to_all(gate_up, "dp", split_axis=0, concat_axis=0, tiled=True)
    kv_gathered = plane_gather(tie(seq_kv, grads_x, grads_y, gate_up), size)
    grads_x, grads_y = tie_all([grads_x, grads_y], *kv_gathered[6])
    far_grads = (swap(grads_y[: rows // 2], 2, size), swap(grads_x[rows // 2 :], 4, size))
    grad_blocks = [(grad_out_b,), None, (grads_x,), None, (grads_y,), None, far_grads, None]
    kv_w, kv_first, second_t, small = assemble(
        kv_gathered, ((1, 2 * kv_width), (1, 2 * rank_all), (groups, rank_all), (1, LANES)), me
    )
    router_w = small[:, :experts]
    gains = small[:, experts : experts + 2].astype(F32).T
    second = own_columns(second_t).T
    first_kv = own_factors(kv_first)
    widths = [query_width, kv_width, kv_width, model, SHARED_HIDDEN, SHARED_HIDDEN, model]
    edges = [sum(widths[:n]) for n in range(len(widths) + 1)]
    b_parts = [second[:, edges[n] : edges[n + 1]] for n in range(len(widths))]

    down_rows = routed_down_weight.shape[1]
    second_cut = rank_all * routed_second_factor.shape[2] // down_rows
    up_shards, down_shards = [], []
    for j in range(local_experts):
        up_parts = [
            routed_gate_up_weight[j].reshape(-1, 2 * EXPERT_HIDDEN),
            routed_first_factor[j].reshape(-1, 2 * rank_all),
        ]
        down_parts = [
            routed_down_weight[j],
            routed_down_first_factor[j],
            routed_second_factor[j].reshape(down_rows, -1),
        ]
        if j == 0:
            up_parts.append(gate_up.reshape(size * shard_rows, 2 * units))
            shared_down = jnp.concatenate([shared_down_weight, shared_down_first_factor], axis=1)
            shared_down = jnp.pad(shared_down, ((0, 0), (0, 16 * LANES - shared_down.shape[1])))
            shared_down = shared_down.reshape(shared_rows, 4, 4 * LANES).transpose(1, 0, 2)
            down_parts.append(shared_down.reshape(down_rows, -1))
        up_shards.append(jnp.concatenate(up_parts, axis=1))
        down_shards.append(jnp.concatenate(down_parts, axis=1))
    first_down = over_seq(tie(down_shards[0], seq_kv))

    x_flat = block_input[0].astype(F32)
    normed = rms_norm(x_flat, gains[0]).astype(BF16)
    low_kv = dot_nn(normed, first_kv).astype(BF16)
    kv_extra = jnp.concatenate([dot_nn(low_kv[:, :rank], b_parts[1]), dot_nn(low_kv[:, rank:], b_parts[2])], axis=1)
    present_tag = jnp.where(key_present == 1, document_number + 1, 0).astype(BF16)
    tag_columns = jnp.broadcast_to(present_tag.reshape(rows, 1), (rows, LANES))
    kv_blocks = [jnp.concatenate([(dot_nn(normed, kv_w) + kv_extra).astype(BF16), tag_columns], axis=1)]
    q_blocks = plane_gather(tie(seq_q, *far_grads), size)
    for k in range(1, size, 2):
        grad_blocks[k] = tuple(swap(piece, 1, size) for piece in grad_blocks[k - 1])
    for h in range(hops):
        block = kv_blocks[-1] if h == 0 else tie(kv_blocks[-1], q_blocks[2][0], q_blocks[4][0], first_down)
        kv_blocks.append(lax.ppermute(block, "seq", forward))
        kv_blocks[h] = block
    kv_all = jnp.concatenate(kv_blocks[::-1], axis=0)
    key_tag = kv_all[:, 2 * kv_width : 2 * kv_width + 1].astype(F32)
    query_tag = (document_number + 1).astype(F32)

    seq_up, seq_down = [over_seq(tie(up_shards[0], kv_blocks[hops]))], [first_down]
    for j in range(1, local_experts):
        seq_up.append(over_seq(tie(up_shards[j], seq_down[j - 1])))
        seq_down.append(over_seq(tie(down_shards[j], seq_up[j - 1])))

    q_w, q_first, out_w = assemble(q_blocks, ((1, query_width), (1, 4 * rank_all), (1, model)), me)
    q_first = own_factors(q_first)
    first_q, first_o, first_gu = q_first[:, :rank], q_first[:, rank : 2 * rank], q_first[:, 2 * rank :]
    low_q = dot_nn(normed, first_q).astype(BF16)
    query = (dot_nn(normed, q_w) + dot_nn(low_q, b_parts[0])).astype(BF16)
    glow_sdown = dot_nt(grad_out_b, b_parts[6]).astype(BF16)
    attn, lse = attend(query, kv_all, query_tag, key_tag, hops, (*grad_blocks[3], *grad_blocks[5], *grad_blocks[7]))
    out_low = dot_nn(attn, first_o).astype(BF16)
    mid = x_flat + dot_nn(attn, out_w) + dot_nn(out_low, b_parts[3])
    normed2 = rms_norm(mid, gains[1]).astype(BF16)

    logits = dot_nn(normed2, router_w)
    top = jnp.max(jnp.where(flags > 0, logits, -jnp.inf), axis=-1, keepdims=True)
    weights = jnp.where(flags > 0, jnp.exp(logits - top), 0.0)
    gates = weights / jnp.sum(weights, axis=-1, keepdims=True)
    gates_hi = gates.astype(BF16)
    gates_lo = (gates - gates_hi.astype(F32)).astype(BF16)
    shared_low = dot_nn(normed2, first_gu).astype(BF16)
    own_adapter = jnp.full((rows, LANES - 3 * experts - 3 * rank), adapter.astype(F32)).astype(BF16)
    payload = jnp.concatenate([normed2, slots, gates_hi, gates_lo, shared_low, glow_sdown, own_adapter], axis=1)
    token_blocks = [None] * size
    token_blocks[0], token_blocks[1] = (payload,), (swap(payload, 1, size),)
    tokens_x, tokens_y = swap(payload, 2, size), swap(payload, 4, size)

    def gather_far(tokens_x, tokens_y, *done):
        tokens_x, tokens_y = tie_all([tokens_x, tokens_y], *done)
        half = rows // 2
        token_blocks[2], token_blocks[3] = (tokens_x,), (swap(tokens_x, 1, size),)
        token_blocks[4], token_blocks[5] = (tokens_y,), (swap(tokens_y, 1, size),)
        return swap(tokens_y[:half], 2, size), swap(tokens_x[half:], 4, size)

    def gather_farthest(far, *done):
        far = tuple(tie_all(far, *done))
        token_blocks[6], token_blocks[7] = far, tuple(swap(piece, 1, size) for piece in far)


    moe_parts, back_parts, grad_sums = [None] * size, [None] * size, []
    wide = model + rank_all

    direct = down_rows == rank_all
    shapes = [None] * local_experts

    def weights_of(j):
        args = [seq_up[j].reshape(model, -1)]
        shapes[j] = [args[0].shape, (EXPERT_HIDDEN, wide), (rank_all, depth * second_cut * down_rows // rank_all)]
        if direct:
            args.append(seq_down[j])
        else:
            second_j = seq_down[j][:, :, wide : wide + second_cut]
            second_j = second_j.reshape(depth, rank_all, -1).transpose(1, 0, 2).reshape(rank_all, -1)
            args += [seq_down[j][:, :, :wide].reshape(EXPERT_HIDDEN, wide), second_j]
        if j == 0:
            if not direct:
                parts = seq_down[j][:, :, wide + second_cut :].reshape(depth, 4, shared_rows, 4 * LANES)
                args.append(parts.transpose(0, 2, 1, 3).reshape(units, -1)[:, :wide])
            slices = [
                lax.dynamic_slice_in_dim(second_t[edges[n] : edges[n + 1]].reshape(depth, size, -1, rank_all), me, 1, 1)
                for n in (4, 5)
            ]
            args.append(jnp.concatenate([part.reshape(units, rank_all) for part in slices], axis=0))
            shapes[j] += [(units, wide), args[-1].shape]
        return args

    def run_expert(j, args, group, prior, deps, packed=False):
        meta = jnp.stack([me * local_experts + j, me]).astype(jnp.int32)
        prior = ([moe_parts[k] for k in group], [back_parts[k] for k in group]) if prior else None
        moe_out, back_out, grads = expert_call(
            meta,
            args,
            shapes[j],
            [token_blocks[k] for k in group],
            [grad_blocks[k] for k in group],
            prior,
            grad_sums[-1],
            packed,
            experts,
            capacity,
            depth,
            deps,
        )
        for n, k in enumerate(group):
            moe_parts[k], back_parts[k] = moe_out[n], back_out[n]
        grad_sums[-1] = list(grads)

    for j in range(local_experts - 1):
        grad_sums.append([])
        args = weights_of(j)
        previous = ()
        for group in ((0, 1), (2, 3), (4, 5), (6, 7)):
            run_expert(j, args, group, j > 0, previous, group == (6, 7))
            previous = (back_parts[group[0]],)
            if j == 0 and group == (0, 1):
                far = gather_far(tokens_x, tokens_y, *previous)
            if j == 0 and group == (2, 3):
                gather_farthest(far, *previous)
    if local_experts == 1:
        gather_farthest(gather_far(tokens_x, tokens_y))

    def scatter(packed):
        return lax.psum_scatter(packed, "seq", scatter_dimension=0, tiled=True)

    packed_sums = [scatter(grads[0]) for grads in grad_sums]
    grad_sums.append([])
    j, prior, half = local_experts - 1, local_experts > 1, (rows + BACK_ROWS) // 2
    args = weights_of(j)
    run_expert(j, args, (6, 7), prior, (back_parts[6],) if prior else ())
    pair_six = add(back_parts[6], swap(back_parts[7], 1, size))
    run_expert(j, args, (2, 3), prior, (back_parts[6],))
    from_diagonal_x, from_diagonal_y = swap(pair_six[:half], 2, size), swap(pair_six[half:], 4, size)
    pair_two = add(back_parts[2], swap(back_parts[3], 1, size))
    run_expert(j, args, (4, 5), prior, (back_parts[2], pair_six))
    pair_four = add(back_parts[4], swap(tie(back_parts[5], from_diagonal_x, from_diagonal_y, *packed_sums), 1, size))
    to_x = jnp.concatenate([pair_two[:half], add(pair_two[half:], from_diagonal_y)], axis=0)
    to_y = jnp.concatenate([add(pair_four[:half], from_diagonal_x), pair_four[half:]], axis=0)
    run_expert(j, args, (0, 1), prior, (to_x, to_y), True)
    packed_sums.append(scatter(grad_sums[-1][0]))
    from_x, from_y = swap(to_x, 2, size), swap(to_y, 4, size)
    grad_mid, grad_mid_b, glow_out, glow_sgu, low_sdown, grad_attn, shared_units = turn(
        [back_parts[0], swap(back_parts[1], 1, size), from_x, from_y, mid, gates, first_gu]
        + [router_w, gains[1:2], grad_out_b, b_parts[3], out_w, first_o],
        (swap(tie(gates_lo[:16], from_x, from_y), 1, size),),
    )

    half = rows // 2
    far_parts = dict(zip((6, 2, 4, 0), tie_all([moe_parts[k + 1] for k in (6, 2, 4, 0)], from_x, from_y)))
    pair = {k: add(moe_parts[k], swap(far_parts[k], 1, size)) for k in (6, 2, 4, 0)}
    moe_to_x = jnp.concatenate([pair[2][:half], add(pair[2][half:], swap(pair[6][half:], 4, size))], axis=0)
    moe_to_y = jnp.concatenate([add(pair[4][:half], swap(pair[6][:half], 2, size)), pair[4][half:]], axis=0)
    moe_from_x, moe_from_y = swap(moe_to_x, 2, size), swap(moe_to_y, 4, size)
    moe = pair[0].astype(F32) + moe_from_x.astype(F32) + moe_from_y.astype(F32)

    def shared_columns(block):
        block = block[:, :SHARED_HIDDEN].reshape(rank, size, depth, units // depth)
        return block.transpose(0, 2, 1, 3).reshape(rank, SHARED_HIDDEN)

    grad_q, grad_kv = attend_back(
        query, kv_all, grad_attn, lse, query_tag, key_tag, hops, 0, KV_HEADS, (pair[6], pair[2], pair[4])
    )
    moving, early_received = grad_kv[:rows], grad_q
    for h in range(hops):
        if h == 1:
            moving = tie(moving, moe_to_x, moe_to_y)
        received = lax.ppermute(moving, "seq", backward)
        moving = add(grad_kv[(h + 1) * rows : (h + 2) * rows], received)
        if h == 0:
            early_received = received
    grad_normed_q, first_query, second_query = query_back(
        [grad_q, normed, low_q, q_w, first_q, b_parts[0]], (early_received,)
    )
    first_early, second_out, second_down = middle(
        [attn, glow_out, normed2, glow_sgu, grad_mid_b, out_low, grad_out_b, low_sdown],
        (early_received,),
    )
    packed_sums = tie_all(packed_sums, early_received)
    owner_rows = model // depth
    firsts, downs, seconds = [], [], []
    for packed in packed_sums:
        packed = packed[0].astype(F32)
        firsts.append(jnp.stack([packed[:owner_rows], packed[owner_rows : 2 * owner_rows]], axis=1))
        at = 2 * owner_rows + down_rows
        downs.append(packed[2 * owner_rows : at])
        seconds.append(packed[at : at + routed_second_factor.shape[2]].T)
    at += routed_second_factor.shape[2]
    grad_expert_a, grad_expert_a_down, grad_expert_b = jnp.stack(firsts), jnp.stack(downs), jnp.stack(seconds)
    grad_first_down = packed_sums[0][0, at : at + shared_rows].astype(F32)

    hidden_out = (mid + moe + dot_nn(low_sdown, b_parts[6])).astype(BF16)[None]
    second_early = jnp.concatenate(
        [second_out, shared_columns(shared_units[:rank]), shared_columns(shared_units[rank:]), second_down], axis=1
    )
    grad_hidden, first_flat, second_flat = last(
        depth * size,
        [moving, normed, low_kv, kv_w, first_kv, b_parts[1], b_parts[2], block_input[0], gains[0:1], grad_mid]
        + [grad_normed_q, first_query, first_early, second_query, second_early, adapter.astype(F32).reshape(1, 1)],
    )
    flat = jnp.concatenate([first_flat.reshape(depth * size, shard_rows, LANES), second_flat], axis=1)
    flat = lax.all_to_all(flat, ("seq", "dp"), split_axis=0, concat_axis=0, tiled=True)
    grad_first, grad_second = spread(flat, depth, shard_rows)
    grad_first = grad_first.reshape(shard_rows, 6, rank_all)
    grad_second = grad_second[:, :second_columns]
    grad_hidden = grad_hidden[None]
    return (
        hidden_out,
        grad_hidden,
        grad_first,
        grad_first_down,
        grad_second,
        grad_expert_a,
        grad_expert_a_down,
        grad_expert_b,
    )


def solution(mesh):
    in_specs = (
        P("dp", "seq", None),
        P("dp", "seq"),
        P("dp", "seq"),
        P("dp", "seq", None),
        P("dp"),
        P("dp", "seq", None),
        P(None, ("seq", "dp")),
        P(("seq", "dp"), None),
        P(("seq", "dp"), None),
        P(("seq", "dp"), None),
        P(("seq", "dp"), None, None),
        P(("seq", "dp"), None),
        P("dp", "seq", None, None),
        P("dp", "seq", None),
        P(("seq", "dp"), None, None),
        P(("seq", "dp"), None),
        P(None, ("seq", "dp")),
        P("dp", "seq", None, None),
        P("dp", "seq", None),
        P("dp", None, "seq"),
    )
    out_specs = (
        P("dp", "seq", None),
        P("dp", "seq", None),
        P(("seq", "dp"), None, None),
        P(("seq", "dp"), None),
        P(None, ("seq", "dp")),
        P("dp", "seq", None, None),
        P("dp", "seq", None),
        P("dp", None, "seq"),
    )
    return jax.shard_map(
        functools.partial(per_device, mesh.shape["seq"], mesh.shape["dp"]),
        mesh=mesh,
        in_specs=in_specs,
        out_specs=out_specs,
        check_vma=False,
    )
```

```python
import functools
import math

import jax
import jax.numpy as jnp
from jax import lax
from jax.experimental import pallas as pl
from jax.experimental.pallas import tpu as pltpu
from jax.sharding import PartitionSpec as P

HEADS = 12
KV_HEADS = 4
HEAD_DIM = 128
EXPERT_HIDDEN = 512
SHARED_HIDDEN = 1024
ADAPTER_RANK = 16
DOCUMENT_SPAN = 1024

EPSILON = 1e-05
MASKED_SCORE = -1e30
LOG2E = 1.4426950408889634
SCALE = HEAD_DIM ** (-0.5)
LANES = 128
VMEM_LIMIT = 60 * 1024 * 1024

F32 = jnp.float32
BF16 = jnp.bfloat16


def dot_nn(left, right):
    return jnp.dot(left, right, preferred_element_type=F32)


def dot_tn(left, right):
    return lax.dot_general(left, right, (((0,), (0,)), ((), ())), preferred_element_type=F32)


def dot_nt(left, right):
    return lax.dot_general(left, right, (((1,), (1,)), ((), ())), preferred_element_type=F32)


def rms_norm(values, gain):
    return values * lax.rsqrt(jnp.mean(values * values, axis=-1, keepdims=True) + EPSILON) * gain


def cost(microseconds):
    return pl.CostEstimate(flops=int(1153500000 * microseconds), bytes_accessed=1000000, transcendentals=0)


def query_tiles(rows, hops):
    tile = math.gcd(rows, 256)
    spans = []
    for first in range(0, rows, tile):
        oldest = max(0, hops * rows + first - (DOCUMENT_SPAN - 1)) // tile * tile
        spans.append((first, tile, oldest, hops * rows + first + tile - oldest))
    return spans


def fill_bias(spans, shift, query_tag, key_tag, bias):
    for first, tile, oldest, span in spans:
        keys = oldest + lax.broadcasted_iota(jnp.int32, (span, tile), 0)
        queries = shift + first + lax.broadcasted_iota(jnp.int32, (span, tile), 1)
        same = key_tag[oldest : oldest + span, :] == query_tag[:, first : first + tile]
        permit = (keys <= queries) & (same | (keys == queries))
        bias[oldest : oldest + span, first : first + tile] = jnp.where(permit, 0.0, MASKED_SCORE)


def attend_kernel(spans, shift, waits, q_ref, k_ref, v_ref, qt_ref, kt_ref, *rest):
    out_ref, lse_ref, bias = rest[waits:]

    @pl.when(pl.program_id(0) == 0)
    def _():
        fill_bias(spans, shift, qt_ref, kt_ref, bias)

    groups = q_ref.shape[1] // HEAD_DIM
    for first, tile, oldest, span in spans:
        keys = k_ref[oldest : oldest + span, :]
        values = v_ref[oldest : oldest + span, :]
        mask = bias[oldest : oldest + span, first : first + tile]
        for h in range(groups):
            columns = slice(h * HEAD_DIM, (h + 1) * HEAD_DIM)
            scores = dot_nt(keys, q_ref[first : first + tile, columns]) * (SCALE * LOG2E) + mask
            top = jnp.max(scores, axis=0, keepdims=True)
            weights = jnp.exp2(scores - top)
            total = jnp.sum(weights, axis=0, keepdims=True)
            mixed = dot_tn(values, weights.astype(BF16)) / total
            out_ref[first : first + tile, columns] = mixed.T.astype(BF16)
            lse_ref[0, h : h + 1, first : first + tile] = top + jnp.log2(total)


def attend(query, kv_all, query_tag, key_tag, hops, deps=()):
    rows = query.shape[0]
    groups = HEADS // KV_HEADS
    span = kv_all.shape[0]
    spans = query_tiles(rows, hops)
    return pl.pallas_call(
        functools.partial(attend_kernel, spans, hops * rows, len(deps)),
        grid=(KV_HEADS,),
        in_specs=[
            pl.BlockSpec((rows, groups * HEAD_DIM), lambda g: (0, g)),
            pl.BlockSpec((span, HEAD_DIM), lambda g: (0, g)),
            pl.BlockSpec((span, HEAD_DIM), lambda g: (0, KV_HEADS + g)),
            pl.BlockSpec((1, rows), lambda g: (0, 0)),
            pl.BlockSpec((span, 1), lambda g: (0, 0)),
        ]
        + [pl.BlockSpec(memory_space=pl.ANY)] * len(deps),
        out_specs=[
            pl.BlockSpec((rows, groups * HEAD_DIM), lambda g: (0, g)),
            pl.BlockSpec((1, groups, rows), lambda g: (g, 0, 0)),
        ],
        out_shape=[
            jax.ShapeDtypeStruct((rows, HEADS * HEAD_DIM), BF16),
            jax.ShapeDtypeStruct((KV_HEADS, groups, rows), F32),
        ],
        scratch_shapes=[pltpu.VMEM((span, rows), F32)],
        compiler_params=pltpu.CompilerParams(vmem_limit_bytes=VMEM_LIMIT),
        cost_estimate=cost(23.0),
        name="attend",
    )(query, kv_all, kv_all, query_tag, key_tag, *deps)


def attend_back_kernel(
    spans, shift, waits, q_ref, k_ref, v_ref, g_ref, lse_ref, qt_ref, kt_ref, *rest
):
    dq_ref, dkv_ref, bias, dk_acc, dv_acc = rest[waits:]

    @pl.when(pl.program_id(0) == 0)
    def _():
        fill_bias(spans, shift, qt_ref, kt_ref, bias)

    dk_acc[...] = jnp.zeros_like(dk_acc)
    dv_acc[...] = jnp.zeros_like(dv_acc)
    groups = q_ref.shape[1] // HEAD_DIM
    for first, tile, oldest, span in spans:
        keys = k_ref[oldest : oldest + span, :]
        values = v_ref[oldest : oldest + span, :]
        mask = bias[oldest : oldest + span, first : first + tile]
        for h in range(groups):
            columns = slice(h * HEAD_DIM, (h + 1) * HEAD_DIM)
            query = q_ref[first : first + tile, columns]
            grad = g_ref[first : first + tile, columns]
            lse = lse_ref[0, h : h + 1, first : first + tile]
            probs = jnp.exp2(dot_nt(keys, query) * (SCALE * LOG2E) + mask - lse)
            dv_acc[oldest : oldest + span, :] += dot_nn(probs.astype(BF16), grad)
            grad_probs = dot_nt(values, grad)
            delta = jnp.sum(probs * grad_probs, axis=0, keepdims=True)
            grad_scores = (probs * (grad_probs - delta)).astype(BF16)
            dk_acc[oldest : oldest + span, :] += dot_nn(grad_scores, query) * SCALE
            dq_ref[first : first + tile, columns] = (dot_tn(grad_scores, keys) * SCALE).astype(BF16)
    dkv_ref[:, :HEAD_DIM] = dk_acc[...].astype(dkv_ref.dtype)
    dkv_ref[:, HEAD_DIM:] = dv_acc[...].astype(dkv_ref.dtype)


def attend_back(query, kv_all, grad_attn, lse, query_tag, key_tag, hops, head, count, deps=()):
    rows = query.shape[0]
    groups = HEADS // KV_HEADS
    span = kv_all.shape[0]
    spans = query_tiles(rows, hops)
    return pl.pallas_call(
        functools.partial(attend_back_kernel, spans, hops * rows, len(deps)),
        grid=(count,),
        in_specs=[
            pl.BlockSpec((rows, groups * HEAD_DIM), lambda g: (0, head + g)),
            pl.BlockSpec((span, HEAD_DIM), lambda g: (0, head + g)),
            pl.BlockSpec((span, HEAD_DIM), lambda g: (0, KV_HEADS + head + g)),
            pl.BlockSpec((rows, groups * HEAD_DIM), lambda g: (0, head + g)),
            pl.BlockSpec((1, groups, rows), lambda g: (head + g, 0, 0)),
            pl.BlockSpec((1, rows), lambda g: (0, 0)),
            pl.BlockSpec((span, 1), lambda g: (0, 0)),
        ]
        + [pl.BlockSpec(memory_space=pl.ANY)] * len(deps),
        out_specs=[
            pl.BlockSpec((rows, groups * HEAD_DIM), lambda g: (0, g)),
            pl.BlockSpec((span, 2 * HEAD_DIM), lambda g: (0, g)),
        ],
        out_shape=[
            jax.ShapeDtypeStruct((rows, count * groups * HEAD_DIM), BF16),
            jax.ShapeDtypeStruct((span, count * 2 * HEAD_DIM), BF16),
        ],
        scratch_shapes=[
            pltpu.VMEM((span, rows), F32),
            pltpu.VMEM((span, HEAD_DIM), F32),
            pltpu.VMEM((span, HEAD_DIM), F32),
        ],
        compiler_params=pltpu.CompilerParams(vmem_limit_bytes=VMEM_LIMIT),
        cost_estimate=cost(2.0 * count),
        name="attend_back",
    )(query, kv_all, kv_all, grad_attn, lse, query_tag, key_tag, *deps)


BACK_ROWS = 2 * ADAPTER_RANK


def expert_kernel(
    count, splits, experts, capacity, depth, direct, with_prior, with_shared, with_sums, packed, waits, *refs
):
    meta, refs = refs[0], refs[1:]
    weight_count = 5 if with_shared else 3
    given = weight_count - (2 if with_shared else 1) if direct else weight_count
    weight_refs, refs = refs[:given], refs[given:]
    token_refs, grad_refs = [], []
    for split in splits:
        token_refs.append(refs[:split])
        refs = refs[split:]
    for split in splits:
        grad_refs.append(refs[:split])
        refs = refs[split:]
    prior_moe, prior_back = (), ()
    if with_prior:
        prior_moe, refs = refs[:count], refs[count:]
        prior_back, refs = refs[:count], refs[count:]
    grad_count = 4 if with_shared else 3
    sums_in = ()
    if with_sums:
        sums_in, refs = refs[:grad_count], refs[grad_count:]
    refs = refs[waits:]
    moe_refs, refs = refs[:count], refs[count:]
    back_refs, refs = refs[:count], refs[count:]
    out_count = 1 if packed else grad_count
    grad_outs, refs = refs[:out_count], refs[out_count:]
    grad_sums, refs = refs[:grad_count], refs[grad_count:]
    first_grad, down_grad, second_grad = grad_sums[:3]
    weight_bufs, refs = refs[:weight_count], refs[weight_count:]
    if packed:
        pack_buf, refs = refs[0], refs[1:]
    tokens_buf, grad_buf, moe_buf, back_buf, in_sem, out_sem, weight_sem, sum_sem, sum_in_sem = refs

    step = pl.program_id(0)
    steps = count // 2
    slots = min(2, steps)
    slot = lax.rem(step, slots)
    rows, wide = tokens_buf.shape[2:]
    model = wide - LANES
    hidden = EXPERT_HIDDEN
    rank = ADAPTER_RANK
    up_ref, down_ref, second_ref = weight_bufs[:3]

    def weight_copies():
        pairs = list(zip(weight_refs, weight_bufs))
        if direct:
            raw, lines = weight_refs[1], weight_refs[1].shape[1]
            pairs, columns = pairs[:1], second_ref.shape[1] // depth
            for z in range(depth):
                pairs.append((raw.at[z, :, pl.ds(0, wide)], down_ref.at[pl.ds(z * lines, lines)]))
                part = raw.at[z, :, pl.ds(wide, columns)]
                pairs.append((part, second_ref.at[:, pl.ds(z * columns, columns)]))
            if with_shared:
                group, size = 4 * LANES, lines // 4
                for z in range(depth):
                    for q in range(4):
                        width = min(group, wide - q * group)
                        part = raw.at[z, pl.ds(q * size, size), pl.ds(wide + columns, width)]
                        target = weight_bufs[3].at[pl.ds(z * size, size), pl.ds(q * group, width)]
                        pairs.append((part, target))
                pairs.append((weight_refs[2], weight_bufs[4]))
        return [pltpu.make_async_copy(src, dst, weight_sem.at[n]) for n, (src, dst) in enumerate(pairs)]

    def incoming(k, i, kinds):
        copies = []
        to, source = k % slots, 2 * k + i
        for n, (refs_of, buf) in enumerate(((token_refs, tokens_buf), (grad_refs, grad_buf))):
            size = rows // len(refs_of[source])
            for p, piece in enumerate(refs_of[source] if n in kinds else ()):
                part = buf.at[to, i, pl.ds(p * size, size)]
                copies.append(pltpu.make_async_copy(piece, part, in_sem.at[to, i, 2 * n + p]))
        if with_prior and 2 in kinds:
            copies.append(pltpu.make_async_copy(prior_moe[source], moe_buf.at[to, i], in_sem.at[to, i, 4]))
            copies.append(pltpu.make_async_copy(prior_back[source], back_buf.at[to, i], in_sem.at[to, i, 5]))
        return copies

    def outgoing(k, i, kinds=(0, 1)):
        at, source = k % slots, 2 * k + i
        pairs = ((moe_buf, moe_refs), (back_buf, back_refs))
        return [pltpu.make_async_copy(pairs[n][0].at[at, i], pairs[n][1][source], out_sem.at[at, i, n]) for n in kinds]

    def at_step(action, first=0, last=steps):
        for k in range(first, last):
            pl.when(step == k)(functools.partial(action, k))

    def wait_in(i, kind):
        def action(k):
            for copy in incoming(k, i, (kind,)):
                copy.wait()

        at_step(action)

    def start_out(i, n):
        at_step(lambda k: outgoing(k, i, (n,))[0].start())

    def turn(k):
        for i in (0, 1):
            if k >= 1:
                for copy in outgoing(k - 1, i):
                    copy.wait()
            if k + 1 < steps:
                for copy in incoming(k + 1, i, (0, 1, 2)):
                    copy.start()

    def sum_copy(n):
        return pltpu.make_async_copy(pack_buf if packed else grad_sums[n], grad_outs[n], sum_sem.at[n])

    def sum_in(n):
        return pltpu.make_async_copy(sums_in[n], grad_sums[n], sum_in_sem.at[n])

    @pl.when(step == 0)
    def _():
        for i in (0, 1):
            for copy in incoming(0, i, (0,)):
                copy.start()
        for i in (0, 1):
            for copy in incoming(0, i, (1,)):
                copy.start()
        for copy in weight_copies():
            copy.start()
        for i in (0, 1):
            for copy in incoming(0, i, (2,)):
                copy.start()
        for n, total in enumerate(grad_sums):
            if with_sums:
                sum_in(n).start()
            else:
                total[...] = jnp.zeros_like(total)

    expert = meta[0]
    lane = lax.broadcasted_iota(jnp.int32, (1, LANES), 1)
    sub = lax.broadcasted_iota(jnp.int32, (LANES, 1), 0)
    places, picks, gates_of, selects, adapters = [], [], [], [], []
    inputs, grad_rows = [], []
    for i in (0, 1):
        wait_in(i, 0)
        extra_b = tokens_buf[slot, i, :, model:]
        extra = extra_b.astype(F32)
        own = 3 * experts + 3 * rank
        adapter = extra[0:1, own : own + 1]
        select = ((lane // rank).astype(F32) == adapter).astype(F32)
        slot_column = jnp.sum(jnp.where(lane == expert, extra, 0.0), axis=1, keepdims=True)
        slot_row = jnp.sum(jnp.where(sub == expert, extra.T, 0.0), axis=0, keepdims=True)
        place = lax.broadcasted_iota(jnp.int32, (rows, capacity), 1).astype(F32) == slot_column
        pick = lax.broadcasted_iota(jnp.int32, (capacity, rows), 0).astype(F32) == slot_row
        place, pick = place.astype(F32).astype(BF16), pick.astype(F32).astype(BF16)
        picked_extra = dot_nn(pick, extra_b)
        chosen = (lane == experts + expert) | (lane == 2 * experts + expert)
        gates_of.append(jnp.sum(jnp.where(chosen, picked_extra, 0.0), axis=1, keepdims=True))
        inputs.append(dot_nn(pick, tokens_buf[slot, i, :, :model]).astype(BF16))
        picks.append(pick)
        places.append(place)
        adapters.append(adapter)
        selects.append(jnp.broadcast_to(select, (capacity, LANES)))
    for i in (0, 1):
        wait_in(i, 1)
        grad_rows.append(dot_nn(picks[i], grad_buf[slot, i]))
    at_step(turn)
    inputs = jnp.concatenate(inputs, axis=0)
    grad_rows = jnp.concatenate(grad_rows, axis=0)
    gate = jnp.concatenate(gates_of, axis=0)
    select = jnp.concatenate(selects, axis=0)
    select_two = jnp.concatenate([select, select], axis=1)

    @pl.when(step == 0)
    def _():
        for copy in weight_copies():
            copy.wait()

    low = (dot_nn(inputs, up_ref[:, 2 * hidden : 2 * hidden + 2 * LANES]) * select_two).astype(BF16)
    gate_part = dot_nn(inputs, up_ref[:, :hidden]) + dot_nn(low[:, :LANES], second_ref[:, :hidden])
    up_part = dot_nn(inputs, up_ref[:, hidden : 2 * hidden]) + dot_nn(low[:, LANES:], second_ref[:, hidden : 2 * hidden])
    sigmoid = 1.0 / (1.0 + jnp.exp(-gate_part))
    silu = gate_part * sigmoid
    act = (silu * up_part).astype(BF16)
    low_down = (dot_nn(act, down_ref[:, model:]) * select).astype(BF16)
    output = (dot_nn(act, down_ref[:, :model]) + dot_nn(low_down, second_ref[:, 2 * hidden :])).astype(BF16).astype(F32)
    grad_gate = jnp.sum(output * grad_rows, axis=1, keepdims=True)
    weighted = (gate * output).astype(BF16)

    if with_sums:

        @pl.when(step == 0)
        def _():
            for n in range(grad_count):
                sum_in(n).wait()

    grad_y = (gate * grad_rows).astype(BF16)
    glow_down = (dot_nt(grad_y, second_ref[:, 2 * hidden :]) * select).astype(BF16)
    second_grad[:, 2 * hidden :] += dot_tn(low_down, grad_y)
    down_grad[...] += dot_tn(act, glow_down)
    grad_act = dot_nt(grad_y, down_ref[:, :model]) + dot_nt(glow_down, down_ref[:, model:])
    grad_up = (grad_act * silu).astype(BF16)
    grad_gp = (grad_act * up_part * (sigmoid * (1.0 + gate_part * (1.0 - sigmoid)))).astype(BF16)
    glow = jnp.concatenate(
        [
            dot_nt(grad_gp, second_ref[:, :hidden]) * select,
            dot_nt(grad_up, second_ref[:, hidden : 2 * hidden]) * select,
        ],
        axis=1,
    ).astype(BF16)
    second_grad[:, :hidden] += dot_tn(low[:, :LANES], grad_gp)
    second_grad[:, hidden : 2 * hidden] += dot_tn(low[:, LANES:], grad_up)
    first_grad[...] += dot_tn(inputs, glow)
    grad_in = (
        dot_nt(grad_gp, up_ref[:, :hidden])
        + dot_nt(grad_up, up_ref[:, hidden : 2 * hidden])
        + dot_nt(glow, up_ref[:, 2 * hidden : 2 * hidden + 2 * LANES])
    ).astype(BF16)
    gate_hi = grad_gate.astype(BF16).astype(F32)
    gate_lo = grad_gate - gate_hi
    extra_out = (
        jnp.where(lane == expert, gate_hi, 0.0) + jnp.where(lane == experts + expert, gate_lo, 0.0)
    ).astype(BF16)

    @pl.when(step == steps - 1)
    def _():
        if not packed:
            for n in range(3):
                sum_copy(n).start()
            return
        second_t = second_grad[...].T
        parts = [first_grad[:, :LANES], first_grad[:, LANES:], down_grad[...], second_t]
        at = 0
        for part in parts:
            size = part.shape[0] // depth
            for z in range(depth):
                pack_buf[z, at : at + size, :] = part[z * size : (z + 1) * size].astype(BF16)
            at += size

    for i in (0, 1):
        mine = slice(i * capacity, (i + 1) * capacity)
        wait_in(i, 2)
        moe = dot_nn(places[i], weighted[mine])
        back = dot_nn(places[i], grad_in[mine])
        back_extra = dot_nn(places[i], extra_out[mine])
        if with_prior:
            moe = moe + moe_buf[slot, i].astype(F32)
            back = back + back_buf[slot, i, :rows, :model].astype(F32)
            back_extra = back_extra + back_buf[slot, i, :rows, model:].astype(F32)
        if not with_prior:
            back_buf[slot, i, rows:, :] = jnp.zeros((BACK_ROWS, wide), BF16)
        if with_shared:
            sdown_ref, sb_ref = weight_bufs[3:]
            units = sdown_ref.shape[0]
            first_gate, first_up, first_down = 3 * experts, 3 * experts + rank, 3 * experts + 2 * rank
            tokens = tokens_buf[slot, i, :, :model]
            extra_b = tokens_buf[slot, i, :, model:]
            grads = grad_buf[slot, i]
            offset = (lane - sub).astype(F32) - adapters[i] * float(rank)

            def spread(base):
                inside = (sub >= base) & (sub < base + rank)
                return (inside & (offset == float(-base))).astype(F32).astype(BF16)

            to_gate = dot_nt(spread(first_gate), sb_ref[:units]).astype(BF16)
            to_up = dot_nt(spread(first_up), sb_ref[units:]).astype(BF16)
            to_down = dot_nt(spread(first_down), sdown_ref[:, model:]).astype(BF16)
            shared_up = up_ref[:, 2 * hidden + 2 * LANES :]
            gate_up = dot_nn(tokens, shared_up)
            s_gate = gate_up[:, :units] + dot_nn(extra_b, to_gate)
            s_up = gate_up[:, units:] + dot_nn(extra_b, to_up)
            s_sig = 1.0 / (1.0 + jnp.exp(-s_gate))
            s_silu = s_gate * s_sig
            s_act = (s_silu * s_up).astype(BF16)
            moe = moe + dot_nn(s_act, sdown_ref[:, :model])
            s_grad = dot_nt(grads, sdown_ref[:, :model]) + dot_nn(extra_b, to_down)
            grad_sums[3][...] += dot_tn(s_act, dot_nn(extra_b, spread(first_down)).astype(BF16))
            s_gu = (s_grad * s_silu).astype(BF16)
            s_gg = (s_grad * s_up * (s_sig * (1.0 + s_gate * (1.0 - s_sig)))).astype(BF16)
            back_extra = back_extra + dot_nt(s_act, to_down) + dot_nt(s_gg, to_gate) + dot_nt(s_gu, to_up)
            back = back + dot_nt(jnp.concatenate([s_gg, s_gu], axis=1), shared_up)
            columns = pl.ds(pl.multiple_of(meta[1] * units, units), units)
            grad_bg = dot_tn(extra_b, s_gg)[first_gate : first_gate + rank]
            grad_bu = dot_tn(extra_b, s_gu)[first_up : first_up + rank]
            back_buf[slot, i, rows : rows + rank, columns] = grad_bg.astype(BF16)
            back_buf[slot, i, rows + rank :, columns] = grad_bu.astype(BF16)
        moe_buf[slot, i] = moe.astype(BF16)
        start_out(i, 0)
        back_buf[slot, i, :rows, :model] = back.astype(BF16)
        back_buf[slot, i, :rows, model:] = back_extra.astype(BF16)
        start_out(i, 1)

    @pl.when(step == steps - 1)
    def _():
        if packed and with_shared:
            size = grad_sums[3].shape[0] // depth
            for z in range(depth):
                part = grad_sums[3][z * size : (z + 1) * size, :]
                if size % 16:
                    part = jnp.concatenate([part, jnp.zeros((16 - size % 16, LANES), F32)], axis=0)
                pack_buf[z, pack_buf.shape[1] - part.shape[0] :, :] = part.astype(BF16)
        for n in range(0 if packed else 3, out_count):
            sum_copy(n).start()
        for i in (0, 1):
            for copy in outgoing(steps - 1, i):
                copy.wait()
        for n in range(out_count):
            sum_copy(n).wait()


def expert_call(meta, weights, shapes, tokens, grads, prior, sums, packed, experts, capacity, depth, deps=()):
    count = len(tokens)
    with_shared = len(shapes) > 3
    direct = len(weights) < len(shapes)
    splits = [len(pieces) for pieces in tokens]
    rows, model = sum(piece.shape[0] for piece in grads[0]), grads[0][0].shape[1]
    wide = model + LANES
    slots = min(2, count // 2)
    anywhere = pl.BlockSpec(memory_space=pl.ANY)
    prior = [] if prior is None else list(prior[0]) + list(prior[1])
    flat = [piece for pieces in tokens for piece in pieces] + [piece for pieces in grads for piece in pieces]
    grad_shapes = [
        jax.ShapeDtypeStruct((model, 2 * LANES), F32),
        jax.ShapeDtypeStruct((EXPERT_HIDDEN, LANES), F32),
        jax.ShapeDtypeStruct(shapes[2], F32),
    ]
    if with_shared:
        grad_shapes.append(jax.ShapeDtypeStruct((shapes[3][0], LANES), F32))
    out_shapes = grad_shapes
    if packed:
        lines = sum(s.shape[0] for s in grad_shapes[:2]) + model + shapes[2][1]
        lines = lines // depth
        if with_shared:
            lines += -(-shapes[3][0] // depth // 16) * 16
        out_shapes = [jax.ShapeDtypeStruct((depth, lines, LANES), BF16)]
    back_rows = rows + BACK_ROWS
    outs = pl.pallas_call(
        functools.partial(
            expert_kernel,
            *(count, splits, experts, capacity, depth, direct, bool(prior), with_shared, bool(sums), packed, len(deps)),
        ),
        grid=(count // 2,),
        in_specs=[pl.BlockSpec(memory_space=pltpu.SMEM)]
        + [anywhere] * (len(weights) + len(flat) + len(prior) + len(sums) + len(deps)),
        out_specs=[anywhere] * (2 * count + len(out_shapes)),
        out_shape=[jax.ShapeDtypeStruct((rows, model), BF16)] * count
        + [jax.ShapeDtypeStruct((back_rows, wide), BF16)] * count
        + out_shapes,
        scratch_shapes=[pltpu.VMEM(s.shape, F32) for s in grad_shapes]
        + [pltpu.VMEM(shape, BF16) for shape in shapes]
        + ([pltpu.VMEM(out_shapes[0].shape, BF16)] if packed else [])
        + [
            pltpu.VMEM((slots, 2, rows, wide), BF16),
            pltpu.VMEM((slots, 2, rows, model), BF16),
            pltpu.VMEM((slots, 2, rows, model), BF16),
            pltpu.VMEM((slots, 2, back_rows, wide), BF16),
            pltpu.SemaphoreType.DMA((slots, 2, 6)),
            pltpu.SemaphoreType.DMA((slots, 2, 2)),
            pltpu.SemaphoreType.DMA((len(shapes) + 6 * depth,)),
            pltpu.SemaphoreType.DMA((len(grad_shapes),)),
            pltpu.SemaphoreType.DMA((len(grad_shapes),)),
        ],
        compiler_params=pltpu.CompilerParams(vmem_limit_bytes=VMEM_LIMIT),
        cost_estimate=cost(12.0 * count),
        name="expert",
    )(meta, *weights, *flat, *prior, *sums, *deps)
    return outs[:count], outs[count : 2 * count], outs[2 * count :]


def swap(array, bit, size):
    return lax.ppermute(array, "dp", [(i, i ^ bit) for i in range(size)])


def plane_gather(array, size):
    half = array.shape[0] // 2
    x, y = swap(array, 2, size), swap(array, 4, size)
    across = {0: (array,), 2: (x,), 4: (y,), 6: (swap(y[:half], 2, size), swap(x[half:], 4, size))}
    blocks = [None] * size
    for k in (0, 2, 4, 6):
        blocks[k] = across[k]
        blocks[k + 1] = tuple(swap(piece, 1, size) for piece in across[k])
    return blocks


def add(*terms):
    total = terms[0].astype(F32)
    for term in terms[1:]:
        total = total + term.astype(F32)
    return total.astype(BF16)


def tie_kernel(*refs):
    del refs


def tie_all(arrays, *others):
    anywhere = pl.BlockSpec(memory_space=pl.ANY)
    return pl.pallas_call(
        tie_kernel,
        in_specs=[anywhere] * (len(arrays) + len(others)),
        out_specs=[anywhere] * len(arrays),
        out_shape=[jax.ShapeDtypeStruct(array.shape, array.dtype) for array in arrays],
        input_output_aliases={n: n for n in range(len(arrays))},
        name="tie",
    )(*arrays, *others)


def tie(array, *others):
    return tie_all([array], *others)[0]


def assemble_kernel(splits, widths, waits, me_ref, *refs):
    pieces, outs = refs[: sum(splits)], refs[sum(splits) + waits : -3]
    whole, in_sem, out_sem = refs[-3:]
    copies, at = [], 0
    for k, split in enumerate(splits):
        start = 0
        for piece in pieces[at : at + split]:
            target = whole.at[pl.ds(start, piece.shape[0]), me_ref[0] ^ k]
            copies.append(pltpu.make_async_copy(piece, target, in_sem.at[len(copies)]))
            start += piece.shape[0]
        at += split
    for copy in copies:
        copy.start()
    for copy in copies:
        copy.wait()
    copies, column = [], 0
    for out, (count, width) in zip(outs, widths):
        for n in range(count):
            source = whole.at[:, :, :, pl.ds(column, width)]
            copies.append(pltpu.make_async_copy(source, out.at[:, :, n], out_sem.at[len(copies)]))
            column += width
    for copy in copies:
        copy.start()
    for copy in copies:
        copy.wait()


def assemble(blocks, widths, me, deps=()):
    depth, rows, _ = blocks[0][0].shape
    size = len(blocks)
    splits = [len(pieces) for pieces in blocks]
    flat = [piece for pieces in blocks for piece in pieces]
    outs = pl.pallas_call(
        functools.partial(assemble_kernel, splits, widths, len(deps)),
        in_specs=[pl.BlockSpec(memory_space=pltpu.SMEM)] + [pl.BlockSpec(memory_space=pl.ANY)] * (len(flat) + len(deps)),
        out_specs=[pl.BlockSpec(memory_space=pl.ANY)] * len(widths),
        out_shape=[jax.ShapeDtypeStruct((depth, size, count, rows, width), BF16) for count, width in widths],
        scratch_shapes=[
            pltpu.VMEM((depth, size, rows, sum(count * width for count, width in widths)), BF16),
            pltpu.SemaphoreType.DMA((len(flat),)),
            pltpu.SemaphoreType.DMA((sum(count for count, _ in widths),)),
        ],
        compiler_params=pltpu.CompilerParams(vmem_limit_bytes=VMEM_LIMIT),
        name="assemble",
    )(me.astype(jnp.int32).reshape(1), *flat, *deps)
    return [out.reshape(-1, out.shape[-1]) for out in outs]


def turn_kernel(
    waits, own, other, from_x, from_y, hidden, gates, first_gu, router, gain, grad_out, second_o, out_w, first_o, *rest
):
    grad_mid_out, grad_mid_b_out, glow_out, glow_sgu, low_sdown, grad_attn, units_out = rest[waits:]
    rows, model = hidden.shape
    experts = gates.shape[1]
    rank = ADAPTER_RANK
    total = own[...].astype(F32) + other[...].astype(F32) + from_x[...].astype(F32) + from_y[...].astype(F32)
    units_out[...] = total[rows:, :]
    tail = total[:rows, model:]
    grad_gates = tail[:, :experts] + tail[:, experts : 2 * experts]
    glow = tail[:, 3 * experts : 3 * experts + 2 * rank].astype(BF16)
    glow_sgu[...] = glow
    low_sdown[...] = tail[:, 3 * experts + 2 * rank : 3 * experts + 3 * rank].astype(BF16)
    gate = gates[...]
    grad_logits = gate * (grad_gates - jnp.sum(gate * grad_gates, axis=-1, keepdims=True))
    logits_hi = grad_logits.astype(BF16)
    left = grad_logits - logits_hi.astype(F32)
    logits_mid = left.astype(BF16)
    logits_lo = (left - logits_mid.astype(F32)).astype(BF16)
    grad_normed = total[:rows, :model] + dot_nt(glow, first_gu[...])
    for part in (logits_hi, logits_mid, logits_lo):
        grad_normed = grad_normed + dot_nt(part, router[...])
    values = hidden[...]
    scale = lax.rsqrt(jnp.mean(values * values, axis=-1, keepdims=True) + EPSILON)
    scaled = grad_normed * gain[...]
    mean = jnp.mean(values * scaled, axis=-1, keepdims=True)
    grad_mid = grad_out[...].astype(F32) + scale * scaled - values * (scale * scale * scale * mean)
    grad_mid_out[...] = grad_mid
    grad_mid_b = grad_mid.astype(BF16)
    grad_mid_b_out[...] = grad_mid_b
    glow = dot_nt(grad_mid_b, second_o[...]).astype(BF16)
    glow_out[...] = glow
    grad_attn[...] = (dot_nt(grad_mid_b, out_w[...]) + dot_nt(glow, first_o[...])).astype(BF16)


def turn(args, deps):
    rows, model = args[4].shape
    rank = ADAPTER_RANK
    vmem = pl.BlockSpec(memory_space=pltpu.VMEM)
    shapes = [
        ((rows, model), F32),
        ((rows, model), BF16),
        ((rows, rank), BF16),
        ((rows, 2 * rank), BF16),
        ((rows, rank), BF16),
        ((rows, HEADS * HEAD_DIM), BF16),
        ((BACK_ROWS, args[0].shape[1]), F32),
    ]
    return pl.pallas_call(
        functools.partial(turn_kernel, len(deps)),
        in_specs=[vmem] * len(args) + [pl.BlockSpec(memory_space=pl.ANY)] * len(deps),
        out_specs=[vmem] * len(shapes),
        out_shape=[jax.ShapeDtypeStruct(shape, dtype) for shape, dtype in shapes],
        compiler_params=pltpu.CompilerParams(vmem_limit_bytes=VMEM_LIMIT),
        cost_estimate=cost(4.0),
        name="turn",
    )(*args, *deps)


def query_back_kernel(waits, grad_q, normed, low_q, q_w, first_q, second_q, *rest):
    grad_normed, first_query, second_query = rest[waits:]
    glow_q = dot_nt(grad_q[...], second_q[...]).astype(BF16)
    grad_normed[...] = dot_nt(grad_q[...], q_w[...]) + dot_nt(glow_q, first_q[...])
    first_query[...] = dot_tn(normed[...], glow_q)
    second_query[...] = dot_tn(low_q[...], grad_q[...])


def query_back(args, deps):
    rows, model = args[1].shape
    vmem = pl.BlockSpec(memory_space=pltpu.VMEM)
    shapes = [(rows, model), (model, ADAPTER_RANK), (ADAPTER_RANK, HEADS * HEAD_DIM)]
    return pl.pallas_call(
        functools.partial(query_back_kernel, len(deps)),
        in_specs=[vmem] * len(args) + [pl.BlockSpec(memory_space=pl.ANY)] * len(deps),
        out_specs=[vmem] * len(shapes),
        out_shape=[jax.ShapeDtypeStruct(shape, F32) for shape in shapes],
        compiler_params=pltpu.CompilerParams(vmem_limit_bytes=VMEM_LIMIT),
        cost_estimate=cost(0.1),
        name="query_back",
    )(*args, *deps)


def middle_kernel(waits, attn, glow_out, normed2, glow_sgu, grad_mid, out_low, grad_out, low_sdown, *rest):
    first_early, second_out, second_down = rest[waits:]
    rank = ADAPTER_RANK
    first_early[:, :rank] = dot_tn(attn[...], glow_out[...])
    first_early[:, rank:] = dot_tn(normed2[...], glow_sgu[...])
    second_out[...] = dot_tn(out_low[...], grad_mid[...])
    second_down[...] = dot_tn(low_sdown[...], grad_out[...])


def middle(args, deps):
    model = args[0].shape[1]
    rank = ADAPTER_RANK
    vmem = pl.BlockSpec(memory_space=pltpu.VMEM)
    shapes = [(model, 3 * rank), (rank, model), (rank, model)]
    return pl.pallas_call(
        functools.partial(middle_kernel, len(deps)),
        in_specs=[vmem] * len(args) + [pl.BlockSpec(memory_space=pl.ANY)] * len(deps),
        out_specs=[vmem] * len(shapes),
        out_shape=[jax.ShapeDtypeStruct(shape, F32) for shape in shapes],
        compiler_params=pltpu.CompilerParams(vmem_limit_bytes=VMEM_LIMIT),
        cost_estimate=cost(0.1),
        name="middle",
    )(*args, *deps)


def last_kernel(
    owners, grad_kv, normed, low_kv, kv_w, first_kv, second_k, second_v, hidden, gain, grad_mid, grad_normed_q,
    first_query, first_early, second_query, second_early, adapter, grad_hidden, first_out, second_out
):
    rank = ADAPTER_RANK
    heads = range(grad_kv.shape[1] // (2 * HEAD_DIM))
    grad_k = jnp.concatenate([grad_kv[:, 2 * n * HEAD_DIM : (2 * n + 1) * HEAD_DIM] for n in heads], axis=1)
    grad_v = jnp.concatenate([grad_kv[:, (2 * n + 1) * HEAD_DIM : (2 * n + 2) * HEAD_DIM] for n in heads], axis=1)
    width = grad_k.shape[1]
    glow_k = dot_nt(grad_k, second_k[...]).astype(BF16)
    glow_v = dot_nt(grad_v, second_v[...]).astype(BF16)
    grad_normed = grad_normed_q[...] + dot_nt(grad_k, kv_w[:, :width]) + dot_nt(grad_v, kv_w[:, width:])
    grad_normed = grad_normed + dot_nt(glow_k, first_kv[:, :rank]) + dot_nt(glow_v, first_kv[:, rank:])
    values = hidden[...].astype(F32)
    scale = lax.rsqrt(jnp.mean(values * values, axis=-1, keepdims=True) + EPSILON)
    scaled = grad_normed * gain[...]
    mean = jnp.mean(values * scaled, axis=-1, keepdims=True)
    grad_hidden[...] = grad_mid[...] + scale * scaled - values * (scale * scale * scale * mean)
    firsts = [first_query[...], dot_tn(normed[...], glow_k), dot_tn(normed[...], glow_v), first_early[...]]
    tags = jnp.broadcast_to(adapter[...], (first_query.shape[0], LANES - 6 * rank))
    first_out[...] = jnp.concatenate(firsts + [tags], axis=1).astype(BF16)
    seconds = [second_query[...], dot_tn(low_kv[:, :rank], grad_k), dot_tn(low_kv[:, rank:], grad_v), second_early[...]]
    seconds = jnp.concatenate(seconds, axis=1)
    columns = seconds.shape[1] // owners
    padding = jnp.zeros((rank, second_out.shape[1] // rank * LANES - columns), F32)
    for n in range(owners):
        piece = jnp.concatenate([seconds[:, n * columns : (n + 1) * columns], padding], axis=1).astype(BF16)
        for c in range(piece.shape[1] // LANES):
            second_out[n, c * rank : (c + 1) * rank, :] = piece[:, c * LANES : (c + 1) * LANES]


def last(owners, args):
    rows, model = args[7].shape
    columns = (args[13].shape[1] + 2 * KV_HEADS * HEAD_DIM + args[14].shape[1]) // owners
    vmem = pl.BlockSpec(memory_space=pltpu.VMEM)
    return pl.pallas_call(
        functools.partial(last_kernel, owners),
        in_specs=[vmem] * len(args),
        out_specs=[vmem] * 3,
        out_shape=[
            jax.ShapeDtypeStruct((rows, model), F32),
            jax.ShapeDtypeStruct((model, LANES), BF16),
            jax.ShapeDtypeStruct((owners, -(-columns // LANES) * ADAPTER_RANK, LANES), BF16),
        ],
        compiler_params=pltpu.CompilerParams(vmem_limit_bytes=VMEM_LIMIT),
        cost_estimate=cost(2.0),
        name="last",
    )(*args)


def spread_kernel(depth, lines, flat, first_out, second_out):
    rank = ADAPTER_RANK
    size = flat.shape[0] // depth
    row = lax.broadcasted_iota(jnp.int32, (LANES, 1), 0).astype(F32)
    column = lax.broadcasted_iota(jnp.int32, (1, first_out.shape[1]), 1)
    inside = column % LANES
    target = (column // LANES * rank + inside).astype(F32)
    owner = (inside // rank).astype(F32)
    short = lax.broadcasted_iota(jnp.int32, (1, rank), 1).astype(F32)
    chunks = (flat.shape[1] - lines) // rank
    first, second = None, [None] * chunks
    for d in range(size):
        adapter = flat[d, 0:1, 6 * rank : 6 * rank + 1].astype(F32)
        total = flat[d].astype(F32)
        for z in range(1, depth):
            total = total + flat[z * size + d].astype(F32)
        total = total.astype(BF16)
        place = ((target - adapter * float(rank) == row) & (owner == adapter)).astype(F32).astype(BF16)
        lift = (row - adapter * float(rank) == short).astype(F32).astype(BF16)
        part = dot_nn(total[:lines], place)
        first = part if first is None else first + part
        for c in range(chunks):
            part = dot_nn(lift, total[lines + c * rank : lines + (c + 1) * rank])
            second[c] = part if second[c] is None else second[c] + part
    first_out[...] = first
    for c in range(chunks):
        second_out[:, c * LANES : (c + 1) * LANES] = second[c]


def spread(flat, depth, lines):
    vmem = pl.BlockSpec(memory_space=pltpu.VMEM)
    chunks = (flat.shape[1] - lines) // ADAPTER_RANK
    return pl.pallas_call(
        functools.partial(spread_kernel, depth, lines),
        in_specs=[vmem],
        out_specs=[vmem] * 2,
        out_shape=[jax.ShapeDtypeStruct((lines, 6 * LANES), F32), jax.ShapeDtypeStruct((LANES, chunks * LANES), F32)],
        compiler_params=pltpu.CompilerParams(vmem_limit_bytes=VMEM_LIMIT),
        cost_estimate=cost(2.0),
        name="spread",
    )(flat)


def per_device(
    depth,
    size,
    block_input,
    document_number,
    key_present,
    routes,
    sequence_adapter,
    output_gradient,
    norm_scale_pair,
    query_key_value_weight,
    attention_output_weight,
    router_weight,
    shared_gate_up_weight,
    shared_down_weight,
    routed_gate_up_weight,
    routed_down_weight,
    dense_first_factor,
    shared_down_first_factor,
    dense_second_factor,
    routed_first_factor,
    routed_down_first_factor,
    routed_second_factor,
):
    _, rows, model = block_input.shape
    topk = routes.shape[2]
    me = lax.axis_index("dp")
    experts = router_weight.shape[1]
    local_experts = routed_gate_up_weight.shape[0]
    shard_rows = query_key_value_weight.shape[0]
    shared_rows = shared_down_weight.shape[0]
    rank_all = dense_second_factor.shape[0]
    second_columns = dense_second_factor.shape[1]
    capacity = 4 * topk * rows // (3 * experts)
    query_width = HEADS * HEAD_DIM
    kv_width = KV_HEADS * HEAD_DIM
    hops = min(depth - 1, -(-(DOCUMENT_SPAN - 1) // rows))
    rank = ADAPTER_RANK
    units = SHARED_HIDDEN // size
    adapter = sequence_adapter[0]
    forward = [(i, i + 1) for i in range(depth - 1)]
    backward = [(i + 1, i) for i in range(depth - 1)]

    def over_seq(shard):
        return lax.all_gather(shard, "seq", axis=0)

    first_shard = dense_first_factor.reshape(shard_rows, 6 * rank_all)
    second_width = second_columns * rank_all // shard_rows
    groups = second_width // rank_all
    pack_kv = jnp.concatenate(
        [
            query_key_value_weight[:, query_width:],
            first_shard[:, rank_all : 3 * rank_all],
            dense_second_factor.T.reshape(groups, shard_rows, rank_all).transpose(1, 0, 2).reshape(shard_rows, -1),
            jnp.pad(
                jnp.concatenate([router_weight, norm_scale_pair.T], axis=1), ((0, 0), (0, LANES - experts - 2))
            ),
        ],
        axis=1,
    )
    pack_q = jnp.concatenate(
        [
            query_key_value_weight[:, :query_width],
            first_shard[:, :rank_all],
            first_shard[:, 3 * rank_all :],
            attention_output_weight,
        ],
        axis=1,
    )
    seq_kv = over_seq(pack_kv)
    seq_q = over_seq(tie(pack_q, seq_kv))

    flags = jnp.sum((routes[0][..., None] == jnp.arange(experts, dtype=jnp.int32)).astype(F32), axis=1)
    before = (jnp.arange(rows)[:, None] > jnp.arange(rows)[None, :]).astype(BF16)
    slots = jnp.where(flags > 0, dot_nn(before, flags.astype(BF16)), -1.0).astype(BF16)

    def own_columns(matrix):
        return lax.dynamic_slice_in_dim(matrix, adapter * rank, rank, 1)

    def own_factors(matrix):
        count = matrix.shape[1] // rank_all
        return jnp.concatenate([own_columns(matrix[:, n * rank_all : (n + 1) * rank_all]) for n in range(count)], axis=1)

    grad_out_b = output_gradient[0]
    grads_x, grads_y = swap(grad_out_b, 2, size), swap(grad_out_b, 4, size)
    gate_up = shared_gate_up_weight.reshape(shard_rows, 2, depth, size, units // depth)
    gate_up = gate_up.transpose(3, 0, 1, 2, 4).reshape(size, shard_rows, 2 * units)
    gate_up = lax.all_to_all(gate_up, "dp", split_axis=0, concat_axis=0, tiled=True)
    kv_gathered = plane_gather(tie(seq_kv, grads_x, grads_y, gate_up), size)
    grads_x, grads_y = tie_all([grads_x, grads_y], *kv_gathered[6])
    far_grads = (swap(grads_y[: rows // 2], 2, size), swap(grads_x[rows // 2 :], 4, size))
    grad_blocks = [(grad_out_b,), None, (grads_x,), None, (grads_y,), None, far_grads, None]
    kv_w, kv_first, second_t, small = assemble(
        kv_gathered, ((1, 2 * kv_width), (1, 2 * rank_all), (groups, rank_all), (1, LANES)), me
    )
    router_w = small[:, :experts]
    gains = small[:, experts : experts + 2].astype(F32).T
    second = own_columns(second_t).T
    first_kv = own_factors(kv_first)
    widths = [query_width, kv_width, kv_width, model, SHARED_HIDDEN, SHARED_HIDDEN, model]
    edges = [sum(widths[:n]) for n in range(len(widths) + 1)]
    b_parts = [second[:, edges[n] : edges[n + 1]] for n in range(len(widths))]

    down_rows = routed_down_weight.shape[1]
    second_cut = rank_all * routed_second_factor.shape[2] // down_rows
    up_shards, down_shards = [], []
    for j in range(local_experts):
        up_parts = [
            routed_gate_up_weight[j].reshape(-1, 2 * EXPERT_HIDDEN),
            routed_first_factor[j].reshape(-1, 2 * rank_all),
        ]
        down_parts = [
            routed_down_weight[j],
            routed_down_first_factor[j],
            routed_second_factor[j].reshape(down_rows, -1),
        ]
        if j == 0:
            up_parts.append(gate_up.reshape(size * shard_rows, 2 * units))
            shared_down = jnp.concatenate([shared_down_weight, shared_down_first_factor], axis=1)
            shared_down = jnp.pad(shared_down, ((0, 0), (0, 16 * LANES - shared_down.shape[1])))
            shared_down = shared_down.reshape(shared_rows, 4, 4 * LANES).transpose(1, 0, 2)
            down_parts.append(shared_down.reshape(down_rows, -1))
        up_shards.append(jnp.concatenate(up_parts, axis=1))
        down_shards.append(jnp.concatenate(down_parts, axis=1))
    first_down = over_seq(tie(down_shards[0], seq_kv))

    x_flat = block_input[0].astype(F32)
    normed = rms_norm(x_flat, gains[0]).astype(BF16)
    select = (jnp.arange(rank_all, dtype=jnp.int32) // rank == adapter).astype(F32)[None, :]

    def masked_low(inputs, factors):
        low = dot_nn(inputs, factors)
        return [
            (low[:, at : at + rank_all] * select).astype(BF16) for at in range(0, factors.shape[1], rank_all)
        ]

    low_k, low_v = masked_low(normed, kv_first)
    low_kv = own_factors(jnp.concatenate([low_k, low_v], axis=1))
    kv_extra = jnp.concatenate(
        [dot_nt(low_k, second_t[edges[1] : edges[2]]), dot_nt(low_v, second_t[edges[2] : edges[3]])], axis=1
    )
    present_tag = jnp.where(key_present == 1, document_number + 1, 0).astype(BF16)
    tag_rows = jnp.broadcast_to(jnp.pad(present_tag, ((0, 0), (0, 2 * kv_width - rows))), (16, 2 * kv_width))
    kv_blocks = [jnp.concatenate([(dot_nn(normed, kv_w) + kv_extra).astype(BF16), tag_rows], axis=0)]
    q_blocks = plane_gather(tie(seq_q, *far_grads), size)
    for k in range(1, size, 2):
        grad_blocks[k] = tuple(swap(piece, 1, size) for piece in grad_blocks[k - 1])
    for h in range(hops):
        block = kv_blocks[-1] if h == 0 else tie(kv_blocks[-1], q_blocks[2][0], q_blocks[4][0], first_down)
        kv_blocks.append(lax.ppermute(block, "seq", forward))
        kv_blocks[h] = block
    kv_all = jnp.concatenate([block[:rows] for block in kv_blocks[::-1]], axis=0)
    key_tag = jnp.concatenate([block[rows, :rows] for block in kv_blocks[::-1]]).astype(F32).reshape(-1, 1)
    query_tag = (document_number + 1).astype(F32)

    seq_up, seq_down = [over_seq(tie(up_shards[0], kv_blocks[hops]))], [first_down]
    for j in range(1, local_experts):
        seq_up.append(over_seq(tie(up_shards[j], seq_down[j - 1])))
        seq_down.append(over_seq(tie(down_shards[j], seq_up[j - 1])))

    q_w, q_first, out_w = assemble(q_blocks, ((1, query_width), (1, 4 * rank_all), (1, model)), me)
    (low_q,) = masked_low(normed, q_first[:, :rank_all])
    first_out = q_first[:, rank_all : 2 * rank_all]
    q_first = own_factors(q_first)
    first_q, first_o, first_gu = q_first[:, :rank], q_first[:, rank : 2 * rank], q_first[:, 2 * rank :]
    query = (dot_nn(normed, q_w) + dot_nt(low_q, second_t[edges[0] : edges[1]])).astype(BF16)
    low_q = own_columns(low_q)
    glow_sdown = dot_nt(grad_out_b, b_parts[6]).astype(BF16)
    attn, lse = attend(query, kv_all, query_tag, key_tag, hops, (*grad_blocks[3], *grad_blocks[5], *grad_blocks[7]))
    (out_low,) = masked_low(attn, first_out)
    mid = x_flat + dot_nn(attn, out_w) + dot_nt(out_low, second_t[edges[3] : edges[4]])
    out_low = own_columns(out_low)
    normed2 = rms_norm(mid, gains[1]).astype(BF16)

    logits = dot_nn(normed2, router_w)
    top = jnp.max(jnp.where(flags > 0, logits, -jnp.inf), axis=-1, keepdims=True)
    weights = jnp.where(flags > 0, jnp.exp(logits - top), 0.0)
    gates = weights / jnp.sum(weights, axis=-1, keepdims=True)
    gates_hi = gates.astype(BF16)
    gates_lo = (gates - gates_hi.astype(F32)).astype(BF16)
    shared_low = dot_nn(normed2, first_gu).astype(BF16)
    own_adapter = jnp.full((rows, LANES - 3 * experts - 3 * rank), adapter.astype(F32)).astype(BF16)
    payload = jnp.concatenate([normed2, slots, gates_hi, gates_lo, shared_low, glow_sdown, own_adapter], axis=1)
    token_blocks = [None] * size
    token_blocks[0], token_blocks[1] = (payload,), (swap(payload, 1, size),)
    tokens_x, tokens_y = swap(payload, 2, size), swap(payload, 4, size)

    def gather_far(tokens_x, tokens_y, *done):
        tokens_x, tokens_y = tie_all([tokens_x, tokens_y], *done)
        half = rows // 2
        token_blocks[2], token_blocks[3] = (tokens_x,), (swap(tokens_x, 1, size),)
        token_blocks[4], token_blocks[5] = (tokens_y,), (swap(tokens_y, 1, size),)
        return swap(tokens_y[:half], 2, size), swap(tokens_x[half:], 4, size)

    def gather_farthest(far, *done):
        far = tuple(tie_all(far, *done))
        token_blocks[6], token_blocks[7] = far, tuple(swap(piece, 1, size) for piece in far)


    moe_parts, back_parts, grad_sums = [None] * size, [None] * size, []
    wide = model + rank_all

    direct = down_rows == rank_all
    shapes = [None] * local_experts

    def weights_of(j):
        args = [seq_up[j].reshape(model, -1)]
        shapes[j] = [args[0].shape, (EXPERT_HIDDEN, wide), (rank_all, depth * second_cut * down_rows // rank_all)]
        if direct:
            args.append(seq_down[j])
        else:
            second_j = seq_down[j][:, :, wide : wide + second_cut]
            second_j = second_j.reshape(depth, rank_all, -1).transpose(1, 0, 2).reshape(rank_all, -1)
            args += [seq_down[j][:, :, :wide].reshape(EXPERT_HIDDEN, wide), second_j]
        if j == 0:
            if not direct:
                parts = seq_down[j][:, :, wide + second_cut :].reshape(depth, 4, shared_rows, 4 * LANES)
                args.append(parts.transpose(0, 2, 1, 3).reshape(units, -1)[:, :wide])
            slices = [
                lax.dynamic_slice_in_dim(second_t[edges[n] : edges[n + 1]].reshape(depth, size, -1, rank_all), me, 1, 1)
                for n in (4, 5)
            ]
            args.append(jnp.concatenate([part.reshape(units, rank_all) for part in slices], axis=0))
            shapes[j] += [(units, wide), args[-1].shape]
        return args

    def run_expert(j, args, group, prior, deps, packed=False):
        meta = jnp.stack([me * local_experts + j, me]).astype(jnp.int32)
        prior = ([moe_parts[k] for k in group], [back_parts[k] for k in group]) if prior else None
        moe_out, back_out, grads = expert_call(
            meta,
            args,
            shapes[j],
            [token_blocks[k] for k in group],
            [grad_blocks[k] for k in group],
            prior,
            grad_sums[-1],
            packed,
            experts,
            capacity,
            depth,
            deps,
        )
        for n, k in enumerate(group):
            moe_parts[k], back_parts[k] = moe_out[n], back_out[n]
        grad_sums[-1] = list(grads)

    for j in range(local_experts - 1):
        grad_sums.append([])
        args = weights_of(j)
        previous = ()
        for group in ((0, 1), (2, 3), (4, 5), (6, 7)):
            run_expert(j, args, group, j > 0, previous, group == (6, 7))
            previous = (back_parts[group[0]],)
            if j == 0 and group == (0, 1):
                far = gather_far(tokens_x, tokens_y, *previous)
            if j == 0 and group == (2, 3):
                gather_farthest(far, *previous)
    if local_experts == 1:
        gather_farthest(gather_far(tokens_x, tokens_y))

    def scatter(packed):
        return lax.psum_scatter(packed, "seq", scatter_dimension=0, tiled=True)

    packed_sums = [scatter(grads[0]) for grads in grad_sums]
    grad_sums.append([])
    j, prior, half = local_experts - 1, local_experts > 1, (rows + BACK_ROWS) // 2
    args = weights_of(j)
    run_expert(j, args, (6, 7), prior, (back_parts[6],) if prior else ())
    pair_six = add(back_parts[6], swap(back_parts[7], 1, size))
    run_expert(j, args, (2, 3), prior, (back_parts[6],))
    from_diagonal_x, from_diagonal_y = swap(pair_six[:half], 2, size), swap(pair_six[half:], 4, size)
    pair_two = add(back_parts[2], swap(back_parts[3], 1, size))
    run_expert(j, args, (4, 5), prior, (back_parts[2], pair_six))
    pair_four = add(back_parts[4], swap(tie(back_parts[5], from_diagonal_x, from_diagonal_y, *packed_sums), 1, size))
    to_x = jnp.concatenate([pair_two[:half], add(pair_two[half:], from_diagonal_y)], axis=0)
    to_y = jnp.concatenate([add(pair_four[:half], from_diagonal_x), pair_four[half:]], axis=0)
    run_expert(j, args, (0, 1), prior, (to_x, to_y), True)
    packed_sums.append(scatter(grad_sums[-1][0]))
    from_x, from_y = swap(to_x, 2, size), swap(to_y, 4, size)
    grad_mid, grad_mid_b, glow_out, glow_sgu, low_sdown, grad_attn, shared_units = turn(
        [back_parts[0], swap(back_parts[1], 1, size), from_x, from_y, mid, gates, first_gu]
        + [router_w, gains[1:2], grad_out_b, b_parts[3], out_w, first_o],
        (swap(tie(gates_lo[:16], from_x, from_y), 1, size),),
    )

    half = rows // 2
    far_parts = dict(zip((6, 2, 4, 0), tie_all([moe_parts[k + 1] for k in (6, 2, 4, 0)], from_x, from_y)))
    pair = {k: add(moe_parts[k], swap(far_parts[k], 1, size)) for k in (6, 2, 4, 0)}
    moe_to_x = jnp.concatenate([pair[2][:half], add(pair[2][half:], swap(pair[6][half:], 4, size))], axis=0)
    moe_to_y = jnp.concatenate([add(pair[4][:half], swap(pair[6][:half], 2, size)), pair[4][half:]], axis=0)
    moe_from_x, moe_from_y = swap(moe_to_x, 2, size), swap(moe_to_y, 4, size)
    moe = pair[0].astype(F32) + moe_from_x.astype(F32) + moe_from_y.astype(F32)

    def shared_columns(block):
        block = block[:, :SHARED_HIDDEN].reshape(rank, size, depth, units // depth)
        return block.transpose(0, 2, 1, 3).reshape(rank, SHARED_HIDDEN)

    grad_q, grad_kv = attend_back(
        query, kv_all, grad_attn, lse, query_tag, key_tag, hops, 0, KV_HEADS, (pair[6], pair[2], pair[4])
    )
    moving, early_received = grad_kv[:rows], grad_q
    for h in range(hops):
        if h == 1:
            moving = tie(moving, moe_to_x, moe_to_y)
        received = lax.ppermute(moving, "seq", backward)
        moving = add(grad_kv[(h + 1) * rows : (h + 2) * rows], received)
        if h == 0:
            early_received = received
    grad_normed_q, first_query, second_query = query_back(
        [grad_q, normed, low_q, q_w, first_q, b_parts[0]], (early_received,)
    )
    first_early, second_out, second_down = middle(
        [attn, glow_out, normed2, glow_sgu, grad_mid_b, out_low, grad_out_b, low_sdown],
        (early_received,),
    )
    packed_sums = tie_all(packed_sums, early_received)
    owner_rows = model // depth
    firsts, downs, seconds = [], [], []
    for packed in packed_sums:
        packed = packed[0].astype(F32)
        firsts.append(jnp.stack([packed[:owner_rows], packed[owner_rows : 2 * owner_rows]], axis=1))
        at = 2 * owner_rows + down_rows
        downs.append(packed[2 * owner_rows : at])
        seconds.append(packed[at : at + routed_second_factor.shape[2]].T)
    at += routed_second_factor.shape[2]
    grad_expert_a, grad_expert_a_down, grad_expert_b = jnp.stack(firsts), jnp.stack(downs), jnp.stack(seconds)
    grad_first_down = packed_sums[0][0, at : at + shared_rows].astype(F32)

    hidden_out = (mid + moe + dot_nn(low_sdown, b_parts[6])).astype(BF16)[None]
    second_early = jnp.concatenate(
        [second_out, shared_columns(shared_units[:rank]), shared_columns(shared_units[rank:]), second_down], axis=1
    )
    grad_hidden, first_flat, second_flat = last(
        depth * size,
        [moving, normed, low_kv, kv_w, first_kv, b_parts[1], b_parts[2], block_input[0], gains[0:1], grad_mid]
        + [grad_normed_q, first_query, first_early, second_query, second_early, adapter.astype(F32).reshape(1, 1)],
    )
    flat = jnp.concatenate([first_flat.reshape(depth * size, shard_rows, LANES), second_flat], axis=1)
    flat = lax.all_to_all(flat, ("seq", "dp"), split_axis=0, concat_axis=0, tiled=True)
    grad_first, grad_second = spread(flat, depth, shard_rows)
    grad_first = grad_first.reshape(shard_rows, 6, rank_all)
    grad_second = grad_second[:, :second_columns]
    grad_hidden = grad_hidden[None]
    return (
        hidden_out,
        grad_hidden,
        grad_first,
        grad_first_down,
        grad_second,
        grad_expert_a,
        grad_expert_a_down,
        grad_expert_b,
    )


def solution(mesh):
    in_specs = (
        P("dp", "seq", None),
        P("dp", "seq"),
        P("dp", "seq"),
        P("dp", "seq", None),
        P("dp"),
        P("dp", "seq", None),
        P(None, ("seq", "dp")),
        P(("seq", "dp"), None),
        P(("seq", "dp"), None),
        P(("seq", "dp"), None),
        P(("seq", "dp"), None, None),
        P(("seq", "dp"), None),
        P("dp", "seq", None, None),
        P("dp", "seq", None),
        P(("seq", "dp"), None, None),
        P(("seq", "dp"), None),
        P(None, ("seq", "dp")),
        P("dp", "seq", None, None),
        P("dp", "seq", None),
        P("dp", None, "seq"),
    )
    out_specs = (
        P("dp", "seq", None),
        P("dp", "seq", None),
        P(("seq", "dp"), None, None),
        P(("seq", "dp"), None),
        P(None, ("seq", "dp")),
        P("dp", "seq", None, None),
        P("dp", "seq", None),
        P("dp", None, "seq"),
    )
    return jax.shard_map(
        functools.partial(per_device, mesh.shape["seq"], mesh.shape["dp"]),
        mesh=mesh,
        in_specs=in_specs,
        out_specs=out_specs,
        check_vma=False,
    )
```

```python
import functools
import math

import jax
import jax.numpy as jnp
from jax import lax
from jax.experimental import pallas as pl
from jax.experimental.pallas import tpu as pltpu
from jax.sharding import PartitionSpec as P

HEADS = 12
KV_HEADS = 4
HEAD_DIM = 128
EXPERT_HIDDEN = 512
SHARED_HIDDEN = 1024
ADAPTER_RANK = 16
DOCUMENT_SPAN = 1024

EPSILON = 1e-05
MASKED_SCORE = -1e30
LOG2E = 1.4426950408889634
SCALE = HEAD_DIM ** (-0.5)
LANES = 128
VMEM_LIMIT = 60 * 1024 * 1024

F32 = jnp.float32
BF16 = jnp.bfloat16


def dot_nn(left, right):
    return jnp.dot(left, right, preferred_element_type=F32)


def dot_tn(left, right):
    return lax.dot_general(left, right, (((0,), (0,)), ((), ())), preferred_element_type=F32)


def dot_nt(left, right):
    return lax.dot_general(left, right, (((1,), (1,)), ((), ())), preferred_element_type=F32)


def rms_norm(values, gain):
    return values * lax.rsqrt(jnp.mean(values * values, axis=-1, keepdims=True) + EPSILON) * gain


def cost(microseconds):
    return pl.CostEstimate(flops=int(1153500000 * microseconds), bytes_accessed=1000000, transcendentals=0)


def query_tiles(rows, hops):
    tile = math.gcd(rows, 256)
    spans = []
    for first in range(0, rows, tile):
        oldest = max(0, hops * rows + first - (DOCUMENT_SPAN - 1)) // tile * tile
        spans.append((first, tile, oldest, hops * rows + first + tile - oldest))
    return spans


def fill_bias(spans, shift, query_tag, key_tag, bias):
    for first, tile, oldest, span in spans:
        keys = oldest + lax.broadcasted_iota(jnp.int32, (span, tile), 0)
        queries = shift + first + lax.broadcasted_iota(jnp.int32, (span, tile), 1)
        same = key_tag[oldest : oldest + span, :] == query_tag[:, first : first + tile]
        permit = (keys <= queries) & (same | (keys == queries))
        bias[oldest : oldest + span, first : first + tile] = jnp.where(permit, 0.0, MASKED_SCORE)


def attend_kernel(spans, shift, waits, q_ref, k_ref, v_ref, qt_ref, kt_ref, *rest):
    out_ref, lse_ref, bias = rest[waits:]

    @pl.when(pl.program_id(0) == 0)
    def _():
        fill_bias(spans, shift, qt_ref, kt_ref, bias)

    groups = q_ref.shape[1] // HEAD_DIM
    for first, tile, oldest, span in spans:
        keys = k_ref[oldest : oldest + span, :]
        values = v_ref[oldest : oldest + span, :]
        mask = bias[oldest : oldest + span, first : first + tile]
        for h in range(groups):
            columns = slice(h * HEAD_DIM, (h + 1) * HEAD_DIM)
            scores = dot_nt(keys, q_ref[first : first + tile, columns]) * (SCALE * LOG2E) + mask
            top = jnp.max(scores, axis=0, keepdims=True)
            weights = jnp.exp2(scores - top)
            total = jnp.sum(weights, axis=0, keepdims=True)
            mixed = dot_tn(values, weights.astype(BF16)) / total
            out_ref[first : first + tile, columns] = mixed.T.astype(BF16)
            lse_ref[0, h : h + 1, first : first + tile] = top + jnp.log2(total)


def attend(query, kv_all, query_tag, key_tag, hops, deps=()):
    rows = query.shape[0]
    groups = HEADS // KV_HEADS
    span = kv_all.shape[0]
    spans = query_tiles(rows, hops)
    return pl.pallas_call(
        functools.partial(attend_kernel, spans, hops * rows, len(deps)),
        grid=(KV_HEADS,),
        in_specs=[
            pl.BlockSpec((rows, groups * HEAD_DIM), lambda g: (0, g)),
            pl.BlockSpec((span, HEAD_DIM), lambda g: (0, g)),
            pl.BlockSpec((span, HEAD_DIM), lambda g: (0, KV_HEADS + g)),
            pl.BlockSpec((1, rows), lambda g: (0, 0)),
            pl.BlockSpec((span, 1), lambda g: (0, 0)),
        ]
        + [pl.BlockSpec(memory_space=pl.ANY)] * len(deps),
        out_specs=[
            pl.BlockSpec((rows, groups * HEAD_DIM), lambda g: (0, g)),
            pl.BlockSpec((1, groups, rows), lambda g: (g, 0, 0)),
        ],
        out_shape=[
            jax.ShapeDtypeStruct((rows, HEADS * HEAD_DIM), BF16),
            jax.ShapeDtypeStruct((KV_HEADS, groups, rows), F32),
        ],
        scratch_shapes=[pltpu.VMEM((span, rows), F32)],
        compiler_params=pltpu.CompilerParams(vmem_limit_bytes=VMEM_LIMIT),
        cost_estimate=cost(23.0),
        name="attend",
    )(query, kv_all, kv_all, query_tag, key_tag, *deps)


def attend_back_kernel(
    spans, shift, waits, q_ref, k_ref, v_ref, g_ref, lse_ref, qt_ref, kt_ref, *rest
):
    dq_ref, dkv_ref, bias, dk_acc, dv_acc = rest[waits:]

    @pl.when(pl.program_id(0) == 0)
    def _():
        fill_bias(spans, shift, qt_ref, kt_ref, bias)

    dk_acc[...] = jnp.zeros_like(dk_acc)
    dv_acc[...] = jnp.zeros_like(dv_acc)
    groups = q_ref.shape[1] // HEAD_DIM
    for first, tile, oldest, span in spans:
        keys = k_ref[oldest : oldest + span, :]
        values = v_ref[oldest : oldest + span, :]
        mask = bias[oldest : oldest + span, first : first + tile]
        for h in range(groups):
            columns = slice(h * HEAD_DIM, (h + 1) * HEAD_DIM)
            query = q_ref[first : first + tile, columns]
            grad = g_ref[first : first + tile, columns]
            lse = lse_ref[0, h : h + 1, first : first + tile]
            probs = jnp.exp2(dot_nt(keys, query) * (SCALE * LOG2E) + mask - lse)
            dv_acc[oldest : oldest + span, :] += dot_nn(probs.astype(BF16), grad)
            grad_probs = dot_nt(values, grad)
            delta = jnp.sum(probs * grad_probs, axis=0, keepdims=True)
            grad_scores = (probs * (grad_probs - delta)).astype(BF16)
            dk_acc[oldest : oldest + span, :] += dot_nn(grad_scores, query) * SCALE
            dq_ref[first : first + tile, columns] = (dot_tn(grad_scores, keys) * SCALE).astype(BF16)
    dkv_ref[:, :HEAD_DIM] = dk_acc[...].astype(dkv_ref.dtype)
    dkv_ref[:, HEAD_DIM:] = dv_acc[...].astype(dkv_ref.dtype)


def attend_back(query, kv_all, grad_attn, lse, query_tag, key_tag, hops, head, count, deps=()):
    rows = query.shape[0]
    groups = HEADS // KV_HEADS
    span = kv_all.shape[0]
    spans = query_tiles(rows, hops)
    return pl.pallas_call(
        functools.partial(attend_back_kernel, spans, hops * rows, len(deps)),
        grid=(count,),
        in_specs=[
            pl.BlockSpec((rows, groups * HEAD_DIM), lambda g: (0, head + g)),
            pl.BlockSpec((span, HEAD_DIM), lambda g: (0, head + g)),
            pl.BlockSpec((span, HEAD_DIM), lambda g: (0, KV_HEADS + head + g)),
            pl.BlockSpec((rows, groups * HEAD_DIM), lambda g: (0, head + g)),
            pl.BlockSpec((1, groups, rows), lambda g: (head + g, 0, 0)),
            pl.BlockSpec((1, rows), lambda g: (0, 0)),
            pl.BlockSpec((span, 1), lambda g: (0, 0)),
        ]
        + [pl.BlockSpec(memory_space=pl.ANY)] * len(deps),
        out_specs=[
            pl.BlockSpec((rows, groups * HEAD_DIM), lambda g: (0, g)),
            pl.BlockSpec((span, 2 * HEAD_DIM), lambda g: (0, g)),
        ],
        out_shape=[
            jax.ShapeDtypeStruct((rows, count * groups * HEAD_DIM), BF16),
            jax.ShapeDtypeStruct((span, count * 2 * HEAD_DIM), BF16),
        ],
        scratch_shapes=[
            pltpu.VMEM((span, rows), F32),
            pltpu.VMEM((span, HEAD_DIM), F32),
            pltpu.VMEM((span, HEAD_DIM), F32),
        ],
        compiler_params=pltpu.CompilerParams(vmem_limit_bytes=VMEM_LIMIT),
        cost_estimate=cost(2.0 * count),
        name="attend_back",
    )(query, kv_all, kv_all, grad_attn, lse, query_tag, key_tag, *deps)


BACK_ROWS = 2 * ADAPTER_RANK


def expert_kernel(
    count, splits, experts, capacity, depth, direct, with_prior, with_shared, with_sums, packed, waits, *refs
):
    meta, refs = refs[0], refs[1:]
    weight_count = 5 if with_shared else 3
    given = weight_count - (2 if with_shared else 1) if direct else weight_count
    weight_refs, refs = refs[:given], refs[given:]
    token_refs, grad_refs = [], []
    for split in splits:
        token_refs.append(refs[:split])
        refs = refs[split:]
    for split in splits:
        grad_refs.append(refs[:split])
        refs = refs[split:]
    prior_moe, prior_back = (), ()
    if with_prior:
        prior_moe, refs = refs[:count], refs[count:]
        prior_back, refs = refs[:count], refs[count:]
    grad_count = 4 if with_shared else 3
    sums_in = ()
    if with_sums:
        sums_in, refs = refs[:grad_count], refs[grad_count:]
    refs = refs[waits:]
    moe_refs, refs = refs[:count], refs[count:]
    back_refs, refs = refs[:count], refs[count:]
    out_count = 1 if packed else grad_count
    grad_outs, refs = refs[:out_count], refs[out_count:]
    grad_sums, refs = refs[:grad_count], refs[grad_count:]
    first_grad, down_grad, second_grad = grad_sums[:3]
    weight_bufs, refs = refs[:weight_count], refs[weight_count:]
    if packed:
        pack_buf, refs = refs[0], refs[1:]
    tokens_buf, grad_buf, moe_buf, back_buf, in_sem, out_sem, weight_sem, sum_sem, sum_in_sem = refs

    step = pl.program_id(0)
    steps = count // 2
    slots = min(2, steps)
    slot = lax.rem(step, slots)
    rows, wide = tokens_buf.shape[2:]
    model = wide - LANES
    hidden = EXPERT_HIDDEN
    rank = ADAPTER_RANK
    up_ref, down_ref, second_ref = weight_bufs[:3]

    def weight_copies():
        pairs = list(zip(weight_refs, weight_bufs))
        if direct:
            raw, lines = weight_refs[1], weight_refs[1].shape[1]
            pairs, columns = pairs[:1], second_ref.shape[1] // depth
            for z in range(depth):
                pairs.append((raw.at[z, :, pl.ds(0, wide)], down_ref.at[pl.ds(z * lines, lines)]))
                part = raw.at[z, :, pl.ds(wide, columns)]
                pairs.append((part, second_ref.at[:, pl.ds(z * columns, columns)]))
            if with_shared:
                group, size = 4 * LANES, lines // 4
                for z in range(depth):
                    for q in range(4):
                        width = min(group, wide - q * group)
                        part = raw.at[z, pl.ds(q * size, size), pl.ds(wide + columns, width)]
                        target = weight_bufs[3].at[pl.ds(z * size, size), pl.ds(q * group, width)]
                        pairs.append((part, target))
                pairs.append((weight_refs[2], weight_bufs[4]))
        return [pltpu.make_async_copy(src, dst, weight_sem.at[n]) for n, (src, dst) in enumerate(pairs)]

    def incoming(k, i, kinds):
        copies = []
        to, source = k % slots, 2 * k + i
        for n, (refs_of, buf) in enumerate(((token_refs, tokens_buf), (grad_refs, grad_buf))):
            size = rows // len(refs_of[source])
            for p, piece in enumerate(refs_of[source] if n in kinds else ()):
                part = buf.at[to, i, pl.ds(p * size, size)]
                copies.append(pltpu.make_async_copy(piece, part, in_sem.at[to, i, 2 * n + p]))
        if with_prior and 2 in kinds:
            copies.append(pltpu.make_async_copy(prior_moe[source], moe_buf.at[to, i], in_sem.at[to, i, 4]))
            copies.append(pltpu.make_async_copy(prior_back[source], back_buf.at[to, i], in_sem.at[to, i, 5]))
        return copies

    def outgoing(k, i, kinds=(0, 1)):
        at, source = k % slots, 2 * k + i
        pairs = ((moe_buf, moe_refs), (back_buf, back_refs))
        return [pltpu.make_async_copy(pairs[n][0].at[at, i], pairs[n][1][source], out_sem.at[at, i, n]) for n in kinds]

    def at_step(action, first=0, last=steps):
        for k in range(first, last):
            pl.when(step == k)(functools.partial(action, k))

    def wait_in(i, kind):
        def action(k):
            for copy in incoming(k, i, (kind,)):
                copy.wait()

        at_step(action)

    def start_out(i, n):
        at_step(lambda k: outgoing(k, i, (n,))[0].start())

    def turn(k):
        for i in (0, 1):
            if k >= 1:
                for copy in outgoing(k - 1, i):
                    copy.wait()
            if k + 1 < steps:
                for copy in incoming(k + 1, i, (0, 1, 2)):
                    copy.start()

    def sum_copy(n):
        return pltpu.make_async_copy(pack_buf if packed else grad_sums[n], grad_outs[n], sum_sem.at[n])

    def sum_in(n):
        return pltpu.make_async_copy(sums_in[n], grad_sums[n], sum_in_sem.at[n])

    @pl.when(step == 0)
    def _():
        for i in (0, 1):
            for copy in incoming(0, i, (0,)):
                copy.start()
        for i in (0, 1):
            for copy in incoming(0, i, (1,)):
                copy.start()
        for copy in weight_copies():
            copy.start()
        for i in (0, 1):
            for copy in incoming(0, i, (2,)):
                copy.start()
        for n, total in enumerate(grad_sums):
            if with_sums:
                sum_in(n).start()
            else:
                total[...] = jnp.zeros_like(total)

    expert = meta[0]
    lane = lax.broadcasted_iota(jnp.int32, (1, LANES), 1)
    sub = lax.broadcasted_iota(jnp.int32, (LANES, 1), 0)
    places, picks, gates_of, selects, adapters = [], [], [], [], []
    inputs, grad_rows = [], []
    for i in (0, 1):
        wait_in(i, 0)
        extra_b = tokens_buf[slot, i, :, model:]
        extra = extra_b.astype(F32)
        own = 3 * experts + 3 * rank
        adapter = extra[0:1, own : own + 1]
        select = ((lane // rank).astype(F32) == adapter).astype(F32)
        slot_column = jnp.sum(jnp.where(lane == expert, extra, 0.0), axis=1, keepdims=True)
        slot_row = jnp.sum(jnp.where(sub == expert, extra.T, 0.0), axis=0, keepdims=True)
        place = lax.broadcasted_iota(jnp.int32, (rows, capacity), 1).astype(F32) == slot_column
        pick = lax.broadcasted_iota(jnp.int32, (capacity, rows), 0).astype(F32) == slot_row
        place, pick = place.astype(F32).astype(BF16), pick.astype(F32).astype(BF16)
        picked_extra = dot_nn(pick, extra_b)
        chosen = (lane == experts + expert) | (lane == 2 * experts + expert)
        gates_of.append(jnp.sum(jnp.where(chosen, picked_extra, 0.0), axis=1, keepdims=True))
        inputs.append(dot_nn(pick, tokens_buf[slot, i, :, :model]).astype(BF16))
        picks.append(pick)
        places.append(place)
        adapters.append(adapter)
        selects.append(jnp.broadcast_to(select, (capacity, LANES)))
    for i in (0, 1):
        wait_in(i, 1)
        grad_rows.append(dot_nn(picks[i], grad_buf[slot, i]))
    at_step(turn)
    inputs = jnp.concatenate(inputs, axis=0)
    grad_rows = jnp.concatenate(grad_rows, axis=0)
    gate = jnp.concatenate(gates_of, axis=0)
    select = jnp.concatenate(selects, axis=0)
    select_two = jnp.concatenate([select, select], axis=1)

    @pl.when(step == 0)
    def _():
        for copy in weight_copies():
            copy.wait()

    low = (dot_nn(inputs, up_ref[:, 2 * hidden : 2 * hidden + 2 * LANES]) * select_two).astype(BF16)
    gate_part = dot_nn(inputs, up_ref[:, :hidden]) + dot_nn(low[:, :LANES], second_ref[:, :hidden])
    up_part = dot_nn(inputs, up_ref[:, hidden : 2 * hidden]) + dot_nn(low[:, LANES:], second_ref[:, hidden : 2 * hidden])
    sigmoid = 1.0 / (1.0 + jnp.exp(-gate_part))
    silu = gate_part * sigmoid
    act = (silu * up_part).astype(BF16)
    low_down = (dot_nn(act, down_ref[:, model:]) * select).astype(BF16)
    output = (dot_nn(act, down_ref[:, :model]) + dot_nn(low_down, second_ref[:, 2 * hidden :])).astype(BF16).astype(F32)
    grad_gate = jnp.sum(output * grad_rows, axis=1, keepdims=True)
    weighted = (gate * output).astype(BF16)

    if with_sums:

        @pl.when(step == 0)
        def _():
            for n in range(grad_count):
                sum_in(n).wait()

    grad_y = (gate * grad_rows).astype(BF16)
    glow_down = (dot_nt(grad_y, second_ref[:, 2 * hidden :]) * select).astype(BF16)
    second_grad[:, 2 * hidden :] += dot_tn(low_down, grad_y)
    down_grad[...] += dot_tn(act, glow_down)
    grad_act = dot_nt(grad_y, down_ref[:, :model]) + dot_nt(glow_down, down_ref[:, model:])
    grad_up = (grad_act * silu).astype(BF16)
    grad_gp = (grad_act * up_part * (sigmoid * (1.0 + gate_part * (1.0 - sigmoid)))).astype(BF16)
    glow = jnp.concatenate(
        [
            dot_nt(grad_gp, second_ref[:, :hidden]) * select,
            dot_nt(grad_up, second_ref[:, hidden : 2 * hidden]) * select,
        ],
        axis=1,
    ).astype(BF16)
    second_grad[:, :hidden] += dot_tn(low[:, :LANES], grad_gp)
    second_grad[:, hidden : 2 * hidden] += dot_tn(low[:, LANES:], grad_up)
    first_grad[...] += dot_tn(inputs, glow)
    grad_in = (
        dot_nt(grad_gp, up_ref[:, :hidden])
        + dot_nt(grad_up, up_ref[:, hidden : 2 * hidden])
        + dot_nt(glow, up_ref[:, 2 * hidden : 2 * hidden + 2 * LANES])
    ).astype(BF16)
    gate_hi = grad_gate.astype(BF16).astype(F32)
    gate_lo = grad_gate - gate_hi
    extra_out = (
        jnp.where(lane == expert, gate_hi, 0.0) + jnp.where(lane == experts + expert, gate_lo, 0.0)
    ).astype(BF16)

    @pl.when(step == steps - 1)
    def _():
        if not packed:
            for n in range(3):
                sum_copy(n).start()
            return
        second_t = second_grad[...].T
        parts = [first_grad[:, :LANES], first_grad[:, LANES:], down_grad[...], second_t]
        at = 0
        for part in parts:
            size = part.shape[0] // depth
            for z in range(depth):
                pack_buf[z, at : at + size, :] = part[z * size : (z + 1) * size].astype(BF16)
            at += size

    for i in (0, 1):
        mine = slice(i * capacity, (i + 1) * capacity)
        wait_in(i, 2)
        moe = dot_nn(places[i], weighted[mine])
        back = dot_nn(places[i], grad_in[mine])
        back_extra = dot_nn(places[i], extra_out[mine])
        if with_prior:
            moe = moe + moe_buf[slot, i].astype(F32)
            back = back + back_buf[slot, i, :rows, :model].astype(F32)
            back_extra = back_extra + back_buf[slot, i, :rows, model:].astype(F32)
        if not with_prior:
            back_buf[slot, i, rows:, :] = jnp.zeros((BACK_ROWS, wide), BF16)
        if with_shared:
            sdown_ref, sb_ref = weight_bufs[3:]
            units = sdown_ref.shape[0]
            first_gate, first_up, first_down = 3 * experts, 3 * experts + rank, 3 * experts + 2 * rank
            tokens = tokens_buf[slot, i, :, :model]
            extra_b = tokens_buf[slot, i, :, model:]
            grads = grad_buf[slot, i]
            offset = (lane - sub).astype(F32) - adapters[i] * float(rank)

            def spread(base):
                inside = (sub >= base) & (sub < base + rank)
                return (inside & (offset == float(-base))).astype(F32).astype(BF16)

            to_gate = dot_nt(spread(first_gate), sb_ref[:units]).astype(BF16)
            to_up = dot_nt(spread(first_up), sb_ref[units:]).astype(BF16)
            to_down = dot_nt(spread(first_down), sdown_ref[:, model:]).astype(BF16)
            shared_up = up_ref[:, 2 * hidden + 2 * LANES :]
            gate_up = dot_nn(tokens, shared_up)
            s_gate = gate_up[:, :units] + dot_nn(extra_b, to_gate)
            s_up = gate_up[:, units:] + dot_nn(extra_b, to_up)
            s_sig = 1.0 / (1.0 + jnp.exp(-s_gate))
            s_silu = s_gate * s_sig
            s_act = (s_silu * s_up).astype(BF16)
            moe = moe + dot_nn(s_act, sdown_ref[:, :model])
            s_grad = dot_nt(grads, sdown_ref[:, :model]) + dot_nn(extra_b, to_down)
            grad_sums[3][...] += dot_tn(s_act, dot_nn(extra_b, spread(first_down)).astype(BF16))
            s_gu = (s_grad * s_silu).astype(BF16)
            s_gg = (s_grad * s_up * (s_sig * (1.0 + s_gate * (1.0 - s_sig)))).astype(BF16)
            back_extra = back_extra + dot_nt(s_act, to_down) + dot_nt(s_gg, to_gate) + dot_nt(s_gu, to_up)
            back = back + dot_nt(jnp.concatenate([s_gg, s_gu], axis=1), shared_up)
            columns = pl.ds(pl.multiple_of(meta[1] * units, units), units)
            grad_bg = dot_tn(extra_b, s_gg)[first_gate : first_gate + rank]
            grad_bu = dot_tn(extra_b, s_gu)[first_up : first_up + rank]
            back_buf[slot, i, rows : rows + rank, columns] = grad_bg.astype(BF16)
            back_buf[slot, i, rows + rank :, columns] = grad_bu.astype(BF16)
        moe_buf[slot, i] = moe.astype(BF16)
        start_out(i, 0)
        back_buf[slot, i, :rows, :model] = back.astype(BF16)
        back_buf[slot, i, :rows, model:] = back_extra.astype(BF16)
        start_out(i, 1)

    @pl.when(step == steps - 1)
    def _():
        if packed and with_shared:
            size = grad_sums[3].shape[0] // depth
            for z in range(depth):
                part = grad_sums[3][z * size : (z + 1) * size, :]
                if size % 16:
                    part = jnp.concatenate([part, jnp.zeros((16 - size % 16, LANES), F32)], axis=0)
                pack_buf[z, pack_buf.shape[1] - part.shape[0] :, :] = part.astype(BF16)
        for n in range(0 if packed else 3, out_count):
            sum_copy(n).start()
        for i in (0, 1):
            for copy in outgoing(steps - 1, i):
                copy.wait()
        for n in range(out_count):
            sum_copy(n).wait()


def expert_call(meta, weights, shapes, tokens, grads, prior, sums, packed, experts, capacity, depth, deps=()):
    count = len(tokens)
    with_shared = len(shapes) > 3
    direct = len(weights) < len(shapes)
    splits = [len(pieces) for pieces in tokens]
    rows, model = sum(piece.shape[0] for piece in grads[0]), grads[0][0].shape[1]
    wide = model + LANES
    slots = min(2, count // 2)
    anywhere = pl.BlockSpec(memory_space=pl.ANY)
    prior = [] if prior is None else list(prior[0]) + list(prior[1])
    flat = [piece for pieces in tokens for piece in pieces] + [piece for pieces in grads for piece in pieces]
    grad_shapes = [
        jax.ShapeDtypeStruct((model, 2 * LANES), F32),
        jax.ShapeDtypeStruct((EXPERT_HIDDEN, LANES), F32),
        jax.ShapeDtypeStruct(shapes[2], F32),
    ]
    if with_shared:
        grad_shapes.append(jax.ShapeDtypeStruct((shapes[3][0], LANES), F32))
    out_shapes = grad_shapes
    if packed:
        lines = sum(s.shape[0] for s in grad_shapes[:2]) + model + shapes[2][1]
        lines = lines // depth
        if with_shared:
            lines += -(-shapes[3][0] // depth // 16) * 16
        out_shapes = [jax.ShapeDtypeStruct((depth, lines, LANES), BF16)]
    back_rows = rows + BACK_ROWS
    outs = pl.pallas_call(
        functools.partial(
            expert_kernel,
            *(count, splits, experts, capacity, depth, direct, bool(prior), with_shared, bool(sums), packed, len(deps)),
        ),
        grid=(count // 2,),
        in_specs=[pl.BlockSpec(memory_space=pltpu.SMEM)]
        + [anywhere] * (len(weights) + len(flat) + len(prior) + len(sums) + len(deps)),
        out_specs=[anywhere] * (2 * count + len(out_shapes)),
        out_shape=[jax.ShapeDtypeStruct((rows, model), BF16)] * count
        + [jax.ShapeDtypeStruct((back_rows, wide), BF16)] * count
        + out_shapes,
        scratch_shapes=[pltpu.VMEM(s.shape, F32) for s in grad_shapes]
        + [pltpu.VMEM(shape, BF16) for shape in shapes]
        + ([pltpu.VMEM(out_shapes[0].shape, BF16)] if packed else [])
        + [
            pltpu.VMEM((slots, 2, rows, wide), BF16),
            pltpu.VMEM((slots, 2, rows, model), BF16),
            pltpu.VMEM((slots, 2, rows, model), BF16),
            pltpu.VMEM((slots, 2, back_rows, wide), BF16),
            pltpu.SemaphoreType.DMA((slots, 2, 6)),
            pltpu.SemaphoreType.DMA((slots, 2, 2)),
            pltpu.SemaphoreType.DMA((len(shapes) + 6 * depth,)),
            pltpu.SemaphoreType.DMA((len(grad_shapes),)),
            pltpu.SemaphoreType.DMA((len(grad_shapes),)),
        ],
        compiler_params=pltpu.CompilerParams(vmem_limit_bytes=VMEM_LIMIT),
        cost_estimate=cost(12.0 * count),
        name="expert",
    )(meta, *weights, *flat, *prior, *sums, *deps)
    return outs[:count], outs[count : 2 * count], outs[2 * count :]


def swap(array, bit, size):
    return lax.ppermute(array, "dp", [(i, i ^ bit) for i in range(size)])


def plane_gather(array, size):
    half = array.shape[0] // 2
    x, y = swap(array, 2, size), swap(array, 4, size)
    across = {0: (array,), 2: (x,), 4: (y,), 6: (swap(y[:half], 2, size), swap(x[half:], 4, size))}
    blocks = [None] * size
    for k in (0, 2, 4, 6):
        blocks[k] = across[k]
        blocks[k + 1] = tuple(swap(piece, 1, size) for piece in across[k])
    return blocks


def add(*terms):
    total = terms[0].astype(F32)
    for term in terms[1:]:
        total = total + term.astype(F32)
    return total.astype(BF16)


def tie_kernel(*refs):
    del refs


def tie_all(arrays, *others):
    anywhere = pl.BlockSpec(memory_space=pl.ANY)
    return pl.pallas_call(
        tie_kernel,
        in_specs=[anywhere] * (len(arrays) + len(others)),
        out_specs=[anywhere] * len(arrays),
        out_shape=[jax.ShapeDtypeStruct(array.shape, array.dtype) for array in arrays],
        input_output_aliases={n: n for n in range(len(arrays))},
        name="tie",
    )(*arrays, *others)


def tie(array, *others):
    return tie_all([array], *others)[0]


def assemble_kernel(splits, widths, waits, me_ref, *refs):
    pieces, outs = refs[: sum(splits)], refs[sum(splits) + waits : -3]
    whole, in_sem, out_sem = refs[-3:]
    copies, at = [], 0
    for k, split in enumerate(splits):
        start = 0
        for piece in pieces[at : at + split]:
            target = whole.at[pl.ds(start, piece.shape[0]), me_ref[0] ^ k]
            copies.append(pltpu.make_async_copy(piece, target, in_sem.at[len(copies)]))
            start += piece.shape[0]
        at += split
    for copy in copies:
        copy.start()
    for copy in copies:
        copy.wait()
    copies, column = [], 0
    for out, (count, width) in zip(outs, widths):
        for n in range(count):
            source = whole.at[:, :, :, pl.ds(column, width)]
            copies.append(pltpu.make_async_copy(source, out.at[:, :, n], out_sem.at[len(copies)]))
            column += width
    for copy in copies:
        copy.start()
    for copy in copies:
        copy.wait()


def assemble(blocks, widths, me, deps=()):
    depth, rows, _ = blocks[0][0].shape
    size = len(blocks)
    splits = [len(pieces) for pieces in blocks]
    flat = [piece for pieces in blocks for piece in pieces]
    outs = pl.pallas_call(
        functools.partial(assemble_kernel, splits, widths, len(deps)),
        in_specs=[pl.BlockSpec(memory_space=pltpu.SMEM)] + [pl.BlockSpec(memory_space=pl.ANY)] * (len(flat) + len(deps)),
        out_specs=[pl.BlockSpec(memory_space=pl.ANY)] * len(widths),
        out_shape=[jax.ShapeDtypeStruct((depth, size, count, rows, width), BF16) for count, width in widths],
        scratch_shapes=[
            pltpu.VMEM((depth, size, rows, sum(count * width for count, width in widths)), BF16),
            pltpu.SemaphoreType.DMA((len(flat),)),
            pltpu.SemaphoreType.DMA((sum(count for count, _ in widths),)),
        ],
        compiler_params=pltpu.CompilerParams(vmem_limit_bytes=VMEM_LIMIT),
        name="assemble",
    )(me.astype(jnp.int32).reshape(1), *flat, *deps)
    return [out.reshape(-1, out.shape[-1]) for out in outs]


def turn_kernel(
    waits, own, other, from_x, from_y, hidden, gates, first_gu, router, gain, grad_out, second_o, out_w, first_o, *rest
):
    grad_mid_out, grad_mid_b_out, glow_out, glow_sgu, low_sdown, grad_attn, units_out = rest[waits:]
    rows, model = hidden.shape
    experts = gates.shape[1]
    rank = ADAPTER_RANK
    total = own[...].astype(F32) + other[...].astype(F32) + from_x[...].astype(F32) + from_y[...].astype(F32)
    units_out[...] = total[rows:, :]
    tail = total[:rows, model:]
    grad_gates = tail[:, :experts] + tail[:, experts : 2 * experts]
    glow = tail[:, 3 * experts : 3 * experts + 2 * rank].astype(BF16)
    glow_sgu[...] = glow
    low_sdown[...] = tail[:, 3 * experts + 2 * rank : 3 * experts + 3 * rank].astype(BF16)
    gate = gates[...]
    grad_logits = gate * (grad_gates - jnp.sum(gate * grad_gates, axis=-1, keepdims=True))
    logits_hi = grad_logits.astype(BF16)
    left = grad_logits - logits_hi.astype(F32)
    logits_mid = left.astype(BF16)
    logits_lo = (left - logits_mid.astype(F32)).astype(BF16)
    grad_normed = total[:rows, :model] + dot_nt(glow, first_gu[...])
    for part in (logits_hi, logits_mid, logits_lo):
        grad_normed = grad_normed + dot_nt(part, router[...])
    values = hidden[...]
    scale = lax.rsqrt(jnp.mean(values * values, axis=-1, keepdims=True) + EPSILON)
    scaled = grad_normed * gain[...]
    mean = jnp.mean(values * scaled, axis=-1, keepdims=True)
    grad_mid = grad_out[...].astype(F32) + scale * scaled - values * (scale * scale * scale * mean)
    grad_mid_out[...] = grad_mid
    grad_mid_b = grad_mid.astype(BF16)
    grad_mid_b_out[...] = grad_mid_b
    glow = dot_nt(grad_mid_b, second_o[...]).astype(BF16)
    glow_out[...] = glow
    grad_attn[...] = (dot_nt(grad_mid_b, out_w[...]) + dot_nt(glow, first_o[...])).astype(BF16)


def turn(args, deps):
    rows, model = args[4].shape
    rank = ADAPTER_RANK
    vmem = pl.BlockSpec(memory_space=pltpu.VMEM)
    shapes = [
        ((rows, model), F32),
        ((rows, model), BF16),
        ((rows, rank), BF16),
        ((rows, 2 * rank), BF16),
        ((rows, rank), BF16),
        ((rows, HEADS * HEAD_DIM), BF16),
        ((BACK_ROWS, args[0].shape[1]), F32),
    ]
    return pl.pallas_call(
        functools.partial(turn_kernel, len(deps)),
        in_specs=[vmem] * len(args) + [pl.BlockSpec(memory_space=pl.ANY)] * len(deps),
        out_specs=[vmem] * len(shapes),
        out_shape=[jax.ShapeDtypeStruct(shape, dtype) for shape, dtype in shapes],
        compiler_params=pltpu.CompilerParams(vmem_limit_bytes=VMEM_LIMIT),
        cost_estimate=cost(4.0),
        name="turn",
    )(*args, *deps)


def query_back_kernel(waits, grad_q, normed, low_q, q_w, first_q, second_q, *rest):
    grad_normed, first_query, second_query = rest[waits:]
    glow_q = dot_nt(grad_q[...], second_q[...]).astype(BF16)
    grad_normed[...] = dot_nt(grad_q[...], q_w[...]) + dot_nt(glow_q, first_q[...])
    first_query[...] = dot_tn(normed[...], glow_q)
    second_query[...] = dot_tn(low_q[...], grad_q[...])


def query_back(args, deps):
    rows, model = args[1].shape
    vmem = pl.BlockSpec(memory_space=pltpu.VMEM)
    shapes = [(rows, model), (model, ADAPTER_RANK), (ADAPTER_RANK, HEADS * HEAD_DIM)]
    return pl.pallas_call(
        functools.partial(query_back_kernel, len(deps)),
        in_specs=[vmem] * len(args) + [pl.BlockSpec(memory_space=pl.ANY)] * len(deps),
        out_specs=[vmem] * len(shapes),
        out_shape=[jax.ShapeDtypeStruct(shape, F32) for shape in shapes],
        compiler_params=pltpu.CompilerParams(vmem_limit_bytes=VMEM_LIMIT),
        cost_estimate=cost(0.1),
        name="query_back",
    )(*args, *deps)


def middle_kernel(waits, attn, glow_out, normed2, glow_sgu, grad_mid, out_low, grad_out, low_sdown, *rest):
    first_early, second_out, second_down = rest[waits:]
    rank = ADAPTER_RANK
    first_early[:, :rank] = dot_tn(attn[...], glow_out[...])
    first_early[:, rank:] = dot_tn(normed2[...], glow_sgu[...])
    second_out[...] = dot_tn(out_low[...], grad_mid[...])
    second_down[...] = dot_tn(low_sdown[...], grad_out[...])


def middle(args, deps):
    model = args[0].shape[1]
    rank = ADAPTER_RANK
    vmem = pl.BlockSpec(memory_space=pltpu.VMEM)
    shapes = [(model, 3 * rank), (rank, model), (rank, model)]
    return pl.pallas_call(
        functools.partial(middle_kernel, len(deps)),
        in_specs=[vmem] * len(args) + [pl.BlockSpec(memory_space=pl.ANY)] * len(deps),
        out_specs=[vmem] * len(shapes),
        out_shape=[jax.ShapeDtypeStruct(shape, F32) for shape in shapes],
        compiler_params=pltpu.CompilerParams(vmem_limit_bytes=VMEM_LIMIT),
        cost_estimate=cost(0.1),
        name="middle",
    )(*args, *deps)


def last_kernel(
    owners, grad_kv, normed, low_kv, kv_w, first_kv, second_k, second_v, hidden, gain, grad_mid, grad_normed_q,
    first_query, first_early, second_query, second_early, adapter, grad_hidden, first_out, second_out
):
    rank = ADAPTER_RANK
    heads = range(grad_kv.shape[1] // (2 * HEAD_DIM))
    grad_k = jnp.concatenate([grad_kv[:, 2 * n * HEAD_DIM : (2 * n + 1) * HEAD_DIM] for n in heads], axis=1)
    grad_v = jnp.concatenate([grad_kv[:, (2 * n + 1) * HEAD_DIM : (2 * n + 2) * HEAD_DIM] for n in heads], axis=1)
    width = grad_k.shape[1]
    glow_k = dot_nt(grad_k, second_k[...]).astype(BF16)
    glow_v = dot_nt(grad_v, second_v[...]).astype(BF16)
    grad_normed = grad_normed_q[...] + dot_nt(grad_k, kv_w[:, :width]) + dot_nt(grad_v, kv_w[:, width:])
    grad_normed = grad_normed + dot_nt(glow_k, first_kv[:, :rank]) + dot_nt(glow_v, first_kv[:, rank:])
    values = hidden[...].astype(F32)
    scale = lax.rsqrt(jnp.mean(values * values, axis=-1, keepdims=True) + EPSILON)
    scaled = grad_normed * gain[...]
    mean = jnp.mean(values * scaled, axis=-1, keepdims=True)
    grad_hidden[...] = grad_mid[...] + scale * scaled - values * (scale * scale * scale * mean)
    firsts = [first_query[...], dot_tn(normed[...], glow_k), dot_tn(normed[...], glow_v), first_early[...]]
    tags = jnp.broadcast_to(adapter[...], (first_query.shape[0], LANES - 6 * rank))
    first_out[...] = jnp.concatenate(firsts + [tags], axis=1).astype(BF16)
    seconds = [second_query[...], dot_tn(low_kv[:, :rank], grad_k), dot_tn(low_kv[:, rank:], grad_v), second_early[...]]
    seconds = jnp.concatenate(seconds, axis=1)
    columns = seconds.shape[1] // owners
    padding = jnp.zeros((rank, second_out.shape[1] // rank * LANES - columns), F32)
    for n in range(owners):
        piece = jnp.concatenate([seconds[:, n * columns : (n + 1) * columns], padding], axis=1).astype(BF16)
        for c in range(piece.shape[1] // LANES):
            second_out[n, c * rank : (c + 1) * rank, :] = piece[:, c * LANES : (c + 1) * LANES]


def last(owners, args):
    rows, model = args[7].shape
    columns = (args[13].shape[1] + 2 * KV_HEADS * HEAD_DIM + args[14].shape[1]) // owners
    vmem = pl.BlockSpec(memory_space=pltpu.VMEM)
    return pl.pallas_call(
        functools.partial(last_kernel, owners),
        in_specs=[vmem] * len(args),
        out_specs=[vmem] * 3,
        out_shape=[
            jax.ShapeDtypeStruct((rows, model), F32),
            jax.ShapeDtypeStruct((model, LANES), BF16),
            jax.ShapeDtypeStruct((owners, -(-columns // LANES) * ADAPTER_RANK, LANES), BF16),
        ],
        compiler_params=pltpu.CompilerParams(vmem_limit_bytes=VMEM_LIMIT),
        cost_estimate=cost(2.0),
        name="last",
    )(*args)


def spread_kernel(depth, lines, flat, first_out, second_out):
    rank = ADAPTER_RANK
    size = flat.shape[0] // depth
    row = lax.broadcasted_iota(jnp.int32, (LANES, 1), 0).astype(F32)
    column = lax.broadcasted_iota(jnp.int32, (1, first_out.shape[1]), 1)
    inside = column % LANES
    target = (column // LANES * rank + inside).astype(F32)
    owner = (inside // rank).astype(F32)
    short = lax.broadcasted_iota(jnp.int32, (1, rank), 1).astype(F32)
    chunks = (flat.shape[1] - lines) // rank
    first, second = None, [None] * chunks
    for d in range(size):
        adapter = flat[d, 0:1, 6 * rank : 6 * rank + 1].astype(F32)
        total = flat[d].astype(F32)
        for z in range(1, depth):
            total = total + flat[z * size + d].astype(F32)
        total = total.astype(BF16)
        place = ((target - adapter * float(rank) == row) & (owner == adapter)).astype(F32).astype(BF16)
        lift = (row - adapter * float(rank) == short).astype(F32).astype(BF16)
        part = dot_nn(total[:lines], place)
        first = part if first is None else first + part
        for c in range(chunks):
            part = dot_nn(lift, total[lines + c * rank : lines + (c + 1) * rank])
            second[c] = part if second[c] is None else second[c] + part
    first_out[...] = first
    for c in range(chunks):
        second_out[:, c * LANES : (c + 1) * LANES] = second[c]


def spread(flat, depth, lines):
    vmem = pl.BlockSpec(memory_space=pltpu.VMEM)
    chunks = (flat.shape[1] - lines) // ADAPTER_RANK
    return pl.pallas_call(
        functools.partial(spread_kernel, depth, lines),
        in_specs=[vmem],
        out_specs=[vmem] * 2,
        out_shape=[jax.ShapeDtypeStruct((lines, 6 * LANES), F32), jax.ShapeDtypeStruct((LANES, chunks * LANES), F32)],
        compiler_params=pltpu.CompilerParams(vmem_limit_bytes=VMEM_LIMIT),
        cost_estimate=cost(2.0),
        name="spread",
    )(flat)


def per_device(
    depth,
    size,
    block_input,
    document_number,
    key_present,
    routes,
    sequence_adapter,
    output_gradient,
    norm_scale_pair,
    query_key_value_weight,
    attention_output_weight,
    router_weight,
    shared_gate_up_weight,
    shared_down_weight,
    routed_gate_up_weight,
    routed_down_weight,
    dense_first_factor,
    shared_down_first_factor,
    dense_second_factor,
    routed_first_factor,
    routed_down_first_factor,
    routed_second_factor,
):
    _, rows, model = block_input.shape
    topk = routes.shape[2]
    me = lax.axis_index("dp")
    experts = router_weight.shape[1]
    local_experts = routed_gate_up_weight.shape[0]
    shard_rows = query_key_value_weight.shape[0]
    shared_rows = shared_down_weight.shape[0]
    rank_all = dense_second_factor.shape[0]
    second_columns = dense_second_factor.shape[1]
    capacity = 4 * topk * rows // (3 * experts)
    query_width = HEADS * HEAD_DIM
    kv_width = KV_HEADS * HEAD_DIM
    hops = min(depth - 1, -(-(DOCUMENT_SPAN - 1) // rows))
    rank = ADAPTER_RANK
    units = SHARED_HIDDEN // size
    adapter = sequence_adapter[0]
    forward = [(i, i + 1) for i in range(depth - 1)]
    backward = [(i + 1, i) for i in range(depth - 1)]

    def over_seq(shard):
        return lax.all_gather(shard, "seq", axis=0)

    first_shard = dense_first_factor.reshape(shard_rows, 6 * rank_all)
    second_width = second_columns * rank_all // shard_rows
    groups = second_width // rank_all
    pack_kv = jnp.concatenate(
        [
            query_key_value_weight[:, query_width:],
            first_shard[:, rank_all : 3 * rank_all],
            dense_second_factor.T.reshape(groups, shard_rows, rank_all).transpose(1, 0, 2).reshape(shard_rows, -1),
            jnp.pad(
                jnp.concatenate([router_weight, norm_scale_pair.T], axis=1), ((0, 0), (0, LANES - experts - 2))
            ),
        ],
        axis=1,
    )
    pack_q = jnp.concatenate(
        [
            query_key_value_weight[:, :query_width],
            first_shard[:, :rank_all],
            first_shard[:, 3 * rank_all :],
            attention_output_weight,
        ],
        axis=1,
    )
    seq_kv = over_seq(pack_kv)
    seq_q = over_seq(tie(pack_q, seq_kv))

    flags = jnp.sum((routes[0][..., None] == jnp.arange(experts, dtype=jnp.int32)).astype(F32), axis=1)
    before = (jnp.arange(rows)[:, None] > jnp.arange(rows)[None, :]).astype(BF16)
    slots = jnp.where(flags > 0, dot_nn(before, flags.astype(BF16)), -1.0).astype(BF16)

    def own_columns(matrix):
        return lax.dynamic_slice_in_dim(matrix, adapter * rank, rank, 1)

    def own_factors(matrix):
        count = matrix.shape[1] // rank_all
        return jnp.concatenate([own_columns(matrix[:, n * rank_all : (n + 1) * rank_all]) for n in range(count)], axis=1)

    grad_out_b = output_gradient[0]
    grads_x, grads_y = swap(grad_out_b, 2, size), swap(grad_out_b, 4, size)
    gate_up = shared_gate_up_weight.reshape(shard_rows, 2, depth, size, units // depth)
    gate_up = gate_up.transpose(3, 0, 1, 2, 4).reshape(size, shard_rows, 2 * units)
    gate_up = lax.all_to_all(gate_up, "dp", split_axis=0, concat_axis=0, tiled=True)
    kv_gathered = plane_gather(tie(seq_kv, grads_x, grads_y, gate_up), size)
    grads_x, grads_y = tie_all([grads_x, grads_y], *kv_gathered[6])
    far_grads = (swap(grads_y[: rows // 2], 2, size), swap(grads_x[rows // 2 :], 4, size))
    grad_blocks = [(grad_out_b,), None, (grads_x,), None, (grads_y,), None, far_grads, None]
    kv_w, kv_first, second_t, small = assemble(
        kv_gathered, ((1, 2 * kv_width), (1, 2 * rank_all), (groups, rank_all), (1, LANES)), me
    )
    router_w = small[:, :experts]
    gains = small[:, experts : experts + 2].astype(F32).T
    second = own_columns(second_t).T
    first_kv = own_factors(kv_first)
    widths = [query_width, kv_width, kv_width, model, SHARED_HIDDEN, SHARED_HIDDEN, model]
    edges = [sum(widths[:n]) for n in range(len(widths) + 1)]
    b_parts = [second[:, edges[n] : edges[n + 1]] for n in range(len(widths))]

    down_rows = routed_down_weight.shape[1]
    second_cut = rank_all * routed_second_factor.shape[2] // down_rows
    up_shards, down_shards = [], []
    for j in range(local_experts):
        up_parts = [
            routed_gate_up_weight[j].reshape(-1, 2 * EXPERT_HIDDEN),
            routed_first_factor[j].reshape(-1, 2 * rank_all),
        ]
        down_parts = [
            routed_down_weight[j],
            routed_down_first_factor[j],
            routed_second_factor[j].reshape(down_rows, -1),
        ]
        if j == 0:
            up_parts.append(gate_up.reshape(size * shard_rows, 2 * units))
            shared_down = jnp.concatenate([shared_down_weight, shared_down_first_factor], axis=1)
            shared_down = jnp.pad(shared_down, ((0, 0), (0, 16 * LANES - shared_down.shape[1])))
            shared_down = shared_down.reshape(shared_rows, 4, 4 * LANES).transpose(1, 0, 2)
            down_parts.append(shared_down.reshape(down_rows, -1))
        up_shards.append(jnp.concatenate(up_parts, axis=1))
        down_shards.append(jnp.concatenate(down_parts, axis=1))
    first_down = over_seq(tie(down_shards[0], seq_kv))

    x_flat = block_input[0].astype(F32)
    normed = rms_norm(x_flat, gains[0]).astype(BF16)
    select = (jnp.arange(rank_all, dtype=jnp.int32) // rank == adapter).astype(F32)[None, :]

    def masked_low(inputs, factors):
        low = dot_nn(inputs, factors)
        return [
            (low[:, at : at + rank_all] * select).astype(BF16) for at in range(0, factors.shape[1], rank_all)
        ]

    low_k, low_v = masked_low(normed, kv_first)
    low_kv = own_factors(jnp.concatenate([low_k, low_v], axis=1))
    kv_extra = jnp.concatenate(
        [dot_nt(low_k, second_t[edges[1] : edges[2]]), dot_nt(low_v, second_t[edges[2] : edges[3]])], axis=1
    )
    present_tag = jnp.where(key_present == 1, document_number + 1, 0).astype(BF16)
    tag_rows = jnp.broadcast_to(jnp.pad(present_tag, ((0, 0), (0, 2 * kv_width - rows))), (16, 2 * kv_width))
    kv_blocks = [jnp.concatenate([(dot_nn(normed, kv_w) + kv_extra).astype(BF16), tag_rows], axis=0)]
    q_blocks = plane_gather(tie(seq_q, *far_grads), size)
    for k in range(1, size, 2):
        grad_blocks[k] = tuple(swap(piece, 1, size) for piece in grad_blocks[k - 1])
    for h in range(hops):
        block = kv_blocks[-1] if h == 0 else tie(kv_blocks[-1], q_blocks[2][0], q_blocks[4][0], first_down)
        kv_blocks.append(lax.ppermute(block, "seq", forward))
        kv_blocks[h] = block
    kv_all = jnp.concatenate([block[:rows] for block in kv_blocks[::-1]], axis=0)
    key_tag = jnp.concatenate([block[rows, :rows] for block in kv_blocks[::-1]]).astype(F32).reshape(-1, 1)
    query_tag = (document_number + 1).astype(F32)

    seq_up, seq_down = [over_seq(tie(up_shards[0], kv_blocks[min(1, hops)]))], [first_down]
    for j in range(1, local_experts):
        seq_up.append(over_seq(tie(up_shards[j], seq_down[j - 1])))
        seq_down.append(over_seq(tie(down_shards[j], seq_up[j - 1])))

    q_w, q_first, out_w = assemble(q_blocks, ((1, query_width), (1, 4 * rank_all), (1, model)), me)
    (low_q,) = masked_low(normed, q_first[:, :rank_all])
    first_out = q_first[:, rank_all : 2 * rank_all]
    q_first = own_factors(q_first)
    first_q, first_o, first_gu = q_first[:, :rank], q_first[:, rank : 2 * rank], q_first[:, 2 * rank :]
    query = (dot_nn(normed, q_w) + dot_nt(low_q, second_t[edges[0] : edges[1]])).astype(BF16)
    low_q = own_columns(low_q)
    glow_sdown = dot_nt(grad_out_b, b_parts[6]).astype(BF16)
    attn, lse = attend(query, kv_all, query_tag, key_tag, hops, (*grad_blocks[3], *grad_blocks[5], *grad_blocks[7]))
    (out_low,) = masked_low(attn, first_out)
    mid = x_flat + dot_nn(attn, out_w) + dot_nt(out_low, second_t[edges[3] : edges[4]])
    out_low = own_columns(out_low)
    normed2 = rms_norm(mid, gains[1]).astype(BF16)

    logits = dot_nn(normed2, router_w)
    top = jnp.max(jnp.where(flags > 0, logits, -jnp.inf), axis=-1, keepdims=True)
    weights = jnp.where(flags > 0, jnp.exp(logits - top), 0.0)
    gates = weights / jnp.sum(weights, axis=-1, keepdims=True)
    gates_hi = gates.astype(BF16)
    gates_lo = (gates - gates_hi.astype(F32)).astype(BF16)
    shared_low = dot_nn(normed2, first_gu).astype(BF16)
    own_adapter = jnp.full((rows, LANES - 3 * experts - 3 * rank), adapter.astype(F32)).astype(BF16)
    payload = jnp.concatenate([normed2, slots, gates_hi, gates_lo, shared_low, glow_sdown, own_adapter], axis=1)
    token_blocks = [None] * size
    token_blocks[0], token_blocks[1] = (payload,), (swap(payload, 1, size),)
    tokens_x, tokens_y = swap(payload, 2, size), swap(payload, 4, size)

    def gather_far(tokens_x, tokens_y, *done):
        tokens_x, tokens_y = tie_all([tokens_x, tokens_y], *done)
        half = rows // 2
        token_blocks[2], token_blocks[3] = (tokens_x,), (swap(tokens_x, 1, size),)
        token_blocks[4], token_blocks[5] = (tokens_y,), (swap(tokens_y, 1, size),)
        return swap(tokens_y[:half], 2, size), swap(tokens_x[half:], 4, size)

    def gather_farthest(far, *done):
        far = tuple(tie_all(far, *done))
        token_blocks[6], token_blocks[7] = far, tuple(swap(piece, 1, size) for piece in far)


    moe_parts, back_parts, grad_sums = [None] * size, [None] * size, []
    wide = model + rank_all

    direct = down_rows == rank_all
    shapes = [None] * local_experts

    def weights_of(j):
        args = [seq_up[j].reshape(model, -1)]
        shapes[j] = [args[0].shape, (EXPERT_HIDDEN, wide), (rank_all, depth * second_cut * down_rows // rank_all)]
        if direct:
            args.append(seq_down[j])
        else:
            second_j = seq_down[j][:, :, wide : wide + second_cut]
            second_j = second_j.reshape(depth, rank_all, -1).transpose(1, 0, 2).reshape(rank_all, -1)
            args += [seq_down[j][:, :, :wide].reshape(EXPERT_HIDDEN, wide), second_j]
        if j == 0:
            if not direct:
                parts = seq_down[j][:, :, wide + second_cut :].reshape(depth, 4, shared_rows, 4 * LANES)
                args.append(parts.transpose(0, 2, 1, 3).reshape(units, -1)[:, :wide])
            slices = [
                lax.dynamic_slice_in_dim(second_t[edges[n] : edges[n + 1]].reshape(depth, size, -1, rank_all), me, 1, 1)
                for n in (4, 5)
            ]
            args.append(jnp.concatenate([part.reshape(units, rank_all) for part in slices], axis=0))
            shapes[j] += [(units, wide), args[-1].shape]
        return args

    def run_expert(j, args, group, prior, deps, packed=False):
        meta = jnp.stack([me * local_experts + j, me]).astype(jnp.int32)
        prior = ([moe_parts[k] for k in group], [back_parts[k] for k in group]) if prior else None
        moe_out, back_out, grads = expert_call(
            meta,
            args,
            shapes[j],
            [token_blocks[k] for k in group],
            [grad_blocks[k] for k in group],
            prior,
            grad_sums[-1],
            packed,
            experts,
            capacity,
            depth,
            deps,
        )
        for n, k in enumerate(group):
            moe_parts[k], back_parts[k] = moe_out[n], back_out[n]
        grad_sums[-1] = list(grads)

    for j in range(local_experts - 1):
        grad_sums.append([])
        args = weights_of(j)
        previous = ()
        for group in ((0, 1), (2, 3), (4, 5), (6, 7)):
            run_expert(j, args, group, j > 0, previous, group == (6, 7))
            previous = (back_parts[group[0]],)
            if j == 0 and group == (0, 1):
                far = gather_far(tokens_x, tokens_y, *previous)
            if j == 0 and group == (2, 3):
                gather_farthest(far, *previous)
    if local_experts == 1:
        gather_farthest(gather_far(tokens_x, tokens_y))

    def scatter(packed):
        return lax.psum_scatter(packed, "seq", scatter_dimension=0, tiled=True)

    packed_sums = [scatter(grads[0]) for grads in grad_sums]
    grad_sums.append([])
    j, prior, half = local_experts - 1, local_experts > 1, (rows + BACK_ROWS) // 2
    args = weights_of(j)
    run_expert(j, args, (6, 7), prior, (back_parts[6],) if prior else ())
    pair_six = add(back_parts[6], swap(back_parts[7], 1, size))
    run_expert(j, args, (2, 3), prior, (back_parts[6],))
    from_diagonal_x, from_diagonal_y = swap(pair_six[:half], 2, size), swap(pair_six[half:], 4, size)
    pair_two = add(back_parts[2], swap(back_parts[3], 1, size))
    run_expert(j, args, (4, 5), prior, (back_parts[2], pair_six))
    pair_four = add(back_parts[4], swap(tie(back_parts[5], from_diagonal_x, from_diagonal_y, *packed_sums), 1, size))
    to_x = jnp.concatenate([pair_two[:half], add(pair_two[half:], from_diagonal_y)], axis=0)
    to_y = jnp.concatenate([add(pair_four[:half], from_diagonal_x), pair_four[half:]], axis=0)
    run_expert(j, args, (0, 1), prior, (to_x, to_y), True)
    packed_sums.append(scatter(grad_sums[-1][0]))
    from_x, from_y = swap(to_x, 2, size), swap(to_y, 4, size)
    grad_mid, grad_mid_b, glow_out, glow_sgu, low_sdown, grad_attn, shared_units = turn(
        [back_parts[0], swap(back_parts[1], 1, size), from_x, from_y, mid, gates, first_gu]
        + [router_w, gains[1:2], grad_out_b, b_parts[3], out_w, first_o],
        (swap(tie(gates_lo[:16], from_x, from_y), 1, size),),
    )

    half = rows // 2
    far_parts = dict(zip((6, 2, 4, 0), tie_all([moe_parts[k + 1] for k in (6, 2, 4, 0)], from_x, from_y)))
    pair = {k: add(moe_parts[k], swap(far_parts[k], 1, size)) for k in (6, 2, 4, 0)}
    moe_to_x = jnp.concatenate([pair[2][:half], add(pair[2][half:], swap(pair[6][half:], 4, size))], axis=0)
    moe_to_y = jnp.concatenate([add(pair[4][:half], swap(pair[6][:half], 2, size)), pair[4][half:]], axis=0)
    moe_from_x, moe_from_y = swap(moe_to_x, 2, size), swap(moe_to_y, 4, size)
    moe = pair[0].astype(F32) + moe_from_x.astype(F32) + moe_from_y.astype(F32)

    def shared_columns(block):
        block = block[:, :SHARED_HIDDEN].reshape(rank, size, depth, units // depth)
        return block.transpose(0, 2, 1, 3).reshape(rank, SHARED_HIDDEN)

    grad_q, grad_kv = attend_back(
        query, kv_all, grad_attn, lse, query_tag, key_tag, hops, 0, KV_HEADS, (pair[6], pair[2], pair[4])
    )
    moving, early_received = grad_kv[:rows], grad_q
    for h in range(hops):
        if h == 1:
            moving = tie(moving, moe_to_x, moe_to_y)
        received = lax.ppermute(moving, "seq", backward)
        moving = add(grad_kv[(h + 1) * rows : (h + 2) * rows], received)
        if h == 0:
            early_received = received
    grad_normed_q, first_query, second_query = query_back(
        [grad_q, normed, low_q, q_w, first_q, b_parts[0]], (early_received,)
    )
    first_early, second_out, second_down = middle(
        [attn, glow_out, normed2, glow_sgu, grad_mid_b, out_low, grad_out_b, low_sdown],
        (early_received,),
    )
    packed_sums = tie_all(packed_sums, early_received)
    owner_rows = model // depth
    firsts, downs, seconds = [], [], []
    for packed in packed_sums:
        packed = packed[0].astype(F32)
        firsts.append(jnp.stack([packed[:owner_rows], packed[owner_rows : 2 * owner_rows]], axis=1))
        at = 2 * owner_rows + down_rows
        downs.append(packed[2 * owner_rows : at])
        seconds.append(packed[at : at + routed_second_factor.shape[2]].T)
    at += routed_second_factor.shape[2]
    grad_expert_a, grad_expert_a_down, grad_expert_b = jnp.stack(firsts), jnp.stack(downs), jnp.stack(seconds)
    grad_first_down = packed_sums[0][0, at : at + shared_rows].astype(F32)

    hidden_out = (mid + moe + dot_nn(low_sdown, b_parts[6])).astype(BF16)[None]
    second_early = jnp.concatenate(
        [second_out, shared_columns(shared_units[:rank]), shared_columns(shared_units[rank:]), second_down], axis=1
    )
    grad_hidden, first_flat, second_flat = last(
        depth * size,
        [moving, normed, low_kv, kv_w, first_kv, b_parts[1], b_parts[2], block_input[0], gains[0:1], grad_mid]
        + [grad_normed_q, first_query, first_early, second_query, second_early, adapter.astype(F32).reshape(1, 1)],
    )
    flat = jnp.concatenate([first_flat.reshape(depth * size, shard_rows, LANES), second_flat], axis=1)
    flat = lax.all_to_all(flat, ("seq", "dp"), split_axis=0, concat_axis=0, tiled=True)
    grad_first, grad_second = spread(flat, depth, shard_rows)
    grad_first = grad_first.reshape(shard_rows, 6, rank_all)
    grad_second = grad_second[:, :second_columns]
    grad_hidden = grad_hidden[None]
    return (
        hidden_out,
        grad_hidden,
        grad_first,
        grad_first_down,
        grad_second,
        grad_expert_a,
        grad_expert_a_down,
        grad_expert_b,
    )


def solution(mesh):
    in_specs = (
        P("dp", "seq", None),
        P("dp", "seq"),
        P("dp", "seq"),
        P("dp", "seq", None),
        P("dp"),
        P("dp", "seq", None),
        P(None, ("seq", "dp")),
        P(("seq", "dp"), None),
        P(("seq", "dp"), None),
        P(("seq", "dp"), None),
        P(("seq", "dp"), None, None),
        P(("seq", "dp"), None),
        P("dp", "seq", None, None),
        P("dp", "seq", None),
        P(("seq", "dp"), None, None),
        P(("seq", "dp"), None),
        P(None, ("seq", "dp")),
        P("dp", "seq", None, None),
        P("dp", "seq", None),
        P("dp", None, "seq"),
    )
    out_specs = (
        P("dp", "seq", None),
        P("dp", "seq", None),
        P(("seq", "dp"), None, None),
        P(("seq", "dp"), None),
        P(None, ("seq", "dp")),
        P("dp", "seq", None, None),
        P("dp", "seq", None),
        P("dp", None, "seq"),
    )
    return jax.shard_map(
        functools.partial(per_device, mesh.shape["seq"], mesh.shape["dp"]),
        mesh=mesh,
        in_specs=in_specs,
        out_specs=out_specs,
        check_vma=False,
    )
```

```python
import functools
import math

import jax
import jax.numpy as jnp
from jax import lax
from jax.experimental import pallas as pl
from jax.experimental.pallas import tpu as pltpu
from jax.sharding import PartitionSpec as P

HEADS = 12
KV_HEADS = 4
HEAD_DIM = 128
EXPERT_HIDDEN = 512
SHARED_HIDDEN = 1024
ADAPTER_RANK = 16
DOCUMENT_SPAN = 1024

EPSILON = 1e-05
MASKED_SCORE = -1e30
LOG2E = 1.4426950408889634
SCALE = HEAD_DIM ** (-0.5)
LANES = 128
VMEM_LIMIT = 60 * 1024 * 1024

F32 = jnp.float32
BF16 = jnp.bfloat16


def dot_nn(left, right):
    return jnp.dot(left, right, preferred_element_type=F32)


def dot_tn(left, right):
    return lax.dot_general(left, right, (((0,), (0,)), ((), ())), preferred_element_type=F32)


def dot_nt(left, right):
    return lax.dot_general(left, right, (((1,), (1,)), ((), ())), preferred_element_type=F32)


def rms_norm(values, gain):
    return values * lax.rsqrt(jnp.mean(values * values, axis=-1, keepdims=True) + EPSILON) * gain


def cost(microseconds):
    return pl.CostEstimate(flops=int(1153500000 * microseconds), bytes_accessed=1000000, transcendentals=0)


def query_tiles(rows, hops):
    tile = math.gcd(rows, 256)
    spans = []
    for first in range(0, rows, tile):
        oldest = max(0, hops * rows + first - (DOCUMENT_SPAN - 1)) // tile * tile
        spans.append((first, tile, oldest, hops * rows + first + tile - oldest))
    return spans


def fill_bias(spans, shift, query_tag, key_tag, bias):
    for first, tile, oldest, span in spans:
        keys = oldest + lax.broadcasted_iota(jnp.int32, (span, tile), 0)
        queries = shift + first + lax.broadcasted_iota(jnp.int32, (span, tile), 1)
        same = key_tag[oldest : oldest + span, :] == query_tag[:, first : first + tile]
        permit = (keys <= queries) & (same | (keys == queries))
        bias[oldest : oldest + span, first : first + tile] = jnp.where(permit, 0.0, MASKED_SCORE)


def attend_kernel(spans, shift, waits, q_ref, k_ref, v_ref, qt_ref, kt_ref, *rest):
    out_ref, lse_ref, bias = rest[waits:]

    @pl.when(pl.program_id(0) == 0)
    def _():
        fill_bias(spans, shift, qt_ref, kt_ref, bias)

    groups = q_ref.shape[1] // HEAD_DIM
    for first, tile, oldest, span in spans:
        keys = k_ref[oldest : oldest + span, :]
        values = v_ref[oldest : oldest + span, :]
        mask = bias[oldest : oldest + span, first : first + tile]
        for h in range(groups):
            columns = slice(h * HEAD_DIM, (h + 1) * HEAD_DIM)
            scores = dot_nt(keys, q_ref[first : first + tile, columns]) * (SCALE * LOG2E) + mask
            top = jnp.max(scores, axis=0, keepdims=True)
            weights = jnp.exp2(scores - top)
            total = jnp.sum(weights, axis=0, keepdims=True)
            mixed = dot_tn(values, weights.astype(BF16)) / total
            out_ref[first : first + tile, columns] = mixed.T.astype(BF16)
            lse_ref[0, h : h + 1, first : first + tile] = top + jnp.log2(total)


def attend(query, kv_all, query_tag, key_tag, hops, deps=()):
    rows = query.shape[0]
    groups = HEADS // KV_HEADS
    span = kv_all.shape[0]
    spans = query_tiles(rows, hops)
    return pl.pallas_call(
        functools.partial(attend_kernel, spans, hops * rows, len(deps)),
        grid=(KV_HEADS,),
        in_specs=[
            pl.BlockSpec((rows, groups * HEAD_DIM), lambda g: (0, g)),
            pl.BlockSpec((span, HEAD_DIM), lambda g: (0, g)),
            pl.BlockSpec((span, HEAD_DIM), lambda g: (0, KV_HEADS + g)),
            pl.BlockSpec((1, rows), lambda g: (0, 0)),
            pl.BlockSpec((span, 1), lambda g: (0, 0)),
        ]
        + [pl.BlockSpec(memory_space=pl.ANY)] * len(deps),
        out_specs=[
            pl.BlockSpec((rows, groups * HEAD_DIM), lambda g: (0, g)),
            pl.BlockSpec((1, groups, rows), lambda g: (g, 0, 0)),
        ],
        out_shape=[
            jax.ShapeDtypeStruct((rows, HEADS * HEAD_DIM), BF16),
            jax.ShapeDtypeStruct((KV_HEADS, groups, rows), F32),
        ],
        scratch_shapes=[pltpu.VMEM((span, rows), F32)],
        compiler_params=pltpu.CompilerParams(vmem_limit_bytes=VMEM_LIMIT),
        cost_estimate=cost(23.0),
        name="attend",
    )(query, kv_all, kv_all, query_tag, key_tag, *deps)


def attend_back_kernel(
    spans, shift, waits, q_ref, k_ref, v_ref, g_ref, lse_ref, qt_ref, kt_ref, *rest
):
    dq_ref, dkv_ref, bias, dk_acc, dv_acc = rest[waits:]

    @pl.when(pl.program_id(0) == 0)
    def _():
        fill_bias(spans, shift, qt_ref, kt_ref, bias)

    dk_acc[...] = jnp.zeros_like(dk_acc)
    dv_acc[...] = jnp.zeros_like(dv_acc)
    groups = q_ref.shape[1] // HEAD_DIM
    for first, tile, oldest, span in spans:
        keys = k_ref[oldest : oldest + span, :]
        values = v_ref[oldest : oldest + span, :]
        mask = bias[oldest : oldest + span, first : first + tile]
        for h in range(groups):
            columns = slice(h * HEAD_DIM, (h + 1) * HEAD_DIM)
            query = q_ref[first : first + tile, columns]
            grad = g_ref[first : first + tile, columns]
            lse = lse_ref[0, h : h + 1, first : first + tile]
            probs = jnp.exp2(dot_nt(keys, query) * (SCALE * LOG2E) + mask - lse)
            dv_acc[oldest : oldest + span, :] += dot_nn(probs.astype(BF16), grad)
            grad_probs = dot_nt(values, grad)
            delta = jnp.sum(probs * grad_probs, axis=0, keepdims=True)
            grad_scores = (probs * (grad_probs - delta)).astype(BF16)
            dk_acc[oldest : oldest + span, :] += dot_nn(grad_scores, query) * SCALE
            dq_ref[first : first + tile, columns] = (dot_tn(grad_scores, keys) * SCALE).astype(BF16)
    dkv_ref[:, :HEAD_DIM] = dk_acc[...].astype(dkv_ref.dtype)
    dkv_ref[:, HEAD_DIM:] = dv_acc[...].astype(dkv_ref.dtype)


def attend_back(query, kv_all, grad_attn, lse, query_tag, key_tag, hops, head, count, deps=()):
    rows = query.shape[0]
    groups = HEADS // KV_HEADS
    span = kv_all.shape[0]
    spans = query_tiles(rows, hops)
    return pl.pallas_call(
        functools.partial(attend_back_kernel, spans, hops * rows, len(deps)),
        grid=(count,),
        in_specs=[
            pl.BlockSpec((rows, groups * HEAD_DIM), lambda g: (0, head + g)),
            pl.BlockSpec((span, HEAD_DIM), lambda g: (0, head + g)),
            pl.BlockSpec((span, HEAD_DIM), lambda g: (0, KV_HEADS + head + g)),
            pl.BlockSpec((rows, groups * HEAD_DIM), lambda g: (0, head + g)),
            pl.BlockSpec((1, groups, rows), lambda g: (head + g, 0, 0)),
            pl.BlockSpec((1, rows), lambda g: (0, 0)),
            pl.BlockSpec((span, 1), lambda g: (0, 0)),
        ]
        + [pl.BlockSpec(memory_space=pl.ANY)] * len(deps),
        out_specs=[
            pl.BlockSpec((rows, groups * HEAD_DIM), lambda g: (0, g)),
            pl.BlockSpec((span, 2 * HEAD_DIM), lambda g: (0, g)),
        ],
        out_shape=[
            jax.ShapeDtypeStruct((rows, count * groups * HEAD_DIM), BF16),
            jax.ShapeDtypeStruct((span, count * 2 * HEAD_DIM), BF16),
        ],
        scratch_shapes=[
            pltpu.VMEM((span, rows), F32),
            pltpu.VMEM((span, HEAD_DIM), F32),
            pltpu.VMEM((span, HEAD_DIM), F32),
        ],
        compiler_params=pltpu.CompilerParams(vmem_limit_bytes=VMEM_LIMIT),
        cost_estimate=cost(2.0 * count),
        name="attend_back",
    )(query, kv_all, kv_all, grad_attn, lse, query_tag, key_tag, *deps)


BACK_ROWS = 2 * ADAPTER_RANK


def expert_kernel(
    count, splits, experts, capacity, depth, direct, with_prior, with_shared, with_sums, packed, waits, *refs
):
    meta, refs = refs[0], refs[1:]
    weight_count = 5 if with_shared else 3
    given = weight_count - (2 if with_shared else 1) if direct else weight_count
    weight_refs, refs = refs[:given], refs[given:]
    token_refs, grad_refs = [], []
    for split in splits:
        token_refs.append(refs[:split])
        refs = refs[split:]
    for split in splits:
        grad_refs.append(refs[:split])
        refs = refs[split:]
    prior_moe, prior_back = (), ()
    if with_prior:
        prior_moe, refs = refs[:count], refs[count:]
        prior_back, refs = refs[:count], refs[count:]
    grad_count = 4 if with_shared else 3
    sums_in = ()
    if with_sums:
        sums_in, refs = refs[:grad_count], refs[grad_count:]
    refs = refs[waits:]
    moe_refs, refs = refs[:count], refs[count:]
    back_refs, refs = refs[:count], refs[count:]
    out_count = 1 if packed else grad_count
    grad_outs, refs = refs[:out_count], refs[out_count:]
    grad_sums, refs = refs[:grad_count], refs[grad_count:]
    first_grad, down_grad, second_grad = grad_sums[:3]
    weight_bufs, refs = refs[:weight_count], refs[weight_count:]
    if packed:
        pack_buf, refs = refs[0], refs[1:]
    tokens_buf, grad_buf, moe_buf, back_buf, in_sem, out_sem, weight_sem, sum_sem, sum_in_sem = refs

    step = pl.program_id(0)
    steps = count // 2
    slots = min(2, steps)
    slot = lax.rem(step, slots)
    rows, wide = tokens_buf.shape[2:]
    model = wide - LANES
    hidden = EXPERT_HIDDEN
    rank = ADAPTER_RANK
    up_ref, down_ref, second_ref = weight_bufs[:3]

    def weight_copies():
        pairs = list(zip(weight_refs, weight_bufs))
        if direct:
            raw, lines = weight_refs[1], weight_refs[1].shape[1]
            pairs, columns = pairs[:1], second_ref.shape[1] // depth
            for z in range(depth):
                pairs.append((raw.at[z, :, pl.ds(0, wide)], down_ref.at[pl.ds(z * lines, lines)]))
                part = raw.at[z, :, pl.ds(wide, columns)]
                pairs.append((part, second_ref.at[:, pl.ds(z * columns, columns)]))
            if with_shared:
                group, size = 4 * LANES, lines // 4
                for z in range(depth):
                    for q in range(4):
                        width = min(group, wide - q * group)
                        part = raw.at[z, pl.ds(q * size, size), pl.ds(wide + columns, width)]
                        target = weight_bufs[3].at[pl.ds(z * size, size), pl.ds(q * group, width)]
                        pairs.append((part, target))
                pairs.append((weight_refs[2], weight_bufs[4]))
        return [pltpu.make_async_copy(src, dst, weight_sem.at[n]) for n, (src, dst) in enumerate(pairs)]

    def incoming(k, i, kinds):
        copies = []
        to, source = k % slots, 2 * k + i
        for n, (refs_of, buf) in enumerate(((token_refs, tokens_buf), (grad_refs, grad_buf))):
            size = rows // len(refs_of[source])
            for p, piece in enumerate(refs_of[source] if n in kinds else ()):
                part = buf.at[to, i, pl.ds(p * size, size)]
                copies.append(pltpu.make_async_copy(piece, part, in_sem.at[to, i, 2 * n + p]))
        if with_prior and 2 in kinds:
            copies.append(pltpu.make_async_copy(prior_moe[source], moe_buf.at[to, i], in_sem.at[to, i, 4]))
            copies.append(pltpu.make_async_copy(prior_back[source], back_buf.at[to, i], in_sem.at[to, i, 5]))
        return copies

    def outgoing(k, i, kinds=(0, 1)):
        at, source = k % slots, 2 * k + i
        pairs = ((moe_buf, moe_refs), (back_buf, back_refs))
        return [pltpu.make_async_copy(pairs[n][0].at[at, i], pairs[n][1][source], out_sem.at[at, i, n]) for n in kinds]

    def at_step(action, first=0, last=steps):
        for k in range(first, last):
            pl.when(step == k)(functools.partial(action, k))

    def wait_in(i, kind):
        def action(k):
            for copy in incoming(k, i, (kind,)):
                copy.wait()

        at_step(action)

    def start_out(i, n):
        at_step(lambda k: outgoing(k, i, (n,))[0].start())

    def turn(k):
        for i in (0, 1):
            if k >= 1:
                for copy in outgoing(k - 1, i):
                    copy.wait()
            if k + 1 < steps:
                for copy in incoming(k + 1, i, (0, 1, 2)):
                    copy.start()

    def sum_copy(n):
        return pltpu.make_async_copy(pack_buf if packed else grad_sums[n], grad_outs[n], sum_sem.at[n])

    def sum_in(n):
        return pltpu.make_async_copy(sums_in[n], grad_sums[n], sum_in_sem.at[n])

    @pl.when(step == 0)
    def _():
        for i in (0, 1):
            for copy in incoming(0, i, (0,)):
                copy.start()
        for copy in weight_copies():
            copy.start()
        for i in (0, 1):
            for copy in incoming(0, i, (1,)):
                copy.start()
        for i in (0, 1):
            for copy in incoming(0, i, (2,)):
                copy.start()
        for n, total in enumerate(grad_sums):
            if with_sums:
                sum_in(n).start()
            else:
                total[...] = jnp.zeros_like(total)

    expert = meta[0]
    lane = lax.broadcasted_iota(jnp.int32, (1, LANES), 1)
    sub = lax.broadcasted_iota(jnp.int32, (LANES, 1), 0)
    places, picks, gates_of, selects, adapters = [], [], [], [], []
    inputs, grad_rows = [], []
    for i in (0, 1):
        wait_in(i, 0)
        extra_b = tokens_buf[slot, i, :, model:]
        extra = extra_b.astype(F32)
        own = 3 * experts + 3 * rank
        adapter = extra[0:1, own : own + 1]
        select = ((lane // rank).astype(F32) == adapter).astype(F32)
        slot_column = jnp.sum(jnp.where(lane == expert, extra, 0.0), axis=1, keepdims=True)
        slot_row = jnp.sum(jnp.where(sub == expert, extra.T, 0.0), axis=0, keepdims=True)
        place = lax.broadcasted_iota(jnp.int32, (rows, capacity), 1).astype(F32) == slot_column
        pick = lax.broadcasted_iota(jnp.int32, (capacity, rows), 0).astype(F32) == slot_row
        place, pick = place.astype(F32).astype(BF16), pick.astype(F32).astype(BF16)
        picked_extra = dot_nn(pick, extra_b)
        chosen = (lane == experts + expert) | (lane == 2 * experts + expert)
        gates_of.append(jnp.sum(jnp.where(chosen, picked_extra, 0.0), axis=1, keepdims=True))
        inputs.append(dot_nn(pick, tokens_buf[slot, i, :, :model]).astype(BF16))
        picks.append(pick)
        places.append(place)
        adapters.append(adapter)
        selects.append(jnp.broadcast_to(select, (capacity, LANES)))
    inputs = jnp.concatenate(inputs, axis=0)
    gate = jnp.concatenate(gates_of, axis=0)
    select = jnp.concatenate(selects, axis=0)
    select_two = jnp.concatenate([select, select], axis=1)

    @pl.when(step == 0)
    def _():
        weight_copies()[0].wait()

    low = (dot_nn(inputs, up_ref[:, 2 * hidden : 2 * hidden + 2 * LANES]) * select_two).astype(BF16)
    gate_part = dot_nn(inputs, up_ref[:, :hidden])
    up_part = dot_nn(inputs, up_ref[:, hidden : 2 * hidden])

    @pl.when(step == 0)
    def _():
        for copy in weight_copies()[1:]:
            copy.wait()

    for i in (0, 1):
        wait_in(i, 1)
        grad_rows.append(dot_nn(picks[i], grad_buf[slot, i]))
    at_step(turn)
    grad_rows = jnp.concatenate(grad_rows, axis=0)
    gate_part = gate_part + dot_nn(low[:, :LANES], second_ref[:, :hidden])
    up_part = up_part + dot_nn(low[:, LANES:], second_ref[:, hidden : 2 * hidden])
    sigmoid = 1.0 / (1.0 + jnp.exp(-gate_part))
    silu = gate_part * sigmoid
    act = (silu * up_part).astype(BF16)
    low_down = (dot_nn(act, down_ref[:, model:]) * select).astype(BF16)
    output = (dot_nn(act, down_ref[:, :model]) + dot_nn(low_down, second_ref[:, 2 * hidden :])).astype(BF16).astype(F32)
    grad_gate = jnp.sum(output * grad_rows, axis=1, keepdims=True)
    weighted = (gate * output).astype(BF16)

    if with_sums:

        @pl.when(step == 0)
        def _():
            for n in range(grad_count):
                sum_in(n).wait()

    grad_y = (gate * grad_rows).astype(BF16)
    glow_down = (dot_nt(grad_y, second_ref[:, 2 * hidden :]) * select).astype(BF16)
    second_grad[:, 2 * hidden :] += dot_tn(low_down, grad_y)
    down_grad[...] += dot_tn(act, glow_down)
    grad_act = dot_nt(grad_y, down_ref[:, :model]) + dot_nt(glow_down, down_ref[:, model:])
    grad_up = (grad_act * silu).astype(BF16)
    grad_gp = (grad_act * up_part * (sigmoid * (1.0 + gate_part * (1.0 - sigmoid)))).astype(BF16)
    glow = jnp.concatenate(
        [
            dot_nt(grad_gp, second_ref[:, :hidden]) * select,
            dot_nt(grad_up, second_ref[:, hidden : 2 * hidden]) * select,
        ],
        axis=1,
    ).astype(BF16)
    second_grad[:, :hidden] += dot_tn(low[:, :LANES], grad_gp)
    second_grad[:, hidden : 2 * hidden] += dot_tn(low[:, LANES:], grad_up)
    first_grad[...] += dot_tn(inputs, glow)
    grad_in = (
        dot_nt(grad_gp, up_ref[:, :hidden])
        + dot_nt(grad_up, up_ref[:, hidden : 2 * hidden])
        + dot_nt(glow, up_ref[:, 2 * hidden : 2 * hidden + 2 * LANES])
    ).astype(BF16)
    gate_hi = grad_gate.astype(BF16).astype(F32)
    gate_lo = grad_gate - gate_hi
    extra_out = (
        jnp.where(lane == expert, gate_hi, 0.0) + jnp.where(lane == experts + expert, gate_lo, 0.0)
    ).astype(BF16)

    @pl.when(step == steps - 1)
    def _():
        if not packed:
            for n in range(3):
                sum_copy(n).start()
            return
        second_t = second_grad[...].T
        parts = [first_grad[:, :LANES], first_grad[:, LANES:], down_grad[...], second_t]
        at = 0
        for part in parts:
            size = part.shape[0] // depth
            for z in range(depth):
                pack_buf[z, at : at + size, :] = part[z * size : (z + 1) * size].astype(BF16)
            at += size

    for i in (0, 1):
        mine = slice(i * capacity, (i + 1) * capacity)
        wait_in(i, 2)
        moe = dot_nn(places[i], weighted[mine])
        back = dot_nn(places[i], grad_in[mine])
        back_extra = dot_nn(places[i], extra_out[mine])
        if with_prior:
            moe = moe + moe_buf[slot, i].astype(F32)
            back = back + back_buf[slot, i, :rows, :model].astype(F32)
            back_extra = back_extra + back_buf[slot, i, :rows, model:].astype(F32)
        if not with_prior:
            back_buf[slot, i, rows:, :] = jnp.zeros((BACK_ROWS, wide), BF16)
        if with_shared:
            sdown_ref, sb_ref = weight_bufs[3:]
            units = sdown_ref.shape[0]
            first_gate, first_up, first_down = 3 * experts, 3 * experts + rank, 3 * experts + 2 * rank
            tokens = tokens_buf[slot, i, :, :model]
            extra_b = tokens_buf[slot, i, :, model:]
            grads = grad_buf[slot, i]
            offset = (lane - sub).astype(F32) - adapters[i] * float(rank)

            def spread(base):
                inside = (sub >= base) & (sub < base + rank)
                return (inside & (offset == float(-base))).astype(F32).astype(BF16)

            to_gate = dot_nt(spread(first_gate), sb_ref[:units]).astype(BF16)
            to_up = dot_nt(spread(first_up), sb_ref[units:]).astype(BF16)
            to_down = dot_nt(spread(first_down), sdown_ref[:, model:]).astype(BF16)
            shared_up = up_ref[:, 2 * hidden + 2 * LANES :]
            gate_up = dot_nn(tokens, shared_up)
            s_gate = gate_up[:, :units] + dot_nn(extra_b, to_gate)
            s_up = gate_up[:, units:] + dot_nn(extra_b, to_up)
            s_sig = 1.0 / (1.0 + jnp.exp(-s_gate))
            s_silu = s_gate * s_sig
            s_act = (s_silu * s_up).astype(BF16)
            moe = moe + dot_nn(s_act, sdown_ref[:, :model])
            s_grad = dot_nt(grads, sdown_ref[:, :model]) + dot_nn(extra_b, to_down)
            grad_sums[3][...] += dot_tn(s_act, dot_nn(extra_b, spread(first_down)).astype(BF16))
            s_gu = (s_grad * s_silu).astype(BF16)
            s_gg = (s_grad * s_up * (s_sig * (1.0 + s_gate * (1.0 - s_sig)))).astype(BF16)
            back_extra = back_extra + dot_nt(s_act, to_down) + dot_nt(s_gg, to_gate) + dot_nt(s_gu, to_up)
            back = back + dot_nt(jnp.concatenate([s_gg, s_gu], axis=1), shared_up)
            columns = pl.ds(pl.multiple_of(meta[1] * units, units), units)
            grad_bg = dot_tn(extra_b, s_gg)[first_gate : first_gate + rank]
            grad_bu = dot_tn(extra_b, s_gu)[first_up : first_up + rank]
            back_buf[slot, i, rows : rows + rank, columns] = grad_bg.astype(BF16)
            back_buf[slot, i, rows + rank :, columns] = grad_bu.astype(BF16)
        moe_buf[slot, i] = moe.astype(BF16)
        start_out(i, 0)
        back_buf[slot, i, :rows, :model] = back.astype(BF16)
        back_buf[slot, i, :rows, model:] = back_extra.astype(BF16)
        start_out(i, 1)

    @pl.when(step == steps - 1)
    def _():
        if packed and with_shared:
            size = grad_sums[3].shape[0] // depth
            for z in range(depth):
                part = grad_sums[3][z * size : (z + 1) * size, :]
                if size % 16:
                    part = jnp.concatenate([part, jnp.zeros((16 - size % 16, LANES), F32)], axis=0)
                pack_buf[z, pack_buf.shape[1] - part.shape[0] :, :] = part.astype(BF16)
        for n in range(0 if packed else 3, out_count):
            sum_copy(n).start()
        for i in (0, 1):
            for copy in outgoing(steps - 1, i):
                copy.wait()
        for n in range(out_count):
            sum_copy(n).wait()


def expert_call(meta, weights, shapes, tokens, grads, prior, sums, packed, experts, capacity, depth, deps=()):
    count = len(tokens)
    with_shared = len(shapes) > 3
    direct = len(weights) < len(shapes)
    splits = [len(pieces) for pieces in tokens]
    rows, model = sum(piece.shape[0] for piece in grads[0]), grads[0][0].shape[1]
    wide = model + LANES
    slots = min(2, count // 2)
    anywhere = pl.BlockSpec(memory_space=pl.ANY)
    prior = [] if prior is None else list(prior[0]) + list(prior[1])
    flat = [piece for pieces in tokens for piece in pieces] + [piece for pieces in grads for piece in pieces]
    grad_shapes = [
        jax.ShapeDtypeStruct((model, 2 * LANES), F32),
        jax.ShapeDtypeStruct((EXPERT_HIDDEN, LANES), F32),
        jax.ShapeDtypeStruct(shapes[2], F32),
    ]
    if with_shared:
        grad_shapes.append(jax.ShapeDtypeStruct((shapes[3][0], LANES), F32))
    out_shapes = grad_shapes
    if packed:
        lines = sum(s.shape[0] for s in grad_shapes[:2]) + model + shapes[2][1]
        lines = lines // depth
        if with_shared:
            lines += -(-shapes[3][0] // depth // 16) * 16
        out_shapes = [jax.ShapeDtypeStruct((depth, lines, LANES), BF16)]
    back_rows = rows + BACK_ROWS
    outs = pl.pallas_call(
        functools.partial(
            expert_kernel,
            *(count, splits, experts, capacity, depth, direct, bool(prior), with_shared, bool(sums), packed, len(deps)),
        ),
        grid=(count // 2,),
        in_specs=[pl.BlockSpec(memory_space=pltpu.SMEM)]
        + [anywhere] * (len(weights) + len(flat) + len(prior) + len(sums) + len(deps)),
        out_specs=[anywhere] * (2 * count + len(out_shapes)),
        out_shape=[jax.ShapeDtypeStruct((rows, model), BF16)] * count
        + [jax.ShapeDtypeStruct((back_rows, wide), BF16)] * count
        + out_shapes,
        scratch_shapes=[pltpu.VMEM(s.shape, F32) for s in grad_shapes]
        + [pltpu.VMEM(shape, BF16) for shape in shapes]
        + ([pltpu.VMEM(out_shapes[0].shape, BF16)] if packed else [])
        + [
            pltpu.VMEM((slots, 2, rows, wide), BF16),
            pltpu.VMEM((slots, 2, rows, model), BF16),
            pltpu.VMEM((slots, 2, rows, model), BF16),
            pltpu.VMEM((slots, 2, back_rows, wide), BF16),
            pltpu.SemaphoreType.DMA((slots, 2, 6)),
            pltpu.SemaphoreType.DMA((slots, 2, 2)),
            pltpu.SemaphoreType.DMA((len(shapes) + 6 * depth,)),
            pltpu.SemaphoreType.DMA((len(grad_shapes),)),
            pltpu.SemaphoreType.DMA((len(grad_shapes),)),
        ],
        compiler_params=pltpu.CompilerParams(vmem_limit_bytes=VMEM_LIMIT),
        cost_estimate=cost(12.0 * count),
        name="expert",
    )(meta, *weights, *flat, *prior, *sums, *deps)
    return outs[:count], outs[count : 2 * count], outs[2 * count :]


def swap(array, bit, size):
    return lax.ppermute(array, "dp", [(i, i ^ bit) for i in range(size)])


def plane_gather(array, size):
    half = array.shape[0] // 2
    x, y = swap(array, 2, size), swap(array, 4, size)
    across = {0: (array,), 2: (x,), 4: (y,), 6: (swap(y[:half], 2, size), swap(x[half:], 4, size))}
    blocks = [None] * size
    for k in (0, 2, 4, 6):
        blocks[k] = across[k]
        blocks[k + 1] = tuple(swap(piece, 1, size) for piece in across[k])
    return blocks


def add(*terms):
    total = terms[0].astype(F32)
    for term in terms[1:]:
        total = total + term.astype(F32)
    return total.astype(BF16)


def tie_kernel(*refs):
    del refs


def tie_all(arrays, *others):
    anywhere = pl.BlockSpec(memory_space=pl.ANY)
    return pl.pallas_call(
        tie_kernel,
        in_specs=[anywhere] * (len(arrays) + len(others)),
        out_specs=[anywhere] * len(arrays),
        out_shape=[jax.ShapeDtypeStruct(array.shape, array.dtype) for array in arrays],
        input_output_aliases={n: n for n in range(len(arrays))},
        name="tie",
    )(*arrays, *others)


def tie(array, *others):
    return tie_all([array], *others)[0]


def assemble_kernel(splits, widths, waits, me_ref, *refs):
    pieces, outs = refs[: sum(splits)], refs[sum(splits) + waits : -3]
    whole, in_sem, out_sem = refs[-3:]
    copies, at = [], 0
    for k, split in enumerate(splits):
        start = 0
        for piece in pieces[at : at + split]:
            target = whole.at[pl.ds(start, piece.shape[0]), me_ref[0] ^ k]
            copies.append(pltpu.make_async_copy(piece, target, in_sem.at[len(copies)]))
            start += piece.shape[0]
        at += split
    for copy in copies:
        copy.start()
    for copy in copies:
        copy.wait()
    copies, column = [], 0
    for out, (count, width) in zip(outs, widths):
        for n in range(count):
            source = whole.at[:, :, :, pl.ds(column, width)]
            copies.append(pltpu.make_async_copy(source, out.at[:, :, n], out_sem.at[len(copies)]))
            column += width
    for copy in copies:
        copy.start()
    for copy in copies:
        copy.wait()


def assemble(blocks, widths, me, deps=()):
    depth, rows, _ = blocks[0][0].shape
    size = len(blocks)
    splits = [len(pieces) for pieces in blocks]
    flat = [piece for pieces in blocks for piece in pieces]
    outs = pl.pallas_call(
        functools.partial(assemble_kernel, splits, widths, len(deps)),
        in_specs=[pl.BlockSpec(memory_space=pltpu.SMEM)] + [pl.BlockSpec(memory_space=pl.ANY)] * (len(flat) + len(deps)),
        out_specs=[pl.BlockSpec(memory_space=pl.ANY)] * len(widths),
        out_shape=[jax.ShapeDtypeStruct((depth, size, count, rows, width), BF16) for count, width in widths],
        scratch_shapes=[
            pltpu.VMEM((depth, size, rows, sum(count * width for count, width in widths)), BF16),
            pltpu.SemaphoreType.DMA((len(flat),)),
            pltpu.SemaphoreType.DMA((sum(count for count, _ in widths),)),
        ],
        compiler_params=pltpu.CompilerParams(vmem_limit_bytes=VMEM_LIMIT),
        name="assemble",
    )(me.astype(jnp.int32).reshape(1), *flat, *deps)
    return [out.reshape(-1, out.shape[-1]) for out in outs]


def turn_kernel(
    waits, own, other, from_x, from_y, hidden, gates, first_gu, router, gain, grad_out, second_o, out_w, first_o, *rest
):
    grad_mid_out, grad_mid_b_out, glow_out, glow_sgu, low_sdown, grad_attn, units_out = rest[waits:]
    rows, model = hidden.shape
    experts = gates.shape[1]
    rank = ADAPTER_RANK
    total = own[...].astype(F32) + other[...].astype(F32) + from_x[...].astype(F32) + from_y[...].astype(F32)
    units_out[...] = total[rows:, :]
    tail = total[:rows, model:]
    grad_gates = tail[:, :experts] + tail[:, experts : 2 * experts]
    glow = tail[:, 3 * experts : 3 * experts + 2 * rank].astype(BF16)
    glow_sgu[...] = glow
    low_sdown[...] = tail[:, 3 * experts + 2 * rank : 3 * experts + 3 * rank].astype(BF16)
    gate = gates[...]
    grad_logits = gate * (grad_gates - jnp.sum(gate * grad_gates, axis=-1, keepdims=True))
    logits_hi = grad_logits.astype(BF16)
    left = grad_logits - logits_hi.astype(F32)
    logits_mid = left.astype(BF16)
    logits_lo = (left - logits_mid.astype(F32)).astype(BF16)
    grad_normed = total[:rows, :model] + dot_nt(glow, first_gu[...])
    for part in (logits_hi, logits_mid, logits_lo):
        grad_normed = grad_normed + dot_nt(part, router[...])
    values = hidden[...]
    scale = lax.rsqrt(jnp.mean(values * values, axis=-1, keepdims=True) + EPSILON)
    scaled = grad_normed * gain[...]
    mean = jnp.mean(values * scaled, axis=-1, keepdims=True)
    grad_mid = grad_out[...].astype(F32) + scale * scaled - values * (scale * scale * scale * mean)
    grad_mid_out[...] = grad_mid
    grad_mid_b = grad_mid.astype(BF16)
    grad_mid_b_out[...] = grad_mid_b
    glow = dot_nt(grad_mid_b, second_o[...]).astype(BF16)
    glow_out[...] = glow
    grad_attn[...] = (dot_nt(grad_mid_b, out_w[...]) + dot_nt(glow, first_o[...])).astype(BF16)


def turn(args, deps):
    rows, model = args[4].shape
    rank = ADAPTER_RANK
    vmem = pl.BlockSpec(memory_space=pltpu.VMEM)
    shapes = [
        ((rows, model), F32),
        ((rows, model), BF16),
        ((rows, rank), BF16),
        ((rows, 2 * rank), BF16),
        ((rows, rank), BF16),
        ((rows, HEADS * HEAD_DIM), BF16),
        ((BACK_ROWS, args[0].shape[1]), F32),
    ]
    return pl.pallas_call(
        functools.partial(turn_kernel, len(deps)),
        in_specs=[vmem] * len(args) + [pl.BlockSpec(memory_space=pl.ANY)] * len(deps),
        out_specs=[vmem] * len(shapes),
        out_shape=[jax.ShapeDtypeStruct(shape, dtype) for shape, dtype in shapes],
        compiler_params=pltpu.CompilerParams(vmem_limit_bytes=VMEM_LIMIT),
        cost_estimate=cost(4.0),
        name="turn",
    )(*args, *deps)


def query_back_kernel(waits, grad_q, normed, low_q, q_w, first_q, second_q, *rest):
    grad_normed, first_query, second_query = rest[waits:]
    glow_q = dot_nt(grad_q[...], second_q[...]).astype(BF16)
    grad_normed[...] = dot_nt(grad_q[...], q_w[...]) + dot_nt(glow_q, first_q[...])
    first_query[...] = dot_tn(normed[...], glow_q)
    second_query[...] = dot_tn(low_q[...], grad_q[...])


def query_back(args, deps):
    rows, model = args[1].shape
    vmem = pl.BlockSpec(memory_space=pltpu.VMEM)
    shapes = [(rows, model), (model, ADAPTER_RANK), (ADAPTER_RANK, HEADS * HEAD_DIM)]
    return pl.pallas_call(
        functools.partial(query_back_kernel, len(deps)),
        in_specs=[vmem] * len(args) + [pl.BlockSpec(memory_space=pl.ANY)] * len(deps),
        out_specs=[vmem] * len(shapes),
        out_shape=[jax.ShapeDtypeStruct(shape, F32) for shape in shapes],
        compiler_params=pltpu.CompilerParams(vmem_limit_bytes=VMEM_LIMIT),
        cost_estimate=cost(0.1),
        name="query_back",
    )(*args, *deps)


def middle_kernel(waits, attn, glow_out, normed2, glow_sgu, grad_mid, out_low, grad_out, low_sdown, *rest):
    first_early, second_out, second_down = rest[waits:]
    rank = ADAPTER_RANK
    first_early[:, :rank] = dot_tn(attn[...], glow_out[...])
    first_early[:, rank:] = dot_tn(normed2[...], glow_sgu[...])
    second_out[...] = dot_tn(out_low[...], grad_mid[...])
    second_down[...] = dot_tn(low_sdown[...], grad_out[...])


def middle(args, deps):
    model = args[0].shape[1]
    rank = ADAPTER_RANK
    vmem = pl.BlockSpec(memory_space=pltpu.VMEM)
    shapes = [(model, 3 * rank), (rank, model), (rank, model)]
    return pl.pallas_call(
        functools.partial(middle_kernel, len(deps)),
        in_specs=[vmem] * len(args) + [pl.BlockSpec(memory_space=pl.ANY)] * len(deps),
        out_specs=[vmem] * len(shapes),
        out_shape=[jax.ShapeDtypeStruct(shape, F32) for shape in shapes],
        compiler_params=pltpu.CompilerParams(vmem_limit_bytes=VMEM_LIMIT),
        cost_estimate=cost(0.1),
        name="middle",
    )(*args, *deps)


def last_kernel(
    owners, grad_kv, normed, low_kv, kv_w, first_kv, second_k, second_v, hidden, gain, grad_mid, grad_normed_q,
    first_query, first_early, second_query, second_early, adapter, grad_hidden, first_out, second_out
):
    rank = ADAPTER_RANK
    heads = range(grad_kv.shape[1] // (2 * HEAD_DIM))
    grad_k = jnp.concatenate([grad_kv[:, 2 * n * HEAD_DIM : (2 * n + 1) * HEAD_DIM] for n in heads], axis=1)
    grad_v = jnp.concatenate([grad_kv[:, (2 * n + 1) * HEAD_DIM : (2 * n + 2) * HEAD_DIM] for n in heads], axis=1)
    width = grad_k.shape[1]
    glow_k = dot_nt(grad_k, second_k[...]).astype(BF16)
    glow_v = dot_nt(grad_v, second_v[...]).astype(BF16)
    grad_normed = grad_normed_q[...] + dot_nt(grad_k, kv_w[:, :width]) + dot_nt(grad_v, kv_w[:, width:])
    grad_normed = grad_normed + dot_nt(glow_k, first_kv[:, :rank]) + dot_nt(glow_v, first_kv[:, rank:])
    values = hidden[...].astype(F32)
    scale = lax.rsqrt(jnp.mean(values * values, axis=-1, keepdims=True) + EPSILON)
    scaled = grad_normed * gain[...]
    mean = jnp.mean(values * scaled, axis=-1, keepdims=True)
    grad_hidden[...] = grad_mid[...] + scale * scaled - values * (scale * scale * scale * mean)
    firsts = [first_query[...], dot_tn(normed[...], glow_k), dot_tn(normed[...], glow_v), first_early[...]]
    tags = jnp.broadcast_to(adapter[...], (first_query.shape[0], LANES - 6 * rank))
    first_out[...] = jnp.concatenate(firsts + [tags], axis=1).astype(BF16)
    seconds = [second_query[...], dot_tn(low_kv[:, :rank], grad_k), dot_tn(low_kv[:, rank:], grad_v), second_early[...]]
    seconds = jnp.concatenate(seconds, axis=1)
    columns = seconds.shape[1] // owners
    padding = jnp.zeros((rank, second_out.shape[1] // rank * LANES - columns), F32)
    for n in range(owners):
        piece = jnp.concatenate([seconds[:, n * columns : (n + 1) * columns], padding], axis=1).astype(BF16)
        for c in range(piece.shape[1] // LANES):
            second_out[n, c * rank : (c + 1) * rank, :] = piece[:, c * LANES : (c + 1) * LANES]


def last(owners, args):
    rows, model = args[7].shape
    columns = (args[13].shape[1] + 2 * KV_HEADS * HEAD_DIM + args[14].shape[1]) // owners
    vmem = pl.BlockSpec(memory_space=pltpu.VMEM)
    return pl.pallas_call(
        functools.partial(last_kernel, owners),
        in_specs=[vmem] * len(args),
        out_specs=[vmem] * 3,
        out_shape=[
            jax.ShapeDtypeStruct((rows, model), F32),
            jax.ShapeDtypeStruct((model, LANES), BF16),
            jax.ShapeDtypeStruct((owners, -(-columns // LANES) * ADAPTER_RANK, LANES), BF16),
        ],
        compiler_params=pltpu.CompilerParams(vmem_limit_bytes=VMEM_LIMIT),
        cost_estimate=cost(2.0),
        name="last",
    )(*args)


def spread_kernel(depth, lines, flat, first_out, second_out):
    rank = ADAPTER_RANK
    size = flat.shape[0] // depth
    row = lax.broadcasted_iota(jnp.int32, (LANES, 1), 0).astype(F32)
    column = lax.broadcasted_iota(jnp.int32, (1, first_out.shape[1]), 1)
    inside = column % LANES
    target = (column // LANES * rank + inside).astype(F32)
    owner = (inside // rank).astype(F32)
    short = lax.broadcasted_iota(jnp.int32, (1, rank), 1).astype(F32)
    chunks = (flat.shape[1] - lines) // rank
    first, second = None, [None] * chunks
    for d in range(size):
        adapter = flat[d, 0:1, 6 * rank : 6 * rank + 1].astype(F32)
        total = flat[d].astype(F32)
        for z in range(1, depth):
            total = total + flat[z * size + d].astype(F32)
        total = total.astype(BF16)
        place = ((target - adapter * float(rank) == row) & (owner == adapter)).astype(F32).astype(BF16)
        lift = (row - adapter * float(rank) == short).astype(F32).astype(BF16)
        part = dot_nn(total[:lines], place)
        first = part if first is None else first + part
        for c in range(chunks):
            part = dot_nn(lift, total[lines + c * rank : lines + (c + 1) * rank])
            second[c] = part if second[c] is None else second[c] + part
    first_out[...] = first
    for c in range(chunks):
        second_out[:, c * LANES : (c + 1) * LANES] = second[c]


def spread(flat, depth, lines):
    vmem = pl.BlockSpec(memory_space=pltpu.VMEM)
    chunks = (flat.shape[1] - lines) // ADAPTER_RANK
    return pl.pallas_call(
        functools.partial(spread_kernel, depth, lines),
        in_specs=[vmem],
        out_specs=[vmem] * 2,
        out_shape=[jax.ShapeDtypeStruct((lines, 6 * LANES), F32), jax.ShapeDtypeStruct((LANES, chunks * LANES), F32)],
        compiler_params=pltpu.CompilerParams(vmem_limit_bytes=VMEM_LIMIT),
        cost_estimate=cost(2.0),
        name="spread",
    )(flat)


def per_device(
    depth,
    size,
    block_input,
    document_number,
    key_present,
    routes,
    sequence_adapter,
    output_gradient,
    norm_scale_pair,
    query_key_value_weight,
    attention_output_weight,
    router_weight,
    shared_gate_up_weight,
    shared_down_weight,
    routed_gate_up_weight,
    routed_down_weight,
    dense_first_factor,
    shared_down_first_factor,
    dense_second_factor,
    routed_first_factor,
    routed_down_first_factor,
    routed_second_factor,
):
    _, rows, model = block_input.shape
    topk = routes.shape[2]
    me = lax.axis_index("dp")
    experts = router_weight.shape[1]
    local_experts = routed_gate_up_weight.shape[0]
    shard_rows = query_key_value_weight.shape[0]
    shared_rows = shared_down_weight.shape[0]
    rank_all = dense_second_factor.shape[0]
    second_columns = dense_second_factor.shape[1]
    capacity = 4 * topk * rows // (3 * experts)
    query_width = HEADS * HEAD_DIM
    kv_width = KV_HEADS * HEAD_DIM
    hops = min(depth - 1, -(-(DOCUMENT_SPAN - 1) // rows))
    rank = ADAPTER_RANK
    units = SHARED_HIDDEN // size
    adapter = sequence_adapter[0]
    forward = [(i, i + 1) for i in range(depth - 1)]
    backward = [(i + 1, i) for i in range(depth - 1)]

    def over_seq(shard):
        return lax.all_gather(shard, "seq", axis=0)

    first_shard = dense_first_factor.reshape(shard_rows, 6 * rank_all)
    second_width = second_columns * rank_all // shard_rows
    groups = second_width // rank_all
    pack_kv = jnp.concatenate(
        [
            query_key_value_weight[:, query_width:],
            first_shard[:, rank_all : 3 * rank_all],
            dense_second_factor.T.reshape(groups, shard_rows, rank_all).transpose(1, 0, 2).reshape(shard_rows, -1),
            jnp.pad(
                jnp.concatenate([router_weight, norm_scale_pair.T], axis=1), ((0, 0), (0, LANES - experts - 2))
            ),
        ],
        axis=1,
    )
    pack_q = jnp.concatenate(
        [
            query_key_value_weight[:, :query_width],
            first_shard[:, :rank_all],
            first_shard[:, 3 * rank_all :],
            attention_output_weight,
        ],
        axis=1,
    )
    seq_kv = over_seq(pack_kv)
    seq_q = over_seq(tie(pack_q, seq_kv))

    flags = jnp.sum((routes[0][..., None] == jnp.arange(experts, dtype=jnp.int32)).astype(F32), axis=1)
    before = (jnp.arange(rows)[:, None] > jnp.arange(rows)[None, :]).astype(BF16)
    slots = jnp.where(flags > 0, dot_nn(before, flags.astype(BF16)), -1.0).astype(BF16)

    def own_columns(matrix):
        return lax.dynamic_slice_in_dim(matrix, adapter * rank, rank, 1)

    def own_factors(matrix):
        count = matrix.shape[1] // rank_all
        return jnp.concatenate([own_columns(matrix[:, n * rank_all : (n + 1) * rank_all]) for n in range(count)], axis=1)

    grad_out_b = output_gradient[0]
    grads_x, grads_y = swap(grad_out_b, 2, size), swap(grad_out_b, 4, size)
    gate_up = shared_gate_up_weight.reshape(shard_rows, 2, depth, size, units // depth)
    gate_up = gate_up.transpose(3, 0, 1, 2, 4).reshape(size, shard_rows, 2 * units)
    gate_up = lax.all_to_all(gate_up, "dp", split_axis=0, concat_axis=0, tiled=True)
    kv_gathered = plane_gather(tie(seq_kv, grads_x, grads_y, gate_up), size)
    grads_x, grads_y = tie_all([grads_x, grads_y], *kv_gathered[6])
    far_grads = (swap(grads_y[: rows // 2], 2, size), swap(grads_x[rows // 2 :], 4, size))
    grad_blocks = [(grad_out_b,), None, (grads_x,), None, (grads_y,), None, far_grads, None]
    kv_w, kv_first, second_t, small = assemble(
        kv_gathered, ((1, 2 * kv_width), (1, 2 * rank_all), (groups, rank_all), (1, LANES)), me
    )
    router_w = small[:, :experts]
    gains = small[:, experts : experts + 2].astype(F32).T
    second = own_columns(second_t).T
    first_kv = own_factors(kv_first)
    widths = [query_width, kv_width, kv_width, model, SHARED_HIDDEN, SHARED_HIDDEN, model]
    edges = [sum(widths[:n]) for n in range(len(widths) + 1)]
    b_parts = [second[:, edges[n] : edges[n + 1]] for n in range(len(widths))]

    down_rows = routed_down_weight.shape[1]
    second_cut = rank_all * routed_second_factor.shape[2] // down_rows
    up_shards, down_shards = [], []
    for j in range(local_experts):
        up_parts = [
            routed_gate_up_weight[j].reshape(-1, 2 * EXPERT_HIDDEN),
            routed_first_factor[j].reshape(-1, 2 * rank_all),
        ]
        down_parts = [
            routed_down_weight[j],
            routed_down_first_factor[j],
            routed_second_factor[j].reshape(down_rows, -1),
        ]
        if j == 0:
            up_parts.append(gate_up.reshape(size * shard_rows, 2 * units))
            shared_down = jnp.concatenate([shared_down_weight, shared_down_first_factor], axis=1)
            shared_down = jnp.pad(shared_down, ((0, 0), (0, 16 * LANES - shared_down.shape[1])))
            shared_down = shared_down.reshape(shared_rows, 4, 4 * LANES).transpose(1, 0, 2)
            down_parts.append(shared_down.reshape(down_rows, -1))
        up_shards.append(jnp.concatenate(up_parts, axis=1))
        down_shards.append(jnp.concatenate(down_parts, axis=1))
    first_down = over_seq(tie(down_shards[0], seq_kv))

    x_flat = block_input[0].astype(F32)
    normed = rms_norm(x_flat, gains[0]).astype(BF16)
    select = (jnp.arange(rank_all, dtype=jnp.int32) // rank == adapter).astype(F32)[None, :]

    def masked_low(inputs, factors):
        low = dot_nn(inputs, factors)
        return [
            (low[:, at : at + rank_all] * select).astype(BF16) for at in range(0, factors.shape[1], rank_all)
        ]

    low_k, low_v = masked_low(normed, kv_first)
    low_kv = own_factors(jnp.concatenate([low_k, low_v], axis=1))
    kv_extra = jnp.concatenate(
        [dot_nt(low_k, second_t[edges[1] : edges[2]]), dot_nt(low_v, second_t[edges[2] : edges[3]])], axis=1
    )
    present_tag = jnp.where(key_present == 1, document_number + 1, 0).astype(BF16)
    tag_rows = jnp.broadcast_to(jnp.pad(present_tag, ((0, 0), (0, 2 * kv_width - rows))), (16, 2 * kv_width))
    kv_blocks = [jnp.concatenate([(dot_nn(normed, kv_w) + kv_extra).astype(BF16), tag_rows], axis=0)]
    q_blocks = plane_gather(tie(seq_q, *far_grads), size)
    for k in range(1, size, 2):
        grad_blocks[k] = tuple(swap(piece, 1, size) for piece in grad_blocks[k - 1])
    for h in range(hops):
        block = kv_blocks[-1] if h == 0 else tie(kv_blocks[-1], q_blocks[2][0], q_blocks[4][0], first_down)
        kv_blocks.append(lax.ppermute(block, "seq", forward))
        kv_blocks[h] = block
    kv_all = jnp.concatenate([block[:rows] for block in kv_blocks[::-1]], axis=0)
    key_tag = jnp.concatenate([block[rows, :rows] for block in kv_blocks[::-1]]).astype(F32).reshape(-1, 1)
    query_tag = (document_number + 1).astype(F32)

    seq_up, seq_down = [over_seq(tie(up_shards[0], kv_blocks[min(1, hops)]))], [first_down]
    for j in range(1, local_experts):
        seq_up.append(over_seq(tie(up_shards[j], seq_down[j - 1])))
        seq_down.append(over_seq(tie(down_shards[j], seq_up[j - 1])))

    q_w, q_first, out_w = assemble(q_blocks, ((1, query_width), (1, 4 * rank_all), (1, model)), me)
    (low_q,) = masked_low(normed, q_first[:, :rank_all])
    first_out = q_first[:, rank_all : 2 * rank_all]
    q_first = own_factors(q_first)
    first_q, first_o, first_gu = q_first[:, :rank], q_first[:, rank : 2 * rank], q_first[:, 2 * rank :]
    query = (dot_nn(normed, q_w) + dot_nt(low_q, second_t[edges[0] : edges[1]])).astype(BF16)
    low_q = own_columns(low_q)
    glow_sdown = dot_nt(grad_out_b, b_parts[6]).astype(BF16)
    attn, lse = attend(query, kv_all, query_tag, key_tag, hops, (*grad_blocks[3], *grad_blocks[5], *grad_blocks[7]))
    (out_low,) = masked_low(attn, first_out)
    mid = x_flat + dot_nn(attn, out_w) + dot_nt(out_low, second_t[edges[3] : edges[4]])
    out_low = own_columns(out_low)
    normed2 = rms_norm(mid, gains[1]).astype(BF16)

    logits = dot_nn(normed2, router_w)
    top = jnp.max(jnp.where(flags > 0, logits, -jnp.inf), axis=-1, keepdims=True)
    weights = jnp.where(flags > 0, jnp.exp(logits - top), 0.0)
    gates = weights / jnp.sum(weights, axis=-1, keepdims=True)
    gates_hi = gates.astype(BF16)
    gates_lo = (gates - gates_hi.astype(F32)).astype(BF16)
    shared_low = dot_nn(normed2, first_gu).astype(BF16)
    own_adapter = jnp.full((rows, LANES - 3 * experts - 3 * rank), adapter.astype(F32)).astype(BF16)
    payload = jnp.concatenate([normed2, slots, gates_hi, gates_lo, shared_low, glow_sdown, own_adapter], axis=1)
    token_blocks = [None] * size
    token_blocks[0], token_blocks[1] = (payload,), (swap(payload, 1, size),)
    tokens_x, tokens_y = swap(payload, 2, size), swap(payload, 4, size)

    def gather_far(tokens_x, tokens_y, *done):
        tokens_x, tokens_y = tie_all([tokens_x, tokens_y], *done)
        half = rows // 2
        token_blocks[2], token_blocks[3] = (tokens_x,), (swap(tokens_x, 1, size),)
        token_blocks[4], token_blocks[5] = (tokens_y,), (swap(tokens_y, 1, size),)
        return swap(tokens_y[:half], 2, size), swap(tokens_x[half:], 4, size)

    def gather_farthest(far, *done):
        far = tuple(tie_all(far, *done))
        token_blocks[6], token_blocks[7] = far, tuple(swap(piece, 1, size) for piece in far)


    moe_parts, back_parts, grad_sums = [None] * size, [None] * size, []
    wide = model + rank_all

    direct = down_rows == rank_all
    shapes = [None] * local_experts

    def weights_of(j):
        args = [seq_up[j].reshape(model, -1)]
        shapes[j] = [args[0].shape, (EXPERT_HIDDEN, wide), (rank_all, depth * second_cut * down_rows // rank_all)]
        if direct:
            args.append(seq_down[j])
        else:
            second_j = seq_down[j][:, :, wide : wide + second_cut]
            second_j = second_j.reshape(depth, rank_all, -1).transpose(1, 0, 2).reshape(rank_all, -1)
            args += [seq_down[j][:, :, :wide].reshape(EXPERT_HIDDEN, wide), second_j]
        if j == 0:
            if not direct:
                parts = seq_down[j][:, :, wide + second_cut :].reshape(depth, 4, shared_rows, 4 * LANES)
                args.append(parts.transpose(0, 2, 1, 3).reshape(units, -1)[:, :wide])
            slices = [
                lax.dynamic_slice_in_dim(second_t[edges[n] : edges[n + 1]].reshape(depth, size, -1, rank_all), me, 1, 1)
                for n in (4, 5)
            ]
            args.append(jnp.concatenate([part.reshape(units, rank_all) for part in slices], axis=0))
            shapes[j] += [(units, wide), args[-1].shape]
        return args

    def run_expert(j, args, group, prior, deps, packed=False):
        meta = jnp.stack([me * local_experts + j, me]).astype(jnp.int32)
        prior = ([moe_parts[k] for k in group], [back_parts[k] for k in group]) if prior else None
        moe_out, back_out, grads = expert_call(
            meta,
            args,
            shapes[j],
            [token_blocks[k] for k in group],
            [grad_blocks[k] for k in group],
            prior,
            grad_sums[-1],
            packed,
            experts,
            capacity,
            depth,
            deps,
        )
        for n, k in enumerate(group):
            moe_parts[k], back_parts[k] = moe_out[n], back_out[n]
        grad_sums[-1] = list(grads)

    for j in range(local_experts - 1):
        grad_sums.append([])
        args = weights_of(j)
        previous = ()
        for group in ((0, 1), (2, 3), (4, 5), (6, 7)):
            run_expert(j, args, group, j > 0, previous, group == (6, 7))
            previous = (back_parts[group[0]],)
            if j == 0 and group == (0, 1):
                far = gather_far(tokens_x, tokens_y, *previous)
            if j == 0 and group == (2, 3):
                gather_farthest(far, *previous)
    if local_experts == 1:
        gather_farthest(gather_far(tokens_x, tokens_y))

    def scatter(packed):
        return lax.psum_scatter(packed, "seq", scatter_dimension=0, tiled=True)

    packed_sums = [scatter(grads[0]) for grads in grad_sums]
    grad_sums.append([])
    j, prior, half = local_experts - 1, local_experts > 1, (rows + BACK_ROWS) // 2
    args = weights_of(j)
    run_expert(j, args, (6, 7), prior, (back_parts[6],) if prior else ())
    pair_six = add(back_parts[6], swap(back_parts[7], 1, size))
    run_expert(j, args, (2, 3), prior, (back_parts[6],))
    from_diagonal_x, from_diagonal_y = swap(pair_six[:half], 2, size), swap(pair_six[half:], 4, size)
    pair_two = add(back_parts[2], swap(back_parts[3], 1, size))
    run_expert(j, args, (4, 5), prior, (back_parts[2], pair_six))
    pair_four = add(back_parts[4], swap(tie(back_parts[5], from_diagonal_x, from_diagonal_y, *packed_sums), 1, size))
    to_x = jnp.concatenate([pair_two[:half], add(pair_two[half:], from_diagonal_y)], axis=0)
    to_y = jnp.concatenate([add(pair_four[:half], from_diagonal_x), pair_four[half:]], axis=0)
    run_expert(j, args, (0, 1), prior, (to_x, to_y), True)
    packed_sums.append(scatter(grad_sums[-1][0]))
    from_x, from_y = swap(to_x, 2, size), swap(to_y, 4, size)
    grad_mid, grad_mid_b, glow_out, glow_sgu, low_sdown, grad_attn, shared_units = turn(
        [back_parts[0], swap(back_parts[1], 1, size), from_x, from_y, mid, gates, first_gu]
        + [router_w, gains[1:2], grad_out_b, b_parts[3], out_w, first_o],
        (swap(tie(gates_lo[:16], from_x, from_y), 1, size),),
    )

    half = rows // 2
    far_parts = dict(zip((6, 2, 4, 0), tie_all([moe_parts[k + 1] for k in (6, 2, 4, 0)], from_x, from_y)))
    pair = {k: add(moe_parts[k], swap(far_parts[k], 1, size)) for k in (6, 2, 4, 0)}
    moe_to_x = jnp.concatenate([pair[2][:half], add(pair[2][half:], swap(pair[6][half:], 4, size))], axis=0)
    moe_to_y = jnp.concatenate([add(pair[4][:half], swap(pair[6][:half], 2, size)), pair[4][half:]], axis=0)
    moe_from_x, moe_from_y = swap(moe_to_x, 2, size), swap(moe_to_y, 4, size)
    moe = pair[0].astype(F32) + moe_from_x.astype(F32) + moe_from_y.astype(F32)

    def shared_columns(block):
        block = block[:, :SHARED_HIDDEN].reshape(rank, size, depth, units // depth)
        return block.transpose(0, 2, 1, 3).reshape(rank, SHARED_HIDDEN)

    grad_q, grad_kv = attend_back(
        query, kv_all, grad_attn, lse, query_tag, key_tag, hops, 0, KV_HEADS, (pair[6], pair[2], pair[4])
    )
    moving, early_received = grad_kv[:rows], grad_q
    for h in range(hops):
        if h == 1:
            moving = tie(moving, moe_to_x, moe_to_y)
        received = lax.ppermute(moving, "seq", backward)
        moving = add(grad_kv[(h + 1) * rows : (h + 2) * rows], received)
        if h == 0:
            early_received = received
    grad_normed_q, first_query, second_query = query_back(
        [grad_q, normed, low_q, q_w, first_q, b_parts[0]], (early_received,)
    )
    first_early, second_out, second_down = middle(
        [attn, glow_out, normed2, glow_sgu, grad_mid_b, out_low, grad_out_b, low_sdown],
        (early_received,),
    )
    packed_sums = tie_all(packed_sums, early_received)
    owner_rows = model // depth
    firsts, downs, seconds = [], [], []
    for packed in packed_sums:
        packed = packed[0].astype(F32)
        firsts.append(jnp.stack([packed[:owner_rows], packed[owner_rows : 2 * owner_rows]], axis=1))
        at = 2 * owner_rows + down_rows
        downs.append(packed[2 * owner_rows : at])
        seconds.append(packed[at : at + routed_second_factor.shape[2]].T)
    at += routed_second_factor.shape[2]
    grad_expert_a, grad_expert_a_down, grad_expert_b = jnp.stack(firsts), jnp.stack(downs), jnp.stack(seconds)
    grad_first_down = packed_sums[0][0, at : at + shared_rows].astype(F32)

    hidden_out = (mid + moe + dot_nn(low_sdown, b_parts[6])).astype(BF16)[None]
    second_early = jnp.concatenate(
        [second_out, shared_columns(shared_units[:rank]), shared_columns(shared_units[rank:]), second_down], axis=1
    )
    grad_hidden, first_flat, second_flat = last(
        depth * size,
        [moving, normed, low_kv, kv_w, first_kv, b_parts[1], b_parts[2], block_input[0], gains[0:1], grad_mid]
        + [grad_normed_q, first_query, first_early, second_query, second_early, adapter.astype(F32).reshape(1, 1)],
    )
    flat = jnp.concatenate([first_flat.reshape(depth * size, shard_rows, LANES), second_flat], axis=1)
    flat = lax.all_to_all(flat, ("seq", "dp"), split_axis=0, concat_axis=0, tiled=True)
    grad_first, grad_second = spread(flat, depth, shard_rows)
    grad_first = grad_first.reshape(shard_rows, 6, rank_all)
    grad_second = grad_second[:, :second_columns]
    grad_hidden = grad_hidden[None]
    return (
        hidden_out,
        grad_hidden,
        grad_first,
        grad_first_down,
        grad_second,
        grad_expert_a,
        grad_expert_a_down,
        grad_expert_b,
    )


def solution(mesh):
    in_specs = (
        P("dp", "seq", None),
        P("dp", "seq"),
        P("dp", "seq"),
        P("dp", "seq", None),
        P("dp"),
        P("dp", "seq", None),
        P(None, ("seq", "dp")),
        P(("seq", "dp"), None),
        P(("seq", "dp"), None),
        P(("seq", "dp"), None),
        P(("seq", "dp"), None, None),
        P(("seq", "dp"), None),
        P("dp", "seq", None, None),
        P("dp", "seq", None),
        P(("seq", "dp"), None, None),
        P(("seq", "dp"), None),
        P(None, ("seq", "dp")),
        P("dp", "seq", None, None),
        P("dp", "seq", None),
        P("dp", None, "seq"),
    )
    out_specs = (
        P("dp", "seq", None),
        P("dp", "seq", None),
        P(("seq", "dp"), None, None),
        P(("seq", "dp"), None),
        P(None, ("seq", "dp")),
        P("dp", "seq", None, None),
        P("dp", "seq", None),
        P("dp", None, "seq"),
    )
    return jax.shard_map(
        functools.partial(per_device, mesh.shape["seq"], mesh.shape["dp"]),
        mesh=mesh,
        in_specs=in_specs,
        out_specs=out_specs,
        check_vma=False,
    )
```
